32 devices in a mesh: seq: 8 (over z, y), head: 4 (over x, core).
Axes of the slice: x: 2, y: 2, z: 4, core: 2. Of those that a mesh axis runs over, the one named last changes fastest.
Arguments:
- queries: bfloat16 [1, 4096, 1024], P(None, 'seq', 'head'), may hold values from -40 to 40
- key_vectors: bfloat16 [1, 4096, 1024], P(None, 'seq', 'head'), may hold values from -40 to 40
- value_vectors: bfloat16 [1, 4096, 1024], P(None, 'seq', 'head'), may hold values from -6 to 6
- out_weight: bfloat16 [1024, 1024], replicated, may hold values from -0.1875 to 0.1875
Outputs:
- layer_output: bfloat16 [1, 4096, 1024], P(None, ('seq', 'head'))
The draws below stay inside these ranges and needn't reach their ends.
All inputs are finite; a program needn't handle non-finite values.
Results may differ from the reference program's by a relative error of at most 0.038.
Values may be sent and summed in bfloat16 or wider, within the bound.
No kernel may reach another device: no remote copies, remote signals or barrier semaphores. Data moves between devices by JAX's collectives and lax.ppermute only.
A program may use at most 192 MiB of HBM per device.

```python
import jax
import jax.numpy as jnp
from jax import lax

HEADS = 16
HD = 64
WIDTH = 1024
BLOCK = 128
LEVELS = 4
BATCH = 1
LENGTH = 4096


def draw_queries(key, part):
    key = jax.random.fold_in(key, 11)
    base = 1.4 * jax.random.truncated_normal(key, -6.0, 6.0, (BATCH, LENGTH, WIDTH), jnp.float32)
    return base.astype(jnp.bfloat16)


def draw_key_vectors(key, part):
    key = jax.random.fold_in(key, 12)
    base = 1.4 * jax.random.truncated_normal(key, -6.0, 6.0, (BATCH, LENGTH, WIDTH), jnp.float32)
    return base.astype(jnp.bfloat16)


def block_scale(rng, shape, cuts, low, high):
    def one(axis_at, parts):
        steps = jax.random.uniform(jax.random.fold_in(jax.random.fold_in(rng, 6), axis_at), (parts,), jnp.float32, low / len(cuts), high / len(cuts))
        return jnp.repeat(jnp.exp(steps), shape[axis_at] // parts).reshape((-1,) + (1,) * (len(shape) - axis_at - 1))

    gain = one(*cuts[0])
    for cut in cuts[1:]:
        gain = gain * one(*cut)
    return gain


def scatter_about(own_key, extent, width, most, pieces=(), held_as=jnp.bfloat16):
    gain = block_scale(own_key, extent, pieces, -0.22, 0.18) if pieces else 1.0
    entries = jax.random.normal(own_key, extent, jnp.float32) * width * gain
    return jnp.minimum(jnp.maximum(entries, -most), most).astype(held_as)


def setup_inputs(seed: int = 0) -> dict:
    key_of = jax.random.split(jax.random.key(seed), 5)
    queries = draw_queries(jax.random.fold_in(key_of[4], 71), 0)
    key_vectors = draw_key_vectors(jax.random.fold_in(key_of[4], 71), 0)
    value_vectors = scatter_about(key_of[2], (BATCH, LENGTH, WIDTH), 1.0, 6.0, ((1, 8), (2, 4)))
    out_weight = scatter_about(key_of[3], (WIDTH, WIDTH), WIDTH ** -0.5, 0.1875)
    return dict(queries=queries, key_vectors=key_vectors, value_vectors=value_vectors, out_weight=out_weight)


neg_fill = -1.0e30
root_half = 0.7071067811865476


def pooled(field):
    return ((field[0::2].astype(jnp.float32) + field[1::2].astype(jnp.float32)) * root_half).astype(jnp.bfloat16)


def attend(query_blocks, key_blocks, value_blocks, allowed):
    scaling = HD ** -0.5
    scores = jnp.einsum("nqd,nkd->nqk", query_blocks.astype(jnp.float32), key_blocks.astype(jnp.float32)) * scaling
    scores = jnp.where(allowed, scores, neg_fill)
    row_max = jnp.max(scores, axis=-1)
    chances = jnp.exp(scores - row_max[..., None]).astype(jnp.bfloat16)
    row_sum = jnp.sum(chances.astype(jnp.float32), axis=-1)
    numerator = jnp.einsum("nqk,nkd->nqd", chances.astype(jnp.float32), value_blocks.astype(jnp.float32))
    return row_max.reshape(-1), numerator.reshape(-1, HD), row_sum.reshape(-1)


def merged(terms, length):
    expanded = [jnp.repeat(record[1], 2 ** record[0], axis=0) for record in terms]
    top_max = expanded[0]
    for other_max in expanded[1:]:
        top_max = jnp.maximum(top_max, other_max)
    numerator = jnp.zeros((length, HD), jnp.float32)
    denominator = jnp.zeros((length,), jnp.float32)
    for record, fine_max in zip(terms, expanded):
        factor = jnp.exp(fine_max - top_max)
        numerator = numerator + jnp.repeat(record[2], 2 ** record[0], axis=0) * factor[:, None]
        denominator = denominator + jnp.repeat(record[3], 2 ** record[0], axis=0) * factor
    return (numerator / denominator[:, None]).astype(jnp.bfloat16)


def one_head(triple):
    query_rows, key_rows, value_rows = triple
    length = query_rows.shape[0]
    blocks = length // BLOCK

    def windowed(field):
        padded = jnp.pad(field, ((BLOCK, BLOCK), (0, 0)))
        return jnp.concatenate([padded[:length].reshape(blocks, BLOCK, HD), padded[BLOCK:length + BLOCK].reshape(blocks, BLOCK, HD), padded[2 * BLOCK:].reshape(blocks, BLOCK, HD)], axis=1)

    block_ids = jnp.arange(blocks)
    left_ok = jnp.broadcast_to((block_ids > 0)[:, None], (blocks, BLOCK))
    right_ok = jnp.broadcast_to((block_ids < blocks - 1)[:, None], (blocks, BLOCK))
    allowed = jnp.concatenate([left_ok, jnp.ones((blocks, BLOCK), jnp.bool_), right_ok], axis=1)[:, None, :]
    terms = [(0,) + attend(query_rows.reshape(blocks, BLOCK, HD), windowed(key_rows), windowed(value_rows), allowed)]
    level_q, level_k, level_v = query_rows, key_rows, value_rows
    for ladder in range(1, LEVELS + 1):
        level_q, level_k, level_v = pooled(level_q), pooled(level_k), pooled(level_v)
        count_now = level_q.shape[0] // BLOCK
        partner_k = level_k.reshape(count_now // 2, 2, BLOCK, HD)[:, ::-1].reshape(count_now, BLOCK, HD)
        partner_v = level_v.reshape(count_now // 2, 2, BLOCK, HD)[:, ::-1].reshape(count_now, BLOCK, HD)
        terms.append((ladder,) + attend(level_q.reshape(count_now, BLOCK, HD), partner_k, partner_v, True))
    terms.append((LEVELS,) + attend(level_q[None], level_k[None], level_v[None], True))
    return merged(terms, length)


def reference(queries, key_vectors, value_vectors, out_weight):
    samples, length, features = queries.shape

    def split_heads(field):
        return jnp.transpose(field.reshape(samples, length, HEADS, HD), (0, 2, 1, 3)).reshape(samples * HEADS, length, HD)

    attended = lax.map(one_head, (split_heads(queries), split_heads(key_vectors), split_heads(value_vectors)))
    attended = jnp.transpose(attended.reshape(samples, HEADS, length, HD), (0, 2, 1, 3)).reshape(samples * length, features)
    projected = jnp.dot(attended, out_weight, preferred_element_type=jnp.float32).astype(jnp.bfloat16)
    return projected.reshape(samples, length, features)
```

```python
import jax
import jax.numpy as jnp
from jax import lax
from jax.experimental import pallas as pl
from jax.experimental.pallas import tpu as pltpu
from jax.sharding import PartitionSpec as P

HD = 64
BLOCK = 128
LEVELS = 4
SLAB = 8
PAIR = 2 * HD

neg_fill = -1e30
root_half = 0.7071067811865476
log2_scale = HD**-0.5 * 1.4426950408889634

FAN = 2**LEVELS


def slabs_of(scratch, block):
    return [scratch[pl.ds(BLOCK * block + j, SLAB, stride=FAN), :] for j in range(FAN)]


def pooled_slabs(slabs):
    return [
        ((low + high) * root_half).astype(jnp.bfloat16).astype(jnp.float32)
        for low, high in zip(slabs[0::2], slabs[1::2])
    ]


def joined(slabs):
    return jnp.concatenate(slabs, axis=0).astype(jnp.bfloat16)


def spill(source, scratch):
    for half in range(scratch.shape[0]):
        scratch[half] = source[:, half * PAIR : (half + 1) * PAIR].astype(jnp.float32)


def pool_kernel(k_ref, v_ref, first_ref, second_ref, one_ref, three_ref, four_ref, scratch):
    rows = k_ref.shape[0]
    blocks = rows // BLOCK
    even = lax.rem(lax.axis_index("seq"), 2) == 0
    for which, ref in enumerate((k_ref, v_ref)):
        head, tail = ref[:BLOCK, :], ref[rows - BLOCK :, :]
        first_ref[2 + which] = jnp.where(even, tail, head)
        second_ref[which] = jnp.where(even, head, tail)
        spill(ref, scratch)
        for half in range(scratch.shape[0]):
            lanes = pl.ds(half * PAIR, PAIR)
            ladder = [[], [], [], [], []]
            for block in range(blocks):
                slabs = slabs_of(scratch.at[half], block)
                for level in range(1, LEVELS + 1):
                    slabs = pooled_slabs(slabs)
                    ladder[level] += slabs
            one_ref[which, :, lanes] = joined(ladder[1])
            first_ref[which, :, lanes] = joined(ladder[2])
            three_ref[which, :, lanes] = joined(ladder[3])
            four_ref[which, :, lanes] = joined(ladder[4])


def term(queries, keys, values, left_open=None, right_open=None):
    rows = queries.shape[0]
    low = lax.broadcasted_iota(jnp.int32, (rows, PAIR), 1) < HD
    zero = jnp.zeros_like(queries)
    both = jnp.concatenate([jnp.where(low, queries, zero), jnp.where(low, zero, queries)], axis=0)
    scores = log2_scale * lax.dot_general(
        both, keys, (((1,), (1,)), ((), ())), preferred_element_type=jnp.float32
    )
    if left_open is not None:
        parts = [scores[:, :BLOCK], scores[:, BLOCK : 2 * BLOCK], scores[:, 2 * BLOCK :]]
        parts[0] = jnp.where(left_open, parts[0], neg_fill)
        parts[2] = jnp.where(right_open, parts[2], neg_fill)
        scores = jnp.concatenate(parts, axis=1)
    top = jnp.max(scores, axis=1, keepdims=True)
    weights = jnp.exp2(scores - top).astype(jnp.bfloat16)
    result = jnp.dot(weights, values, preferred_element_type=jnp.float32)
    return (
        jnp.where(low, top[:rows], top[rows:]),
        jnp.where(low, result[:rows, :PAIR], result[rows:, :PAIR]),
        jnp.where(low, result[:rows, PAIR:], result[rows:, PAIR:]),
    )


def merged(fine, coarse):
    top = jnp.maximum(fine[0], coarse[0])
    keep = jnp.exp2(fine[0] - top)
    join = jnp.exp2(coarse[0] - top)
    return top, fine[1] * keep + coarse[1] * join, fine[2] * keep + coarse[2] * join


def doubled(field):
    rows, lanes = field.shape
    slabs = field.reshape(rows // SLAB, 1, SLAB, lanes)
    return jnp.broadcast_to(slabs, (rows // SLAB, 2, SLAB, lanes)).reshape(2 * rows, lanes)


def with_ones(values, weight=1.0):
    if weight != 1.0:
        values = values * jnp.bfloat16(weight)
    return jnp.concatenate([values, jnp.full(values.shape, weight, jnp.bfloat16)], axis=1)


def attend_kernel(
    q_ref, k_ref, v_ref, one_ref, first_ref, second_ref, three_a, three_b, four_ref, rest_ref,
    *tail,
):
    outs, (scratch, fine_q, padded, state) = tail[:-4], tail[-4:]
    rows = q_ref.shape[0]
    blocks = rows // BLOCK
    position = lax.axis_index("seq")
    even = lax.rem(position, 2) == 0
    left_open = position > 0
    right_open = position < lax.axis_size("seq") - 1
    own = lax.axis_index("head")

    for which, ref in enumerate((k_ref, v_ref)):
        inner, outer = first_ref[2 + which], second_ref[which]
        padded[which, :BLOCK, :] = jnp.where(even, outer, inner)
        padded[which, BLOCK : BLOCK + rows, :] = ref[...]
        padded[which, BLOCK + rows :, :] = jnp.where(even, inner, outer)

    spill(q_ref, scratch)
    pairs = scratch.shape[0]
    for pair in range(pairs):
        lanes = pl.ds(pair * PAIR, PAIR)
        ladder = [[], [], [], [], []]
        for block in range(blocks):
            slabs = slabs_of(scratch.at[pair], block)
            ladder[0] += slabs
            for level in range(1, LEVELS + 1):
                slabs = pooled_slabs(slabs)
                ladder[level] += slabs
        fine_q[:, lanes] = joined(ladder[0])
        coarse_q = [None] + [joined(ladder[level]) for level in range(1, LEVELS + 1)]

        sibling = 4 * (rows >> LEVELS)
        ours, others = four_ref[:, :, lanes], rest_ref[:, :, lanes]
        keys = jnp.concatenate([ours[0], others[0]], axis=0)
        values = jnp.concatenate(
            [with_ones(ours[1]), with_ones(others[1, :sibling], 2.0)]
            + ([with_ones(others[1, sibling:])] if others.shape[1] > sibling else []),
            axis=0,
        )
        now = term(coarse_q[4], keys, values)
        keys = jnp.concatenate([three_a[0, :, lanes], three_b[0, :, lanes]], axis=0)
        values = jnp.concatenate([three_a[1, :, lanes], three_b[1, :, lanes]], axis=0)
        now = merged(term(coarse_q[3], keys, with_ones(values)), [doubled(x) for x in now])
        now = merged(
            term(coarse_q[2], first_ref[0, :, lanes], with_ones(first_ref[1, :, lanes])),
            [doubled(x) for x in now],
        )
        up = [doubled(x) for x in now]
        for half in range(2):
            there = pl.ds((1 - half) * BLOCK, BLOCK)
            here = slice(half * BLOCK, (half + 1) * BLOCK)
            done = merged(
                term(coarse_q[1][here], one_ref[0, there, lanes], with_ones(one_ref[1, there, lanes])),
                [x[here] for x in up],
            )
            for index, field in enumerate(done):
                state[index, here, lanes] = field

    for step, out in enumerate(outs):
        block = own ^ step
        start = pl.multiple_of(block * BLOCK, BLOCK)
        half_start = pl.multiple_of(block * (BLOCK // 2), BLOCK // 2)
        left = jnp.logical_or(left_open, block > 0)
        right = jnp.logical_or(right_open, block < blocks - 1)
        for pair in range(pairs):
            lanes = pl.ds(pair * PAIR, PAIR)
            near = term(
                fine_q[pl.ds(start, BLOCK), lanes],
                padded[0, pl.ds(start, 3 * BLOCK), lanes],
                with_ones(padded[1, pl.ds(start, 3 * BLOCK), lanes]),
                left,
                right,
            )
            coarse = [doubled(state[index, pl.ds(half_start, BLOCK // 2), lanes]) for index in range(3)]
            _, numer, rowsum = merged(near, coarse)
            out[:, lanes] = (numer / rowsum).astype(jnp.bfloat16)


def project_kernel(*refs):
    parts, (weight_ref, out_ref, scratch) = refs[:-3], refs[-3:]
    own = lax.axis_index("head")
    total = None
    for step, part in enumerate(parts):
        start = pl.multiple_of((own ^ step) * part.shape[1], part.shape[1])
        product = jnp.dot(
            part[...], weight_ref[pl.ds(start, part.shape[1]), :], preferred_element_type=jnp.float32
        )
        total = product if total is None else total + product
    count = scratch.shape[0]
    for column in range(count):
        scratch[column] = total[:, column * PAIR : (column + 1) * PAIR]
    for column in range(count):
        for i in range(SLAB):
            out_ref[i * FAN : (i + 1) * FAN, column * PAIR : (column + 1) * PAIR] = scratch[
                column, pl.ds(i, FAN, stride=SLAB), :
            ].astype(jnp.bfloat16)


def swapped(block, axis, mask):
    return lax.ppermute(block, axis, [(i, i ^ mask) for i in range(lax.axis_size(axis))])


def across(block, axis):
    count = lax.axis_size(axis)
    route = []
    for low in range(1, count - 1, 2):
        route += [(low, low + 1), (low + 1, low)]
    return lax.ppermute(block, axis, route)


def per_device(queries, key_vectors, value_vectors, out_weight):
    rows, features = queries.shape[1:]
    queries, key_vectors, value_vectors = queries[0], key_vectors[0], value_vectors[0]
    pairs = features // PAIR
    seq_count, head_count = lax.axis_size("seq"), lax.axis_size("head")
    bf16 = lambda *shape: jax.ShapeDtypeStruct(shape, jnp.bfloat16)
    params = pltpu.CompilerParams(vmem_limit_bytes=32 * 1024 * 1024)

    first, second, one, three, four = pl.pallas_call(
        pool_kernel,
        out_shape=[
            bf16(4, BLOCK, features),
            bf16(2, BLOCK, features),
            bf16(2, rows // 2, features),
            bf16(2, rows // 8, features),
            bf16(2, rows // 16, features),
        ],
        scratch_shapes=[pltpu.VMEM((pairs, rows, PAIR), jnp.float32)],
        compiler_params=params,
        name="pool",
    )(key_vectors, value_vectors)

    first = swapped(first, "seq", 1)
    second = across(second, "seq")
    three_a, three_b = swapped(three, "seq", 2), swapped(three, "seq", 3)
    fours = [swapped(four, "seq", mask) for mask in range(1, 8)]
    ours = jnp.concatenate([four] + fours[:3], axis=1)
    rest = jnp.concatenate(fours[3:], axis=1)
    group = 8
    while group < seq_count:
        known = jnp.concatenate([ours, rest], axis=1)
        rest = jnp.concatenate([rest, swapped(known, "seq", group)], axis=1)
        group *= 2

    outs = pl.pallas_call(
        attend_kernel,
        out_shape=[bf16(BLOCK, features) for _ in range(head_count)],
        scratch_shapes=[
            pltpu.VMEM((pairs, rows, PAIR), jnp.float32),
            pltpu.VMEM((rows, features), jnp.bfloat16),
            pltpu.VMEM((2, rows + 2 * BLOCK, features), jnp.bfloat16),
            pltpu.VMEM((3, rows // 2, features), jnp.float32),
        ],
        compiler_params=params,
        name="attend",
    )(queries, key_vectors, value_vectors, one, first, second, three_a, three_b, ours, rest)

    parts = [part if step == 0 else swapped(part, "head", step) for step, part in enumerate(outs)]
    width = out_weight.shape[1]
    result = pl.pallas_call(
        project_kernel,
        out_shape=bf16(BLOCK, width),
        scratch_shapes=[pltpu.VMEM((width // PAIR, BLOCK, PAIR), jnp.float32)],
        compiler_params=params,
        name="project",
    )(*parts, out_weight)
    return result[None]


def solution(mesh):
    return jax.shard_map(
        per_device,
        mesh=mesh,
        in_specs=(P(None, "seq", "head"), P(None, "seq", "head"), P(None, "seq", "head"), P()),
        out_specs=P(None, ("seq", "head"), None),
        check_vma=False,
    )
```

```python
import jax
import jax.numpy as jnp
from jax import lax
from jax.experimental import pallas as pl
from jax.experimental.pallas import tpu as pltpu
from jax.sharding import PartitionSpec as P

HD = 64
BLOCK = 128
LEVELS = 4
SLAB = 8
PAIR = 2 * HD

neg_fill = -1e30
root_half = 0.7071067811865476
log2_scale = HD**-0.5 * 1.4426950408889634

FAN = 2**LEVELS


def slabs_of(scratch, block):
    return [scratch[pl.ds(BLOCK * block + j, SLAB, stride=FAN), :] for j in range(FAN)]


def pooled_slabs(slabs):
    return [
        ((low + high) * root_half).astype(jnp.bfloat16).astype(jnp.float32)
        for low, high in zip(slabs[0::2], slabs[1::2])
    ]


def joined(slabs):
    return jnp.concatenate(slabs, axis=0).astype(jnp.bfloat16)


def spill(source, scratch):
    for half in range(scratch.shape[0]):
        scratch[half] = source[:, half * PAIR : (half + 1) * PAIR].astype(jnp.float32)


def pool_kernel(
    k_hbm, v_hbm, q_hbm, k_ref, v_ref, q_ref, first_ref, second_ref, one_ref, three_ref, four_ref,
    scratch, sems,
):
    rows = k_ref.shape[0]
    blocks = rows // BLOCK
    copies = [
        pltpu.make_async_copy(source.at[0], target, sems.at[index])
        for index, (source, target) in enumerate(
            ((k_hbm, k_ref), (v_hbm, v_ref), (q_hbm, q_ref))
        )
    ]
    for copy in copies:
        copy.start()
    even = lax.rem(lax.axis_index("seq"), 2) == 0
    for which, ref in enumerate((k_ref, v_ref)):
        copies[which].wait()
        head, tail = ref[:BLOCK, :], ref[rows - BLOCK :, :]
        first_ref[2 + which] = jnp.where(even, tail, head)
        second_ref[which] = jnp.where(even, head, tail)
        spill(ref, scratch)
        for half in range(scratch.shape[0]):
            lanes = pl.ds(half * PAIR, PAIR)
            ladder = [[], [], [], [], []]
            for block in range(blocks):
                slabs = slabs_of(scratch.at[half], block)
                for level in range(1, LEVELS + 1):
                    slabs = pooled_slabs(slabs)
                    ladder[level] += slabs
            one_ref[which, :, lanes] = joined(ladder[1])
            first_ref[which, :, lanes] = joined(ladder[2])
            three_ref[which, :, lanes] = joined(ladder[3])
            four_ref[which, :, lanes] = joined(ladder[4])
    copies[2].wait()


def repooled(field):
    rows, lanes = field.shape
    slabs = field.astype(jnp.float32).reshape(rows // (2 * SLAB), 2, SLAB, lanes)
    return ((slabs[:, 0] + slabs[:, 1]) * root_half).reshape(rows // 2, lanes).astype(jnp.bfloat16)


def term(queries, keys, values, is_open=None):
    rows = queries.shape[0]
    low = lax.broadcasted_iota(jnp.int32, (rows, PAIR), 1) < HD
    zero = jnp.zeros_like(queries)
    both = jnp.concatenate([jnp.where(low, queries, zero), jnp.where(low, zero, queries)], axis=0)
    scores = log2_scale * lax.dot_general(
        both, keys, (((1,), (1,)), ((), ())), preferred_element_type=jnp.float32
    )
    if is_open is not None:
        scores = jnp.where(is_open, scores, neg_fill)
    top = jnp.max(scores, axis=1, keepdims=True)
    weights = jnp.exp2(scores - top).astype(jnp.bfloat16)
    result = jnp.dot(weights, values, preferred_element_type=jnp.float32)
    return (
        jnp.where(low, top[:rows], top[rows:]),
        jnp.where(low, result[:rows, :PAIR], result[rows:, :PAIR]),
        jnp.where(low, result[:rows, PAIR:], result[rows:, PAIR:]),
    )


def merged(fine, coarse):
    top = jnp.maximum(fine[0], coarse[0])
    keep = jnp.exp2(fine[0] - top)
    join = jnp.exp2(coarse[0] - top)
    return top, fine[1] * keep + coarse[1] * join, fine[2] * keep + coarse[2] * join


def doubled(field):
    rows, lanes = field.shape
    slabs = field.reshape(rows // SLAB, 1, SLAB, lanes)
    return jnp.broadcast_to(slabs, (rows // SLAB, 2, SLAB, lanes)).reshape(2 * rows, lanes)


def with_ones(values, weight=1.0):
    if weight != 1.0:
        values = values * jnp.bfloat16(weight)
    return jnp.concatenate([values, jnp.full(values.shape, weight, jnp.bfloat16)], axis=1)


def local_kernel(
    q_ref, k_ref, v_ref, one_ref, four_ref, w_hbm,
    edge_q, two_q, three_q, four_q, state, four_out, w_ref,
    scratch, sem,
):
    rows = q_ref.shape[0]
    blocks = rows // BLOCK
    weight_copy = pltpu.make_async_copy(w_hbm, w_ref, sem.at[0])
    weight_copy.start()
    four_out[...] = four_ref[...]
    spill(q_ref, scratch)
    for pair in range(scratch.shape[0]):
        lanes = pl.ds(pair * PAIR, PAIR)
        ladder = [[], [], [], [], []]
        for block in range(blocks):
            slabs = slabs_of(scratch.at[pair], block)
            ladder[0].append(joined(slabs))
            for level in range(1, LEVELS + 1):
                slabs = pooled_slabs(slabs)
                ladder[level] += slabs
        edge_q[0, :, lanes] = ladder[0][0]
        edge_q[1, :, lanes] = ladder[0][-1]
        two_q[:, lanes] = joined(ladder[2])
        three_q[:, lanes] = joined(ladder[3])
        four_q[:, lanes] = joined(ladder[4])
        for half in range(blocks // 2):
            there = pl.ds((half ^ 1) * BLOCK, BLOCK)
            here = BLOCK // SLAB * half
            coarse = term(
                joined(ladder[1][here : here + BLOCK // SLAB]),
                one_ref[0, there, lanes],
                with_ones(one_ref[1, there, lanes]),
            )
            up = [doubled(x) for x in coarse]
            for part in range(2):
                block = 2 * half + part
                low, high = max(block - 1, 0) * BLOCK, min(block + 2, blocks) * BLOCK
                near = term(
                    ladder[0][block], k_ref[low:high, lanes], with_ones(v_ref[low:high, lanes])
                )
                done = merged(near, [x[part * BLOCK : (part + 1) * BLOCK] for x in up])
                for index, field in enumerate(done):
                    state[index, block * BLOCK : (block + 1) * BLOCK, lanes] = field
    weight_copy.wait()


def finish_kernel(
    edge_q, two_q, three_q, four_q, state, first_ref, second_ref, three_a, three_b, four_ref, *refs
):
    others, refs = refs[:-5], refs[-5:]
    outs, attended = refs[:-1], refs[-1]
    rows = state.shape[1]
    blocks = rows // BLOCK
    position = lax.axis_index("seq")
    even = lax.rem(position, 2) == 0
    own = lax.axis_index("head")
    sides = ((0, position > 0, second_ref, first_ref), (blocks - 1, position < lax.axis_size("seq") - 1, first_ref, second_ref))

    for pair in range(two_q.shape[1] // PAIR):
        lanes = pl.ds(pair * PAIR, PAIR)
        three = [three_a[:, :, lanes], three_b[:, :, lanes]]
        ours, theirs = [], []
        for which in range(2):
            ours.append(
                [four_ref[which, :, lanes], repooled(repooled(first_ref[which, :, lanes]))]
                + [repooled(field[which]) for field in three]
            )
            theirs.append([other[which, :, lanes] for other in others])
        now = term(
            four_q[:, lanes],
            jnp.concatenate(ours[0] + theirs[0], axis=0),
            jnp.concatenate(
                [with_ones(field) for field in ours[1]]
                + [with_ones(field, 2.0) for field in theirs[1][:4]]
                + [with_ones(field) for field in theirs[1][4:]],
                axis=0,
            ),
        )
        now = merged(
            term(
                three_q[:, lanes],
                jnp.concatenate([three[0][0], three[1][0]], axis=0),
                with_ones(jnp.concatenate([three[0][1], three[1][1]], axis=0)),
            ),
            [doubled(x) for x in now],
        )
        now = merged(
            term(two_q[:, lanes], first_ref[0, :, lanes], with_ones(first_ref[1, :, lanes])),
            [doubled(x) for x in now],
        )
        for block in range(blocks):
            here = slice(block * BLOCK, (block + 1) * BLOCK)
            quarter = slice(block * BLOCK // 4, (block + 1) * BLOCK // 4)
            done = merged(
                [state[index, here, lanes] for index in range(3)],
                [doubled(doubled(x[quarter])) for x in now],
            )
            for side, (edge, is_open, if_even, if_odd) in enumerate(sides):
                if block == edge:
                    halo = [
                        jnp.where(
                            even,
                            if_even[if_even.shape[0] - 2 + which, :, lanes],
                            if_odd[if_odd.shape[0] - 2 + which, :, lanes],
                        )
                        for which in range(2)
                    ]
                    done = merged(done, term(edge_q[side, :, lanes], halo[0], with_ones(halo[1]), is_open))
            attended[block, :, lanes] = (done[1] / done[2]).astype(jnp.bfloat16)
    for step, out in enumerate(outs):
        out[...] = attended[own ^ step]


def project_kernel(*refs):
    parts, (weight_ref, out_ref, scratch) = refs[:-3], refs[-3:]
    own = lax.axis_index("head")
    total = None
    for step, part in enumerate(parts):
        start = pl.multiple_of((own ^ step) * part.shape[1], part.shape[1])
        product = jnp.dot(
            part[...], weight_ref[pl.ds(start, part.shape[1]), :], preferred_element_type=jnp.float32
        )
        total = product if total is None else total + product
    count = scratch.shape[0]
    for column in range(count):
        scratch[column] = total[:, column * PAIR : (column + 1) * PAIR]
    for column in range(count):
        for i in range(SLAB):
            out_ref[i * FAN : (i + 1) * FAN, column * PAIR : (column + 1) * PAIR] = scratch[
                column, pl.ds(i, FAN, stride=SLAB), :
            ].astype(jnp.bfloat16)


def repool_outside(field, times):
    for _ in range(times):
        which, rows, lanes = field.shape
        slabs = field.astype(jnp.float32).reshape(which, rows // (2 * SLAB), 2, SLAB, lanes)
        field = ((slabs[:, :, 0] + slabs[:, :, 1]) * root_half).reshape(which, rows // 2, lanes).astype(jnp.bfloat16)
    return field


def swapped(block, axis, mask):
    return lax.ppermute(block, axis, [(i, i ^ mask) for i in range(lax.axis_size(axis))])


def across(block, axis):
    count = lax.axis_size(axis)
    route = []
    for low in range(1, count - 1, 2):
        route += [(low, low + 1), (low + 1, low)]
    return lax.ppermute(block, axis, route)


def per_device(queries, key_vectors, value_vectors, out_weight):
    rows, features = queries.shape[1:]
    queries, key_vectors, value_vectors, out_weight = [
        pltpu.with_memory_space_constraint(x, pltpu.HBM)
        for x in (queries, key_vectors, value_vectors, out_weight)
    ]
    pairs = features // PAIR
    seq_count, head_count = lax.axis_size("seq"), lax.axis_size("head")
    bf16 = lambda *shape: jax.ShapeDtypeStruct(shape, jnp.bfloat16)
    params = pltpu.CompilerParams(vmem_limit_bytes=32 * 1024 * 1024)

    hbm = pl.BlockSpec(memory_space=pltpu.HBM)
    vmem = pl.BlockSpec(memory_space=pltpu.VMEM)
    keys, values, ours, first, second, one, three, four = pl.pallas_call(
        pool_kernel,
        in_specs=[hbm] * 3,
        out_shape=[
            bf16(rows, features),
            bf16(rows, features),
            bf16(rows, features),
            bf16(4, BLOCK, features),
            bf16(2, BLOCK, features),
            bf16(2, rows // 2, features),
            bf16(2, rows // 8, features),
            bf16(2, rows // 16, features),
        ],
        scratch_shapes=[
            pltpu.VMEM((pairs, rows, PAIR), jnp.float32),
            pltpu.SemaphoreType.DMA((3,)),
        ],
        compiler_params=params,
        name="pool",
    )(key_vectors, value_vectors, queries)

    first_in = swapped(first, "seq", 1)
    second_in = across(second, "seq")
    three_in = [swapped(three, "seq", mask) for mask in (2, 3)]

    edge_q, two_q, three_q, four_q, state, four_late, weight = pl.pallas_call(
        local_kernel,
        in_specs=[vmem] * 5 + [hbm],
        out_shape=[
            bf16(2, BLOCK, features),
            bf16(rows // 4, features),
            bf16(rows // 8, features),
            bf16(rows // 16, features),
            jax.ShapeDtypeStruct((3, rows, features), jnp.float32),
            bf16(2, rows // 16, features),
            bf16(*out_weight.shape),
        ],
        scratch_shapes=[
            pltpu.VMEM((pairs, rows, PAIR), jnp.float32),
            pltpu.SemaphoreType.DMA((1,)),
        ],
        compiler_params=params,
        name="local",
    )(ours, keys, values, one, four, out_weight)

    others = [swapped(four_late, "seq", mask) for mask in range(4, 8)]
    known = seq_count if seq_count < 8 else 8
    if known < seq_count:
        mine = [four, repool_outside(first_in[:2], 2)] + [repool_outside(x, 1) for x in three_in]
        group = jnp.concatenate(mine + others, axis=1)
        while known < seq_count:
            fresh = swapped(group, "seq", known)
            others.append(fresh)
            group = jnp.concatenate([group, fresh], axis=1)
            known *= 2

    outs = pl.pallas_call(
        finish_kernel,
        out_shape=[bf16(BLOCK, features) for _ in range(head_count)],
        scratch_shapes=[pltpu.VMEM((rows // BLOCK, BLOCK, features), jnp.bfloat16)],
        compiler_params=params,
        name="finish",
    )(edge_q, two_q, three_q, four_q, state, first_in, second_in, *three_in, four, *others)

    parts = [part if step == 0 else swapped(part, "head", step) for step, part in enumerate(outs)]
    width = out_weight.shape[1]
    result = pl.pallas_call(
        project_kernel,
        out_shape=bf16(BLOCK, width),
        scratch_shapes=[pltpu.VMEM((width // PAIR, BLOCK, PAIR), jnp.float32)],
        compiler_params=params,
        name="project",
    )(*parts, weight)
    return result[None]


def solution(mesh):
    return jax.shard_map(
        per_device,
        mesh=mesh,
        in_specs=(P(None, "seq", "head"), P(None, "seq", "head"), P(None, "seq", "head"), P()),
        out_specs=P(None, ("seq", "head"), None),
        check_vma=False,
    )
```

```python
import jax
import jax.numpy as jnp
from jax import lax
from jax.experimental import pallas as pl
from jax.experimental.pallas import tpu as pltpu
from jax.sharding import PartitionSpec as P

HD = 64
BLOCK = 128
LEVELS = 4
SLAB = 8
PAIR = 2 * HD

neg_fill = -1e30
root_half = 0.7071067811865476
log2_scale = HD**-0.5 * 1.4426950408889634

FAN = 2**LEVELS


def slabs_of(scratch, block):
    return [scratch[pl.ds(BLOCK * block + j, SLAB, stride=FAN), :] for j in range(FAN)]


def pooled_slabs(slabs):
    return [
        ((low + high) * root_half).astype(jnp.bfloat16).astype(jnp.float32)
        for low, high in zip(slabs[0::2], slabs[1::2])
    ]


def joined(slabs):
    return jnp.concatenate(slabs, axis=0).astype(jnp.bfloat16)


def spill(source, scratch):
    for half in range(scratch.shape[0]):
        scratch[half] = source[:, half * PAIR : (half + 1) * PAIR].astype(jnp.float32)


def pool_kernel(
    k_hbm, v_hbm, q_hbm, k_ref, v_ref, q_ref, first_ref, second_ref, one_ref, three_ref, four_ref,
    scratch, sems,
):
    rows = k_ref.shape[0]
    blocks = rows // BLOCK
    copies = [
        pltpu.make_async_copy(source.at[0], target, sems.at[index])
        for index, (source, target) in enumerate(
            ((k_hbm, k_ref), (v_hbm, v_ref), (q_hbm, q_ref))
        )
    ]
    for copy in copies:
        copy.start()
    even = lax.rem(lax.axis_index("seq"), 2) == 0
    for which, ref in enumerate((k_ref, v_ref)):
        copies[which].wait()
        head, tail = ref[:BLOCK, :], ref[rows - BLOCK :, :]
        first_ref[2 + which] = jnp.where(even, tail, head)
        second_ref[which] = jnp.where(even, head, tail)
        spill(ref, scratch)
        for half in range(scratch.shape[0]):
            lanes = pl.ds(half * PAIR, PAIR)
            ladder = [[], [], [], [], []]
            for block in range(blocks):
                slabs = slabs_of(scratch.at[half], block)
                for level in range(1, LEVELS + 1):
                    slabs = pooled_slabs(slabs)
                    ladder[level] += slabs
            one_ref[which, :, lanes] = joined(ladder[1])
            first_ref[which, :, lanes] = joined(ladder[2])
            three_ref[which, :, lanes] = joined(ladder[3])
            four_ref[which, :, lanes] = joined(ladder[4])
    copies[2].wait()


def repooled(field):
    rows, lanes = field.shape
    slabs = field.astype(jnp.float32).reshape(rows // (2 * SLAB), 2, SLAB, lanes)
    return ((slabs[:, 0] + slabs[:, 1]) * root_half).reshape(rows // 2, lanes).astype(jnp.bfloat16)


def term(queries, keys, values, is_open=None):
    rows = queries.shape[0]
    low = lax.broadcasted_iota(jnp.int32, (rows, PAIR), 1) < HD
    zero = jnp.zeros_like(queries)
    both = jnp.concatenate([jnp.where(low, queries, zero), jnp.where(low, zero, queries)], axis=0)
    scores = log2_scale * lax.dot_general(
        both, keys, (((1,), (1,)), ((), ())), preferred_element_type=jnp.float32
    )
    if is_open is not None:
        scores = jnp.where(is_open, scores, neg_fill)
    top = jnp.max(scores, axis=1, keepdims=True)
    weights = jnp.exp2(scores - top).astype(jnp.bfloat16)
    result = jnp.dot(weights, values, preferred_element_type=jnp.float32)
    return (
        jnp.where(low, top[:rows], top[rows:]),
        jnp.where(low, result[:rows, :PAIR], result[rows:, :PAIR]),
        jnp.where(low, result[:rows, PAIR:], result[rows:, PAIR:]),
    )


def merged(fine, coarse):
    top = jnp.maximum(fine[0], coarse[0])
    keep = jnp.exp2(fine[0] - top)
    join = jnp.exp2(coarse[0] - top)
    return top, fine[1] * keep + coarse[1] * join, fine[2] * keep + coarse[2] * join


def doubled(field):
    rows, lanes = field.shape
    slabs = field.reshape(rows // SLAB, 1, SLAB, lanes)
    return jnp.broadcast_to(slabs, (rows // SLAB, 2, SLAB, lanes)).reshape(2 * rows, lanes)


def with_ones(values, weight=1.0):
    if weight != 1.0:
        values = values * jnp.bfloat16(weight)
    return jnp.concatenate([values, jnp.full(values.shape, weight, jnp.bfloat16)], axis=1)


def local_kernel(
    q_ref, k_ref, v_ref, one_ref, edge_q, two_q, three_q, four_q, state, scratch
):
    rows = q_ref.shape[0]
    blocks = rows // BLOCK
    spill(q_ref, scratch)
    for pair in range(scratch.shape[0]):
        lanes = pl.ds(pair * PAIR, PAIR)
        ladder = [[], [], [], [], []]
        for block in range(blocks):
            slabs = slabs_of(scratch.at[pair], block)
            ladder[0].append(joined(slabs))
            for level in range(1, LEVELS + 1):
                slabs = pooled_slabs(slabs)
                ladder[level] += slabs
        edge_q[0, :, lanes] = ladder[0][0]
        edge_q[1, :, lanes] = ladder[0][-1]
        two_q[:, lanes] = joined(ladder[2])
        three_q[:, lanes] = joined(ladder[3])
        four_q[:, lanes] = joined(ladder[4])
        for half in range(blocks // 2):
            there = pl.ds((half ^ 1) * BLOCK, BLOCK)
            here = BLOCK // SLAB * half
            coarse = term(
                joined(ladder[1][here : here + BLOCK // SLAB]),
                one_ref[0, there, lanes],
                with_ones(one_ref[1, there, lanes]),
            )
            up = [doubled(x) for x in coarse]
            for part in range(2):
                block = 2 * half + part
                low, high = max(block - 1, 0) * BLOCK, min(block + 2, blocks) * BLOCK
                near = term(
                    ladder[0][block], k_ref[low:high, lanes], with_ones(v_ref[low:high, lanes])
                )
                done = merged(near, [x[part * BLOCK : (part + 1) * BLOCK] for x in up])
                for index, field in enumerate(done):
                    state[index, block * BLOCK : (block + 1) * BLOCK, lanes] = field


def finish_kernel(
    edge_q, two_q, three_q, four_q, state, first_ref, second_ref, four_ref, relay_a, relay_b, *refs
):
    far, refs = refs[:-5], refs[-5:]
    outs, attended = refs[:-1], refs[-1]
    rows = state.shape[1]
    blocks = rows // BLOCK
    position = lax.axis_index("seq")
    even = lax.rem(position, 2) == 0
    own = lax.axis_index("head")
    sides = ((0, position > 0, second_ref, first_ref), (blocks - 1, position < lax.axis_size("seq") - 1, first_ref, second_ref))

    for pair in range(two_q.shape[1] // PAIR):
        lanes = pl.ds(pair * PAIR, PAIR)
        relays = [relay_a[:, :, lanes], relay_b[:, :, lanes]]
        eighth = rows // 8
        three, ours, theirs, beyond = [], [], [], []
        for which in range(2):
            three.append([relay[which, :eighth] for relay in relays])
            ours.append(
                [four_ref[which, :, lanes], repooled(repooled(first_ref[which, :, lanes]))]
                + [repooled(field) for field in three[which]]
            )
            theirs.append([relay[which, eighth:] for relay in relays])
            beyond.append([field[which, :, lanes] for field in far])
        now = term(
            four_q[:, lanes],
            jnp.concatenate(ours[0] + theirs[0] + beyond[0], axis=0),
            jnp.concatenate(
                [with_ones(field) for field in ours[1]]
                + [with_ones(field, 2.0) for field in theirs[1]]
                + [with_ones(field) for field in beyond[1]],
                axis=0,
            ),
        )
        now = merged(
            term(
                three_q[:, lanes],
                jnp.concatenate(three[0], axis=0),
                with_ones(jnp.concatenate(three[1], axis=0)),
            ),
            [doubled(x) for x in now],
        )
        now = merged(
            term(two_q[:, lanes], first_ref[0, :, lanes], with_ones(first_ref[1, :, lanes])),
            [doubled(x) for x in now],
        )
        for block in range(blocks):
            here = slice(block * BLOCK, (block + 1) * BLOCK)
            quarter = slice(block * BLOCK // 4, (block + 1) * BLOCK // 4)
            done = merged(
                [state[index, here, lanes] for index in range(3)],
                [doubled(doubled(x[quarter])) for x in now],
            )
            for side, (edge, is_open, if_even, if_odd) in enumerate(sides):
                if block == edge:
                    halo = [
                        jnp.where(
                            even,
                            if_even[if_even.shape[0] - 2 + which, :, lanes],
                            if_odd[if_odd.shape[0] - 2 + which, :, lanes],
                        )
                        for which in range(2)
                    ]
                    done = merged(done, term(edge_q[side, :, lanes], halo[0], with_ones(halo[1]), is_open))
            attended[block, :, lanes] = (done[1] / done[2]).astype(jnp.bfloat16)
    for step, out in enumerate(outs):
        out[...] = attended[own ^ step]


def project_kernel(*refs):
    parts, (weight_ref, out_ref, scratch) = refs[:-3], refs[-3:]
    own = lax.axis_index("head")
    total = None
    for step, part in enumerate(parts):
        start = pl.multiple_of((own ^ step) * part.shape[1], part.shape[1])
        product = jnp.dot(
            part[...], weight_ref[pl.ds(start, part.shape[1]), :], preferred_element_type=jnp.float32
        )
        total = product if total is None else total + product
    count = scratch.shape[0]
    for column in range(count):
        scratch[column] = total[:, column * PAIR : (column + 1) * PAIR]
    for column in range(count):
        for i in range(SLAB):
            out_ref[i * FAN : (i + 1) * FAN, column * PAIR : (column + 1) * PAIR] = scratch[
                column, pl.ds(i, FAN, stride=SLAB), :
            ].astype(jnp.bfloat16)


def repool_outside(field, times):
    for _ in range(times):
        which, rows, lanes = field.shape
        slabs = field.astype(jnp.float32).reshape(which, rows // (2 * SLAB), 2, SLAB, lanes)
        field = ((slabs[:, :, 0] + slabs[:, :, 1]) * root_half).reshape(which, rows // 2, lanes).astype(jnp.bfloat16)
    return field


def swapped(block, axis, mask):
    return lax.ppermute(block, axis, [(i, i ^ mask) for i in range(lax.axis_size(axis))])


def across(block, axis):
    count = lax.axis_size(axis)
    route = []
    for low in range(1, count - 1, 2):
        route += [(low, low + 1), (low + 1, low)]
    return lax.ppermute(block, axis, route)


def per_device(queries, key_vectors, value_vectors, out_weight):
    rows, features = queries.shape[1:]
    queries, key_vectors, value_vectors = [
        pltpu.with_memory_space_constraint(x, pltpu.HBM)
        for x in (queries, key_vectors, value_vectors)
    ]
    pairs = features // PAIR
    seq_count, head_count = lax.axis_size("seq"), lax.axis_size("head")
    bf16 = lambda *shape: jax.ShapeDtypeStruct(shape, jnp.bfloat16)
    params = pltpu.CompilerParams(vmem_limit_bytes=32 * 1024 * 1024)

    hbm = pl.BlockSpec(memory_space=pltpu.HBM)
    vmem = pl.BlockSpec(memory_space=pltpu.VMEM)
    keys, values, ours, first, second, one, three, four = pl.pallas_call(
        pool_kernel,
        in_specs=[hbm] * 3,
        out_shape=[
            bf16(rows, features),
            bf16(rows, features),
            bf16(rows, features),
            bf16(4, BLOCK, features),
            bf16(2, BLOCK, features),
            bf16(2, rows // 2, features),
            bf16(2, rows // 8, features),
            bf16(2, rows // 16, features),
        ],
        scratch_shapes=[
            pltpu.VMEM((pairs, rows, PAIR), jnp.float32),
            pltpu.SemaphoreType.DMA((3,)),
        ],
        compiler_params=params,
        name="pool",
    )(key_vectors, value_vectors, queries)

    first_in = swapped(first, "seq", 1)
    second_in = across(second, "seq")
    three_in = swapped(three, "seq", 2)
    fours_in = [swapped(four, "seq", mask) for mask in (4, 6)]
    relayed = jnp.concatenate([three_in] + fours_in, axis=1)
    relayed_in = swapped(relayed, "seq", 1)

    edge_q, two_q, three_q, four_q, state = pl.pallas_call(
        local_kernel,
        out_shape=[
            bf16(2, BLOCK, features),
            bf16(rows // 4, features),
            bf16(rows // 8, features),
            bf16(rows // 16, features),
            jax.ShapeDtypeStruct((3, rows, features), jnp.float32),
        ],
        scratch_shapes=[pltpu.VMEM((pairs, rows, PAIR), jnp.float32)],
        compiler_params=params,
        name="local",
    )(ours, keys, values, one)

    far = []
    known = 8
    if known < seq_count:
        eighth = rows // 8
        near = [four, repool_outside(first_in[:2], 2), repool_outside(three_in, 1)]
        near += [repool_outside(relayed_in[:, :eighth], 1), relayed_in[:, eighth:]] + fours_in
        group = jnp.concatenate(near, axis=1)
        while known < seq_count:
            fresh = swapped(group, "seq", known)
            far.append(fresh)
            group = jnp.concatenate([group, fresh], axis=1)
            known *= 2

    outs = pl.pallas_call(
        finish_kernel,
        out_shape=[bf16(BLOCK, features) for _ in range(head_count)],
        scratch_shapes=[pltpu.VMEM((rows // BLOCK, BLOCK, features), jnp.bfloat16)],
        compiler_params=params,
        name="finish",
    )(edge_q, two_q, three_q, four_q, state, first_in, second_in, four, relayed, relayed_in, *far)

    parts = [part if step == 0 else swapped(part, "head", step) for step, part in enumerate(outs)]
    width = out_weight.shape[1]
    result = pl.pallas_call(
        project_kernel,
        out_shape=bf16(BLOCK, width),
        scratch_shapes=[pltpu.VMEM((width // PAIR, BLOCK, PAIR), jnp.float32)],
        compiler_params=params,
        name="project",
    )(*parts, out_weight)
    return result[None]


def solution(mesh):
    return jax.shard_map(
        per_device,
        mesh=mesh,
        in_specs=(P(None, "seq", "head"), P(None, "seq", "head"), P(None, "seq", "head"), P()),
        out_specs=P(None, ("seq", "head"), None),
        check_vma=False,
    )
```

```python
import jax
import jax.numpy as jnp
from jax import lax
from jax.experimental import pallas as pl
from jax.experimental.pallas import tpu as pltpu
from jax.sharding import PartitionSpec as P

HD = 64
BLOCK = 128
LEVELS = 4
SLAB = 8
PAIR = 2 * HD

neg_fill = -1e30
root_half = 0.7071067811865476
log2_scale = HD**-0.5 * 1.4426950408889634

FAN = 2**LEVELS


def slabs_of(scratch, block):
    return [scratch[pl.ds(BLOCK * block + j, SLAB, stride=FAN), :] for j in range(FAN)]


def pooled_slabs(slabs):
    return [
        ((low + high) * root_half).astype(jnp.bfloat16).astype(jnp.float32)
        for low, high in zip(slabs[0::2], slabs[1::2])
    ]


def joined(slabs):
    return jnp.concatenate(slabs, axis=0).astype(jnp.bfloat16)


def spill(source, scratch):
    for half in range(scratch.shape[0]):
        scratch[half] = source[:, half * PAIR : (half + 1) * PAIR].astype(jnp.float32)


def pool_kernel(
    k_hbm, v_hbm, q_hbm, k_ref, v_ref, q_ref, first_ref, one_ref, scratch, sems
):
    rows = k_ref.shape[0]
    blocks = rows // BLOCK
    copies = [
        pltpu.make_async_copy(source.at[0], target, sems.at[index])
        for index, (source, target) in enumerate(
            ((k_hbm, k_ref), (v_hbm, v_ref), (q_hbm, q_ref))
        )
    ]
    for copy in copies:
        copy.start()
    even = lax.rem(lax.axis_index("seq"), 2) == 0
    for which, ref in enumerate((k_ref, v_ref)):
        copies[which].wait()
        head, tail = ref[:BLOCK, :], ref[rows - BLOCK :, :]
        first_ref[2 + which] = jnp.where(even, tail, head)
        spill(ref, scratch)
        for half in range(scratch.shape[0]):
            lanes = pl.ds(half * PAIR, PAIR)
            one, two = [], []
            for block in range(blocks):
                slabs = pooled_slabs(slabs_of(scratch.at[half], block))
                one += slabs
                two += pooled_slabs(slabs)
            one_ref[which, :, lanes] = joined(one)
            first_ref[which, :, lanes] = joined(two)
    copies[2].wait()


def deeper_kernel(k_ref, v_ref, first_ref, second_ref, three_ref, four_ref):
    rows = k_ref.shape[0]
    even = lax.rem(lax.axis_index("seq"), 2) == 0
    for which, ref in enumerate((k_ref, v_ref)):
        second_ref[which] = jnp.where(even, ref[:BLOCK, :], ref[rows - BLOCK :, :])
        three = repooled(first_ref[which])
        three_ref[which] = three
        four_ref[which] = repooled(three)


def repooled(field):
    rows, lanes = field.shape
    slabs = field.astype(jnp.float32).reshape(rows // (2 * SLAB), 2, SLAB, lanes)
    return ((slabs[:, 0] + slabs[:, 1]) * root_half).reshape(rows // 2, lanes).astype(jnp.bfloat16)


def term(queries, keys, values, is_open=None):
    rows = queries.shape[0]
    low = lax.broadcasted_iota(jnp.int32, (rows, PAIR), 1) < HD
    zero = jnp.zeros_like(queries)
    both = jnp.concatenate([jnp.where(low, queries, zero), jnp.where(low, zero, queries)], axis=0)
    scores = log2_scale * lax.dot_general(
        both, keys, (((1,), (1,)), ((), ())), preferred_element_type=jnp.float32
    )
    if is_open is not None:
        scores = jnp.where(is_open, scores, neg_fill)
    top = jnp.max(scores, axis=1, keepdims=True)
    weights = jnp.exp2(scores - top).astype(jnp.bfloat16)
    result = jnp.dot(weights, values, preferred_element_type=jnp.float32)
    return (
        jnp.where(low, top[:rows], top[rows:]),
        jnp.where(low, result[:rows, :PAIR], result[rows:, :PAIR]),
        jnp.where(low, result[:rows, PAIR:], result[rows:, PAIR:]),
    )


def merged(fine, coarse):
    top = jnp.maximum(fine[0], coarse[0])
    keep = jnp.exp2(fine[0] - top)
    join = jnp.exp2(coarse[0] - top)
    return top, fine[1] * keep + coarse[1] * join, fine[2] * keep + coarse[2] * join


def doubled(field):
    rows, lanes = field.shape
    slabs = field.reshape(rows // SLAB, 1, SLAB, lanes)
    return jnp.broadcast_to(slabs, (rows // SLAB, 2, SLAB, lanes)).reshape(2 * rows, lanes)


def with_ones(values, weight=1.0):
    if weight != 1.0:
        values = values * jnp.bfloat16(weight)
    return jnp.concatenate([values, jnp.full(values.shape, weight, jnp.bfloat16)], axis=1)


def local_kernel(
    q_ref, k_ref, v_ref, one_ref, edge_q, two_q, three_q, four_q, state, scratch
):
    rows = q_ref.shape[0]
    blocks = rows // BLOCK
    spill(q_ref, scratch)
    for pair in range(scratch.shape[0]):
        lanes = pl.ds(pair * PAIR, PAIR)
        ladder = [[], [], [], [], []]
        for block in range(blocks):
            slabs = slabs_of(scratch.at[pair], block)
            ladder[0].append(joined(slabs))
            for level in range(1, LEVELS + 1):
                slabs = pooled_slabs(slabs)
                ladder[level] += slabs
        edge_q[0, :, lanes] = ladder[0][0]
        edge_q[1, :, lanes] = ladder[0][-1]
        two_q[:, lanes] = joined(ladder[2])
        three_q[:, lanes] = joined(ladder[3])
        four_q[:, lanes] = joined(ladder[4])
        for half in range(blocks // 2):
            there = pl.ds((half ^ 1) * BLOCK, BLOCK)
            here = BLOCK // SLAB * half
            coarse = term(
                joined(ladder[1][here : here + BLOCK // SLAB]),
                one_ref[0, there, lanes],
                with_ones(one_ref[1, there, lanes]),
            )
            up = [doubled(x) for x in coarse]
            for part in range(2):
                block = 2 * half + part
                low, high = max(block - 1, 0) * BLOCK, min(block + 2, blocks) * BLOCK
                near = term(
                    ladder[0][block], k_ref[low:high, lanes], with_ones(v_ref[low:high, lanes])
                )
                done = merged(near, [x[part * BLOCK : (part + 1) * BLOCK] for x in up])
                for index, field in enumerate(done):
                    state[index, block * BLOCK : (block + 1) * BLOCK, lanes] = field


def mid_kernel(edge_q, two_q, state, first_ref, second_ref, out):
    rows = state.shape[1]
    blocks = rows // BLOCK
    position = lax.axis_index("seq")
    last = lax.axis_size("seq") - 1
    even = lax.rem(position, 2) == 0
    sides = ((0, position > 0, second_ref, first_ref), (blocks - 1, position < last, first_ref, second_ref))
    for pair in range(two_q.shape[1] // PAIR):
        lanes = pl.ds(pair * PAIR, PAIR)
        two = term(two_q[:, lanes], first_ref[0, :, lanes], with_ones(first_ref[1, :, lanes]))
        for block in range(blocks):
            here = slice(block * BLOCK, (block + 1) * BLOCK)
            quarter = slice(block * BLOCK // 4, (block + 1) * BLOCK // 4)
            done = merged(
                [state[index, here, lanes] for index in range(3)],
                [doubled(doubled(x[quarter])) for x in two],
            )
            for side, (edge, is_open, if_even, if_odd) in enumerate(sides):
                if block == edge:
                    halo = [
                        jnp.where(
                            even,
                            if_even[if_even.shape[0] - 2 + which, :, lanes],
                            if_odd[if_odd.shape[0] - 2 + which, :, lanes],
                        )
                        for which in range(2)
                    ]
                    done = merged(done, term(edge_q[side, :, lanes], halo[0], with_ones(halo[1]), is_open))
            for index, field in enumerate(done):
                out[index, here, lanes] = field


def finish_kernel(three_q, four_q, state, first_ref, four_ref, relay_a, relay_b, *refs):
    far, refs = refs[:-5], refs[-5:]
    outs, attended = refs[:-1], refs[-1]
    rows = state.shape[1]
    blocks = rows // BLOCK
    own = lax.axis_index("head")
    for pair in range(three_q.shape[1] // PAIR):
        lanes = pl.ds(pair * PAIR, PAIR)
        relays = [relay_a[:, :, lanes], relay_b[:, :, lanes]]
        eighth = rows // 8
        three, ours, theirs, beyond = [], [], [], []
        for which in range(2):
            three.append([relay[which, :eighth] for relay in relays])
            ours.append(
                [four_ref[which, :, lanes], repooled(repooled(first_ref[which, :, lanes]))]
                + [repooled(field) for field in three[which]]
            )
            theirs.append([relay[which, eighth:] for relay in relays])
            beyond.append([field[which, :, lanes] for field in far])
        now = term(
            four_q[:, lanes],
            jnp.concatenate(ours[0] + theirs[0] + beyond[0], axis=0),
            jnp.concatenate(
                [with_ones(field) for field in ours[1]]
                + [with_ones(field, 2.0) for field in theirs[1]]
                + [with_ones(field) for field in beyond[1]],
                axis=0,
            ),
        )
        now = merged(
            term(
                three_q[:, lanes],
                jnp.concatenate(three[0], axis=0),
                with_ones(jnp.concatenate(three[1], axis=0)),
            ),
            [doubled(x) for x in now],
        )
        for block in range(blocks):
            here = slice(block * BLOCK, (block + 1) * BLOCK)
            eighth_here = slice(block * BLOCK // 8, (block + 1) * BLOCK // 8)
            _, numer, rowsum = merged(
                [state[index, here, lanes] for index in range(3)],
                [doubled(doubled(doubled(x[eighth_here]))) for x in now],
            )
            attended[block, :, lanes] = (numer / rowsum).astype(jnp.bfloat16)
    for step, out in enumerate(outs):
        out[...] = attended[own ^ step]


def project_kernel(*refs):
    parts, (weight_ref, out_ref, scratch) = refs[:-3], refs[-3:]
    own = lax.axis_index("head")
    total = None
    for step, part in enumerate(parts):
        start = pl.multiple_of((own ^ step) * part.shape[1], part.shape[1])
        product = jnp.dot(
            part[...], weight_ref[pl.ds(start, part.shape[1]), :], preferred_element_type=jnp.float32
        )
        total = product if total is None else total + product
    count = scratch.shape[0]
    for column in range(count):
        scratch[column] = total[:, column * PAIR : (column + 1) * PAIR]
    for column in range(count):
        for i in range(SLAB):
            out_ref[i * FAN : (i + 1) * FAN, column * PAIR : (column + 1) * PAIR] = scratch[
                column, pl.ds(i, FAN, stride=SLAB), :
            ].astype(jnp.bfloat16)


def repool_outside(field, times):
    for _ in range(times):
        which, rows, lanes = field.shape
        slabs = field.astype(jnp.float32).reshape(which, rows // (2 * SLAB), 2, SLAB, lanes)
        field = ((slabs[:, :, 0] + slabs[:, :, 1]) * root_half).reshape(which, rows // 2, lanes).astype(jnp.bfloat16)
    return field


def swapped(block, axis, mask):
    return lax.ppermute(block, axis, [(i, i ^ mask) for i in range(lax.axis_size(axis))])


def across(block, axis):
    count = lax.axis_size(axis)
    route = []
    for low in range(1, count - 1, 2):
        route += [(low, low + 1), (low + 1, low)]
    return lax.ppermute(block, axis, route)


def per_device(queries, key_vectors, value_vectors, out_weight):
    rows, features = queries.shape[1:]
    queries, key_vectors, value_vectors = [
        pltpu.with_memory_space_constraint(x, pltpu.HBM)
        for x in (queries, key_vectors, value_vectors)
    ]
    pairs = features // PAIR
    seq_count, head_count = lax.axis_size("seq"), lax.axis_size("head")
    bf16 = lambda *shape: jax.ShapeDtypeStruct(shape, jnp.bfloat16)
    params = pltpu.CompilerParams(vmem_limit_bytes=32 * 1024 * 1024)

    hbm = pl.BlockSpec(memory_space=pltpu.HBM)
    vmem = pl.BlockSpec(memory_space=pltpu.VMEM)
    keys, values, ours, first, one = pl.pallas_call(
        pool_kernel,
        in_specs=[hbm] * 3,
        out_shape=[
            bf16(rows, features),
            bf16(rows, features),
            bf16(rows, features),
            bf16(4, BLOCK, features),
            bf16(2, rows // 2, features),
        ],
        scratch_shapes=[
            pltpu.VMEM((pairs, rows, PAIR), jnp.float32),
            pltpu.SemaphoreType.DMA((3,)),
        ],
        compiler_params=params,
        name="pool",
    )(key_vectors, value_vectors, queries)
    second, three, four = pl.pallas_call(
        deeper_kernel,
        out_shape=[
            bf16(2, BLOCK, features),
            bf16(2, rows // 8, features),
            bf16(2, rows // 16, features),
        ],
        compiler_params=params,
        name="deeper",
    )(keys, values, first)

    first_in = swapped(first, "seq", 1)
    second_in = across(second, "seq")
    three_in = swapped(three, "seq", 2)
    fours_in = [swapped(four, "seq", mask) for mask in (4, 6)]
    relayed = jnp.concatenate([three_in] + fours_in, axis=1)
    relayed_in = swapped(relayed, "seq", 1)

    edge_q, two_q, three_q, four_q, state = pl.pallas_call(
        local_kernel,
        out_shape=[
            bf16(2, BLOCK, features),
            bf16(rows // 4, features),
            bf16(rows // 8, features),
            bf16(rows // 16, features),
            jax.ShapeDtypeStruct((3, rows, features), jnp.float32),
        ],
        scratch_shapes=[pltpu.VMEM((pairs, rows, PAIR), jnp.float32)],
        compiler_params=params,
        name="local",
    )(ours, keys, values, one)

    far = []
    known = 8
    if known < seq_count:
        eighth = rows // 8
        near = [four, repool_outside(first_in[:2], 2), repool_outside(three_in, 1)]
        near += [repool_outside(relayed_in[:, :eighth], 1), relayed_in[:, eighth:]] + fours_in
        group = jnp.concatenate(near, axis=1)
        while known < seq_count:
            fresh = swapped(group, "seq", known)
            far.append(fresh)
            group = jnp.concatenate([group, fresh], axis=1)
            known *= 2

    state = pl.pallas_call(
        mid_kernel,
        out_shape=jax.ShapeDtypeStruct((3, rows, features), jnp.float32),
        input_output_aliases={2: 0},
        compiler_params=params,
        name="mid",
    )(edge_q, two_q, state, first_in, second_in)
    outs = pl.pallas_call(
        finish_kernel,
        out_shape=[bf16(BLOCK, features) for _ in range(head_count)],
        scratch_shapes=[pltpu.VMEM((rows // BLOCK, BLOCK, features), jnp.bfloat16)],
        compiler_params=params,
        name="finish",
    )(three_q, four_q, state, first_in, four, relayed, relayed_in, *far)

    parts = [part if step == 0 else swapped(part, "head", step) for step, part in enumerate(outs)]
    width = out_weight.shape[1]
    result = pl.pallas_call(
        project_kernel,
        out_shape=bf16(BLOCK, width),
        scratch_shapes=[pltpu.VMEM((width // PAIR, BLOCK, PAIR), jnp.float32)],
        compiler_params=params,
        name="project",
    )(*parts, out_weight)
    return result[None]


def solution(mesh):
    return jax.shard_map(
        per_device,
        mesh=mesh,
        in_specs=(P(None, "seq", "head"), P(None, "seq", "head"), P(None, "seq", "head"), P()),
        out_specs=P(None, ("seq", "head"), None),
        check_vma=False,
    )
```

```python
import jax
import jax.numpy as jnp
from jax import lax
from jax.experimental import pallas as pl
from jax.experimental.pallas import tpu as pltpu
from jax.sharding import PartitionSpec as P

HD = 64
BLOCK = 128
LEVELS = 4
SLAB = 8
PAIR = 2 * HD

neg_fill = -1e30
root_half = 0.7071067811865476
log2_scale = HD**-0.5 * 1.4426950408889634

FAN = 2**LEVELS


def slabs_of(scratch, block):
    return [scratch[pl.ds(BLOCK * block + j, SLAB, stride=FAN), :] for j in range(FAN)]


def pooled_slabs(slabs):
    return [
        ((low + high) * root_half).astype(jnp.bfloat16).astype(jnp.float32)
        for low, high in zip(slabs[0::2], slabs[1::2])
    ]


def joined(slabs):
    return jnp.concatenate(slabs, axis=0).astype(jnp.bfloat16)


def spill(source, scratch):
    for half in range(scratch.shape[0]):
        scratch[half] = source[:, half * PAIR : (half + 1) * PAIR].astype(jnp.float32)


def pool_kernel(
    k_hbm, v_hbm, q_hbm, k_ref, v_ref, q_ref, first_ref, one_ref, scratch, sems, q_sem
):
    rows = k_ref.shape[0]
    blocks = rows // BLOCK
    arrivals = []
    for block in range(blocks):
        here = pl.ds(block * BLOCK, BLOCK)
        for which, (source, target) in enumerate(((k_hbm, k_ref), (v_hbm, v_ref))):
            copy = pltpu.make_async_copy(
                source.at[0, here, :], target.at[here, :], sems.at[which, block]
            )
            copy.start()
            arrivals.append((block, which, target, copy))
    q_copy = pltpu.make_async_copy(q_hbm.at[0], q_ref, q_sem.at[0])
    q_copy.start()
    even = lax.rem(lax.axis_index("seq"), 2) == 0
    for block, which, ref, copy in arrivals:
        copy.wait()
        here = pl.ds(block * BLOCK, BLOCK)
        spill(ref.at[here, :], scratch.at[which, block])
        for half in range(scratch.shape[2]):
            lanes = pl.ds(half * PAIR, PAIR)
            one = pooled_slabs(slabs_of(scratch.at[which, block, half], 0))
            one_ref[which, pl.ds(block * BLOCK // 2, BLOCK // 2), lanes] = joined(one)
            first_ref[which, pl.ds(block * BLOCK // 4, BLOCK // 4), lanes] = joined(pooled_slabs(one))
    for which, ref in enumerate((k_ref, v_ref)):
        first_ref[2 + which] = jnp.where(even, ref[rows - BLOCK :, :], ref[:BLOCK, :])
    q_copy.wait()


def repooled(field):
    rows, lanes = field.shape
    slabs = field.astype(jnp.float32).reshape(rows // (2 * SLAB), 2, SLAB, lanes)
    return ((slabs[:, 0] + slabs[:, 1]) * root_half).reshape(rows // 2, lanes).astype(jnp.bfloat16)


def deeper_kernel(k_ref, v_ref, first_ref, second_ref, three_ref, four_ref):
    rows = k_ref.shape[0]
    even = lax.rem(lax.axis_index("seq"), 2) == 0
    for which, ref in enumerate((k_ref, v_ref)):
        second_ref[which] = jnp.where(even, ref[:BLOCK, :], ref[rows - BLOCK :, :])
        three = repooled(first_ref[which])
        three_ref[which] = three
        four_ref[which] = repooled(three)


def repooled(field):
    rows, lanes = field.shape
    slabs = field.astype(jnp.float32).reshape(rows // (2 * SLAB), 2, SLAB, lanes)
    return ((slabs[:, 0] + slabs[:, 1]) * root_half).reshape(rows // 2, lanes).astype(jnp.bfloat16)


def term(queries, keys, values, is_open=None):
    rows = queries.shape[0]
    low = lax.broadcasted_iota(jnp.int32, (rows, PAIR), 1) < HD
    zero = jnp.zeros_like(queries)
    both = jnp.concatenate([jnp.where(low, queries, zero), jnp.where(low, zero, queries)], axis=0)
    scores = log2_scale * lax.dot_general(
        both, keys, (((1,), (1,)), ((), ())), preferred_element_type=jnp.float32
    )
    if is_open is not None:
        scores = jnp.where(is_open, scores, neg_fill)
    top = jnp.max(scores, axis=1, keepdims=True)
    weights = jnp.exp2(scores - top).astype(jnp.bfloat16)
    result = jnp.dot(weights, values, preferred_element_type=jnp.float32)
    return (
        jnp.where(low, top[:rows], top[rows:]),
        jnp.where(low, result[:rows, :PAIR], result[rows:, :PAIR]),
        jnp.where(low, result[:rows, PAIR:], result[rows:, PAIR:]),
    )


def merged(fine, coarse):
    top = jnp.maximum(fine[0], coarse[0])
    keep = jnp.exp2(fine[0] - top)
    join = jnp.exp2(coarse[0] - top)
    return top, fine[1] * keep + coarse[1] * join, fine[2] * keep + coarse[2] * join


def doubled(field):
    rows, lanes = field.shape
    slabs = field.reshape(rows // SLAB, 1, SLAB, lanes)
    return jnp.broadcast_to(slabs, (rows // SLAB, 2, SLAB, lanes)).reshape(2 * rows, lanes)


def with_ones(values, weight=1.0):
    if weight != 1.0:
        values = values * jnp.bfloat16(weight)
    return jnp.concatenate([values, jnp.full(values.shape, weight, jnp.bfloat16)], axis=1)


def local_kernel(
    q_ref, k_ref, v_ref, one_ref, edge_q, two_q, three_q, four_q, state, scratch
):
    rows = q_ref.shape[0]
    blocks = rows // BLOCK
    spill(q_ref, scratch)
    for pair in range(scratch.shape[0]):
        lanes = pl.ds(pair * PAIR, PAIR)
        ladder = [[], [], [], [], []]
        for block in range(blocks):
            slabs = slabs_of(scratch.at[pair], block)
            ladder[0].append(joined(slabs))
            for level in range(1, LEVELS + 1):
                slabs = pooled_slabs(slabs)
                ladder[level] += slabs
        edge_q[0, :, lanes] = ladder[0][0]
        edge_q[1, :, lanes] = ladder[0][-1]
        two_q[:, lanes] = joined(ladder[2])
        three_q[:, lanes] = joined(ladder[3])
        four_q[:, lanes] = joined(ladder[4])
        for half in range(blocks // 2):
            there = pl.ds((half ^ 1) * BLOCK, BLOCK)
            here = BLOCK // SLAB * half
            coarse = term(
                joined(ladder[1][here : here + BLOCK // SLAB]),
                one_ref[0, there, lanes],
                with_ones(one_ref[1, there, lanes]),
            )
            up = [doubled(x) for x in coarse]
            for part in range(2):
                block = 2 * half + part
                low, high = max(block - 1, 0) * BLOCK, min(block + 2, blocks) * BLOCK
                near = term(
                    ladder[0][block], k_ref[low:high, lanes], with_ones(v_ref[low:high, lanes])
                )
                done = merged(near, [x[part * BLOCK : (part + 1) * BLOCK] for x in up])
                for index, field in enumerate(done):
                    state[index, block * BLOCK : (block + 1) * BLOCK, lanes] = field


def mid_kernel(edge_q, two_q, state, first_ref, second_ref, out):
    rows = state.shape[1]
    blocks = rows // BLOCK
    position = lax.axis_index("seq")
    last = lax.axis_size("seq") - 1
    even = lax.rem(position, 2) == 0
    sides = ((0, position > 0, second_ref, first_ref), (blocks - 1, position < last, first_ref, second_ref))
    for pair in range(two_q.shape[1] // PAIR):
        lanes = pl.ds(pair * PAIR, PAIR)
        two = term(two_q[:, lanes], first_ref[0, :, lanes], with_ones(first_ref[1, :, lanes]))
        for block in range(blocks):
            here = slice(block * BLOCK, (block + 1) * BLOCK)
            quarter = slice(block * BLOCK // 4, (block + 1) * BLOCK // 4)
            done = merged(
                [state[index, here, lanes] for index in range(3)],
                [doubled(doubled(x[quarter])) for x in two],
            )
            for side, (edge, is_open, if_even, if_odd) in enumerate(sides):
                if block == edge:
                    halo = [
                        jnp.where(
                            even,
                            if_even[if_even.shape[0] - 2 + which, :, lanes],
                            if_odd[if_odd.shape[0] - 2 + which, :, lanes],
                        )
                        for which in range(2)
                    ]
                    done = merged(done, term(edge_q[side, :, lanes], halo[0], with_ones(halo[1]), is_open))
            for index, field in enumerate(done):
                out[index, here, lanes] = field


def finish_kernel(three_q, four_q, state, first_ref, four_ref, relay_a, relay_b, *refs):
    far, refs = refs[:-5], refs[-5:]
    outs, attended = refs[:-1], refs[-1]
    rows = state.shape[1]
    blocks = rows // BLOCK
    own = lax.axis_index("head")
    for pair in range(three_q.shape[1] // PAIR):
        lanes = pl.ds(pair * PAIR, PAIR)
        relays = [relay_a[:, :, lanes], relay_b[:, :, lanes]]
        eighth = rows // 8
        three, ours, theirs, beyond = [], [], [], []
        for which in range(2):
            three.append([relay[which, :eighth] for relay in relays])
            ours.append(
                [four_ref[which, :, lanes], repooled(repooled(first_ref[which, :, lanes]))]
                + [repooled(field) for field in three[which]]
            )
            theirs.append([relay[which, eighth:] for relay in relays])
            beyond.append([field[which, :, lanes] for field in far])
        now = term(
            four_q[:, lanes],
            jnp.concatenate(ours[0] + theirs[0] + beyond[0], axis=0),
            jnp.concatenate(
                [with_ones(field) for field in ours[1]]
                + [with_ones(field, 2.0) for field in theirs[1]]
                + [with_ones(field) for field in beyond[1]],
                axis=0,
            ),
        )
        now = merged(
            term(
                three_q[:, lanes],
                jnp.concatenate(three[0], axis=0),
                with_ones(jnp.concatenate(three[1], axis=0)),
            ),
            [doubled(x) for x in now],
        )
        for block in range(blocks):
            here = slice(block * BLOCK, (block + 1) * BLOCK)
            eighth_here = slice(block * BLOCK // 8, (block + 1) * BLOCK // 8)
            _, numer, rowsum = merged(
                [state[index, here, lanes] for index in range(3)],
                [doubled(doubled(doubled(x[eighth_here]))) for x in now],
            )
            attended[block, :, lanes] = (numer / rowsum).astype(jnp.bfloat16)
    for step, out in enumerate(outs):
        out[...] = attended[own ^ step]


def project_kernel(*refs):
    parts, (weight_ref, out_hbm, scratch, staged, sems) = refs[:-5], refs[-5:]
    own = lax.axis_index("head")
    features = parts[0].shape[1]
    chunk = staged.shape[2]
    copies = []
    for index in range(staged.shape[0]):
        columns = pl.ds(index * chunk, chunk)
        total = None
        for step, part in enumerate(parts):
            start = pl.multiple_of((own ^ step) * features, features)
            product = jnp.dot(
                part[...],
                weight_ref[pl.ds(start, features), columns],
                preferred_element_type=jnp.float32,
            )
            total = product if total is None else total + product
        for half in range(chunk // PAIR):
            lanes = slice(half * PAIR, (half + 1) * PAIR)
            scratch[index, half] = total[:, lanes]
            for i in range(SLAB):
                staged[index, i * FAN : (i + 1) * FAN, lanes] = scratch[
                    index, half, pl.ds(i, FAN, stride=SLAB), :
                ].astype(jnp.bfloat16)
        copy = pltpu.make_async_copy(staged.at[index], out_hbm.at[:, columns], sems.at[index])
        copy.start()
        copies.append(copy)
    for copy in copies:
        copy.wait()


def repool_outside(field, times):
    for _ in range(times):
        which, rows, lanes = field.shape
        slabs = field.astype(jnp.float32).reshape(which, rows // (2 * SLAB), 2, SLAB, lanes)
        field = ((slabs[:, :, 0] + slabs[:, :, 1]) * root_half).reshape(which, rows // 2, lanes).astype(jnp.bfloat16)
    return field


def swapped(block, axis, mask):
    return lax.ppermute(block, axis, [(i, i ^ mask) for i in range(lax.axis_size(axis))])


def across(block, axis):
    count = lax.axis_size(axis)
    route = []
    for low in range(1, count - 1, 2):
        route += [(low, low + 1), (low + 1, low)]
    return lax.ppermute(block, axis, route)


def per_device(queries, key_vectors, value_vectors, out_weight):
    rows, features = queries.shape[1:]
    queries, key_vectors, value_vectors = [
        pltpu.with_memory_space_constraint(x, pltpu.HBM)
        for x in (queries, key_vectors, value_vectors)
    ]
    pairs = features // PAIR
    seq_count, head_count = lax.axis_size("seq"), lax.axis_size("head")
    bf16 = lambda *shape: jax.ShapeDtypeStruct(shape, jnp.bfloat16)
    params = pltpu.CompilerParams(vmem_limit_bytes=32 * 1024 * 1024)

    hbm = pl.BlockSpec(memory_space=pltpu.HBM)
    vmem = pl.BlockSpec(memory_space=pltpu.VMEM)
    keys, values, ours, first, one = pl.pallas_call(
        pool_kernel,
        in_specs=[hbm] * 3,
        out_shape=[
            bf16(rows, features),
            bf16(rows, features),
            bf16(rows, features),
            bf16(4, BLOCK, features),
            bf16(2, rows // 2, features),
        ],
        scratch_shapes=[
            pltpu.VMEM((2, rows // BLOCK, pairs, BLOCK, PAIR), jnp.float32),
            pltpu.SemaphoreType.DMA((2, rows // BLOCK)),
            pltpu.SemaphoreType.DMA((1,)),
        ],
        compiler_params=params,
        name="pool",
    )(key_vectors, value_vectors, queries)
    second, three, four = pl.pallas_call(
        deeper_kernel,
        out_shape=[
            bf16(2, BLOCK, features),
            bf16(2, rows // 8, features),
            bf16(2, rows // 16, features),
        ],
        compiler_params=params,
        cost_estimate=pl.CostEstimate(flops=2**31, bytes_accessed=2**23, transcendentals=0),
        name="deeper",
    )(keys, values, first)

    first_in = swapped(first, "seq", 1)
    second_in = across(second, "seq")
    fours_in = [swapped(four, "seq", mask) for mask in (6, 4)]
    three_in = swapped(three, "seq", 2)
    relayed = jnp.concatenate([three_in] + fours_in, axis=1)
    relayed_in = swapped(relayed, "seq", 1)

    edge_q, two_q, three_q, four_q, state = pl.pallas_call(
        local_kernel,
        out_shape=[
            bf16(2, BLOCK, features),
            bf16(rows // 4, features),
            bf16(rows // 8, features),
            bf16(rows // 16, features),
            jax.ShapeDtypeStruct((3, rows, features), jnp.float32),
        ],
        scratch_shapes=[pltpu.VMEM((pairs, rows, PAIR), jnp.float32)],
        compiler_params=params,
        name="local",
    )(ours, keys, values, one)

    far = []
    known = 8
    if known < seq_count:
        eighth = rows // 8
        near = [four, repool_outside(first_in[:2], 2), repool_outside(three_in, 1)]
        near += [repool_outside(relayed_in[:, :eighth], 1), relayed_in[:, eighth:]] + fours_in
        group = jnp.concatenate(near, axis=1)
        while known < seq_count:
            fresh = swapped(group, "seq", known)
            far.append(fresh)
            group = jnp.concatenate([group, fresh], axis=1)
            known *= 2

    state = pl.pallas_call(
        mid_kernel,
        out_shape=jax.ShapeDtypeStruct((3, rows, features), jnp.float32),
        input_output_aliases={2: 0},
        compiler_params=params,
        name="mid",
    )(edge_q, two_q, state, first_in, second_in)
    outs = pl.pallas_call(
        finish_kernel,
        out_shape=[bf16(BLOCK, features) for _ in range(head_count)],
        scratch_shapes=[pltpu.VMEM((rows // BLOCK, BLOCK, features), jnp.bfloat16)],
        compiler_params=params,
        name="finish",
    )(three_q, four_q, state, first_in, four, relayed, relayed_in, *far)

    parts = [part if step == 0 else swapped(part, "head", step) for step, part in enumerate(outs)]
    width = out_weight.shape[1]
    chunk = 2 * PAIR
    result = pl.pallas_call(
        project_kernel,
        in_specs=[vmem] * (len(parts) + 1),
        out_specs=hbm,
        out_shape=bf16(BLOCK, width),
        scratch_shapes=[
            pltpu.VMEM((width // chunk, 2, BLOCK, PAIR), jnp.float32),
            pltpu.VMEM((width // chunk, BLOCK, chunk), jnp.bfloat16),
            pltpu.SemaphoreType.DMA((width // chunk,)),
        ],
        compiler_params=params,
        name="project",
    )(*parts, out_weight)
    return result[None]


def solution(mesh):
    return jax.shard_map(
        per_device,
        mesh=mesh,
        in_specs=(P(None, "seq", "head"), P(None, "seq", "head"), P(None, "seq", "head"), P()),
        out_specs=P(None, ("seq", "head"), None),
        check_vma=False,
    )
```

```python
import jax
import jax.numpy as jnp
from jax import lax
from jax.experimental import pallas as pl
from jax.experimental.pallas import tpu as pltpu
from jax.sharding import PartitionSpec as P

HD = 64
BLOCK = 128
LEVELS = 4
SLAB = 8
PAIR = 2 * HD

neg_fill = -1e30
root_half = 0.7071067811865476
log2_scale = HD**-0.5 * 1.4426950408889634

FAN = 2**LEVELS


def slabs_of(scratch, block):
    return [scratch[pl.ds(BLOCK * block + j, SLAB, stride=FAN), :] for j in range(FAN)]


def pooled_slabs(slabs):
    return [
        ((low + high) * root_half).astype(jnp.bfloat16).astype(jnp.float32)
        for low, high in zip(slabs[0::2], slabs[1::2])
    ]


def joined(slabs):
    return jnp.concatenate(slabs, axis=0).astype(jnp.bfloat16)


def spill(source, scratch):
    for half in range(scratch.shape[0]):
        scratch[half] = source[:, half * PAIR : (half + 1) * PAIR].astype(jnp.float32)


def pool_kernel(
    k_hbm, v_hbm, q_hbm, k_ref, v_ref, q_ref, first_ref, one_ref, two_ref, scratch, sems, q_sem
):
    rows = k_ref.shape[0]
    blocks = rows // BLOCK
    arrivals = []
    for block in range(blocks):
        here = pl.ds(block * BLOCK, BLOCK)
        for which, (source, target) in enumerate(((k_hbm, k_ref), (v_hbm, v_ref))):
            copy = pltpu.make_async_copy(
                source.at[0, here, :], target.at[here, :], sems.at[which, block]
            )
            copy.start()
            arrivals.append((block, which, target, copy))
    q_copy = pltpu.make_async_copy(q_hbm.at[0], q_ref, q_sem.at[0])
    q_copy.start()
    even = lax.rem(lax.axis_index("seq"), 2) == 0
    for block, which, ref, copy in arrivals:
        copy.wait()
        here = pl.ds(block * BLOCK, BLOCK)
        spill(ref.at[here, :], scratch.at[which, block])
        for half in range(scratch.shape[2]):
            lanes = pl.ds(half * PAIR, PAIR)
            one = pooled_slabs(slabs_of(scratch.at[which, block, half], 0))
            one_ref[which, pl.ds(block * BLOCK // 2, BLOCK // 2), lanes] = joined(one)
            two_ref[which, pl.ds(block * BLOCK // 4, BLOCK // 4), lanes] = joined(pooled_slabs(one))
    inner = rows // 4 - BLOCK // 4
    for which, ref in enumerate((k_ref, v_ref)):
        first_ref[which, :BLOCK, :] = jnp.where(even, ref[rows - BLOCK :, :], ref[:BLOCK, :])
        first_ref[which, BLOCK:, :] = jnp.where(
            even, two_ref[which, :inner, :], two_ref[which, BLOCK // 4 :, :]
        )
    q_copy.wait()


def repooled(field):
    rows, lanes = field.shape
    slabs = field.astype(jnp.float32).reshape(rows // (2 * SLAB), 2, SLAB, lanes)
    return ((slabs[:, 0] + slabs[:, 1]) * root_half).reshape(rows // 2, lanes).astype(jnp.bfloat16)


def deeper_kernel(k_ref, v_ref, two_ref, second_ref, three_ref, four_ref):
    rows = k_ref.shape[0]
    even = lax.rem(lax.axis_index("seq"), 2) == 0
    for which, ref in enumerate((k_ref, v_ref)):
        second_ref[which] = jnp.where(even, ref[:BLOCK, :], ref[rows - BLOCK :, :])
        three = repooled(two_ref[which])
        three_ref[which] = three
        four_ref[which] = repooled(three)


def repooled(field):
    rows, lanes = field.shape
    slabs = field.astype(jnp.float32).reshape(rows // (2 * SLAB), 2, SLAB, lanes)
    return ((slabs[:, 0] + slabs[:, 1]) * root_half).reshape(rows // 2, lanes).astype(jnp.bfloat16)


def score(queries, keys, hold, is_open=None):
    rows = queries.shape[0]
    low = lax.broadcasted_iota(jnp.int32, (rows, PAIR), 1) < HD
    zero = jnp.zeros_like(queries)
    both = jnp.concatenate([jnp.where(low, queries, zero), jnp.where(low, zero, queries)], axis=0)
    raw = lax.dot_general(both, keys, (((1,), (1,)), ((), ())), preferred_element_type=jnp.float32)
    if is_open is not None:
        raw = jnp.where(is_open, raw, neg_fill)
    hold[...] = raw
    return jnp.max(raw, axis=1, keepdims=True)


def weigh(hold, top, values):
    rows = top.shape[0] // 2
    low = lax.broadcasted_iota(jnp.int32, (rows, PAIR), 1) < HD
    weights = jnp.exp2((hold[...] - top) * log2_scale).astype(jnp.bfloat16)
    result = jnp.dot(weights, values, preferred_element_type=jnp.float32)
    return (
        log2_scale * jnp.where(low, top[:rows], top[rows:]),
        jnp.where(low, result[:rows, :PAIR], result[rows:, :PAIR]),
        jnp.where(low, result[:rows, PAIR:], result[rows:, PAIR:]),
    )


def merged(fine, coarse):
    top = jnp.maximum(fine[0], coarse[0])
    keep = jnp.exp2(fine[0] - top)
    join = jnp.exp2(coarse[0] - top)
    return top, fine[1] * keep + coarse[1] * join, fine[2] * keep + coarse[2] * join


def doubled(field):
    rows, lanes = field.shape
    slabs = field.reshape(rows // SLAB, 1, SLAB, lanes)
    return jnp.broadcast_to(slabs, (rows // SLAB, 2, SLAB, lanes)).reshape(2 * rows, lanes)


def with_ones(values, weight=1.0):
    if weight != 1.0:
        values = values * jnp.bfloat16(weight)
    return jnp.concatenate([values, jnp.full(values.shape, weight, jnp.bfloat16)], axis=1)


def local_kernel(
    q_ref, k_ref, v_ref, one_ref, edge_q, two_q, three_q, four_q, state,
    scratch, near_hold, coarse_hold,
):
    rows = q_ref.shape[0]
    blocks = rows // BLOCK
    pairs = scratch.shape[0]
    spill(q_ref, scratch)
    fine, one_q = [], []
    for pair in range(pairs):
        lanes = pl.ds(pair * PAIR, PAIR)
        ladder = [[], [], [], [], []]
        for block in range(blocks):
            slabs = slabs_of(scratch.at[pair], block)
            ladder[0].append(joined(slabs))
            for level in range(1, LEVELS + 1):
                slabs = pooled_slabs(slabs)
                ladder[level] += slabs
        edge_q[0, :, lanes] = ladder[0][0]
        edge_q[1, :, lanes] = ladder[0][-1]
        two_q[:, lanes] = joined(ladder[2])
        three_q[:, lanes] = joined(ladder[3])
        four_q[:, lanes] = joined(ladder[4])
        fine.append(ladder[0])
        one_q.append([joined(ladder[1][n : n + FAN]) for n in range(0, len(ladder[1]), FAN)])
    windows = [(max(n - 1, 0) * BLOCK, min(n + 2, blocks) * BLOCK) for n in range(blocks)]
    tops = {}
    for pair in range(pairs):
        lanes = pl.ds(pair * PAIR, PAIR)
        for half in range(blocks // 2):
            there = pl.ds((half ^ 1) * BLOCK, BLOCK)
            tops[pair, half] = score(
                one_q[pair][half], one_ref[0, there, lanes], coarse_hold.at[pair, half]
            )
            for block in (2 * half, 2 * half + 1):
                low, high = windows[block]
                hold = near_hold.at[pair, block, :, : high - low]
                tops[pair, half, block] = score(fine[pair][block], k_ref[low:high, lanes], hold)
    for pair in range(pairs):
        lanes = pl.ds(pair * PAIR, PAIR)
        for half in range(blocks // 2):
            there = pl.ds((half ^ 1) * BLOCK, BLOCK)
            coarse = weigh(
                coarse_hold.at[pair, half], tops[pair, half], with_ones(one_ref[1, there, lanes])
            )
            for block in (2 * half, 2 * half + 1):
                low, high = windows[block]
                hold = near_hold.at[pair, block, :, : high - low]
                near = weigh(hold, tops[pair, half, block], with_ones(v_ref[low:high, lanes]))
                part = slice((block - 2 * half) * BLOCK // 2, (block - 2 * half + 1) * BLOCK // 2)
                done = merged(near, [doubled(x[part]) for x in coarse])
                for index, field in enumerate(done):
                    state[index, block * BLOCK : (block + 1) * BLOCK, lanes] = field


def relay_kernel(first_ref, three_ref, six_ref, four_ref, relay_ref, two_ref, near_ref, scratch):
    eighth, sixteenth = three_ref.shape[1], four_ref.shape[1]
    relay_ref[:, :eighth, :] = three_ref[...]
    relay_ref[:, eighth : eighth + sixteenth, :] = six_ref[...]
    relay_ref[:, eighth + sixteenth :, :] = four_ref[...]
    inner = first_ref.shape[1] - BLOCK
    two_ref[:, :inner, :] = first_ref[:, BLOCK:, :]
    for which in range(2):
        spill(first_ref.at[which, pl.ds(0, BLOCK), :], scratch.at[which])
        for half in range(scratch.shape[1]):
            lanes = pl.ds(half * PAIR, PAIR)
            slabs = slabs_of(scratch.at[which, half], 0)
            two_ref[which, inner:, lanes] = joined(pooled_slabs(pooled_slabs(slabs)))
        near_ref[which] = repooled(repooled(two_ref[which]))


def mid_kernel(edge_q, two_q, state, first_ref, second_ref, two_ref, out, holds):
    rows = state.shape[1]
    blocks = rows // BLOCK
    position = lax.axis_index("seq")
    last = lax.axis_size("seq") - 1
    even = lax.rem(position, 2) == 0
    opens = (position > 0, position < last)
    pairs = two_q.shape[1] // PAIR
    steps = {}
    for pair in range(pairs):
        lanes = pl.ds(pair * PAIR, PAIR)
        inner = [first_ref[which, :BLOCK, lanes] for which in range(2)]
        outer = [second_ref[which, :, lanes] for which in range(2)]
        steps[pair, 2] = (
            score(two_q[:, lanes], two_ref[0, :, lanes], holds.at[pair, 2]),
            with_ones(two_ref[1, :, lanes]),
        )
        for side in range(2):
            halo = [
                jnp.where(even, *((outer[which], inner[which])[:: 1 - 2 * side]))
                for which in range(2)
            ]
            steps[pair, side] = (
                score(edge_q[side, :, lanes], halo[0], holds.at[pair, side], opens[side]),
                with_ones(halo[1]),
            )
    for pair in range(pairs):
        lanes = pl.ds(pair * PAIR, PAIR)
        two = weigh(holds.at[pair, 2], *steps[pair, 2])
        for block in range(blocks):
            here = slice(block * BLOCK, (block + 1) * BLOCK)
            quarter = slice(block * BLOCK // 4, (block + 1) * BLOCK // 4)
            done = merged(
                [state[index, here, lanes] for index in range(3)],
                [doubled(doubled(x[quarter])) for x in two],
            )
            for side, edge in enumerate((0, blocks - 1)):
                if block == edge:
                    done = merged(done, weigh(holds.at[pair, side], *steps[pair, side]))
            for index, field in enumerate(done):
                out[index, here, lanes] = field


def finish_kernel(three_q, four_q, state, four_ref, near_ref, relay_a, relay_b, *refs):
    far, refs = refs[:-7], refs[-7:]
    outs, (attended, three_hold, four_hold) = refs[:-3], refs[-3:]
    rows = state.shape[1]
    blocks = rows // BLOCK
    own = lax.axis_index("head")
    pairs = three_q.shape[1] // PAIR
    eighth = rows // 8
    steps = {}
    for pair in range(pairs):
        lanes = pl.ds(pair * PAIR, PAIR)
        relays = [relay_a[:, :, lanes], relay_b[:, :, lanes]]
        three, ours, theirs, beyond = [], [], [], []
        for which in range(2):
            three.append([relay[which, :eighth] for relay in relays])
            ours.append(
                [four_ref[which, :, lanes], near_ref[which, :, lanes]]
                + [repooled(field) for field in three[which]]
            )
            theirs.append([relay[which, eighth:] for relay in relays])
            beyond.append([field[which, :, lanes] for field in far])
        steps[pair, 3] = (
            score(three_q[:, lanes], jnp.concatenate(three[0], axis=0), three_hold.at[pair]),
            with_ones(jnp.concatenate(three[1], axis=0)),
        )
        steps[pair, 4] = (
            score(
                four_q[:, lanes],
                jnp.concatenate(ours[0] + theirs[0] + beyond[0], axis=0),
                four_hold.at[pair],
            ),
            jnp.concatenate(
                [with_ones(field) for field in ours[1]]
                + [with_ones(field, 2.0) for field in theirs[1]]
                + [with_ones(field) for field in beyond[1]],
                axis=0,
            ),
        )
    for pair in range(pairs):
        lanes = pl.ds(pair * PAIR, PAIR)
        four = weigh(four_hold.at[pair], *steps[pair, 4])
        now = merged(weigh(three_hold.at[pair], *steps[pair, 3]), [doubled(x) for x in four])
        for block in range(blocks):
            here = slice(block * BLOCK, (block + 1) * BLOCK)
            eighth_here = slice(block * BLOCK // 8, (block + 1) * BLOCK // 8)
            _, numer, rowsum = merged(
                [state[index, here, lanes] for index in range(3)],
                [doubled(doubled(doubled(x[eighth_here]))) for x in now],
            )
            attended[block, :, lanes] = (numer / rowsum).astype(jnp.bfloat16)
    for step, out in enumerate(outs):
        out[...] = attended[own ^ step]


def project_kernel(*refs):
    parts, (weight_ref, out_hbm, scratch, staged, sems) = refs[:-5], refs[-5:]
    own = lax.axis_index("head")
    features = parts[0].shape[1]
    chunk = staged.shape[2]
    copies = []
    for index in range(staged.shape[0]):
        columns = pl.ds(index * chunk, chunk)
        total = None
        for step, part in enumerate(parts):
            start = pl.multiple_of((own ^ step) * features, features)
            product = jnp.dot(
                part[...],
                weight_ref[pl.ds(start, features), columns],
                preferred_element_type=jnp.float32,
            )
            total = product if total is None else total + product
        for half in range(chunk // PAIR):
            lanes = slice(half * PAIR, (half + 1) * PAIR)
            scratch[index, half] = total[:, lanes]
            for i in range(SLAB):
                staged[index, i * FAN : (i + 1) * FAN, lanes] = scratch[
                    index, half, pl.ds(i, FAN, stride=SLAB), :
                ].astype(jnp.bfloat16)
        copy = pltpu.make_async_copy(staged.at[index], out_hbm.at[:, columns], sems.at[index])
        copy.start()
        copies.append(copy)
    for copy in copies:
        copy.wait()


def repool_outside(field):
    which, rows, lanes = field.shape
    slabs = field.astype(jnp.float32).reshape(which, rows // (2 * SLAB), 2, SLAB, lanes)
    sums = (slabs[:, :, 0] + slabs[:, :, 1]) * root_half
    return sums.reshape(which, rows // 2, lanes).astype(jnp.bfloat16)


def swapped(block, axis, mask):
    return lax.ppermute(block, axis, [(i, i ^ mask) for i in range(lax.axis_size(axis))])


def across(block, axis):
    count = lax.axis_size(axis)
    route = []
    for low in range(1, count - 1, 2):
        route += [(low, low + 1), (low + 1, low)]
    return lax.ppermute(block, axis, route)


def per_device(queries, key_vectors, value_vectors, out_weight):
    rows, features = queries.shape[1:]
    queries, key_vectors, value_vectors = [
        pltpu.with_memory_space_constraint(x, pltpu.HBM)
        for x in (queries, key_vectors, value_vectors)
    ]
    pairs = features // PAIR
    seq_count, head_count = lax.axis_size("seq"), lax.axis_size("head")
    bf16 = lambda *shape: jax.ShapeDtypeStruct(shape, jnp.bfloat16)
    params = pltpu.CompilerParams(vmem_limit_bytes=32 * 1024 * 1024)

    hbm = pl.BlockSpec(memory_space=pltpu.HBM)
    vmem = pl.BlockSpec(memory_space=pltpu.VMEM)
    keys, values, ours, first, one, two = pl.pallas_call(
        pool_kernel,
        in_specs=[hbm] * 3,
        out_shape=[
            bf16(rows, features),
            bf16(rows, features),
            bf16(rows, features),
            bf16(2, BLOCK + rows // 4 - BLOCK // 4, features),
            bf16(2, rows // 2, features),
            bf16(2, rows // 4, features),
        ],
        scratch_shapes=[
            pltpu.VMEM((2, rows // BLOCK, pairs, BLOCK, PAIR), jnp.float32),
            pltpu.SemaphoreType.DMA((2, rows // BLOCK)),
            pltpu.SemaphoreType.DMA((1,)),
        ],
        compiler_params=params,
        name="pool",
    )(key_vectors, value_vectors, queries)
    second, three, four = pl.pallas_call(
        deeper_kernel,
        out_shape=[
            bf16(2, BLOCK, features),
            bf16(2, rows // 8, features),
            bf16(2, rows // 16, features),
        ],
        compiler_params=params,
        cost_estimate=pl.CostEstimate(flops=2**31, bytes_accessed=2**23, transcendentals=0),
        name="deeper",
    )(keys, values, two)

    first_in = swapped(first, "seq", 1)
    second_in = across(second, "seq")
    fours_in = [swapped(four, "seq", mask) for mask in (6, 4)]
    three_in = swapped(three, "seq", 2)
    relayed, two_in, near = pl.pallas_call(
        relay_kernel,
        out_shape=[
            bf16(2, rows // 4, features),
            bf16(2, rows // 4, features),
            bf16(2, rows // 16, features),
        ],
        scratch_shapes=[pltpu.VMEM((2, pairs, BLOCK, PAIR), jnp.float32)],
        compiler_params=params,
        name="relay",
    )(first_in, three_in, *fours_in)
    relayed_in = swapped(relayed, "seq", 1)

    edge_q, two_q, three_q, four_q, state = pl.pallas_call(
        local_kernel,
        out_shape=[
            bf16(2, BLOCK, features),
            bf16(rows // 4, features),
            bf16(rows // 8, features),
            bf16(rows // 16, features),
            jax.ShapeDtypeStruct((3, rows, features), jnp.float32),
        ],
        scratch_shapes=[
            pltpu.VMEM((pairs, rows, PAIR), jnp.float32),
            pltpu.VMEM((pairs, rows // BLOCK, 2 * BLOCK, 3 * BLOCK), jnp.float32),
            pltpu.VMEM((pairs, rows // BLOCK // 2, 2 * BLOCK, BLOCK), jnp.float32),
        ],
        compiler_params=params,
        name="local",
    )(ours, keys, values, one)

    state = pl.pallas_call(
        mid_kernel,
        out_shape=jax.ShapeDtypeStruct((3, rows, features), jnp.float32),
        input_output_aliases={2: 0},
        scratch_shapes=[pltpu.VMEM((pairs, 3, 2 * BLOCK, BLOCK), jnp.float32)],
        compiler_params=params,
        name="mid",
    )(edge_q, two_q, state, first_in, second_in, two_in)

    far = []
    known = 8
    if known < seq_count:
        eighth = rows // 8
        group = [four, near, repool_outside(three_in), repool_outside(relayed_in[:, :eighth])]
        group = jnp.concatenate(group + fours_in + [relayed_in[:, eighth:]], axis=1)
        while known < seq_count:
            fresh = swapped(group, "seq", known)
            far.append(fresh)
            group = jnp.concatenate([group, fresh], axis=1)
            known *= 2

    outs = pl.pallas_call(
        finish_kernel,
        out_shape=[bf16(BLOCK, features) for _ in range(head_count)],
        scratch_shapes=[
            pltpu.VMEM((rows // BLOCK, BLOCK, features), jnp.bfloat16),
            pltpu.VMEM((pairs, rows // 4, BLOCK), jnp.float32),
            pltpu.VMEM((pairs, rows // 8, rows // 16 * seq_count), jnp.float32),
        ],
        compiler_params=params,
        name="finish",
    )(three_q, four_q, state, four, near, relayed, relayed_in, *far)

    parts = [part if step == 0 else swapped(part, "head", step) for step, part in enumerate(outs)]
    width = out_weight.shape[1]
    chunk = 2 * PAIR
    result = pl.pallas_call(
        project_kernel,
        in_specs=[vmem] * (len(parts) + 1),
        out_specs=hbm,
        out_shape=bf16(BLOCK, width),
        scratch_shapes=[
            pltpu.VMEM((width // chunk, 2, BLOCK, PAIR), jnp.float32),
            pltpu.VMEM((width // chunk, BLOCK, chunk), jnp.bfloat16),
            pltpu.SemaphoreType.DMA((width // chunk,)),
        ],
        compiler_params=params,
        name="project",
    )(*parts, out_weight)
    return result[None]


def solution(mesh):
    return jax.shard_map(
        per_device,
        mesh=mesh,
        in_specs=(P(None, "seq", "head"), P(None, "seq", "head"), P(None, "seq", "head"), P()),
        out_specs=P(None, ("seq", "head"), None),
        check_vma=False,
    )
```

```python
import jax
import jax.numpy as jnp
from jax import lax
from jax.experimental import pallas as pl
from jax.experimental.pallas import tpu as pltpu
from jax.sharding import PartitionSpec as P

HD = 64
BLOCK = 128
LEVELS = 4
SLAB = 8
PAIR = 2 * HD

neg_fill = -1e30
root_half = 0.7071067811865476
log2_scale = HD**-0.5 * 1.4426950408889634

FAN = 2**LEVELS


def slabs_of(scratch, block):
    return [scratch[pl.ds(BLOCK * block + j, SLAB, stride=FAN), :] for j in range(FAN)]


def pooled_slabs(slabs):
    return [
        ((low + high) * root_half).astype(jnp.bfloat16).astype(jnp.float32)
        for low, high in zip(slabs[0::2], slabs[1::2])
    ]


def joined(slabs):
    return jnp.concatenate(slabs, axis=0).astype(jnp.bfloat16)


def spill(source, scratch):
    for half in range(scratch.shape[0]):
        scratch[half] = source[:, half * PAIR : (half + 1) * PAIR].astype(jnp.float32)


def pool_kernel(
    k_hbm, v_hbm, q_hbm, k_ref, v_ref, q_ref, first_ref, one_ref, two_ref, scratch, sems, q_sem
):
    rows = k_ref.shape[0]
    blocks = rows // BLOCK
    arrivals = []
    for block in range(blocks):
        here = pl.ds(block * BLOCK, BLOCK)
        for which, (source, target) in enumerate(((k_hbm, k_ref), (v_hbm, v_ref))):
            copy = pltpu.make_async_copy(
                source.at[0, here, :], target.at[here, :], sems.at[which, block]
            )
            copy.start()
            arrivals.append((block, which, target, copy))
    q_copy = pltpu.make_async_copy(q_hbm.at[0], q_ref, q_sem.at[0])
    q_copy.start()
    even = lax.rem(lax.axis_index("seq"), 2) == 0
    for block, which, ref, copy in arrivals:
        copy.wait()
        here = pl.ds(block * BLOCK, BLOCK)
        spill(ref.at[here, :], scratch.at[which, block])
        for half in range(scratch.shape[2]):
            lanes = pl.ds(half * PAIR, PAIR)
            one = pooled_slabs(slabs_of(scratch.at[which, block, half], 0))
            one_ref[which, pl.ds(block * BLOCK // 2, BLOCK // 2), lanes] = joined(one)
            two_ref[which, pl.ds(block * BLOCK // 4, BLOCK // 4), lanes] = joined(pooled_slabs(one))
    inner = rows // 4 - BLOCK // 4
    for which, ref in enumerate((k_ref, v_ref)):
        first_ref[which, :BLOCK, :] = jnp.where(even, ref[rows - BLOCK :, :], ref[:BLOCK, :])
        first_ref[which, BLOCK:, :] = jnp.where(
            even, two_ref[which, :inner, :], two_ref[which, BLOCK // 4 :, :]
        )
    q_copy.wait()


def repooled(field):
    rows, lanes = field.shape
    slabs = field.astype(jnp.float32).reshape(rows // (2 * SLAB), 2, SLAB, lanes)
    return ((slabs[:, 0] + slabs[:, 1]) * root_half).reshape(rows // 2, lanes).astype(jnp.bfloat16)


def deeper_kernel(k_ref, v_ref, two_ref, second_ref, three_ref, four_ref):
    rows = k_ref.shape[0]
    even = lax.rem(lax.axis_index("seq"), 2) == 0
    for which, ref in enumerate((k_ref, v_ref)):
        second_ref[which] = jnp.where(even, ref[:BLOCK, :], ref[rows - BLOCK :, :])
        three = repooled(two_ref[which])
        three_ref[which] = three
        four_ref[which] = repooled(three)


def repooled(field):
    rows, lanes = field.shape
    slabs = field.astype(jnp.float32).reshape(rows // (2 * SLAB), 2, SLAB, lanes)
    return ((slabs[:, 0] + slabs[:, 1]) * root_half).reshape(rows // 2, lanes).astype(jnp.bfloat16)


def score(queries, keys, hold, is_open=None):
    rows = queries.shape[0]
    low = lax.broadcasted_iota(jnp.int32, (rows, PAIR), 1) < HD
    zero = jnp.zeros_like(queries)
    both = jnp.concatenate([jnp.where(low, queries, zero), jnp.where(low, zero, queries)], axis=0)
    raw = lax.dot_general(both, keys, (((1,), (1,)), ((), ())), preferred_element_type=jnp.float32)
    if is_open is not None:
        raw = jnp.where(is_open, raw, neg_fill)
    hold[...] = raw
    return jnp.max(raw, axis=1, keepdims=True)


def weigh(hold, top, values):
    rows = top.shape[0] // 2
    low = lax.broadcasted_iota(jnp.int32, (rows, PAIR), 1) < HD
    weights = jnp.exp2((hold[...] - top) * log2_scale).astype(jnp.bfloat16)
    result = jnp.dot(weights, values, preferred_element_type=jnp.float32)
    return (
        log2_scale * jnp.where(low, top[:rows], top[rows:]),
        jnp.where(low, result[:rows, :PAIR], result[rows:, :PAIR]),
        jnp.where(low, result[:rows, PAIR:], result[rows:, PAIR:]),
    )


def merged(fine, coarse):
    top = jnp.maximum(fine[0], coarse[0])
    keep = jnp.exp2(fine[0] - top)
    join = jnp.exp2(coarse[0] - top)
    return top, fine[1] * keep + coarse[1] * join, fine[2] * keep + coarse[2] * join


def doubled(field):
    rows, lanes = field.shape
    slabs = field.reshape(rows // SLAB, 1, SLAB, lanes)
    return jnp.broadcast_to(slabs, (rows // SLAB, 2, SLAB, lanes)).reshape(2 * rows, lanes)


def with_ones(values, weight=1.0):
    if weight != 1.0:
        values = values * jnp.bfloat16(weight)
    return jnp.concatenate([values, jnp.full(values.shape, weight, jnp.bfloat16)], axis=1)


def local_kernel(
    q_ref, k_ref, v_ref, one_ref, edge_q, two_q, three_q, four_q, state,
    scratch, near_hold, coarse_hold,
):
    rows = q_ref.shape[0]
    blocks = rows // BLOCK
    pairs = scratch.shape[0]
    spill(q_ref, scratch)
    fine, one_q = [], []
    for pair in range(pairs):
        lanes = pl.ds(pair * PAIR, PAIR)
        ladder = [[], [], [], [], []]
        for block in range(blocks):
            slabs = slabs_of(scratch.at[pair], block)
            ladder[0].append(joined(slabs))
            for level in range(1, LEVELS + 1):
                slabs = pooled_slabs(slabs)
                ladder[level] += slabs
        edge_q[0, :, lanes] = ladder[0][0]
        edge_q[1, :, lanes] = ladder[0][-1]
        two_q[:, lanes] = joined(ladder[2])
        three_q[:, lanes] = joined(ladder[3])
        four_q[:, lanes] = joined(ladder[4])
        fine.append(ladder[0])
        one_q.append([joined(ladder[1][n : n + FAN]) for n in range(0, len(ladder[1]), FAN)])
    windows = [(max(n - 1, 0) * BLOCK, min(n + 2, blocks) * BLOCK) for n in range(blocks)]
    tops = {}
    for pair in range(pairs):
        lanes = pl.ds(pair * PAIR, PAIR)
        for half in range(blocks // 2):
            there = pl.ds((half ^ 1) * BLOCK, BLOCK)
            tops[pair, half] = score(
                one_q[pair][half], one_ref[0, there, lanes], coarse_hold.at[pair, half]
            )
            for block in (2 * half, 2 * half + 1):
                low, high = windows[block]
                hold = near_hold.at[pair, block, :, : high - low]
                tops[pair, half, block] = score(fine[pair][block], k_ref[low:high, lanes], hold)
    for pair in range(pairs):
        lanes = pl.ds(pair * PAIR, PAIR)
        for half in range(blocks // 2):
            there = pl.ds((half ^ 1) * BLOCK, BLOCK)
            coarse = weigh(
                coarse_hold.at[pair, half], tops[pair, half], with_ones(one_ref[1, there, lanes])
            )
            for block in (2 * half, 2 * half + 1):
                low, high = windows[block]
                hold = near_hold.at[pair, block, :, : high - low]
                near = weigh(hold, tops[pair, half, block], with_ones(v_ref[low:high, lanes]))
                part = slice((block - 2 * half) * BLOCK // 2, (block - 2 * half + 1) * BLOCK // 2)
                done = merged(near, [doubled(x[part]) for x in coarse])
                for index, field in enumerate(done):
                    state[index, block * BLOCK : (block + 1) * BLOCK, lanes] = field


def relay_kernel(first_ref, packet_ref, four_ref, relay_ref, two_ref, near_ref, scratch):
    held = packet_ref.shape[1]
    relay_ref[:, :held, :] = packet_ref[...]
    relay_ref[:, held:, :] = four_ref[...]
    inner = first_ref.shape[1] - BLOCK
    two_ref[:, :inner, :] = first_ref[:, BLOCK:, :]
    for which in range(2):
        spill(first_ref.at[which, pl.ds(0, BLOCK), :], scratch.at[which])
        for half in range(scratch.shape[1]):
            lanes = pl.ds(half * PAIR, PAIR)
            slabs = slabs_of(scratch.at[which, half], 0)
            two_ref[which, inner:, lanes] = joined(pooled_slabs(pooled_slabs(slabs)))
        near_ref[which] = repooled(repooled(two_ref[which]))


def mid_kernel(edge_q, two_q, state, first_ref, second_ref, two_ref, out, holds):
    rows = state.shape[1]
    blocks = rows // BLOCK
    position = lax.axis_index("seq")
    last = lax.axis_size("seq") - 1
    even = lax.rem(position, 2) == 0
    opens = (position > 0, position < last)
    pairs = two_q.shape[1] // PAIR
    steps = {}
    for pair in range(pairs):
        lanes = pl.ds(pair * PAIR, PAIR)
        inner = [first_ref[which, :BLOCK, lanes] for which in range(2)]
        outer = [second_ref[which, :, lanes] for which in range(2)]
        steps[pair, 2] = (
            score(two_q[:, lanes], two_ref[0, :, lanes], holds.at[pair, 2]),
            with_ones(two_ref[1, :, lanes]),
        )
        for side in range(2):
            halo = [
                jnp.where(even, *((outer[which], inner[which])[:: 1 - 2 * side]))
                for which in range(2)
            ]
            steps[pair, side] = (
                score(edge_q[side, :, lanes], halo[0], holds.at[pair, side], opens[side]),
                with_ones(halo[1]),
            )
    for pair in range(pairs):
        lanes = pl.ds(pair * PAIR, PAIR)
        two = weigh(holds.at[pair, 2], *steps[pair, 2])
        for block in range(blocks):
            here = slice(block * BLOCK, (block + 1) * BLOCK)
            quarter = slice(block * BLOCK // 4, (block + 1) * BLOCK // 4)
            done = merged(
                [state[index, here, lanes] for index in range(3)],
                [doubled(doubled(x[quarter])) for x in two],
            )
            for side, edge in enumerate((0, blocks - 1)):
                if block == edge:
                    done = merged(done, weigh(holds.at[pair, side], *steps[pair, side]))
            for index, field in enumerate(done):
                out[index, here, lanes] = field


def finish_kernel(three_q, four_q, state, four_ref, near_ref, relay_a, relay_b, *refs):
    far, refs = refs[:-7], refs[-7:]
    outs, (attended, three_hold, four_hold) = refs[:-3], refs[-3:]
    rows = state.shape[1]
    blocks = rows // BLOCK
    own = lax.axis_index("head")
    pairs = three_q.shape[1] // PAIR
    eighth = rows // 8
    steps = {}
    for pair in range(pairs):
        lanes = pl.ds(pair * PAIR, PAIR)
        relays = [relay_a[:, :, lanes], relay_b[:, :, lanes]]
        three, ours, theirs, beyond = [], [], [], []
        for which in range(2):
            three.append([relay[which, :eighth] for relay in relays])
            ours.append(
                [four_ref[which, :, lanes], near_ref[which, :, lanes]]
                + [repooled(field) for field in three[which]]
            )
            theirs.append([relay[which, eighth:] for relay in relays])
            beyond.append([field[which, :, lanes] for field in far])
        steps[pair, 3] = (
            score(three_q[:, lanes], jnp.concatenate(three[0], axis=0), three_hold.at[pair]),
            with_ones(jnp.concatenate(three[1], axis=0)),
        )
        steps[pair, 4] = (
            score(
                four_q[:, lanes],
                jnp.concatenate(ours[0] + theirs[0] + beyond[0], axis=0),
                four_hold.at[pair],
            ),
            jnp.concatenate(
                [with_ones(field) for field in ours[1]]
                + [with_ones(field, 2.0) for field in theirs[1]]
                + [with_ones(field) for field in beyond[1]],
                axis=0,
            ),
        )
    for pair in range(pairs):
        lanes = pl.ds(pair * PAIR, PAIR)
        four = weigh(four_hold.at[pair], *steps[pair, 4])
        now = merged(weigh(three_hold.at[pair], *steps[pair, 3]), [doubled(x) for x in four])
        for block in range(blocks):
            here = slice(block * BLOCK, (block + 1) * BLOCK)
            eighth_here = slice(block * BLOCK // 8, (block + 1) * BLOCK // 8)
            _, numer, rowsum = merged(
                [state[index, here, lanes] for index in range(3)],
                [doubled(doubled(doubled(x[eighth_here]))) for x in now],
            )
            attended[block, :, lanes] = (numer / rowsum).astype(jnp.bfloat16)
    for step, out in enumerate(outs):
        out[...] = attended[own ^ step]


def project_kernel(*refs):
    parts, (weight_ref, out_hbm, scratch, staged, sems) = refs[:-5], refs[-5:]
    own = lax.axis_index("head")
    features = parts[0].shape[1]
    chunk = staged.shape[2]
    copies = []
    for index in range(staged.shape[0]):
        columns = pl.ds(index * chunk, chunk)
        total = None
        for step, part in enumerate(parts):
            start = pl.multiple_of((own ^ step) * features, features)
            product = jnp.dot(
                part[...],
                weight_ref[pl.ds(start, features), columns],
                preferred_element_type=jnp.float32,
            )
            total = product if total is None else total + product
        for half in range(chunk // PAIR):
            lanes = slice(half * PAIR, (half + 1) * PAIR)
            scratch[index, half] = total[:, lanes]
            for i in range(SLAB):
                staged[index, i * FAN : (i + 1) * FAN, lanes] = scratch[
                    index, half, pl.ds(i, FAN, stride=SLAB), :
                ].astype(jnp.bfloat16)
        copy = pltpu.make_async_copy(staged.at[index], out_hbm.at[:, columns], sems.at[index])
        copy.start()
        copies.append(copy)
    for copy in copies:
        copy.wait()


def repool_outside(field):
    which, rows, lanes = field.shape
    slabs = field.astype(jnp.float32).reshape(which, rows // (2 * SLAB), 2, SLAB, lanes)
    sums = (slabs[:, :, 0] + slabs[:, :, 1]) * root_half
    return sums.reshape(which, rows // 2, lanes).astype(jnp.bfloat16)


def swapped(block, axis, mask):
    return lax.ppermute(block, axis, [(i, i ^ mask) for i in range(lax.axis_size(axis))])


def across(block, axis):
    count = lax.axis_size(axis)
    route = []
    for low in range(1, count - 1, 2):
        route += [(low, low + 1), (low + 1, low)]
    return lax.ppermute(block, axis, route)


def per_device(queries, key_vectors, value_vectors, out_weight):
    rows, features = queries.shape[1:]
    queries, key_vectors, value_vectors = [
        pltpu.with_memory_space_constraint(x, pltpu.HBM)
        for x in (queries, key_vectors, value_vectors)
    ]
    pairs = features // PAIR
    seq_count, head_count = lax.axis_size("seq"), lax.axis_size("head")
    bf16 = lambda *shape: jax.ShapeDtypeStruct(shape, jnp.bfloat16)
    params = pltpu.CompilerParams(vmem_limit_bytes=32 * 1024 * 1024)

    hbm = pl.BlockSpec(memory_space=pltpu.HBM)
    vmem = pl.BlockSpec(memory_space=pltpu.VMEM)
    keys, values, ours, first, one, two = pl.pallas_call(
        pool_kernel,
        in_specs=[hbm] * 3,
        out_shape=[
            bf16(rows, features),
            bf16(rows, features),
            bf16(rows, features),
            bf16(2, BLOCK + rows // 4 - BLOCK // 4, features),
            bf16(2, rows // 2, features),
            bf16(2, rows // 4, features),
        ],
        scratch_shapes=[
            pltpu.VMEM((2, rows // BLOCK, pairs, BLOCK, PAIR), jnp.float32),
            pltpu.SemaphoreType.DMA((2, rows // BLOCK)),
            pltpu.SemaphoreType.DMA((1,)),
        ],
        compiler_params=params,
        name="pool",
    )(key_vectors, value_vectors, queries)
    second, three, four = pl.pallas_call(
        deeper_kernel,
        out_shape=[
            bf16(2, BLOCK, features),
            bf16(2, rows // 8, features),
            bf16(2, rows // 16, features),
        ],
        compiler_params=params,
        cost_estimate=pl.CostEstimate(flops=2**31, bytes_accessed=2**23, transcendentals=0),
        name="deeper",
    )(keys, values, two)

    first_in = swapped(first, "seq", 1)
    second_in = across(second, "seq")
    four_in = swapped(four, "seq", 4)
    packet_in = swapped(jnp.concatenate([three, four_in], axis=1), "seq", 2)
    relayed, two_in, near = pl.pallas_call(
        relay_kernel,
        out_shape=[
            bf16(2, rows // 4, features),
            bf16(2, rows // 4, features),
            bf16(2, rows // 16, features),
        ],
        scratch_shapes=[pltpu.VMEM((2, pairs, BLOCK, PAIR), jnp.float32)],
        compiler_params=params,
        name="relay",
    )(first_in, packet_in, four_in)
    relayed_in = swapped(relayed, "seq", 1)

    edge_q, two_q, three_q, four_q, state = pl.pallas_call(
        local_kernel,
        out_shape=[
            bf16(2, BLOCK, features),
            bf16(rows // 4, features),
            bf16(rows // 8, features),
            bf16(rows // 16, features),
            jax.ShapeDtypeStruct((3, rows, features), jnp.float32),
        ],
        scratch_shapes=[
            pltpu.VMEM((pairs, rows, PAIR), jnp.float32),
            pltpu.VMEM((pairs, rows // BLOCK, 2 * BLOCK, 3 * BLOCK), jnp.float32),
            pltpu.VMEM((pairs, rows // BLOCK // 2, 2 * BLOCK, BLOCK), jnp.float32),
        ],
        compiler_params=params,
        name="local",
    )(ours, keys, values, one)

    state = pl.pallas_call(
        mid_kernel,
        out_shape=jax.ShapeDtypeStruct((3, rows, features), jnp.float32),
        input_output_aliases={2: 0},
        scratch_shapes=[pltpu.VMEM((pairs, 3, 2 * BLOCK, BLOCK), jnp.float32)],
        compiler_params=params,
        name="mid",
    )(edge_q, two_q, state, first_in, second_in, two_in)

    far = []
    known = 8
    if known < seq_count:
        eighth = rows // 8
        group = [four, near, repool_outside(relayed[:, :eighth]), repool_outside(relayed_in[:, :eighth])]
        group = jnp.concatenate(group + [relayed[:, eighth:], relayed_in[:, eighth:]], axis=1)
        while known < seq_count:
            fresh = swapped(group, "seq", known)
            far.append(fresh)
            group = jnp.concatenate([group, fresh], axis=1)
            known *= 2

    outs = pl.pallas_call(
        finish_kernel,
        out_shape=[bf16(BLOCK, features) for _ in range(head_count)],
        scratch_shapes=[
            pltpu.VMEM((rows // BLOCK, BLOCK, features), jnp.bfloat16),
            pltpu.VMEM((pairs, rows // 4, BLOCK), jnp.float32),
            pltpu.VMEM((pairs, rows // 8, rows // 16 * seq_count), jnp.float32),
        ],
        compiler_params=params,
        name="finish",
    )(three_q, four_q, state, four, near, relayed, relayed_in, *far)

    parts = [part if step == 0 else swapped(part, "head", step) for step, part in enumerate(outs)]
    width = out_weight.shape[1]
    chunk = 2 * PAIR
    result = pl.pallas_call(
        project_kernel,
        in_specs=[vmem] * (len(parts) + 1),
        out_specs=hbm,
        out_shape=bf16(BLOCK, width),
        scratch_shapes=[
            pltpu.VMEM((width // chunk, 2, BLOCK, PAIR), jnp.float32),
            pltpu.VMEM((width // chunk, BLOCK, chunk), jnp.bfloat16),
            pltpu.SemaphoreType.DMA((width // chunk,)),
        ],
        compiler_params=params,
        name="project",
    )(*parts, out_weight)
    return result[None]


def solution(mesh):
    return jax.shard_map(
        per_device,
        mesh=mesh,
        in_specs=(P(None, "seq", "head"), P(None, "seq", "head"), P(None, "seq", "head"), P()),
        out_specs=P(None, ("seq", "head"), None),
        check_vma=False,
    )
```

```python
import jax
import jax.numpy as jnp
from jax import lax
from jax.experimental import pallas as pl
from jax.experimental.pallas import tpu as pltpu
from jax.sharding import PartitionSpec as P

HD = 64
BLOCK = 128
LEVELS = 4
SLAB = 8
PAIR = 2 * HD

neg_fill = -1e30
root_half = 0.7071067811865476
log2_scale = HD**-0.5 * 1.4426950408889634

FAN = 2**LEVELS


def slabs_of(scratch, block):
    return [scratch[pl.ds(BLOCK * block + j, SLAB, stride=FAN), :] for j in range(FAN)]


def pooled_slabs(slabs):
    return [
        ((low + high) * root_half).astype(jnp.bfloat16).astype(jnp.float32)
        for low, high in zip(slabs[0::2], slabs[1::2])
    ]


def joined(slabs):
    return jnp.concatenate(slabs, axis=0).astype(jnp.bfloat16)


def spill(source, scratch):
    for half in range(scratch.shape[0]):
        scratch[half] = source[:, half * PAIR : (half + 1) * PAIR].astype(jnp.float32)


def pool_kernel(
    k_hbm, v_hbm, q_hbm, k_ref, v_ref, q_ref, first_ref, one_ref, two_ref, scratch, sems, q_sem
):
    rows = k_ref.shape[0]
    blocks = rows // BLOCK
    arrivals = []
    for block in range(blocks):
        here = pl.ds(block * BLOCK, BLOCK)
        for which, (source, target) in enumerate(((k_hbm, k_ref), (v_hbm, v_ref))):
            copy = pltpu.make_async_copy(
                source.at[0, here, :], target.at[here, :], sems.at[which, block]
            )
            copy.start()
            arrivals.append((block, which, target, copy))
    q_copy = pltpu.make_async_copy(q_hbm.at[0], q_ref, q_sem.at[0])
    q_copy.start()
    even = lax.rem(lax.axis_index("seq"), 2) == 0
    for block, which, ref, copy in arrivals:
        copy.wait()
        here = pl.ds(block * BLOCK, BLOCK)
        spill(ref.at[here, :], scratch.at[which, block])
        for half in range(scratch.shape[2]):
            lanes = pl.ds(half * PAIR, PAIR)
            one = pooled_slabs(slabs_of(scratch.at[which, block, half], 0))
            one_ref[which, pl.ds(block * BLOCK // 2, BLOCK // 2), lanes] = joined(one)
            two_ref[which, pl.ds(block * BLOCK // 4, BLOCK // 4), lanes] = joined(pooled_slabs(one))
    inner = rows // 4 - BLOCK // 4
    for which, ref in enumerate((k_ref, v_ref)):
        first_ref[which, :BLOCK, :] = jnp.where(even, ref[rows - BLOCK :, :], ref[:BLOCK, :])
        first_ref[which, BLOCK:, :] = jnp.where(
            even, two_ref[which, :inner, :], two_ref[which, BLOCK // 4 :, :]
        )
    q_copy.wait()


def repooled(field):
    rows, lanes = field.shape
    slabs = field.astype(jnp.float32).reshape(rows // (2 * SLAB), 2, SLAB, lanes)
    return ((slabs[:, 0] + slabs[:, 1]) * root_half).reshape(rows // 2, lanes).astype(jnp.bfloat16)


def deeper_kernel(k_ref, v_ref, two_ref, second_ref, three_ref, four_ref):
    rows = k_ref.shape[0]
    even = lax.rem(lax.axis_index("seq"), 2) == 0
    for which, ref in enumerate((k_ref, v_ref)):
        second_ref[which] = jnp.where(even, ref[:BLOCK, :], ref[rows - BLOCK :, :])
        three = repooled(two_ref[which])
        three_ref[which] = three
        four_ref[which] = repooled(three)


def repooled(field):
    rows, lanes = field.shape
    slabs = field.astype(jnp.float32).reshape(rows // (2 * SLAB), 2, SLAB, lanes)
    return ((slabs[:, 0] + slabs[:, 1]) * root_half).reshape(rows // 2, lanes).astype(jnp.bfloat16)


def score(queries, keys, hold, is_open=None):
    rows = queries.shape[0]
    low = lax.broadcasted_iota(jnp.int32, (rows, PAIR), 1) < HD
    zero = jnp.zeros_like(queries)
    both = jnp.concatenate([jnp.where(low, queries, zero), jnp.where(low, zero, queries)], axis=0)
    raw = lax.dot_general(both, keys, (((1,), (1,)), ((), ())), preferred_element_type=jnp.float32)
    if is_open is not None:
        raw = jnp.where(is_open, raw, neg_fill)
    hold[...] = raw
    return jnp.max(raw, axis=1, keepdims=True)


def weigh(hold, top, values):
    rows = top.shape[0] // 2
    low = lax.broadcasted_iota(jnp.int32, (rows, PAIR), 1) < HD
    weights = jnp.exp2((hold[...] - top) * log2_scale).astype(jnp.bfloat16)
    result = jnp.dot(weights, values, preferred_element_type=jnp.float32)
    return (
        log2_scale * jnp.where(low, top[:rows], top[rows:]),
        jnp.where(low, result[:rows, :PAIR], result[rows:, :PAIR]),
        jnp.where(low, result[:rows, PAIR:], result[rows:, PAIR:]),
    )


def merged(fine, coarse):
    top = jnp.maximum(fine[0], coarse[0])
    keep = jnp.exp2(fine[0] - top)
    join = jnp.exp2(coarse[0] - top)
    return top, fine[1] * keep + coarse[1] * join, fine[2] * keep + coarse[2] * join


def doubled(field):
    rows, lanes = field.shape
    slabs = field.reshape(rows // SLAB, 1, SLAB, lanes)
    return jnp.broadcast_to(slabs, (rows // SLAB, 2, SLAB, lanes)).reshape(2 * rows, lanes)


def with_ones(values, weight=1.0):
    if weight != 1.0:
        values = values * jnp.bfloat16(weight)
    return jnp.concatenate([values, jnp.full(values.shape, weight, jnp.bfloat16)], axis=1)


def local_kernel(
    q_ref, k_ref, v_ref, one_ref, edge_q, two_q, three_q, four_q, state,
    scratch, near_hold, coarse_hold,
):
    rows = q_ref.shape[0]
    blocks = rows // BLOCK
    pairs = scratch.shape[0]
    spill(q_ref, scratch)
    fine, one_q = [], []
    for pair in range(pairs):
        lanes = pl.ds(pair * PAIR, PAIR)
        ladder = [[], [], [], [], []]
        for block in range(blocks):
            slabs = slabs_of(scratch.at[pair], block)
            ladder[0].append(joined(slabs))
            for level in range(1, LEVELS + 1):
                slabs = pooled_slabs(slabs)
                ladder[level] += slabs
        edge_q[0, :, lanes] = ladder[0][0]
        edge_q[1, :, lanes] = ladder[0][-1]
        two_q[:, lanes] = joined(ladder[2])
        three_q[:, lanes] = joined(ladder[3])
        four_q[:, lanes] = joined(ladder[4])
        fine.append(ladder[0])
        one_q.append([joined(ladder[1][n : n + FAN]) for n in range(0, len(ladder[1]), FAN)])
    windows = [(max(n - 1, 0) * BLOCK, min(n + 2, blocks) * BLOCK) for n in range(blocks)]
    tops = {}
    for pair in range(pairs):
        lanes = pl.ds(pair * PAIR, PAIR)
        for half in range(blocks // 2):
            there = pl.ds((half ^ 1) * BLOCK, BLOCK)
            tops[pair, half] = score(
                one_q[pair][half], one_ref[0, there, lanes], coarse_hold.at[pair, half]
            )
            for block in (2 * half, 2 * half + 1):
                low, high = windows[block]
                hold = near_hold.at[pair, block, :, : high - low]
                tops[pair, half, block] = score(fine[pair][block], k_ref[low:high, lanes], hold)
    for pair in range(pairs):
        lanes = pl.ds(pair * PAIR, PAIR)
        for half in range(blocks // 2):
            there = pl.ds((half ^ 1) * BLOCK, BLOCK)
            coarse = weigh(
                coarse_hold.at[pair, half], tops[pair, half], with_ones(one_ref[1, there, lanes])
            )
            for block in (2 * half, 2 * half + 1):
                low, high = windows[block]
                hold = near_hold.at[pair, block, :, : high - low]
                near = weigh(hold, tops[pair, half, block], with_ones(v_ref[low:high, lanes]))
                part = slice((block - 2 * half) * BLOCK // 2, (block - 2 * half + 1) * BLOCK // 2)
                done = merged(near, [doubled(x[part]) for x in coarse])
                for index, field in enumerate(done):
                    state[index, block * BLOCK : (block + 1) * BLOCK, lanes] = field


def relay_kernel(first_ref, six_ref, four_ref, pack_ref, two_ref, near_ref, scratch):
    sixteenth = four_ref.shape[1]
    pack_ref[:, :sixteenth, :] = six_ref[...]
    pack_ref[:, sixteenth:, :] = four_ref[...]
    inner = first_ref.shape[1] - BLOCK
    two_ref[:, :inner, :] = first_ref[:, BLOCK:, :]
    for which in range(2):
        spill(first_ref.at[which, pl.ds(0, BLOCK), :], scratch.at[which])
        for half in range(scratch.shape[1]):
            lanes = pl.ds(half * PAIR, PAIR)
            slabs = slabs_of(scratch.at[which, half], 0)
            two_ref[which, inner:, lanes] = joined(pooled_slabs(pooled_slabs(slabs)))
        near_ref[which] = repooled(repooled(two_ref[which]))


def join_kernel(pack_ref, three_ref, relay_ref):
    eighth = three_ref.shape[1]
    relay_ref[:, :eighth, :] = three_ref[...]
    relay_ref[:, eighth:, :] = pack_ref[...]


def mid_kernel(edge_q, two_q, state, first_ref, second_ref, two_ref, out, holds):
    rows = state.shape[1]
    blocks = rows // BLOCK
    position = lax.axis_index("seq")
    last = lax.axis_size("seq") - 1
    even = lax.rem(position, 2) == 0
    opens = (position > 0, position < last)
    pairs = two_q.shape[1] // PAIR
    steps = {}
    for pair in range(pairs):
        lanes = pl.ds(pair * PAIR, PAIR)
        inner = [first_ref[which, :BLOCK, lanes] for which in range(2)]
        outer = [second_ref[which, :, lanes] for which in range(2)]
        steps[pair, 2] = (
            score(two_q[:, lanes], two_ref[0, :, lanes], holds.at[pair, 2]),
            with_ones(two_ref[1, :, lanes]),
        )
        for side in range(2):
            halo = [
                jnp.where(even, *((outer[which], inner[which])[:: 1 - 2 * side]))
                for which in range(2)
            ]
            steps[pair, side] = (
                score(edge_q[side, :, lanes], halo[0], holds.at[pair, side], opens[side]),
                with_ones(halo[1]),
            )
    for pair in range(pairs):
        lanes = pl.ds(pair * PAIR, PAIR)
        two = weigh(holds.at[pair, 2], *steps[pair, 2])
        for block in range(blocks):
            here = slice(block * BLOCK, (block + 1) * BLOCK)
            quarter = slice(block * BLOCK // 4, (block + 1) * BLOCK // 4)
            done = merged(
                [state[index, here, lanes] for index in range(3)],
                [doubled(doubled(x[quarter])) for x in two],
            )
            for side, edge in enumerate((0, blocks - 1)):
                if block == edge:
                    done = merged(done, weigh(holds.at[pair, side], *steps[pair, side]))
            for index, field in enumerate(done):
                out[index, here, lanes] = field


def finish_kernel(three_q, four_q, state, four_ref, near_ref, relay_a, relay_b, *refs):
    far, refs = refs[:-7], refs[-7:]
    outs, (attended, three_hold, four_hold) = refs[:-3], refs[-3:]
    rows = state.shape[1]
    blocks = rows // BLOCK
    own = lax.axis_index("head")
    pairs = three_q.shape[1] // PAIR
    eighth = rows // 8
    steps = {}
    for pair in range(pairs):
        lanes = pl.ds(pair * PAIR, PAIR)
        relays = [relay_a[:, :, lanes], relay_b[:, :, lanes]]
        three, ours, theirs, beyond = [], [], [], []
        for which in range(2):
            three.append([relay[which, :eighth] for relay in relays])
            ours.append(
                [four_ref[which, :, lanes], near_ref[which, :, lanes]]
                + [repooled(field) for field in three[which]]
            )
            theirs.append([relay[which, eighth:] for relay in relays])
            beyond.append([field[which, :, lanes] for field in far])
        steps[pair, 3] = (
            score(three_q[:, lanes], jnp.concatenate(three[0], axis=0), three_hold.at[pair]),
            with_ones(jnp.concatenate(three[1], axis=0)),
        )
        steps[pair, 4] = (
            score(
                four_q[:, lanes],
                jnp.concatenate(ours[0] + theirs[0] + beyond[0], axis=0),
                four_hold.at[pair],
            ),
            jnp.concatenate(
                [with_ones(field) for field in ours[1]]
                + [with_ones(field, 2.0) for field in theirs[1]]
                + [with_ones(field) for field in beyond[1]],
                axis=0,
            ),
        )
    for pair in range(pairs):
        lanes = pl.ds(pair * PAIR, PAIR)
        four = weigh(four_hold.at[pair], *steps[pair, 4])
        now = merged(weigh(three_hold.at[pair], *steps[pair, 3]), [doubled(x) for x in four])
        for block in range(blocks):
            here = slice(block * BLOCK, (block + 1) * BLOCK)
            eighth_here = slice(block * BLOCK // 8, (block + 1) * BLOCK // 8)
            _, numer, rowsum = merged(
                [state[index, here, lanes] for index in range(3)],
                [doubled(doubled(doubled(x[eighth_here]))) for x in now],
            )
            attended[block, :, lanes] = (numer / rowsum).astype(jnp.bfloat16)
    for step, out in enumerate(outs):
        out[...] = attended[own ^ step]


def partial_kernel(near_ref, next_ref, weight_ref, out_ref):
    own = lax.axis_index("head")
    features = near_ref.shape[1]
    total = None
    for step, part in enumerate((near_ref, next_ref)):
        start = pl.multiple_of((own ^ step) * features, features)
        product = jnp.dot(
            part[...], weight_ref[pl.ds(start, features), :], preferred_element_type=jnp.float32
        )
        total = product if total is None else total + product
    out_ref[...] = total


def project_kernel(partial_ref, *refs):
    parts, (weight_ref, out_hbm, scratch, staged, sems) = refs[:-5], refs[-5:]
    own = lax.axis_index("head")
    features = parts[0].shape[1]
    chunk = staged.shape[2]
    copies = []
    for index in range(staged.shape[0]):
        columns = pl.ds(index * chunk, chunk)
        total = partial_ref[:, columns]
        for step, part in enumerate(parts, 2):
            start = pl.multiple_of((own ^ step) * features, features)
            total += jnp.dot(
                part[...],
                weight_ref[pl.ds(start, features), columns],
                preferred_element_type=jnp.float32,
            )
        for half in range(chunk // PAIR):
            lanes = slice(half * PAIR, (half + 1) * PAIR)
            scratch[index, half] = total[:, lanes]
            for i in range(SLAB):
                staged[index, i * FAN : (i + 1) * FAN, lanes] = scratch[
                    index, half, pl.ds(i, FAN, stride=SLAB), :
                ].astype(jnp.bfloat16)
        copy = pltpu.make_async_copy(staged.at[index], out_hbm.at[:, columns], sems.at[index])
        copy.start()
        copies.append(copy)
    for copy in copies:
        copy.wait()


def repool_outside(field):
    which, rows, lanes = field.shape
    slabs = field.astype(jnp.float32).reshape(which, rows // (2 * SLAB), 2, SLAB, lanes)
    sums = (slabs[:, :, 0] + slabs[:, :, 1]) * root_half
    return sums.reshape(which, rows // 2, lanes).astype(jnp.bfloat16)


def swapped(block, axis, mask):
    return lax.ppermute(block, axis, [(i, i ^ mask) for i in range(lax.axis_size(axis))])


def across(block, axis):
    count = lax.axis_size(axis)
    route = []
    for low in range(1, count - 1, 2):
        route += [(low, low + 1), (low + 1, low)]
    return lax.ppermute(block, axis, route)


def per_device(queries, key_vectors, value_vectors, out_weight):
    rows, features = queries.shape[1:]
    queries, key_vectors, value_vectors = [
        pltpu.with_memory_space_constraint(x, pltpu.HBM)
        for x in (queries, key_vectors, value_vectors)
    ]
    pairs = features // PAIR
    seq_count, head_count = lax.axis_size("seq"), lax.axis_size("head")
    bf16 = lambda *shape: jax.ShapeDtypeStruct(shape, jnp.bfloat16)
    params = pltpu.CompilerParams(vmem_limit_bytes=32 * 1024 * 1024)

    hbm = pl.BlockSpec(memory_space=pltpu.HBM)
    vmem = pl.BlockSpec(memory_space=pltpu.VMEM)
    keys, values, ours, first, one, two = pl.pallas_call(
        pool_kernel,
        in_specs=[hbm] * 3,
        out_shape=[
            bf16(rows, features),
            bf16(rows, features),
            bf16(rows, features),
            bf16(2, BLOCK + rows // 4 - BLOCK // 4, features),
            bf16(2, rows // 2, features),
            bf16(2, rows // 4, features),
        ],
        scratch_shapes=[
            pltpu.VMEM((2, rows // BLOCK, pairs, BLOCK, PAIR), jnp.float32),
            pltpu.SemaphoreType.DMA((2, rows // BLOCK)),
            pltpu.SemaphoreType.DMA((1,)),
        ],
        compiler_params=params,
        name="pool",
    )(key_vectors, value_vectors, queries)
    second, three, four = pl.pallas_call(
        deeper_kernel,
        out_shape=[
            bf16(2, BLOCK, features),
            bf16(2, rows // 8, features),
            bf16(2, rows // 16, features),
        ],
        compiler_params=params,
        cost_estimate=pl.CostEstimate(flops=2**31, bytes_accessed=2**23, transcendentals=0),
        name="deeper",
    )(keys, values, two)

    first_in = swapped(first, "seq", 1)
    second_in = across(second, "seq")
    fours_in = [swapped(four, "seq", mask) for mask in (6, 4)]
    three_in = swapped(three, "seq", 2)
    pack, two_in, near = pl.pallas_call(
        relay_kernel,
        out_shape=[
            bf16(2, rows // 8, features),
            bf16(2, rows // 4, features),
            bf16(2, rows // 16, features),
        ],
        scratch_shapes=[pltpu.VMEM((2, pairs, BLOCK, PAIR), jnp.float32)],
        compiler_params=params,
        cost_estimate=pl.CostEstimate(flops=2**29, bytes_accessed=2**20, transcendentals=0),
        name="relay",
    )(first_in, *fours_in)
    relayed = pl.pallas_call(
        join_kernel,
        out_shape=bf16(2, rows // 4, features),
        compiler_params=params,
        name="join",
    )(pack, three_in)
    relayed_in = swapped(relayed, "seq", 1)

    edge_q, two_q, three_q, four_q, state = pl.pallas_call(
        local_kernel,
        out_shape=[
            bf16(2, BLOCK, features),
            bf16(rows // 4, features),
            bf16(rows // 8, features),
            bf16(rows // 16, features),
            jax.ShapeDtypeStruct((3, rows, features), jnp.float32),
        ],
        scratch_shapes=[
            pltpu.VMEM((pairs, rows, PAIR), jnp.float32),
            pltpu.VMEM((pairs, rows // BLOCK, 2 * BLOCK, 3 * BLOCK), jnp.float32),
            pltpu.VMEM((pairs, rows // BLOCK // 2, 2 * BLOCK, BLOCK), jnp.float32),
        ],
        compiler_params=params,
        name="local",
    )(ours, keys, values, one)

    state = pl.pallas_call(
        mid_kernel,
        out_shape=jax.ShapeDtypeStruct((3, rows, features), jnp.float32),
        input_output_aliases={2: 0},
        scratch_shapes=[pltpu.VMEM((pairs, 3, 2 * BLOCK, BLOCK), jnp.float32)],
        compiler_params=params,
        name="mid",
    )(edge_q, two_q, state, first_in, second_in, two_in)

    far = []
    known = 8
    if known < seq_count:
        eighth = rows // 8
        group = [four, near, repool_outside(relayed[:, :eighth]), repool_outside(relayed_in[:, :eighth])]
        group = jnp.concatenate(group + [relayed[:, eighth:], relayed_in[:, eighth:]], axis=1)
        while known < seq_count:
            fresh = swapped(group, "seq", known)
            far.append(fresh)
            group = jnp.concatenate([group, fresh], axis=1)
            known *= 2

    outs = pl.pallas_call(
        finish_kernel,
        out_shape=[bf16(BLOCK, features) for _ in range(head_count)],
        scratch_shapes=[
            pltpu.VMEM((rows // BLOCK, BLOCK, features), jnp.bfloat16),
            pltpu.VMEM((pairs, rows // 4, BLOCK), jnp.float32),
            pltpu.VMEM((pairs, rows // 8, rows // 16 * seq_count), jnp.float32),
        ],
        compiler_params=params,
        name="finish",
    )(three_q, four_q, state, four, near, relayed, relayed_in, *far)

    parts = [part if step == 0 else swapped(part, "head", step) for step, part in enumerate(outs)]
    width = out_weight.shape[1]
    partial = pl.pallas_call(
        partial_kernel,
        out_shape=jax.ShapeDtypeStruct((BLOCK, width), jnp.float32),
        compiler_params=params,
        name="partial",
    )(*parts[:2], out_weight)
    chunk = 2 * PAIR
    result = pl.pallas_call(
        project_kernel,
        in_specs=[vmem] * len(parts),
        out_specs=hbm,
        out_shape=bf16(BLOCK, width),
        scratch_shapes=[
            pltpu.VMEM((width // chunk, 2, BLOCK, PAIR), jnp.float32),
            pltpu.VMEM((width // chunk, BLOCK, chunk), jnp.bfloat16),
            pltpu.SemaphoreType.DMA((width // chunk,)),
        ],
        compiler_params=params,
        name="project",
    )(partial, *parts[2:], out_weight)
    return result[None]


def solution(mesh):
    return jax.shard_map(
        per_device,
        mesh=mesh,
        in_specs=(P(None, "seq", "head"), P(None, "seq", "head"), P(None, "seq", "head"), P()),
        out_specs=P(None, ("seq", "head"), None),
        check_vma=False,
    )
```

```python
import jax
import jax.numpy as jnp
from jax import lax
from jax.experimental import pallas as pl
from jax.experimental.pallas import tpu as pltpu
from jax.sharding import PartitionSpec as P

HD = 64
BLOCK = 128
LEVELS = 4
SLAB = 8
PAIR = 2 * HD

neg_fill = -1e30
root_half = 0.7071067811865476
log2_scale = HD**-0.5 * 1.4426950408889634

FAN = 2**LEVELS


def slabs_of(scratch, block):
    return [scratch[pl.ds(BLOCK * block + j, SLAB, stride=FAN), :] for j in range(FAN)]


def pooled_slabs(slabs):
    return [
        ((low + high) * root_half).astype(jnp.bfloat16).astype(jnp.float32)
        for low, high in zip(slabs[0::2], slabs[1::2])
    ]


def joined(slabs):
    return jnp.concatenate(slabs, axis=0).astype(jnp.bfloat16)


def spill(source, scratch):
    for half in range(scratch.shape[0]):
        scratch[half] = source[:, half * PAIR : (half + 1) * PAIR].astype(jnp.float32)


def pool_kernel(
    k_hbm, v_hbm, q_hbm, k_ref, v_ref, q_ref, first_ref, one_ref, two_ref, scratch, sems, q_sem
):
    rows = k_ref.shape[0]
    blocks = rows // BLOCK
    arrivals = []
    for block in range(blocks):
        here = pl.ds(block * BLOCK, BLOCK)
        for which, (source, target) in enumerate(((k_hbm, k_ref), (v_hbm, v_ref))):
            copy = pltpu.make_async_copy(
                source.at[0, here, :], target.at[here, :], sems.at[which, block]
            )
            copy.start()
            arrivals.append((block, which, target, copy))
    q_copy = pltpu.make_async_copy(q_hbm.at[0], q_ref, q_sem.at[0])
    q_copy.start()
    even = lax.rem(lax.axis_index("seq"), 2) == 0
    for block, which, ref, copy in arrivals:
        copy.wait()
        here = pl.ds(block * BLOCK, BLOCK)
        spill(ref.at[here, :], scratch.at[which, block])
        for half in range(scratch.shape[2]):
            lanes = pl.ds(half * PAIR, PAIR)
            one = pooled_slabs(slabs_of(scratch.at[which, block, half], 0))
            one_ref[which, pl.ds(block * BLOCK // 2, BLOCK // 2), lanes] = joined(one)
            two_ref[which, pl.ds(block * BLOCK // 4, BLOCK // 4), lanes] = joined(pooled_slabs(one))
    inner = rows // 4 - BLOCK // 4
    for which, ref in enumerate((k_ref, v_ref)):
        first_ref[which, :BLOCK, :] = jnp.where(even, ref[rows - BLOCK :, :], ref[:BLOCK, :])
        first_ref[which, BLOCK:, :] = jnp.where(
            even, two_ref[which, :inner, :], two_ref[which, BLOCK // 4 :, :]
        )
    q_copy.wait()


def repooled(field):
    rows, lanes = field.shape
    slabs = field.astype(jnp.float32).reshape(rows // (2 * SLAB), 2, SLAB, lanes)
    return ((slabs[:, 0] + slabs[:, 1]) * root_half).reshape(rows // 2, lanes).astype(jnp.bfloat16)


def deeper_kernel(k_ref, v_ref, two_ref, second_ref, three_ref, four_ref):
    rows = k_ref.shape[0]
    even = lax.rem(lax.axis_index("seq"), 2) == 0
    for which, ref in enumerate((k_ref, v_ref)):
        second_ref[which] = jnp.where(even, ref[:BLOCK, :], ref[rows - BLOCK :, :])
        three = repooled(two_ref[which])
        three_ref[which] = three
        four_ref[which] = repooled(three)


def repooled(field):
    rows, lanes = field.shape
    slabs = field.astype(jnp.float32).reshape(rows // (2 * SLAB), 2, SLAB, lanes)
    return ((slabs[:, 0] + slabs[:, 1]) * root_half).reshape(rows // 2, lanes).astype(jnp.bfloat16)


def score(queries, keys, hold, is_open=None):
    rows = queries.shape[0]
    low = lax.broadcasted_iota(jnp.int32, (rows, PAIR), 1) < HD
    zero = jnp.zeros_like(queries)
    both = jnp.concatenate([jnp.where(low, queries, zero), jnp.where(low, zero, queries)], axis=0)
    raw = lax.dot_general(both, keys, (((1,), (1,)), ((), ())), preferred_element_type=jnp.float32)
    if is_open is not None:
        raw = jnp.where(is_open, raw, neg_fill)
    hold[...] = raw
    return jnp.max(raw, axis=1, keepdims=True)


def weigh(hold, top, values):
    rows = top.shape[0] // 2
    low = lax.broadcasted_iota(jnp.int32, (rows, PAIR), 1) < HD
    weights = jnp.exp2((hold[...] - top) * log2_scale).astype(jnp.bfloat16)
    result = jnp.dot(weights, values, preferred_element_type=jnp.float32)
    return (
        log2_scale * jnp.where(low, top[:rows], top[rows:]),
        jnp.where(low, result[:rows, :PAIR], result[rows:, :PAIR]),
        jnp.where(low, result[:rows, PAIR:], result[rows:, PAIR:]),
    )


def merged(fine, coarse):
    top = jnp.maximum(fine[0], coarse[0])
    keep = jnp.exp2(fine[0] - top)
    join = jnp.exp2(coarse[0] - top)
    return top, fine[1] * keep + coarse[1] * join, fine[2] * keep + coarse[2] * join


def doubled(field):
    rows, lanes = field.shape
    slabs = field.reshape(rows // SLAB, 1, SLAB, lanes)
    return jnp.broadcast_to(slabs, (rows // SLAB, 2, SLAB, lanes)).reshape(2 * rows, lanes)


def with_ones(values, weight=1.0):
    if weight != 1.0:
        values = values * jnp.bfloat16(weight)
    return jnp.concatenate([values, jnp.full(values.shape, weight, jnp.bfloat16)], axis=1)


def local_kernel(
    q_ref, k_ref, v_ref, one_ref, edge_q, two_q, three_q, four_q, state,
    scratch, near_hold, coarse_hold,
):
    rows = q_ref.shape[0]
    blocks = rows // BLOCK
    pairs = scratch.shape[0]
    spill(q_ref, scratch)
    fine, one_q = [], []
    for pair in range(pairs):
        lanes = pl.ds(pair * PAIR, PAIR)
        ladder = [[], [], [], [], []]
        for block in range(blocks):
            slabs = slabs_of(scratch.at[pair], block)
            ladder[0].append(joined(slabs))
            for level in range(1, LEVELS + 1):
                slabs = pooled_slabs(slabs)
                ladder[level] += slabs
        edge_q[0, :, lanes] = ladder[0][0]
        edge_q[1, :, lanes] = ladder[0][-1]
        two_q[:, lanes] = joined(ladder[2])
        three_q[:, lanes] = joined(ladder[3])
        four_q[:, lanes] = joined(ladder[4])
        fine.append(ladder[0])
        one_q.append([joined(ladder[1][n : n + FAN]) for n in range(0, len(ladder[1]), FAN)])
    windows = [(max(n - 1, 0) * BLOCK, min(n + 2, blocks) * BLOCK) for n in range(blocks)]
    tops = {}
    for pair in range(pairs):
        lanes = pl.ds(pair * PAIR, PAIR)
        for half in range(blocks // 2):
            there = pl.ds((half ^ 1) * BLOCK, BLOCK)
            tops[pair, half] = score(
                one_q[pair][half], one_ref[0, there, lanes], coarse_hold.at[pair, half]
            )
            for block in (2 * half, 2 * half + 1):
                low, high = windows[block]
                hold = near_hold.at[pair, block, :, : high - low]
                tops[pair, half, block] = score(fine[pair][block], k_ref[low:high, lanes], hold)
    for pair in range(pairs):
        lanes = pl.ds(pair * PAIR, PAIR)
        for half in range(blocks // 2):
            there = pl.ds((half ^ 1) * BLOCK, BLOCK)
            coarse = weigh(
                coarse_hold.at[pair, half], tops[pair, half], with_ones(one_ref[1, there, lanes])
            )
            for block in (2 * half, 2 * half + 1):
                low, high = windows[block]
                hold = near_hold.at[pair, block, :, : high - low]
                near = weigh(hold, tops[pair, half, block], with_ones(v_ref[low:high, lanes]))
                part = slice((block - 2 * half) * BLOCK // 2, (block - 2 * half + 1) * BLOCK // 2)
                done = merged(near, [doubled(x[part]) for x in coarse])
                for index, field in enumerate(done):
                    state[index, block * BLOCK : (block + 1) * BLOCK, lanes] = field


def relay_kernel(first_ref, six_ref, four_ref, pack_ref, two_ref, near_ref, scratch):
    sixteenth = four_ref.shape[1]
    pack_ref[:, :sixteenth, :] = six_ref[...]
    pack_ref[:, sixteenth:, :] = four_ref[...]
    inner = first_ref.shape[1] - BLOCK
    two_ref[:, :inner, :] = first_ref[:, BLOCK:, :]
    for which in range(2):
        spill(first_ref.at[which, pl.ds(0, BLOCK), :], scratch.at[which])
        for half in range(scratch.shape[1]):
            lanes = pl.ds(half * PAIR, PAIR)
            slabs = slabs_of(scratch.at[which, half], 0)
            two_ref[which, inner:, lanes] = joined(pooled_slabs(pooled_slabs(slabs)))
        near_ref[which] = repooled(repooled(two_ref[which]))


def join_kernel(pack_ref, three_ref, relay_ref):
    eighth = three_ref.shape[1]
    relay_ref[:, :eighth, :] = three_ref[...]
    relay_ref[:, eighth:, :] = pack_ref[...]


def mid_kernel(edge_q, two_q, state, first_ref, second_ref, two_ref, out, holds):
    rows = state.shape[1]
    blocks = rows // BLOCK
    position = lax.axis_index("seq")
    last = lax.axis_size("seq") - 1
    even = lax.rem(position, 2) == 0
    opens = (position > 0, position < last)
    pairs = two_q.shape[1] // PAIR
    steps = {}
    for pair in range(pairs):
        lanes = pl.ds(pair * PAIR, PAIR)
        inner = [first_ref[which, :BLOCK, lanes] for which in range(2)]
        outer = [second_ref[which, :, lanes] for which in range(2)]
        steps[pair, 2] = (
            score(two_q[:, lanes], two_ref[0, :, lanes], holds.at[pair, 2]),
            with_ones(two_ref[1, :, lanes]),
        )
        for side in range(2):
            halo = [
                jnp.where(even, *((outer[which], inner[which])[:: 1 - 2 * side]))
                for which in range(2)
            ]
            steps[pair, side] = (
                score(edge_q[side, :, lanes], halo[0], holds.at[pair, side], opens[side]),
                with_ones(halo[1]),
            )
    for pair in range(pairs):
        lanes = pl.ds(pair * PAIR, PAIR)
        two = weigh(holds.at[pair, 2], *steps[pair, 2])
        for block in range(blocks):
            here = slice(block * BLOCK, (block + 1) * BLOCK)
            quarter = slice(block * BLOCK // 4, (block + 1) * BLOCK // 4)
            done = merged(
                [state[index, here, lanes] for index in range(3)],
                [doubled(doubled(x[quarter])) for x in two],
            )
            for side, edge in enumerate((0, blocks - 1)):
                if block == edge:
                    done = merged(done, weigh(holds.at[pair, side], *steps[pair, side]))
            for index, field in enumerate(done):
                out[index, here, lanes] = field


def finish_kernel(three_q, four_q, state, four_ref, near_ref, relay_a, relay_b, *refs):
    far, refs = refs[:-7], refs[-7:]
    outs, (attended, three_hold, four_hold) = refs[:-3], refs[-3:]
    rows = state.shape[1]
    blocks = rows // BLOCK
    own = lax.axis_index("head")
    pairs = three_q.shape[1] // PAIR
    eighth = rows // 8
    steps = {}
    for pair in range(pairs):
        lanes = pl.ds(pair * PAIR, PAIR)
        relays = [relay_a[:, :, lanes], relay_b[:, :, lanes]]
        three, ours, theirs, beyond = [], [], [], []
        for which in range(2):
            three.append([relay[which, :eighth] for relay in relays])
            ours.append(
                [four_ref[which, :, lanes], near_ref[which, :, lanes]]
                + [repooled(field) for field in three[which]]
            )
            theirs.append([relay[which, eighth:] for relay in relays])
            beyond.append([field[which, :, lanes] for field in far])
        steps[pair, 3] = (
            score(three_q[:, lanes], jnp.concatenate(three[0], axis=0), three_hold.at[pair]),
            with_ones(jnp.concatenate(three[1], axis=0)),
        )
        steps[pair, 4] = (
            score(
                four_q[:, lanes],
                jnp.concatenate(ours[0] + theirs[0] + beyond[0], axis=0),
                four_hold.at[pair],
            ),
            jnp.concatenate(
                [with_ones(field) for field in ours[1]]
                + [with_ones(field, 2.0) for field in theirs[1]]
                + [with_ones(field) for field in beyond[1]],
                axis=0,
            ),
        )
    for pair in range(pairs):
        lanes = pl.ds(pair * PAIR, PAIR)
        four = weigh(four_hold.at[pair], *steps[pair, 4])
        now = merged(weigh(three_hold.at[pair], *steps[pair, 3]), [doubled(x) for x in four])
        for block in range(blocks):
            here = slice(block * BLOCK, (block + 1) * BLOCK)
            eighth_here = slice(block * BLOCK // 8, (block + 1) * BLOCK // 8)
            _, numer, rowsum = merged(
                [state[index, here, lanes] for index in range(3)],
                [doubled(doubled(doubled(x[eighth_here]))) for x in now],
            )
            attended[block, :, lanes] = (numer / rowsum).astype(jnp.bfloat16)
    for step, out in enumerate(outs):
        out[...] = attended[own ^ step]


def partial_kernel(near_ref, next_ref, weight_ref, out_ref):
    own = lax.axis_index("head")
    features = near_ref.shape[1]
    total = None
    for step, part in enumerate((near_ref, next_ref)):
        start = pl.multiple_of((own ^ step) * features, features)
        product = jnp.dot(
            part[...], weight_ref[pl.ds(start, features), :], preferred_element_type=jnp.float32
        )
        total = product if total is None else total + product
    out_ref[...] = total


def project_kernel(partial_ref, *refs):
    parts, (weight_ref, out_hbm, scratch, staged, sems) = refs[:-5], refs[-5:]
    own = lax.axis_index("head")
    features = parts[0].shape[1]
    chunk = staged.shape[2]
    copies = []
    for index in range(staged.shape[0]):
        columns = pl.ds(index * chunk, chunk)
        total = partial_ref[:, columns]
        for step, part in enumerate(parts, 2):
            start = pl.multiple_of((own ^ step) * features, features)
            total += jnp.dot(
                part[...],
                weight_ref[pl.ds(start, features), columns],
                preferred_element_type=jnp.float32,
            )
        for half in range(chunk // PAIR):
            lanes = slice(half * PAIR, (half + 1) * PAIR)
            scratch[index, half] = total[:, lanes]
            for i in range(SLAB):
                staged[index, i * FAN : (i + 1) * FAN, lanes] = scratch[
                    index, half, pl.ds(i, FAN, stride=SLAB), :
                ].astype(jnp.bfloat16)
        copy = pltpu.make_async_copy(staged.at[index], out_hbm.at[:, columns], sems.at[index])
        copy.start()
        copies.append(copy)
    for copy in copies:
        copy.wait()


def repool_outside(field):
    which, rows, lanes = field.shape
    slabs = field.astype(jnp.float32).reshape(which, rows // (2 * SLAB), 2, SLAB, lanes)
    sums = (slabs[:, :, 0] + slabs[:, :, 1]) * root_half
    return sums.reshape(which, rows // 2, lanes).astype(jnp.bfloat16)


def swapped(block, axis, mask):
    return lax.ppermute(block, axis, [(i, i ^ mask) for i in range(lax.axis_size(axis))])


def across(block, axis):
    count = lax.axis_size(axis)
    route = [(0, 0), (count - 1, count - 1)]
    for low in range(1, count - 1, 2):
        route += [(low, low + 1), (low + 1, low)]
    return lax.ppermute(block, axis, route)


def per_device(queries, key_vectors, value_vectors, out_weight):
    rows, features = queries.shape[1:]
    queries, key_vectors, value_vectors = [
        pltpu.with_memory_space_constraint(x, pltpu.HBM)
        for x in (queries, key_vectors, value_vectors)
    ]
    pairs = features // PAIR
    seq_count, head_count = lax.axis_size("seq"), lax.axis_size("head")
    bf16 = lambda *shape: jax.ShapeDtypeStruct(shape, jnp.bfloat16)
    params = pltpu.CompilerParams(vmem_limit_bytes=32 * 1024 * 1024)

    hbm = pl.BlockSpec(memory_space=pltpu.HBM)
    vmem = pl.BlockSpec(memory_space=pltpu.VMEM)
    keys, values, ours, first, one, two = pl.pallas_call(
        pool_kernel,
        in_specs=[hbm] * 3,
        out_shape=[
            bf16(rows, features),
            bf16(rows, features),
            bf16(rows, features),
            bf16(2, BLOCK + rows // 4 - BLOCK // 4, features),
            bf16(2, rows // 2, features),
            bf16(2, rows // 4, features),
        ],
        scratch_shapes=[
            pltpu.VMEM((2, rows // BLOCK, pairs, BLOCK, PAIR), jnp.float32),
            pltpu.SemaphoreType.DMA((2, rows // BLOCK)),
            pltpu.SemaphoreType.DMA((1,)),
        ],
        compiler_params=params,
        name="pool",
    )(key_vectors, value_vectors, queries)
    second, three, four = pl.pallas_call(
        deeper_kernel,
        out_shape=[
            bf16(2, BLOCK, features),
            bf16(2, rows // 8, features),
            bf16(2, rows // 16, features),
        ],
        compiler_params=params,
        cost_estimate=pl.CostEstimate(flops=2**31, bytes_accessed=2**23, transcendentals=0),
        name="deeper",
    )(keys, values, two)

    first_in = swapped(first, "seq", 1)
    second_in = across(second, "seq")
    fours_in = [swapped(four, "seq", mask) for mask in (6, 4)]
    three_in = swapped(three, "seq", 2)
    pack, two_in, near = pl.pallas_call(
        relay_kernel,
        out_shape=[
            bf16(2, rows // 8, features),
            bf16(2, rows // 4, features),
            bf16(2, rows // 16, features),
        ],
        scratch_shapes=[pltpu.VMEM((2, pairs, BLOCK, PAIR), jnp.float32)],
        compiler_params=params,
        cost_estimate=pl.CostEstimate(flops=2**29, bytes_accessed=2**20, transcendentals=0),
        name="relay",
    )(first_in, *fours_in)
    relayed = pl.pallas_call(
        join_kernel,
        out_shape=bf16(2, rows // 4, features),
        compiler_params=params,
        name="join",
    )(pack, three_in)
    relayed_in = swapped(relayed, "seq", 1)

    edge_q, two_q, three_q, four_q, state = pl.pallas_call(
        local_kernel,
        out_shape=[
            bf16(2, BLOCK, features),
            bf16(rows // 4, features),
            bf16(rows // 8, features),
            bf16(rows // 16, features),
            jax.ShapeDtypeStruct((3, rows, features), jnp.float32),
        ],
        scratch_shapes=[
            pltpu.VMEM((pairs, rows, PAIR), jnp.float32),
            pltpu.VMEM((pairs, rows // BLOCK, 2 * BLOCK, 3 * BLOCK), jnp.float32),
            pltpu.VMEM((pairs, rows // BLOCK // 2, 2 * BLOCK, BLOCK), jnp.float32),
        ],
        compiler_params=params,
        name="local",
    )(ours, keys, values, one)

    state = pl.pallas_call(
        mid_kernel,
        out_shape=jax.ShapeDtypeStruct((3, rows, features), jnp.float32),
        input_output_aliases={2: 0},
        scratch_shapes=[pltpu.VMEM((pairs, 3, 2 * BLOCK, BLOCK), jnp.float32)],
        compiler_params=params,
        name="mid",
    )(edge_q, two_q, state, first_in, second_in, two_in)

    far = []
    known = 8
    if known < seq_count:
        eighth = rows // 8
        group = [four, near, repool_outside(relayed[:, :eighth]), repool_outside(relayed_in[:, :eighth])]
        group = jnp.concatenate(group + [relayed[:, eighth:], relayed_in[:, eighth:]], axis=1)
        while known < seq_count:
            fresh = swapped(group, "seq", known)
            far.append(fresh)
            group = jnp.concatenate([group, fresh], axis=1)
            known *= 2

    outs = pl.pallas_call(
        finish_kernel,
        out_shape=[bf16(BLOCK, features) for _ in range(head_count)],
        scratch_shapes=[
            pltpu.VMEM((rows // BLOCK, BLOCK, features), jnp.bfloat16),
            pltpu.VMEM((pairs, rows // 4, BLOCK), jnp.float32),
            pltpu.VMEM((pairs, rows // 8, rows // 16 * seq_count), jnp.float32),
        ],
        compiler_params=params,
        name="finish",
    )(three_q, four_q, state, four, near, relayed, relayed_in, *far)

    parts = [part if step == 0 else swapped(part, "head", step) for step, part in enumerate(outs)]
    width = out_weight.shape[1]
    partial = pl.pallas_call(
        partial_kernel,
        out_shape=jax.ShapeDtypeStruct((BLOCK, width), jnp.float32),
        compiler_params=params,
        name="partial",
    )(*parts[:2], out_weight)
    chunk = 2 * PAIR
    result = pl.pallas_call(
        project_kernel,
        in_specs=[vmem] * len(parts),
        out_specs=hbm,
        out_shape=bf16(BLOCK, width),
        scratch_shapes=[
            pltpu.VMEM((width // chunk, 2, BLOCK, PAIR), jnp.float32),
            pltpu.VMEM((width // chunk, BLOCK, chunk), jnp.bfloat16),
            pltpu.SemaphoreType.DMA((width // chunk,)),
        ],
        compiler_params=params,
        name="project",
    )(partial, *parts[2:], out_weight)
    return result[None]


def solution(mesh):
    return jax.shard_map(
        per_device,
        mesh=mesh,
        in_specs=(P(None, "seq", "head"), P(None, "seq", "head"), P(None, "seq", "head"), P()),
        out_specs=P(None, ("seq", "head"), None),
        check_vma=False,
    )
```

```python
import jax
import jax.numpy as jnp
from jax import lax
from jax.experimental import pallas as pl
from jax.experimental.pallas import tpu as pltpu
from jax.sharding import PartitionSpec as P

HD = 64
BLOCK = 128
LEVELS = 4
SLAB = 8
PAIR = 2 * HD

neg_fill = -1e30
root_half = 0.7071067811865476
log2_scale = HD**-0.5 * 1.4426950408889634

FAN = 2**LEVELS


def slabs_of(scratch, block):
    return [scratch[pl.ds(BLOCK * block + j, SLAB, stride=FAN), :] for j in range(FAN)]


def pooled_slabs(slabs):
    return [
        ((low + high) * root_half).astype(jnp.bfloat16).astype(jnp.float32)
        for low, high in zip(slabs[0::2], slabs[1::2])
    ]


def joined(slabs):
    return jnp.concatenate(slabs, axis=0).astype(jnp.bfloat16)


def spill(source, scratch):
    for half in range(scratch.shape[0]):
        scratch[half] = source[:, half * PAIR : (half + 1) * PAIR].astype(jnp.float32)


def pool_kernel(
    k_hbm, v_hbm, q_hbm, k_ref, v_ref, q_ref, first_ref, one_ref, two_ref, scratch, sems, q_sem
):
    rows = k_ref.shape[0]
    blocks = rows // BLOCK
    arrivals = []
    for block in range(blocks):
        here = pl.ds(block * BLOCK, BLOCK)
        for which, (source, target) in enumerate(((k_hbm, k_ref), (v_hbm, v_ref))):
            copy = pltpu.make_async_copy(
                source.at[0, here, :], target.at[here, :], sems.at[which, block]
            )
            copy.start()
            arrivals.append((block, which, target, copy))
    q_copy = pltpu.make_async_copy(q_hbm.at[0], q_ref, q_sem.at[0])
    q_copy.start()
    even = lax.rem(lax.axis_index("seq"), 2) == 0
    for block, which, ref, copy in arrivals:
        copy.wait()
        here = pl.ds(block * BLOCK, BLOCK)
        spill(ref.at[here, :], scratch.at[which, block])
        for half in range(scratch.shape[2]):
            lanes = pl.ds(half * PAIR, PAIR)
            one = pooled_slabs(slabs_of(scratch.at[which, block, half], 0))
            one_ref[which, pl.ds(block * BLOCK // 2, BLOCK // 2), lanes] = joined(one)
            two_ref[which, pl.ds(block * BLOCK // 4, BLOCK // 4), lanes] = joined(pooled_slabs(one))
    inner = rows // 4 - BLOCK // 4
    for which, ref in enumerate((k_ref, v_ref)):
        first_ref[which, :BLOCK, :] = jnp.where(even, ref[rows - BLOCK :, :], ref[:BLOCK, :])
        first_ref[which, BLOCK:, :] = jnp.where(
            even, two_ref[which, :inner, :], two_ref[which, BLOCK // 4 :, :]
        )
    q_copy.wait()


def repooled(field):
    rows, lanes = field.shape
    slabs = field.astype(jnp.float32).reshape(rows // (2 * SLAB), 2, SLAB, lanes)
    return ((slabs[:, 0] + slabs[:, 1]) * root_half).reshape(rows // 2, lanes).astype(jnp.bfloat16)


def deeper_kernel(k_ref, v_ref, two_ref, second_ref, three_ref, four_ref):
    rows = k_ref.shape[0]
    even = lax.rem(lax.axis_index("seq"), 2) == 0
    for which, ref in enumerate((k_ref, v_ref)):
        second_ref[which] = jnp.where(even, ref[:BLOCK, :], ref[rows - BLOCK :, :])
        three = repooled(two_ref[which])
        three_ref[which] = three
        four_ref[which] = repooled(three)


def repooled(field):
    rows, lanes = field.shape
    slabs = field.astype(jnp.float32).reshape(rows // (2 * SLAB), 2, SLAB, lanes)
    return ((slabs[:, 0] + slabs[:, 1]) * root_half).reshape(rows // 2, lanes).astype(jnp.bfloat16)


def score(queries, keys, hold, is_open=None):
    rows = queries.shape[0]
    low = lax.broadcasted_iota(jnp.int32, (rows, PAIR), 1) < HD
    zero = jnp.zeros_like(queries)
    both = jnp.concatenate([jnp.where(low, queries, zero), jnp.where(low, zero, queries)], axis=0)
    raw = lax.dot_general(both, keys, (((1,), (1,)), ((), ())), preferred_element_type=jnp.float32)
    if is_open is not None:
        raw = jnp.where(is_open, raw, neg_fill)
    hold[...] = raw
    return jnp.max(raw, axis=1, keepdims=True)


def weigh(hold, top, values):
    rows = top.shape[0] // 2
    low = lax.broadcasted_iota(jnp.int32, (rows, PAIR), 1) < HD
    weights = jnp.exp2((hold[...] - top) * log2_scale).astype(jnp.bfloat16)
    result = jnp.dot(weights, values, preferred_element_type=jnp.float32)
    return (
        log2_scale * jnp.where(low, top[:rows], top[rows:]),
        jnp.where(low, result[:rows, :PAIR], result[rows:, :PAIR]),
        jnp.where(low, result[:rows, PAIR:], result[rows:, PAIR:]),
    )


def merged(fine, coarse):
    top = jnp.maximum(fine[0], coarse[0])
    keep = jnp.exp2(fine[0] - top)
    join = jnp.exp2(coarse[0] - top)
    return top, fine[1] * keep + coarse[1] * join, fine[2] * keep + coarse[2] * join


def doubled(field):
    rows, lanes = field.shape
    slabs = field.reshape(rows // SLAB, 1, SLAB, lanes)
    return jnp.broadcast_to(slabs, (rows // SLAB, 2, SLAB, lanes)).reshape(2 * rows, lanes)


def with_ones(values, weight=1.0):
    if weight != 1.0:
        values = values * jnp.bfloat16(weight)
    return jnp.concatenate([values, jnp.full(values.shape, weight, jnp.bfloat16)], axis=1)


def local_kernel(
    q_ref, k_ref, v_ref, one_ref, edge_q, two_q, three_q, four_q, state,
    scratch, near_hold, coarse_hold,
):
    rows = q_ref.shape[0]
    blocks = rows // BLOCK
    pairs = scratch.shape[0]
    spill(q_ref, scratch)
    fine, one_q = [], []
    for pair in range(pairs):
        lanes = pl.ds(pair * PAIR, PAIR)
        ladder = [[], [], [], [], []]
        for block in range(blocks):
            slabs = slabs_of(scratch.at[pair], block)
            ladder[0].append(joined(slabs))
            for level in range(1, LEVELS + 1):
                slabs = pooled_slabs(slabs)
                ladder[level] += slabs
        edge_q[0, :, lanes] = ladder[0][0]
        edge_q[1, :, lanes] = ladder[0][-1]
        two_q[:, lanes] = joined(ladder[2])
        three_q[:, lanes] = joined(ladder[3])
        four_q[:, lanes] = joined(ladder[4])
        fine.append(ladder[0])
        one_q.append([joined(ladder[1][n : n + FAN]) for n in range(0, len(ladder[1]), FAN)])
    windows = [(max(n - 1, 0) * BLOCK, min(n + 2, blocks) * BLOCK) for n in range(blocks)]
    tops = {}
    for pair in range(pairs):
        lanes = pl.ds(pair * PAIR, PAIR)
        for half in range(blocks // 2):
            there = pl.ds((half ^ 1) * BLOCK, BLOCK)
            tops[pair, half] = score(
                one_q[pair][half], one_ref[0, there, lanes], coarse_hold.at[pair, half]
            )
            for block in (2 * half, 2 * half + 1):
                low, high = windows[block]
                hold = near_hold.at[pair, block, :, : high - low]
                tops[pair, half, block] = score(fine[pair][block], k_ref[low:high, lanes], hold)
    for pair in range(pairs):
        lanes = pl.ds(pair * PAIR, PAIR)
        for half in range(blocks // 2):
            there = pl.ds((half ^ 1) * BLOCK, BLOCK)
            coarse = weigh(
                coarse_hold.at[pair, half], tops[pair, half], with_ones(one_ref[1, there, lanes])
            )
            for block in (2 * half, 2 * half + 1):
                low, high = windows[block]
                hold = near_hold.at[pair, block, :, : high - low]
                near = weigh(hold, tops[pair, half, block], with_ones(v_ref[low:high, lanes]))
                part = slice((block - 2 * half) * BLOCK // 2, (block - 2 * half + 1) * BLOCK // 2)
                done = merged(near, [doubled(x[part]) for x in coarse])
                for index, field in enumerate(done):
                    state[index, block * BLOCK : (block + 1) * BLOCK, lanes] = field


def relay_kernel(first_ref, six_ref, four_ref, pack_ref, two_ref, near_ref, scratch):
    sixteenth = four_ref.shape[1]
    pack_ref[:, :sixteenth, :] = six_ref[...]
    pack_ref[:, sixteenth:, :] = four_ref[...]
    inner = first_ref.shape[1] - BLOCK
    two_ref[:, :inner, :] = first_ref[:, BLOCK:, :]
    for which in range(2):
        spill(first_ref.at[which, pl.ds(0, BLOCK), :], scratch.at[which])
        for half in range(scratch.shape[1]):
            lanes = pl.ds(half * PAIR, PAIR)
            slabs = slabs_of(scratch.at[which, half], 0)
            two_ref[which, inner:, lanes] = joined(pooled_slabs(pooled_slabs(slabs)))
        near_ref[which] = repooled(repooled(two_ref[which]))


def join_kernel(pack_ref, three_ref, relay_ref):
    eighth = three_ref.shape[1]
    relay_ref[:, :eighth, :] = three_ref[...]
    relay_ref[:, eighth:, :] = pack_ref[...]


def mid_kernel(edge_q, two_q, state, first_ref, second_ref, two_ref, out, holds):
    rows = state.shape[1]
    blocks = rows // BLOCK
    position = lax.axis_index("seq")
    last = lax.axis_size("seq") - 1
    even = lax.rem(position, 2) == 0
    opens = (position > 0, position < last)
    pairs = two_q.shape[1] // PAIR
    steps = {}
    for pair in range(pairs):
        lanes = pl.ds(pair * PAIR, PAIR)
        inner = [first_ref[which, :BLOCK, lanes] for which in range(2)]
        outer = [second_ref[which, :, lanes] for which in range(2)]
        steps[pair, 2] = (
            score(two_q[:, lanes], two_ref[0, :, lanes], holds.at[pair, 2]),
            with_ones(two_ref[1, :, lanes]),
        )
        for side in range(2):
            halo = [
                jnp.where(even, *((outer[which], inner[which])[:: 1 - 2 * side]))
                for which in range(2)
            ]
            steps[pair, side] = (
                score(edge_q[side, :, lanes], halo[0], holds.at[pair, side], opens[side]),
                with_ones(halo[1]),
            )
    for pair in range(pairs):
        lanes = pl.ds(pair * PAIR, PAIR)
        two = weigh(holds.at[pair, 2], *steps[pair, 2])
        for block in range(blocks):
            here = slice(block * BLOCK, (block + 1) * BLOCK)
            quarter = slice(block * BLOCK // 4, (block + 1) * BLOCK // 4)
            done = merged(
                [state[index, here, lanes] for index in range(3)],
                [doubled(doubled(x[quarter])) for x in two],
            )
            for side, edge in enumerate((0, blocks - 1)):
                if block == edge:
                    done = merged(done, weigh(holds.at[pair, side], *steps[pair, side]))
            for index, field in enumerate(done):
                out[index, here, lanes] = field


def finish_kernel(three_q, four_q, state, four_ref, near_ref, relay_a, relay_b, *refs):
    far, refs = refs[:-7], refs[-7:]
    outs, (attended, three_hold, four_hold) = refs[:-3], refs[-3:]
    rows = state.shape[1]
    blocks = rows // BLOCK
    own = lax.axis_index("head")
    pairs = three_q.shape[1] // PAIR
    eighth = rows // 8
    steps = {}
    for pair in range(pairs):
        lanes = pl.ds(pair * PAIR, PAIR)
        relays = [relay_a[:, :, lanes], relay_b[:, :, lanes]]
        three, ours, theirs, beyond = [], [], [], []
        for which in range(2):
            three.append([relay[which, :eighth] for relay in relays])
            ours.append(
                [four_ref[which, :, lanes], near_ref[which, :, lanes]]
                + [repooled(field) for field in three[which]]
            )
            theirs.append([relay[which, eighth:] for relay in relays])
            beyond.append([field[which, :, lanes] for field in far])
        steps[pair, 3] = (
            score(three_q[:, lanes], jnp.concatenate(three[0], axis=0), three_hold.at[pair]),
            with_ones(jnp.concatenate(three[1], axis=0)),
        )
        steps[pair, 4] = (
            score(
                four_q[:, lanes],
                jnp.concatenate(ours[0] + theirs[0] + beyond[0], axis=0),
                four_hold.at[pair],
            ),
            jnp.concatenate(
                [with_ones(field) for field in ours[1]]
                + [with_ones(field, 2.0) for field in theirs[1]]
                + [with_ones(field) for field in beyond[1]],
                axis=0,
            ),
        )
    for pair in range(pairs):
        lanes = pl.ds(pair * PAIR, PAIR)
        four = weigh(four_hold.at[pair], *steps[pair, 4])
        now = merged(weigh(three_hold.at[pair], *steps[pair, 3]), [doubled(x) for x in four])
        for block in range(blocks):
            here = slice(block * BLOCK, (block + 1) * BLOCK)
            eighth_here = slice(block * BLOCK // 8, (block + 1) * BLOCK // 8)
            _, numer, rowsum = merged(
                [state[index, here, lanes] for index in range(3)],
                [doubled(doubled(doubled(x[eighth_here]))) for x in now],
            )
            attended[block, :, lanes] = (numer / rowsum).astype(jnp.bfloat16)
    for step, out in enumerate(outs):
        out[...] = attended[own ^ step]


def partial_kernel(near_ref, next_ref, weight_ref, out_ref):
    own = lax.axis_index("head")
    features = near_ref.shape[1]
    total = None
    for step, part in enumerate((near_ref, next_ref)):
        start = pl.multiple_of((own ^ step) * features, features)
        product = jnp.dot(
            part[...], weight_ref[pl.ds(start, features), :], preferred_element_type=jnp.float32
        )
        total = product if total is None else total + product
    out_ref[...] = total


def project_kernel(partial_ref, *refs):
    parts, (weight_ref, out_hbm, scratch, staged, sems) = refs[:-5], refs[-5:]
    own = lax.axis_index("head")
    features = parts[0].shape[1]
    chunk = staged.shape[2]
    copies = []
    for index in range(staged.shape[0]):
        columns = pl.ds(index * chunk, chunk)
        total = partial_ref[:, columns]
        for step, part in enumerate(parts, 2):
            start = pl.multiple_of((own ^ step) * features, features)
            total += jnp.dot(
                part[...],
                weight_ref[pl.ds(start, features), columns],
                preferred_element_type=jnp.float32,
            )
        for half in range(chunk // PAIR):
            lanes = slice(half * PAIR, (half + 1) * PAIR)
            scratch[index, half] = total[:, lanes]
            for i in range(SLAB):
                staged[index, i * FAN : (i + 1) * FAN, lanes] = scratch[
                    index, half, pl.ds(i, FAN, stride=SLAB), :
                ].astype(jnp.bfloat16)
        copy = pltpu.make_async_copy(staged.at[index], out_hbm.at[:, columns], sems.at[index])
        copy.start()
        copies.append(copy)
    for copy in copies:
        copy.wait()


def repool_outside(field):
    which, rows, lanes = field.shape
    slabs = field.astype(jnp.float32).reshape(which, rows // (2 * SLAB), 2, SLAB, lanes)
    sums = (slabs[:, :, 0] + slabs[:, :, 1]) * root_half
    return sums.reshape(which, rows // 2, lanes).astype(jnp.bfloat16)


def swapped(block, axis, mask):
    return lax.ppermute(block, axis, [(i, i ^ mask) for i in range(lax.axis_size(axis))])


def across(block):
    count, heads = lax.axis_size("seq"), lax.axis_size("head")
    route = []
    for seq in range(count):
        end = seq in (0, count - 1)
        other = seq if end else seq + 1 if seq % 2 else seq - 1
        for head in range(heads):
            route.append((seq * heads + head, other * heads + (head ^ 1 if end else head)))
    return lax.ppermute(block, ("seq", "head"), route)


def per_device(queries, key_vectors, value_vectors, out_weight):
    rows, features = queries.shape[1:]
    queries, key_vectors, value_vectors = [
        pltpu.with_memory_space_constraint(x, pltpu.HBM)
        for x in (queries, key_vectors, value_vectors)
    ]
    pairs = features // PAIR
    seq_count, head_count = lax.axis_size("seq"), lax.axis_size("head")
    bf16 = lambda *shape: jax.ShapeDtypeStruct(shape, jnp.bfloat16)
    params = pltpu.CompilerParams(vmem_limit_bytes=32 * 1024 * 1024)

    hbm = pl.BlockSpec(memory_space=pltpu.HBM)
    vmem = pl.BlockSpec(memory_space=pltpu.VMEM)
    keys, values, ours, first, one, two = pl.pallas_call(
        pool_kernel,
        in_specs=[hbm] * 3,
        out_shape=[
            bf16(rows, features),
            bf16(rows, features),
            bf16(rows, features),
            bf16(2, BLOCK + rows // 4 - BLOCK // 4, features),
            bf16(2, rows // 2, features),
            bf16(2, rows // 4, features),
        ],
        scratch_shapes=[
            pltpu.VMEM((2, rows // BLOCK, pairs, BLOCK, PAIR), jnp.float32),
            pltpu.SemaphoreType.DMA((2, rows // BLOCK)),
            pltpu.SemaphoreType.DMA((1,)),
        ],
        compiler_params=params,
        name="pool",
    )(key_vectors, value_vectors, queries)
    second, three, four = pl.pallas_call(
        deeper_kernel,
        out_shape=[
            bf16(2, BLOCK, features),
            bf16(2, rows // 8, features),
            bf16(2, rows // 16, features),
        ],
        compiler_params=params,
        cost_estimate=pl.CostEstimate(flops=2**31, bytes_accessed=2**23, transcendentals=0),
        name="deeper",
    )(keys, values, two)

    first_in = swapped(first, "seq", 1)
    second_in = across(second)
    fours_in = [swapped(four, "seq", mask) for mask in (6, 4)]
    three_in = swapped(three, "seq", 2)
    pack, two_in, near = pl.pallas_call(
        relay_kernel,
        out_shape=[
            bf16(2, rows // 8, features),
            bf16(2, rows // 4, features),
            bf16(2, rows // 16, features),
        ],
        scratch_shapes=[pltpu.VMEM((2, pairs, BLOCK, PAIR), jnp.float32)],
        compiler_params=params,
        cost_estimate=pl.CostEstimate(flops=2**29, bytes_accessed=2**20, transcendentals=0),
        name="relay",
    )(first_in, *fours_in)
    relayed = pl.pallas_call(
        join_kernel,
        out_shape=bf16(2, rows // 4, features),
        compiler_params=params,
        name="join",
    )(pack, three_in)
    relayed_in = swapped(relayed, "seq", 1)

    edge_q, two_q, three_q, four_q, state = pl.pallas_call(
        local_kernel,
        out_shape=[
            bf16(2, BLOCK, features),
            bf16(rows // 4, features),
            bf16(rows // 8, features),
            bf16(rows // 16, features),
            jax.ShapeDtypeStruct((3, rows, features), jnp.float32),
        ],
        scratch_shapes=[
            pltpu.VMEM((pairs, rows, PAIR), jnp.float32),
            pltpu.VMEM((pairs, rows // BLOCK, 2 * BLOCK, 3 * BLOCK), jnp.float32),
            pltpu.VMEM((pairs, rows // BLOCK // 2, 2 * BLOCK, BLOCK), jnp.float32),
        ],
        compiler_params=params,
        name="local",
    )(ours, keys, values, one)

    state = pl.pallas_call(
        mid_kernel,
        out_shape=jax.ShapeDtypeStruct((3, rows, features), jnp.float32),
        input_output_aliases={2: 0},
        scratch_shapes=[pltpu.VMEM((pairs, 3, 2 * BLOCK, BLOCK), jnp.float32)],
        compiler_params=params,
        name="mid",
    )(edge_q, two_q, state, first_in, second_in, two_in)

    far = []
    known = 8
    if known < seq_count:
        eighth = rows // 8
        group = [four, near, repool_outside(relayed[:, :eighth]), repool_outside(relayed_in[:, :eighth])]
        group = jnp.concatenate(group + [relayed[:, eighth:], relayed_in[:, eighth:]], axis=1)
        while known < seq_count:
            fresh = swapped(group, "seq", known)
            far.append(fresh)
            group = jnp.concatenate([group, fresh], axis=1)
            known *= 2

    outs = pl.pallas_call(
        finish_kernel,
        out_shape=[bf16(BLOCK, features) for _ in range(head_count)],
        scratch_shapes=[
            pltpu.VMEM((rows // BLOCK, BLOCK, features), jnp.bfloat16),
            pltpu.VMEM((pairs, rows // 4, BLOCK), jnp.float32),
            pltpu.VMEM((pairs, rows // 8, rows // 16 * seq_count), jnp.float32),
        ],
        compiler_params=params,
        name="finish",
    )(three_q, four_q, state, four, near, relayed, relayed_in, *far)

    parts = [part if step == 0 else swapped(part, "head", step) for step, part in enumerate(outs)]
    width = out_weight.shape[1]
    partial = pl.pallas_call(
        partial_kernel,
        out_shape=jax.ShapeDtypeStruct((BLOCK, width), jnp.float32),
        compiler_params=params,
        name="partial",
    )(*parts[:2], out_weight)
    chunk = 2 * PAIR
    result = pl.pallas_call(
        project_kernel,
        in_specs=[vmem] * len(parts),
        out_specs=hbm,
        out_shape=bf16(BLOCK, width),
        scratch_shapes=[
            pltpu.VMEM((width // chunk, 2, BLOCK, PAIR), jnp.float32),
            pltpu.VMEM((width // chunk, BLOCK, chunk), jnp.bfloat16),
            pltpu.SemaphoreType.DMA((width // chunk,)),
        ],
        compiler_params=params,
        name="project",
    )(partial, *parts[2:], out_weight)
    return result[None]


def solution(mesh):
    return jax.shard_map(
        per_device,
        mesh=mesh,
        in_specs=(P(None, "seq", "head"), P(None, "seq", "head"), P(None, "seq", "head"), P()),
        out_specs=P(None, ("seq", "head"), None),
        check_vma=False,
    )
```

```python
import jax
import jax.numpy as jnp
from jax import lax
from jax.experimental import pallas as pl
from jax.experimental.pallas import tpu as pltpu
from jax.sharding import PartitionSpec as P

HD = 64
BLOCK = 128
LEVELS = 4
SLAB = 8
PAIR = 2 * HD

neg_fill = -1e30
root_half = 0.7071067811865476
log2_scale = HD**-0.5 * 1.4426950408889634

FAN = 2**LEVELS


def slabs_of(scratch, block):
    return [scratch[pl.ds(BLOCK * block + j, SLAB, stride=FAN), :] for j in range(FAN)]


def pooled_slabs(slabs):
    return [
        ((low + high) * root_half).astype(jnp.bfloat16).astype(jnp.float32)
        for low, high in zip(slabs[0::2], slabs[1::2])
    ]


def joined(slabs):
    return jnp.concatenate(slabs, axis=0).astype(jnp.bfloat16)


def spill(source, scratch):
    for half in range(scratch.shape[0]):
        scratch[half] = source[:, half * PAIR : (half + 1) * PAIR].astype(jnp.float32)


def pool_kernel(
    k_hbm, v_hbm, q_hbm, k_ref, v_ref, q_ref, first_ref, one_ref, two_ref, scratch, sems, q_sem
):
    rows = k_ref.shape[0]
    blocks = rows // BLOCK
    arrivals = []
    for block in range(blocks):
        here = pl.ds(block * BLOCK, BLOCK)
        for which, (source, target) in enumerate(((k_hbm, k_ref), (v_hbm, v_ref))):
            copy = pltpu.make_async_copy(
                source.at[0, here, :], target.at[here, :], sems.at[which, block]
            )
            copy.start()
            arrivals.append((block, which, target, copy))
    q_copy = pltpu.make_async_copy(q_hbm.at[0], q_ref, q_sem.at[0])
    q_copy.start()
    even = lax.rem(lax.axis_index("seq"), 2) == 0
    for block, which, ref, copy in arrivals:
        copy.wait()
        here = pl.ds(block * BLOCK, BLOCK)
        spill(ref.at[here, :], scratch.at[which, block])
        for half in range(scratch.shape[2]):
            lanes = pl.ds(half * PAIR, PAIR)
            one = pooled_slabs(slabs_of(scratch.at[which, block, half], 0))
            one_ref[which, pl.ds(block * BLOCK // 2, BLOCK // 2), lanes] = joined(one)
            two_ref[which, pl.ds(block * BLOCK // 4, BLOCK // 4), lanes] = joined(pooled_slabs(one))
    inner = rows // 4 - BLOCK // 4
    for which, ref in enumerate((k_ref, v_ref)):
        first_ref[which, :BLOCK, :] = jnp.where(even, ref[rows - BLOCK :, :], ref[:BLOCK, :])
        first_ref[which, BLOCK:, :] = jnp.where(
            even, two_ref[which, :inner, :], two_ref[which, BLOCK // 4 :, :]
        )
    q_copy.wait()


def repooled(field):
    rows, lanes = field.shape
    slabs = field.astype(jnp.float32).reshape(rows // (2 * SLAB), 2, SLAB, lanes)
    return ((slabs[:, 0] + slabs[:, 1]) * root_half).reshape(rows // 2, lanes).astype(jnp.bfloat16)


def deeper_kernel(k_ref, v_ref, two_ref, second_ref, three_ref, four_ref):
    rows = k_ref.shape[0]
    even = lax.rem(lax.axis_index("seq"), 2) == 0
    for which, ref in enumerate((k_ref, v_ref)):
        second_ref[which] = jnp.where(even, ref[:BLOCK, :], ref[rows - BLOCK :, :])
        three = repooled(two_ref[which])
        three_ref[which] = three
        four_ref[which] = repooled(three)


def repooled(field):
    rows, lanes = field.shape
    slabs = field.astype(jnp.float32).reshape(rows // (2 * SLAB), 2, SLAB, lanes)
    return ((slabs[:, 0] + slabs[:, 1]) * root_half).reshape(rows // 2, lanes).astype(jnp.bfloat16)


def score(queries, keys, hold, is_open=None):
    rows = queries.shape[0]
    low = lax.broadcasted_iota(jnp.int32, (rows, PAIR), 1) < HD
    zero = jnp.zeros_like(queries)
    both = jnp.concatenate([jnp.where(low, queries, zero), jnp.where(low, zero, queries)], axis=0)
    raw = lax.dot_general(both, keys, (((1,), (1,)), ((), ())), preferred_element_type=jnp.float32)
    if is_open is not None:
        raw = jnp.where(is_open, raw, neg_fill)
    hold[...] = raw
    return jnp.max(raw, axis=1, keepdims=True)


def weigh(hold, top, values):
    rows = top.shape[0] // 2
    low = lax.broadcasted_iota(jnp.int32, (rows, PAIR), 1) < HD
    weights = jnp.exp2((hold[...] - top) * log2_scale).astype(jnp.bfloat16)
    result = jnp.dot(weights, values, preferred_element_type=jnp.float32)
    return (
        log2_scale * jnp.where(low, top[:rows], top[rows:]),
        jnp.where(low, result[:rows, :PAIR], result[rows:, :PAIR]),
        jnp.where(low, result[:rows, PAIR:], result[rows:, PAIR:]),
    )


def merged(fine, coarse):
    top = jnp.maximum(fine[0], coarse[0])
    keep = jnp.exp2(fine[0] - top)
    join = jnp.exp2(coarse[0] - top)
    return top, fine[1] * keep + coarse[1] * join, fine[2] * keep + coarse[2] * join


def doubled(field):
    rows, lanes = field.shape
    slabs = field.reshape(rows // SLAB, 1, SLAB, lanes)
    return jnp.broadcast_to(slabs, (rows // SLAB, 2, SLAB, lanes)).reshape(2 * rows, lanes)


def with_ones(values, weight=1.0):
    if weight != 1.0:
        values = values * jnp.bfloat16(weight)
    return jnp.concatenate([values, jnp.full(values.shape, weight, jnp.bfloat16)], axis=1)


def local_kernel(
    q_ref, k_ref, v_ref, one_ref, edge_q, two_q, three_q, four_q, state,
    scratch, near_hold, coarse_hold,
):
    rows = q_ref.shape[0]
    blocks = rows // BLOCK
    pairs = scratch.shape[0]
    spill(q_ref, scratch)
    fine, one_q = [], []
    for pair in range(pairs):
        lanes = pl.ds(pair * PAIR, PAIR)
        ladder = [[], [], [], [], []]
        for block in range(blocks):
            slabs = slabs_of(scratch.at[pair], block)
            ladder[0].append(joined(slabs))
            for level in range(1, LEVELS + 1):
                slabs = pooled_slabs(slabs)
                ladder[level] += slabs
        edge_q[0, :, lanes] = ladder[0][0]
        edge_q[1, :, lanes] = ladder[0][-1]
        two_q[:, lanes] = joined(ladder[2])
        three_q[:, lanes] = joined(ladder[3])
        four_q[:, lanes] = joined(ladder[4])
        fine.append(ladder[0])
        one_q.append([joined(ladder[1][n : n + FAN]) for n in range(0, len(ladder[1]), FAN)])
    windows = [(max(n - 1, 0) * BLOCK, min(n + 2, blocks) * BLOCK) for n in range(blocks)]
    tops = {}
    for pair in range(pairs):
        lanes = pl.ds(pair * PAIR, PAIR)
        for half in range(blocks // 2):
            there = pl.ds((half ^ 1) * BLOCK, BLOCK)
            tops[pair, half] = score(
                one_q[pair][half], one_ref[0, there, lanes], coarse_hold.at[pair, half]
            )
            for block in (2 * half, 2 * half + 1):
                low, high = windows[block]
                hold = near_hold.at[pair, block, :, : high - low]
                tops[pair, half, block] = score(fine[pair][block], k_ref[low:high, lanes], hold)
    for pair in range(pairs):
        lanes = pl.ds(pair * PAIR, PAIR)
        for half in range(blocks // 2):
            there = pl.ds((half ^ 1) * BLOCK, BLOCK)
            coarse = weigh(
                coarse_hold.at[pair, half], tops[pair, half], with_ones(one_ref[1, there, lanes])
            )
            for block in (2 * half, 2 * half + 1):
                low, high = windows[block]
                hold = near_hold.at[pair, block, :, : high - low]
                near = weigh(hold, tops[pair, half, block], with_ones(v_ref[low:high, lanes]))
                part = slice((block - 2 * half) * BLOCK // 2, (block - 2 * half + 1) * BLOCK // 2)
                done = merged(near, [doubled(x[part]) for x in coarse])
                for index, field in enumerate(done):
                    state[index, block * BLOCK : (block + 1) * BLOCK, lanes] = field


def near_kernel(first_ref, two_ref, near_ref, scratch):
    inner = first_ref.shape[1] - BLOCK
    two_ref[:, :inner, :] = first_ref[:, BLOCK:, :]
    for which in range(2):
        spill(first_ref.at[which, pl.ds(0, BLOCK), :], scratch.at[which])
        for half in range(scratch.shape[1]):
            lanes = pl.ds(half * PAIR, PAIR)
            slabs = slabs_of(scratch.at[which, half], 0)
            two_ref[which, inner:, lanes] = joined(pooled_slabs(pooled_slabs(slabs)))
        near_ref[which] = repooled(repooled(two_ref[which]))


def join_kernel(four_ref, six_ref, query_ref, out):
    sixteenth = four_ref.shape[1]
    out[:, :sixteenth, :] = four_ref[...]
    out[:, sixteenth:, :] = six_ref[...]


def mid_kernel(
    edge_q, two_q, state, three_q, first_ref, second_ref, two_ref, three_a, three_b, out,
    holds, three_hold,
):
    rows = state.shape[1]
    blocks = rows // BLOCK
    position = lax.axis_index("seq")
    last = lax.axis_size("seq") - 1
    even = lax.rem(position, 2) == 0
    opens = (position > 0, position < last)
    pairs = two_q.shape[1] // PAIR
    steps = {}
    for pair in range(pairs):
        lanes = pl.ds(pair * PAIR, PAIR)
        inner = [first_ref[which, :BLOCK, lanes] for which in range(2)]
        outer = [second_ref[which, :, lanes] for which in range(2)]
        steps[pair, 2] = (
            score(two_q[:, lanes], two_ref[0, :, lanes], holds.at[pair, 2]),
            with_ones(two_ref[1, :, lanes]),
        )
        three = [
            jnp.concatenate([three_a[which, :, lanes], three_b[which, :, lanes]], axis=0)
            for which in range(2)
        ]
        steps[pair, 3] = (
            score(three_q[:, lanes], three[0], three_hold.at[pair]), with_ones(three[1])
        )
        for side in range(2):
            halo = [
                jnp.where(even, *((outer[which], inner[which])[:: 1 - 2 * side]))
                for which in range(2)
            ]
            steps[pair, side] = (
                score(edge_q[side, :, lanes], halo[0], holds.at[pair, side], opens[side]),
                with_ones(halo[1]),
            )
    for pair in range(pairs):
        lanes = pl.ds(pair * PAIR, PAIR)
        three = weigh(three_hold.at[pair], *steps[pair, 3])
        two = merged(weigh(holds.at[pair, 2], *steps[pair, 2]), [doubled(x) for x in three])
        for block in range(blocks):
            here = slice(block * BLOCK, (block + 1) * BLOCK)
            quarter = slice(block * BLOCK // 4, (block + 1) * BLOCK // 4)
            done = merged(
                [state[index, here, lanes] for index in range(3)],
                [doubled(doubled(x[quarter])) for x in two],
            )
            for side, edge in enumerate((0, blocks - 1)):
                if block == edge:
                    done = merged(done, weigh(holds.at[pair, side], *steps[pair, side]))
            for index, field in enumerate(done):
                out[index, here, lanes] = field


def finish_kernel(
    four_q, state, four_ref, near_ref, three_a, three_b, fours_a, fours_b, *refs
):
    far, refs = refs[:-6], refs[-6:]
    outs, (attended, four_hold) = refs[:-2], refs[-2:]
    rows = state.shape[1]
    blocks = rows // BLOCK
    own = lax.axis_index("head")
    pairs = four_q.shape[1] // PAIR
    steps = {}
    for pair in range(pairs):
        lanes = pl.ds(pair * PAIR, PAIR)
        ours, theirs, beyond = [], [], []
        for which in range(2):
            ours.append(
                [four_ref[which, :, lanes], near_ref[which, :, lanes]]
                + [repooled(field[which, :, lanes]) for field in (three_a, three_b)]
            )
            theirs.append([field[which, :, lanes] for field in (fours_a, fours_b)])
            beyond.append([field[which, :, lanes] for field in far])
        steps[pair] = (
            score(
                four_q[:, lanes],
                jnp.concatenate(ours[0] + theirs[0] + beyond[0], axis=0),
                four_hold.at[pair],
            ),
            jnp.concatenate(
                [with_ones(field) for field in ours[1]]
                + [with_ones(field, 2.0) for field in theirs[1]]
                + [with_ones(field) for field in beyond[1]],
                axis=0,
            ),
        )
    for pair in range(pairs):
        lanes = pl.ds(pair * PAIR, PAIR)
        four = weigh(four_hold.at[pair], *steps[pair])
        for block in range(blocks):
            here = slice(block * BLOCK, (block + 1) * BLOCK)
            coarse = [x[block * SLAB : (block + 1) * SLAB] for x in four]
            for _ in range(LEVELS):
                coarse = [doubled(x) for x in coarse]
            _, numer, rowsum = merged([state[index, here, lanes] for index in range(3)], coarse)
            attended[block, :, lanes] = (numer / rowsum).astype(jnp.bfloat16)
    for step, out in enumerate(outs):
        out[...] = attended[own ^ step]


def partial_kernel(near_ref, next_ref, weight_ref, out_ref):
    own = lax.axis_index("head")
    features = near_ref.shape[1]
    total = None
    for step, part in enumerate((near_ref, next_ref)):
        start = pl.multiple_of((own ^ step) * features, features)
        product = jnp.dot(
            part[...], weight_ref[pl.ds(start, features), :], preferred_element_type=jnp.float32
        )
        total = product if total is None else total + product
    out_ref[...] = total


def project_kernel(partial_ref, *refs):
    parts, (weight_ref, out_hbm, scratch, staged, sems) = refs[:-5], refs[-5:]
    own = lax.axis_index("head")
    features = parts[0].shape[1]
    chunk = staged.shape[2]
    copies = []
    for index in range(staged.shape[0]):
        columns = pl.ds(index * chunk, chunk)
        total = partial_ref[:, columns]
        for step, part in enumerate(parts, 2):
            start = pl.multiple_of((own ^ step) * features, features)
            total += jnp.dot(
                part[...],
                weight_ref[pl.ds(start, features), columns],
                preferred_element_type=jnp.float32,
            )
        for half in range(chunk // PAIR):
            lanes = slice(half * PAIR, (half + 1) * PAIR)
            scratch[index, half] = total[:, lanes]
            for i in range(SLAB):
                staged[index, i * FAN : (i + 1) * FAN, lanes] = scratch[
                    index, half, pl.ds(i, FAN, stride=SLAB), :
                ].astype(jnp.bfloat16)
        copy = pltpu.make_async_copy(staged.at[index], out_hbm.at[:, columns], sems.at[index])
        copy.start()
        copies.append(copy)
    for copy in copies:
        copy.wait()


def repool_outside(field):
    which, rows, lanes = field.shape
    slabs = field.astype(jnp.float32).reshape(which, rows // (2 * SLAB), 2, SLAB, lanes)
    sums = (slabs[:, :, 0] + slabs[:, :, 1]) * root_half
    return sums.reshape(which, rows // 2, lanes).astype(jnp.bfloat16)


def swapped(block, axis, mask):
    return lax.ppermute(block, axis, [(i, i ^ mask) for i in range(lax.axis_size(axis))])


def across(block):
    count, heads = lax.axis_size("seq"), lax.axis_size("head")
    route = []
    for seq in range(count):
        end = seq in (0, count - 1)
        other = seq if end else seq + 1 if seq % 2 else seq - 1
        for head in range(heads):
            route.append((seq * heads + head, other * heads + (head ^ 1 if end else head)))
    return lax.ppermute(block, ("seq", "head"), route)


def per_device(queries, key_vectors, value_vectors, out_weight):
    rows, features = queries.shape[1:]
    queries, key_vectors, value_vectors = [
        pltpu.with_memory_space_constraint(x, pltpu.HBM)
        for x in (queries, key_vectors, value_vectors)
    ]
    pairs = features // PAIR
    seq_count, head_count = lax.axis_size("seq"), lax.axis_size("head")
    bf16 = lambda *shape: jax.ShapeDtypeStruct(shape, jnp.bfloat16)
    params = pltpu.CompilerParams(vmem_limit_bytes=32 * 1024 * 1024)

    hbm = pl.BlockSpec(memory_space=pltpu.HBM)
    vmem = pl.BlockSpec(memory_space=pltpu.VMEM)
    keys, values, ours, first, one, two = pl.pallas_call(
        pool_kernel,
        in_specs=[hbm] * 3,
        out_shape=[
            bf16(rows, features),
            bf16(rows, features),
            bf16(rows, features),
            bf16(2, BLOCK + rows // 4 - BLOCK // 4, features),
            bf16(2, rows // 2, features),
            bf16(2, rows // 4, features),
        ],
        scratch_shapes=[
            pltpu.VMEM((2, rows // BLOCK, pairs, BLOCK, PAIR), jnp.float32),
            pltpu.SemaphoreType.DMA((2, rows // BLOCK)),
            pltpu.SemaphoreType.DMA((1,)),
        ],
        compiler_params=params,
        name="pool",
    )(key_vectors, value_vectors, queries)
    second, three, four = pl.pallas_call(
        deeper_kernel,
        out_shape=[
            bf16(2, BLOCK, features),
            bf16(2, rows // 8, features),
            bf16(2, rows // 16, features),
        ],
        compiler_params=params,
        cost_estimate=pl.CostEstimate(flops=2**31, bytes_accessed=2**23, transcendentals=0),
        name="deeper",
    )(keys, values, two)

    first_in = swapped(first, "seq", 1)
    second_in = across(second)
    four_in = swapped(four, "seq", 4)
    six_in = swapped(four, "seq", 6)
    threes_in = [swapped(three, "seq", mask) for mask in (3, 2)]
    edge_q, two_q, three_q, four_q, state = pl.pallas_call(
        local_kernel,
        out_shape=[
            bf16(2, BLOCK, features),
            bf16(rows // 4, features),
            bf16(rows // 8, features),
            bf16(rows // 16, features),
            jax.ShapeDtypeStruct((3, rows, features), jnp.float32),
        ],
        scratch_shapes=[
            pltpu.VMEM((pairs, rows, PAIR), jnp.float32),
            pltpu.VMEM((pairs, rows // BLOCK, 2 * BLOCK, 3 * BLOCK), jnp.float32),
            pltpu.VMEM((pairs, rows // BLOCK // 2, 2 * BLOCK, BLOCK), jnp.float32),
        ],
        compiler_params=params,
        name="local",
    )(ours, keys, values, one)

    fours = pl.pallas_call(
        join_kernel,
        out_shape=bf16(2, rows // 8, features),
        compiler_params=params,
        cost_estimate=pl.CostEstimate(flops=2**29, bytes_accessed=2**20, transcendentals=0),
        name="join",
    )(four_in, six_in, four_q)
    fours_in = swapped(fours, "seq", 1)
    two_in, near = pl.pallas_call(
        near_kernel,
        out_shape=[bf16(2, rows // 4, features), bf16(2, rows // 16, features)],
        scratch_shapes=[pltpu.VMEM((2, pairs, BLOCK, PAIR), jnp.float32)],
        compiler_params=params,
        name="near",
    )(first_in)

    state = pl.pallas_call(
        mid_kernel,
        out_shape=jax.ShapeDtypeStruct((3, rows, features), jnp.float32),
        input_output_aliases={2: 0},
        scratch_shapes=[
            pltpu.VMEM((pairs, 3, 2 * BLOCK, BLOCK), jnp.float32),
            pltpu.VMEM((pairs, rows // 4, BLOCK), jnp.float32),
        ],
        compiler_params=params,
        name="mid",
    )(edge_q, two_q, state, three_q, first_in, second_in, two_in, *threes_in)

    far = []
    known = 8
    if known < seq_count:
        group = [four, near] + [repool_outside(field) for field in threes_in]
        group = jnp.concatenate(group + [fours, fours_in], axis=1)
        while known < seq_count:
            fresh = swapped(group, "seq", known)
            far.append(fresh)
            group = jnp.concatenate([group, fresh], axis=1)
            known *= 2

    outs = pl.pallas_call(
        finish_kernel,
        out_shape=[bf16(BLOCK, features) for _ in range(head_count)],
        scratch_shapes=[
            pltpu.VMEM((rows // BLOCK, BLOCK, features), jnp.bfloat16),
            pltpu.VMEM((pairs, rows // 8, rows // 16 * seq_count), jnp.float32),
        ],
        compiler_params=params,
        name="finish",
    )(four_q, state, four, near, *threes_in, fours, fours_in, *far)

    parts = [part if step == 0 else swapped(part, "head", step) for step, part in enumerate(outs)]
    width = out_weight.shape[1]
    partial = pl.pallas_call(
        partial_kernel,
        out_shape=jax.ShapeDtypeStruct((BLOCK, width), jnp.float32),
        compiler_params=params,
        name="partial",
    )(*parts[:2], out_weight)
    chunk = 2 * PAIR
    result = pl.pallas_call(
        project_kernel,
        in_specs=[vmem] * len(parts),
        out_specs=hbm,
        out_shape=bf16(BLOCK, width),
        scratch_shapes=[
            pltpu.VMEM((width // chunk, 2, BLOCK, PAIR), jnp.float32),
            pltpu.VMEM((width // chunk, BLOCK, chunk), jnp.bfloat16),
            pltpu.SemaphoreType.DMA((width // chunk,)),
        ],
        compiler_params=params,
        name="project",
    )(partial, *parts[2:], out_weight)
    return result[None]


def solution(mesh):
    return jax.shard_map(
        per_device,
        mesh=mesh,
        in_specs=(P(None, "seq", "head"), P(None, "seq", "head"), P(None, "seq", "head"), P()),
        out_specs=P(None, ("seq", "head"), None),
        check_vma=False,
    )
```

```python
import jax
import jax.numpy as jnp
from jax import lax
from jax.experimental import pallas as pl
from jax.experimental.pallas import tpu as pltpu
from jax.sharding import PartitionSpec as P

HD = 64
BLOCK = 128
LEVELS = 4
SLAB = 8
PAIR = 2 * HD

neg_fill = -1e30
root_half = 0.7071067811865476
log2_scale = HD**-0.5 * 1.4426950408889634

FAN = 2**LEVELS


def slabs_of(scratch, block):
    return [scratch[pl.ds(BLOCK * block + j, SLAB, stride=FAN), :] for j in range(FAN)]


def pooled_slabs(slabs):
    return [
        ((low + high) * root_half).astype(jnp.bfloat16).astype(jnp.float32)
        for low, high in zip(slabs[0::2], slabs[1::2])
    ]


def joined(slabs):
    return jnp.concatenate(slabs, axis=0).astype(jnp.bfloat16)


def spill(source, scratch):
    for half in range(scratch.shape[0]):
        scratch[half] = source[:, half * PAIR : (half + 1) * PAIR].astype(jnp.float32)


def pool_kernel(
    k_hbm, v_hbm, q_hbm, k_ref, v_ref, q_ref, first_ref, one_ref, two_ref, scratch, sems, q_sem
):
    rows = k_ref.shape[0]
    blocks = rows // BLOCK
    arrivals = []
    for block in range(blocks):
        here = pl.ds(block * BLOCK, BLOCK)
        for which, (source, target) in enumerate(((k_hbm, k_ref), (v_hbm, v_ref))):
            copy = pltpu.make_async_copy(
                source.at[0, here, :], target.at[here, :], sems.at[which, block]
            )
            copy.start()
            arrivals.append((block, which, target, copy))
    q_copy = pltpu.make_async_copy(q_hbm.at[0], q_ref, q_sem.at[0])
    q_copy.start()
    even = lax.rem(lax.axis_index("seq"), 2) == 0
    for block, which, ref, copy in arrivals:
        copy.wait()
        here = pl.ds(block * BLOCK, BLOCK)
        spill(ref.at[here, :], scratch.at[which, block])
        for half in range(scratch.shape[2]):
            lanes = pl.ds(half * PAIR, PAIR)
            one = pooled_slabs(slabs_of(scratch.at[which, block, half], 0))
            one_ref[which, pl.ds(block * BLOCK // 2, BLOCK // 2), lanes] = joined(one)
            two_ref[which, pl.ds(block * BLOCK // 4, BLOCK // 4), lanes] = joined(pooled_slabs(one))
    inner = rows // 4 - BLOCK // 4
    for which, ref in enumerate((k_ref, v_ref)):
        first_ref[which, :BLOCK, :] = jnp.where(even, ref[rows - BLOCK :, :], ref[:BLOCK, :])
        first_ref[which, BLOCK:, :] = jnp.where(
            even, two_ref[which, :inner, :], two_ref[which, BLOCK // 4 :, :]
        )
    q_copy.wait()


def repooled(field):
    rows, lanes = field.shape
    slabs = field.astype(jnp.float32).reshape(rows // (2 * SLAB), 2, SLAB, lanes)
    return ((slabs[:, 0] + slabs[:, 1]) * root_half).reshape(rows // 2, lanes).astype(jnp.bfloat16)


def deeper_kernel(k_ref, v_ref, two_ref, second_ref, three_ref, four_ref):
    rows = k_ref.shape[0]
    even = lax.rem(lax.axis_index("seq"), 2) == 0
    for which, ref in enumerate((k_ref, v_ref)):
        second_ref[which] = jnp.where(even, ref[:BLOCK, :], ref[rows - BLOCK :, :])
        three = repooled(two_ref[which])
        three_ref[which] = three
        four_ref[which] = repooled(three)


def repooled(field):
    rows, lanes = field.shape
    slabs = field.astype(jnp.float32).reshape(rows // (2 * SLAB), 2, SLAB, lanes)
    return ((slabs[:, 0] + slabs[:, 1]) * root_half).reshape(rows // 2, lanes).astype(jnp.bfloat16)


def score(queries, keys, hold, is_open=None):
    rows = queries.shape[0]
    low = lax.broadcasted_iota(jnp.int32, (rows, PAIR), 1) < HD
    zero = jnp.zeros_like(queries)
    both = jnp.concatenate([jnp.where(low, queries, zero), jnp.where(low, zero, queries)], axis=0)
    raw = lax.dot_general(both, keys, (((1,), (1,)), ((), ())), preferred_element_type=jnp.float32)
    if is_open is not None:
        raw = jnp.where(is_open, raw, neg_fill)
    hold[...] = raw
    return jnp.max(raw, axis=1, keepdims=True)


def weigh(hold, top, values):
    rows = top.shape[0] // 2
    low = lax.broadcasted_iota(jnp.int32, (rows, PAIR), 1) < HD
    weights = jnp.exp2((hold[...] - top) * log2_scale).astype(jnp.bfloat16)
    result = jnp.dot(weights, values, preferred_element_type=jnp.float32)
    return (
        log2_scale * jnp.where(low, top[:rows], top[rows:]),
        jnp.where(low, result[:rows, :PAIR], result[rows:, :PAIR]),
        jnp.where(low, result[:rows, PAIR:], result[rows:, PAIR:]),
    )


def merged(fine, coarse):
    top = jnp.maximum(fine[0], coarse[0])
    keep = jnp.exp2(fine[0] - top)
    join = jnp.exp2(coarse[0] - top)
    return top, fine[1] * keep + coarse[1] * join, fine[2] * keep + coarse[2] * join


def doubled(field):
    rows, lanes = field.shape
    slabs = field.reshape(rows // SLAB, 1, SLAB, lanes)
    return jnp.broadcast_to(slabs, (rows // SLAB, 2, SLAB, lanes)).reshape(2 * rows, lanes)


def with_ones(values, weight=1.0):
    if weight != 1.0:
        values = values * jnp.bfloat16(weight)
    return jnp.concatenate([values, jnp.full(values.shape, weight, jnp.bfloat16)], axis=1)


def local_kernel(
    q_ref, k_ref, v_ref, one_ref, four_ref, edge_q, two_q, three_q, four_q, state,
    scratch, near_hold, coarse_hold,
):
    rows = q_ref.shape[0]
    blocks = rows // BLOCK
    pairs = scratch.shape[0]
    spill(q_ref, scratch)
    fine, one_q = [], []
    for pair in range(pairs):
        lanes = pl.ds(pair * PAIR, PAIR)
        ladder = [[], [], [], [], []]
        for block in range(blocks):
            slabs = slabs_of(scratch.at[pair], block)
            ladder[0].append(joined(slabs))
            for level in range(1, LEVELS + 1):
                slabs = pooled_slabs(slabs)
                ladder[level] += slabs
        edge_q[0, :, lanes] = ladder[0][0]
        edge_q[1, :, lanes] = ladder[0][-1]
        two_q[:, lanes] = joined(ladder[2])
        three_q[:, lanes] = joined(ladder[3])
        four_q[:, lanes] = joined(ladder[4])
        fine.append(ladder[0])
        one_q.append([joined(ladder[1][n : n + FAN]) for n in range(0, len(ladder[1]), FAN)])
    windows = [(max(n - 1, 0) * BLOCK, min(n + 2, blocks) * BLOCK) for n in range(blocks)]
    tops = {}
    for pair in range(pairs):
        lanes = pl.ds(pair * PAIR, PAIR)
        for half in range(blocks // 2):
            there = pl.ds((half ^ 1) * BLOCK, BLOCK)
            tops[pair, half] = score(
                one_q[pair][half], one_ref[0, there, lanes], coarse_hold.at[pair, half]
            )
            for block in (2 * half, 2 * half + 1):
                low, high = windows[block]
                hold = near_hold.at[pair, block, :, : high - low]
                tops[pair, half, block] = score(fine[pair][block], k_ref[low:high, lanes], hold)
    for pair in range(pairs):
        lanes = pl.ds(pair * PAIR, PAIR)
        for half in range(blocks // 2):
            there = pl.ds((half ^ 1) * BLOCK, BLOCK)
            coarse = weigh(
                coarse_hold.at[pair, half], tops[pair, half], with_ones(one_ref[1, there, lanes])
            )
            for block in (2 * half, 2 * half + 1):
                low, high = windows[block]
                hold = near_hold.at[pair, block, :, : high - low]
                near = weigh(hold, tops[pair, half, block], with_ones(v_ref[low:high, lanes]))
                part = slice((block - 2 * half) * BLOCK // 2, (block - 2 * half + 1) * BLOCK // 2)
                done = merged(near, [doubled(x[part]) for x in coarse])
                for index, field in enumerate(done):
                    state[index, block * BLOCK : (block + 1) * BLOCK, lanes] = field


def join_kernel(four_ref, six_ref, query_ref, out):
    sixteenth = four_ref.shape[1]
    out[:, :sixteenth, :] = four_ref[...]
    out[:, sixteenth:, :] = six_ref[...]


def coarse_kernel(
    two_q, three_q, first_ref, three_a, three_b, coarse, near_ref, scratch, two_ref, two_hold, three_hold
):
    inner = first_ref.shape[1] - BLOCK
    pairs = scratch.shape[1]
    two_ref[:, :inner, :] = first_ref[:, BLOCK:, :]
    for which in range(2):
        spill(first_ref.at[which, pl.ds(0, BLOCK), :], scratch.at[which])
        for half in range(pairs):
            lanes = pl.ds(half * PAIR, PAIR)
            slabs = slabs_of(scratch.at[which, half], 0)
            two_ref[which, inner:, lanes] = joined(pooled_slabs(pooled_slabs(slabs)))
        near_ref[which] = repooled(repooled(two_ref[which]))
    steps = {}
    for pair in range(pairs):
        lanes = pl.ds(pair * PAIR, PAIR)
        three = [
            jnp.concatenate([three_a[which, :, lanes], three_b[which, :, lanes]], axis=0)
            for which in range(2)
        ]
        steps[pair, 3] = (
            score(three_q[:, lanes], three[0], three_hold.at[pair]), with_ones(three[1])
        )
        steps[pair, 2] = (
            score(two_q[:, lanes], two_ref[0, :, lanes], two_hold.at[pair]),
            with_ones(two_ref[1, :, lanes]),
        )
    for pair in range(pairs):
        three = weigh(three_hold.at[pair], *steps[pair, 3])
        two = merged(weigh(two_hold.at[pair], *steps[pair, 2]), [doubled(x) for x in three])
        for index, field in enumerate(two):
            coarse[index, :, pl.ds(pair * PAIR, PAIR)] = field


def mid_kernel(edge_q, coarse, state, first_ref, second_ref, out, holds):
    rows = state.shape[1]
    blocks = rows // BLOCK
    position = lax.axis_index("seq")
    last = lax.axis_size("seq") - 1
    even = lax.rem(position, 2) == 0
    opens = (position > 0, position < last)
    pairs = holds.shape[0]
    steps = {}
    for pair in range(pairs):
        lanes = pl.ds(pair * PAIR, PAIR)
        inner = [first_ref[which, :BLOCK, lanes] for which in range(2)]
        outer = [second_ref[which, :, lanes] for which in range(2)]
        for side in range(2):
            halo = [
                jnp.where(even, *((outer[which], inner[which])[:: 1 - 2 * side]))
                for which in range(2)
            ]
            steps[pair, side] = (
                score(edge_q[side, :, lanes], halo[0], holds.at[pair, side], opens[side]),
                with_ones(halo[1]),
            )
    for pair in range(pairs):
        lanes = pl.ds(pair * PAIR, PAIR)
        for block in range(blocks):
            here = slice(block * BLOCK, (block + 1) * BLOCK)
            quarter = slice(block * BLOCK // 4, (block + 1) * BLOCK // 4)
            done = merged(
                [state[index, here, lanes] for index in range(3)],
                [doubled(doubled(coarse[index, quarter, lanes])) for index in range(3)],
            )
            for side, edge in enumerate((0, blocks - 1)):
                if block == edge:
                    done = merged(done, weigh(holds.at[pair, side], *steps[pair, side]))
            for index, field in enumerate(done):
                out[index, here, lanes] = field


def finish_kernel(
    four_q, state, four_ref, near_ref, three_a, three_b, fours_a, fours_b, *refs
):
    far, refs = refs[:-6], refs[-6:]
    outs, (attended, four_hold) = refs[:-2], refs[-2:]
    rows = state.shape[1]
    blocks = rows // BLOCK
    own = lax.axis_index("head")
    pairs = four_q.shape[1] // PAIR
    steps = {}
    for pair in range(pairs):
        lanes = pl.ds(pair * PAIR, PAIR)
        ours, theirs, beyond = [], [], []
        for which in range(2):
            ours.append(
                [four_ref[which, :, lanes], near_ref[which, :, lanes]]
                + [repooled(field[which, :, lanes]) for field in (three_a, three_b)]
            )
            theirs.append([field[which, :, lanes] for field in (fours_a, fours_b)])
            beyond.append([field[which, :, lanes] for field in far])
        steps[pair] = (
            score(
                four_q[:, lanes],
                jnp.concatenate(ours[0] + theirs[0] + beyond[0], axis=0),
                four_hold.at[pair],
            ),
            jnp.concatenate(
                [with_ones(field) for field in ours[1]]
                + [with_ones(field, 2.0) for field in theirs[1]]
                + [with_ones(field) for field in beyond[1]],
                axis=0,
            ),
        )
    for pair in range(pairs):
        lanes = pl.ds(pair * PAIR, PAIR)
        four = weigh(four_hold.at[pair], *steps[pair])
        for block in range(blocks):
            here = slice(block * BLOCK, (block + 1) * BLOCK)
            coarse = [x[block * SLAB : (block + 1) * SLAB] for x in four]
            for _ in range(LEVELS):
                coarse = [doubled(x) for x in coarse]
            _, numer, rowsum = merged([state[index, here, lanes] for index in range(3)], coarse)
            attended[block, :, lanes] = (numer / rowsum).astype(jnp.bfloat16)
    for step, out in enumerate(outs):
        out[...] = attended[own ^ step]


def partial_kernel(near_ref, next_ref, weight_ref, out_ref):
    own = lax.axis_index("head")
    features = near_ref.shape[1]
    total = None
    for step, part in enumerate((near_ref, next_ref)):
        start = pl.multiple_of((own ^ step) * features, features)
        product = jnp.dot(
            part[...], weight_ref[pl.ds(start, features), :], preferred_element_type=jnp.float32
        )
        total = product if total is None else total + product
    out_ref[...] = total


def project_kernel(partial_ref, *refs):
    parts, (weight_ref, out_hbm, scratch, staged, sems) = refs[:-5], refs[-5:]
    own = lax.axis_index("head")
    features = parts[0].shape[1]
    chunk = staged.shape[2]
    copies = []
    for index in range(staged.shape[0]):
        columns = pl.ds(index * chunk, chunk)
        total = partial_ref[:, columns]
        for step, part in enumerate(parts, 2):
            start = pl.multiple_of((own ^ step) * features, features)
            total += jnp.dot(
                part[...],
                weight_ref[pl.ds(start, features), columns],
                preferred_element_type=jnp.float32,
            )
        for half in range(chunk // PAIR):
            lanes = slice(half * PAIR, (half + 1) * PAIR)
            scratch[index, half] = total[:, lanes]
            for i in range(SLAB):
                staged[index, i * FAN : (i + 1) * FAN, lanes] = scratch[
                    index, half, pl.ds(i, FAN, stride=SLAB), :
                ].astype(jnp.bfloat16)
        copy = pltpu.make_async_copy(staged.at[index], out_hbm.at[:, columns], sems.at[index])
        copy.start()
        copies.append(copy)
    for copy in copies:
        copy.wait()


def repool_outside(field):
    which, rows, lanes = field.shape
    slabs = field.astype(jnp.float32).reshape(which, rows // (2 * SLAB), 2, SLAB, lanes)
    sums = (slabs[:, :, 0] + slabs[:, :, 1]) * root_half
    return sums.reshape(which, rows // 2, lanes).astype(jnp.bfloat16)


def swapped(block, axis, mask):
    return lax.ppermute(block, axis, [(i, i ^ mask) for i in range(lax.axis_size(axis))])


def across(block):
    count, heads = lax.axis_size("seq"), lax.axis_size("head")
    route = []
    for seq in range(count):
        end = seq in (0, count - 1)
        other = seq if end else seq + 1 if seq % 2 else seq - 1
        for head in range(heads):
            route.append((seq * heads + head, other * heads + (head ^ 1 if end else head)))
    return lax.ppermute(block, ("seq", "head"), route)


def per_device(queries, key_vectors, value_vectors, out_weight):
    rows, features = queries.shape[1:]
    queries, key_vectors, value_vectors = [
        pltpu.with_memory_space_constraint(x, pltpu.HBM)
        for x in (queries, key_vectors, value_vectors)
    ]
    pairs = features // PAIR
    seq_count, head_count = lax.axis_size("seq"), lax.axis_size("head")
    bf16 = lambda *shape: jax.ShapeDtypeStruct(shape, jnp.bfloat16)
    params = pltpu.CompilerParams(vmem_limit_bytes=32 * 1024 * 1024)

    hbm = pl.BlockSpec(memory_space=pltpu.HBM)
    vmem = pl.BlockSpec(memory_space=pltpu.VMEM)
    keys, values, ours, first, one, two = pl.pallas_call(
        pool_kernel,
        in_specs=[hbm] * 3,
        out_shape=[
            bf16(rows, features),
            bf16(rows, features),
            bf16(rows, features),
            bf16(2, BLOCK + rows // 4 - BLOCK // 4, features),
            bf16(2, rows // 2, features),
            bf16(2, rows // 4, features),
        ],
        scratch_shapes=[
            pltpu.VMEM((2, rows // BLOCK, pairs, BLOCK, PAIR), jnp.float32),
            pltpu.SemaphoreType.DMA((2, rows // BLOCK)),
            pltpu.SemaphoreType.DMA((1,)),
        ],
        compiler_params=params,
        name="pool",
    )(key_vectors, value_vectors, queries)
    second, three, four = pl.pallas_call(
        deeper_kernel,
        out_shape=[
            bf16(2, BLOCK, features),
            bf16(2, rows // 8, features),
            bf16(2, rows // 16, features),
        ],
        compiler_params=params,
        cost_estimate=pl.CostEstimate(flops=2**31, bytes_accessed=2**23, transcendentals=0),
        name="deeper",
    )(keys, values, two)

    first_in = swapped(first, "seq", 1)
    second_in = across(second)
    four_in = swapped(four, "seq", 4)
    six_in = swapped(four, "seq", 6)
    threes_in = [swapped(three, "seq", mask) for mask in (3, 2)]
    edge_q, two_q, three_q, four_q, state = pl.pallas_call(
        local_kernel,
        out_shape=[
            bf16(2, BLOCK, features),
            bf16(rows // 4, features),
            bf16(rows // 8, features),
            bf16(rows // 16, features),
            jax.ShapeDtypeStruct((3, rows, features), jnp.float32),
        ],
        scratch_shapes=[
            pltpu.VMEM((pairs, rows, PAIR), jnp.float32),
            pltpu.VMEM((pairs, rows // BLOCK, 2 * BLOCK, 3 * BLOCK), jnp.float32),
            pltpu.VMEM((pairs, rows // BLOCK // 2, 2 * BLOCK, BLOCK), jnp.float32),
        ],
        compiler_params=params,
        name="local",
    )(ours, keys, values, one, four_in)

    fours = pl.pallas_call(
        join_kernel,
        out_shape=bf16(2, rows // 8, features),
        compiler_params=params,
        cost_estimate=pl.CostEstimate(flops=2**29, bytes_accessed=2**20, transcendentals=0),
        name="join",
    )(four_in, six_in, four_q)
    fours_in = swapped(fours, "seq", 1)
    coarse, near = pl.pallas_call(
        coarse_kernel,
        out_shape=[
            jax.ShapeDtypeStruct((3, rows // 4, features), jnp.float32),
            bf16(2, rows // 16, features),
        ],
        scratch_shapes=[
            pltpu.VMEM((2, pairs, BLOCK, PAIR), jnp.float32),
            pltpu.VMEM((2, rows // 4, features), jnp.bfloat16),
            pltpu.VMEM((pairs, rows // 2, BLOCK), jnp.float32),
            pltpu.VMEM((pairs, rows // 4, BLOCK), jnp.float32),
        ],
        compiler_params=params,
        cost_estimate=pl.CostEstimate(flops=2**31, bytes_accessed=2**21, transcendentals=0),
        name="coarse",
    )(two_q, three_q, first_in, *threes_in)
    state = pl.pallas_call(
        mid_kernel,
        out_shape=jax.ShapeDtypeStruct((3, rows, features), jnp.float32),
        input_output_aliases={2: 0},
        scratch_shapes=[pltpu.VMEM((pairs, 2, 2 * BLOCK, BLOCK), jnp.float32)],
        compiler_params=params,
        name="mid",
    )(edge_q, coarse, state, first_in, second_in)

    far = []
    known = 8
    if known < seq_count:
        group = [four, near] + [repool_outside(field) for field in threes_in]
        group = jnp.concatenate(group + [fours, fours_in], axis=1)
        while known < seq_count:
            fresh = swapped(group, "seq", known)
            far.append(fresh)
            group = jnp.concatenate([group, fresh], axis=1)
            known *= 2

    outs = pl.pallas_call(
        finish_kernel,
        out_shape=[bf16(BLOCK, features) for _ in range(head_count)],
        scratch_shapes=[
            pltpu.VMEM((rows // BLOCK, BLOCK, features), jnp.bfloat16),
            pltpu.VMEM((pairs, rows // 8, rows // 16 * seq_count), jnp.float32),
        ],
        compiler_params=params,
        name="finish",
    )(four_q, state, four, near, *threes_in, fours, fours_in, *far)

    parts = [part if step == 0 else swapped(part, "head", step) for step, part in enumerate(outs)]
    width = out_weight.shape[1]
    partial = pl.pallas_call(
        partial_kernel,
        out_shape=jax.ShapeDtypeStruct((BLOCK, width), jnp.float32),
        compiler_params=params,
        name="partial",
    )(*parts[:2], out_weight)
    chunk = 2 * PAIR
    result = pl.pallas_call(
        project_kernel,
        in_specs=[vmem] * len(parts),
        out_specs=hbm,
        out_shape=bf16(BLOCK, width),
        scratch_shapes=[
            pltpu.VMEM((width // chunk, 2, BLOCK, PAIR), jnp.float32),
            pltpu.VMEM((width // chunk, BLOCK, chunk), jnp.bfloat16),
            pltpu.SemaphoreType.DMA((width // chunk,)),
        ],
        compiler_params=params,
        name="project",
    )(partial, *parts[2:], out_weight)
    return result[None]


def solution(mesh):
    return jax.shard_map(
        per_device,
        mesh=mesh,
        in_specs=(P(None, "seq", "head"), P(None, "seq", "head"), P(None, "seq", "head"), P()),
        out_specs=P(None, ("seq", "head"), None),
        check_vma=False,
    )
```

```python
import jax
import jax.numpy as jnp
from jax import lax
from jax.experimental import pallas as pl
from jax.experimental.pallas import tpu as pltpu
from jax.sharding import PartitionSpec as P

HD = 64
BLOCK = 128
LEVELS = 4
SLAB = 8
PAIR = 2 * HD

neg_fill = -1e30
root_half = 0.7071067811865476
log2_e = 1.4426950408889634
log2_scale = HD**-0.5 * log2_e
least_share = 2.0**-100
CORES = 2

FAN = 2**LEVELS


def slabs_of(scratch, block):
    return [scratch[pl.ds(BLOCK * block + j, SLAB, stride=FAN), :] for j in range(FAN)]


def pooled_slabs(slabs):
    return [
        ((low + high) * root_half).astype(jnp.bfloat16).astype(jnp.float32)
        for low, high in zip(slabs[0::2], slabs[1::2])
    ]


def joined(slabs):
    return jnp.concatenate(slabs, axis=0).astype(jnp.bfloat16)


def spill(source, scratch):
    for half in range(scratch.shape[0]):
        scratch[half] = source[:, half * PAIR : (half + 1) * PAIR].astype(jnp.float32)


def pool_kernel(
    k_hbm, v_hbm, q_hbm, k_ref, v_ref, q_ref, first_ref, one_ref, two_ref, scratch, sems, q_sem
):
    rows = k_ref.shape[0]
    blocks = rows // BLOCK
    arrivals = []
    for block in range(blocks):
        here = pl.ds(block * BLOCK, BLOCK)
        for which, (source, target) in enumerate(((k_hbm, k_ref), (v_hbm, v_ref))):
            copy = pltpu.make_async_copy(
                source.at[0, here, :], target.at[here, :], sems.at[which, block]
            )
            copy.start()
            arrivals.append((block, which, target, copy))
    q_copy = pltpu.make_async_copy(q_hbm.at[0], q_ref, q_sem.at[0])
    q_copy.start()
    even = lax.rem(lax.axis_index("seq"), 2) == 0
    for block, which, ref, copy in arrivals:
        copy.wait()
        here = pl.ds(block * BLOCK, BLOCK)
        spill(ref.at[here, :], scratch.at[which, block])
        for half in range(scratch.shape[2]):
            lanes = pl.ds(half * PAIR, PAIR)
            one = pooled_slabs(slabs_of(scratch.at[which, block, half], 0))
            one_ref[which, pl.ds(block * BLOCK // 2, BLOCK // 2), lanes] = joined(one)
            two_ref[which, pl.ds(block * BLOCK // 4, BLOCK // 4), lanes] = joined(pooled_slabs(one))
    inner = rows // 4 - BLOCK // 4
    for which, ref in enumerate((k_ref, v_ref)):
        first_ref[which, :BLOCK, :] = jnp.where(even, ref[rows - BLOCK :, :], ref[:BLOCK, :])
        first_ref[which, BLOCK:, :] = jnp.where(
            even, two_ref[which, :inner, :], two_ref[which, BLOCK // 4 :, :]
        )
    q_copy.wait()


def repooled(field):
    rows, lanes = field.shape
    slabs = field.astype(jnp.float32).reshape(rows // (2 * SLAB), 2, SLAB, lanes)
    return ((slabs[:, 0] + slabs[:, 1]) * root_half).reshape(rows // 2, lanes).astype(jnp.bfloat16)


def deeper_kernel(k_ref, v_ref, two_ref, second_ref, three_ref, four_ref):
    rows = k_ref.shape[0]
    even = lax.rem(lax.axis_index("seq"), 2) == 0
    for which, ref in enumerate((k_ref, v_ref)):
        second_ref[which] = jnp.where(even, ref[:BLOCK, :], ref[rows - BLOCK :, :])
        three = repooled(two_ref[which])
        three_ref[which] = three
        four_ref[which] = repooled(three)


def repooled(field):
    rows, lanes = field.shape
    slabs = field.astype(jnp.float32).reshape(rows // (2 * SLAB), 2, SLAB, lanes)
    return ((slabs[:, 0] + slabs[:, 1]) * root_half).reshape(rows // 2, lanes).astype(jnp.bfloat16)


def score(queries, keys, hold, is_open=None):
    rows = queries.shape[0]
    low = lax.broadcasted_iota(jnp.int32, (rows, PAIR), 1) < HD
    zero = jnp.zeros_like(queries)
    both = jnp.concatenate([jnp.where(low, queries, zero), jnp.where(low, zero, queries)], axis=0)
    raw = lax.dot_general(both, keys, (((1,), (1,)), ((), ())), preferred_element_type=jnp.float32)
    if is_open is not None:
        raw = jnp.where(is_open, raw, neg_fill)
    hold[...] = raw
    return jnp.max(raw, axis=1, keepdims=True)


def weigh(hold, top, values):
    rows = top.shape[0] // 2
    low = lax.broadcasted_iota(jnp.int32, (rows, PAIR), 1) < HD
    weights = jnp.exp2((hold[...] - top) * log2_scale).astype(jnp.bfloat16)
    result = jnp.dot(weights, values, preferred_element_type=jnp.float32)
    return (
        log2_scale * jnp.where(low, top[:rows], top[rows:]),
        jnp.where(low, result[:rows, :PAIR], result[rows:, :PAIR]),
        jnp.where(low, result[:rows, PAIR:], result[rows:, PAIR:]),
    )


def merged(fine, coarse):
    top = jnp.maximum(fine[0], coarse[0])
    keep = jnp.exp2(fine[0] - top)
    join = jnp.exp2(coarse[0] - top)
    return top, fine[1] * keep + coarse[1] * join, fine[2] * keep + coarse[2] * join


def doubled(field):
    rows, lanes = field.shape
    slabs = field.reshape(rows // SLAB, 1, SLAB, lanes)
    return jnp.broadcast_to(slabs, (rows // SLAB, 2, SLAB, lanes)).reshape(2 * rows, lanes)


def with_ones(values, weight=1.0):
    if weight != 1.0:
        values = values * jnp.bfloat16(weight)
    return jnp.concatenate([values, jnp.full(values.shape, weight, jnp.bfloat16)], axis=1)


def local_kernel(
    q_ref, k_ref, v_ref, one_ref, four_ref, edge_q, two_q, three_q, four_q, state,
    scratch, near_hold, coarse_hold,
):
    rows = q_ref.shape[0]
    blocks = rows // BLOCK
    pairs = scratch.shape[0]
    spill(q_ref, scratch)
    fine, one_q = [], []
    for pair in range(pairs):
        lanes = pl.ds(pair * PAIR, PAIR)
        ladder = [[], [], [], [], []]
        for block in range(blocks):
            slabs = slabs_of(scratch.at[pair], block)
            ladder[0].append(joined(slabs))
            for level in range(1, LEVELS + 1):
                slabs = pooled_slabs(slabs)
                ladder[level] += slabs
        edge_q[0, :, lanes] = ladder[0][0]
        edge_q[1, :, lanes] = ladder[0][-1]
        two_q[:, lanes] = joined(ladder[2])
        three_q[:, lanes] = joined(ladder[3])
        four_q[:, lanes] = joined(ladder[4])
        fine.append(ladder[0])
        one_q.append([joined(ladder[1][n : n + FAN]) for n in range(0, len(ladder[1]), FAN)])
    windows = [(max(n - 1, 0) * BLOCK, min(n + 2, blocks) * BLOCK) for n in range(blocks)]
    tops = {}
    for pair in range(pairs):
        lanes = pl.ds(pair * PAIR, PAIR)
        for half in range(blocks // 2):
            there = pl.ds((half ^ 1) * BLOCK, BLOCK)
            tops[pair, half] = score(
                one_q[pair][half], one_ref[0, there, lanes], coarse_hold.at[pair, half]
            )
            for block in (2 * half, 2 * half + 1):
                low, high = windows[block]
                hold = near_hold.at[pair, block, :, : high - low]
                tops[pair, half, block] = score(fine[pair][block], k_ref[low:high, lanes], hold)
    for pair in range(pairs):
        lanes = pl.ds(pair * PAIR, PAIR)
        for half in range(blocks // 2):
            there = pl.ds((half ^ 1) * BLOCK, BLOCK)
            coarse = weigh(
                coarse_hold.at[pair, half], tops[pair, half], with_ones(one_ref[1, there, lanes])
            )
            for block in (2 * half, 2 * half + 1):
                low, high = windows[block]
                hold = near_hold.at[pair, block, :, : high - low]
                near = weigh(hold, tops[pair, half, block], with_ones(v_ref[low:high, lanes]))
                part = slice((block - 2 * half) * BLOCK // 2, (block - 2 * half + 1) * BLOCK // 2)
                done = merged(near, [doubled(x[part]) for x in coarse])
                for index, field in enumerate(done):
                    state[index, block * BLOCK : (block + 1) * BLOCK, lanes] = field


def join_kernel(four_ref, six_ref, query_ref, out):
    sixteenth = four_ref.shape[1]
    out[:, :sixteenth, :] = four_ref[...]
    out[:, sixteenth:, :] = six_ref[...]


def coarse_kernel(
    two_q, three_q, first_ref, three_a, three_b, coarse, near_ref, scratch, two_ref, two_hold, three_hold
):
    inner = first_ref.shape[1] - BLOCK
    pairs = scratch.shape[1]
    two_ref[:, :inner, :] = first_ref[:, BLOCK:, :]
    for which in range(2):
        spill(first_ref.at[which, pl.ds(0, BLOCK), :], scratch.at[which])
        for half in range(pairs):
            lanes = pl.ds(half * PAIR, PAIR)
            slabs = slabs_of(scratch.at[which, half], 0)
            two_ref[which, inner:, lanes] = joined(pooled_slabs(pooled_slabs(slabs)))
        near_ref[which] = repooled(repooled(two_ref[which]))
    steps = {}
    for pair in range(pairs):
        lanes = pl.ds(pair * PAIR, PAIR)
        three = [
            jnp.concatenate([three_a[which, :, lanes], three_b[which, :, lanes]], axis=0)
            for which in range(2)
        ]
        steps[pair, 3] = (
            score(three_q[:, lanes], three[0], three_hold.at[pair]), with_ones(three[1])
        )
        steps[pair, 2] = (
            score(two_q[:, lanes], two_ref[0, :, lanes], two_hold.at[pair]),
            with_ones(two_ref[1, :, lanes]),
        )
    for pair in range(pairs):
        three = weigh(three_hold.at[pair], *steps[pair, 3])
        two = merged(weigh(two_hold.at[pair], *steps[pair, 2]), [doubled(x) for x in three])
        for index, field in enumerate(two):
            coarse[index, :, pl.ds(pair * PAIR, PAIR)] = field


def mid_kernel(edge_q, coarse, state, first_ref, second_ref, fine, *refs):
    outs, (ready, holds) = refs[:-2], refs[-2:]
    own = lax.axis_index("head")
    rows = state.shape[1]
    blocks = rows // BLOCK
    position = lax.axis_index("seq")
    last = lax.axis_size("seq") - 1
    even = lax.rem(position, 2) == 0
    opens = (position > 0, position < last)
    pairs = holds.shape[0]
    steps = {}
    for pair in range(pairs):
        lanes = pl.ds(pair * PAIR, PAIR)
        inner = [first_ref[which, :BLOCK, lanes] for which in range(2)]
        outer = [second_ref[which, :, lanes] for which in range(2)]
        for side in range(2):
            halo = [
                jnp.where(even, *((outer[which], inner[which])[:: 1 - 2 * side]))
                for which in range(2)
            ]
            steps[pair, side] = (
                score(edge_q[side, :, lanes], halo[0], holds.at[pair, side], opens[side]),
                with_ones(halo[1]),
            )
    for pair in range(pairs):
        lanes = pl.ds(pair * PAIR, PAIR)
        for block in range(blocks):
            here = slice(block * BLOCK, (block + 1) * BLOCK)
            quarter = slice(block * BLOCK // 4, (block + 1) * BLOCK // 4)
            done = merged(
                [state[index, here, lanes] for index in range(3)],
                [doubled(doubled(coarse[index, quarter, lanes])) for index in range(3)],
            )
            for side, edge in enumerate((0, blocks - 1)):
                if block == edge:
                    done = merged(done, weigh(holds.at[pair, side], *steps[pair, side]))
            result = done[1] / done[2]
            fine[0, here, lanes] = result
            fine[1, here, lanes] = done[0] + jnp.log(done[2]) * log2_e
            ready[block, :, lanes] = result.astype(jnp.bfloat16)
    for step, out in enumerate(outs, CORES):
        out[...] = ready[own ^ step]


def repeated(field):
    return jnp.concatenate([field] * FAN, axis=0)


def share(ahead, behind):
    return 1.0 / (1.0 + jnp.exp2(behind - ahead))


def finish_kernel(
    four_q, fine, four_ref, near_ref, three_a, three_b, fours_a, fours_b, *refs
):
    refs, (coarse, four_hold) = refs[:-2], refs[-2:]
    heads = lax.axis_size("head")
    far, outs = refs[:-heads], refs[-heads:]
    own = lax.axis_index("head")
    features = four_q.shape[1]
    pairs = four_q.shape[1] // PAIR
    steps = {}
    for pair in range(pairs):
        lanes = pl.ds(pair * PAIR, PAIR)
        ours, theirs, beyond = [], [], []
        for which in range(2):
            ours.append(
                [four_ref[which, :, lanes], near_ref[which, :, lanes]]
                + [repooled(field[which, :, lanes]) for field in (three_a, three_b)]
            )
            theirs.append([field[which, :, lanes] for field in (fours_a, fours_b)])
            beyond.append([field[which, :, lanes] for field in far])
        steps[pair] = (
            score(
                four_q[:, lanes],
                jnp.concatenate(ours[0] + theirs[0] + beyond[0], axis=0),
                four_hold.at[pair],
            ),
            jnp.concatenate(
                [with_ones(field) for field in ours[1]]
                + [with_ones(field, 2.0) for field in theirs[1]]
                + [with_ones(field) for field in beyond[1]],
                axis=0,
            ),
        )
    for pair in range(pairs):
        lanes = pl.ds(pair * PAIR, PAIR)
        top, numer, rowsum = weigh(four_hold.at[pair], *steps[pair])
        coarse[0, :, lanes] = numer / rowsum
        coarse[1, :, lanes] = top + jnp.log(rowsum) * log2_e
    for step, out in enumerate(outs):
        block = own ^ step
        here = pl.ds(pl.multiple_of(block * BLOCK, BLOCK), BLOCK)
        few = pl.ds(pl.multiple_of(block * SLAB, SLAB), SLAB)
        shares = []
        for pair in range(pairs):
            lanes = pl.ds(pair * PAIR, PAIR)
            fine_sum, coarse_sum = fine[1, here, lanes], repeated(coarse[1, few, lanes])
            keep, join = share(fine_sum, coarse_sum), share(coarse_sum, fine_sum)
            if step < CORES:
                result = keep * fine[0, here, lanes] + join * repeated(coarse[0, few, lanes])
                out[:, lanes] = result.astype(jnp.bfloat16)
            else:
                signed = jnp.where(fine_sum <= coarse_sum, keep, -jnp.maximum(join, least_share))
                shares.append(signed.astype(jnp.bfloat16))
        if step >= CORES:
            pick = lax.broadcasted_iota(jnp.int32, (2 * SLAB, features), 1) == HD * (
                lax.broadcasted_iota(jnp.int32, (2 * SLAB, features), 0)
            )
            by_head = lax.dot_general(
                pick.astype(jnp.bfloat16),
                jnp.concatenate(shares, axis=1),
                (((1,), (1,)), ((), ())),
                preferred_element_type=jnp.float32,
            )[:SLAB]
            blank = jnp.zeros((SLAB, features - BLOCK), jnp.float32)
            out[...] = jnp.concatenate(
                [coarse[0, few, :], jnp.concatenate([by_head, blank], axis=1)], axis=0
            ).astype(jnp.bfloat16)


def joined_parts(early, late_ref):
    features = early.shape[1]
    late = late_ref[...].astype(jnp.float32)
    spread = lax.broadcasted_iota(jnp.int32, (SLAB, features), 1) // HD == (
        lax.broadcasted_iota(jnp.int32, (SLAB, features), 0)
    )
    signed = lax.dot_general(
        late[SLAB:, :BLOCK].astype(jnp.bfloat16),
        spread.astype(jnp.bfloat16),
        (((0,), (0,)), ((), ())),
        preferred_element_type=jnp.float32,
    )
    keep = jnp.where(signed >= 0, signed, 1.0 + signed)
    join = jnp.where(signed >= 0, 1.0 - signed, -signed)
    result = keep * early + join * repeated(late[:SLAB])
    return result.astype(jnp.bfloat16)


def stack_kernel(*refs):
    for index, ref in enumerate(refs[:-1]):
        refs[-1][index] = ref[...].astype(jnp.float32)


def partial_kernel(near_ref, next_ref, early_ref, weight_ref, out_ref):
    own = lax.axis_index("head")
    features = near_ref.shape[1]
    total = None
    for step, part in enumerate((near_ref, next_ref)):
        start = pl.multiple_of((own ^ step) * features, features)
        product = jnp.dot(
            part[...], weight_ref[pl.ds(start, features), :], preferred_element_type=jnp.float32
        )
        total = product if total is None else total + product
    out_ref[...] = total


def project_kernel(partial_ref, early_ref, *refs):
    refs, (weight_ref, out_hbm, scratch, staged, sems) = refs[:-5], refs[-5:]
    own = lax.axis_index("head")
    parts = [joined_parts(early_ref[index], late) for index, late in enumerate(refs)]
    features = parts[0].shape[1]
    chunk = staged.shape[2]
    copies = []
    for index in range(staged.shape[0]):
        columns = pl.ds(index * chunk, chunk)
        total = partial_ref[:, columns]
        for step, part in enumerate(parts, CORES):
            start = pl.multiple_of((own ^ step) * features, features)
            total += jnp.dot(
                part,
                weight_ref[pl.ds(start, features), columns],
                preferred_element_type=jnp.float32,
            )
        for half in range(chunk // PAIR):
            lanes = slice(half * PAIR, (half + 1) * PAIR)
            scratch[index, half] = total[:, lanes]
            for i in range(SLAB):
                staged[index, i * FAN : (i + 1) * FAN, lanes] = scratch[
                    index, half, pl.ds(i, FAN, stride=SLAB), :
                ].astype(jnp.bfloat16)
        copy = pltpu.make_async_copy(staged.at[index], out_hbm.at[:, columns], sems.at[index])
        copy.start()
        copies.append(copy)
    for copy in copies:
        copy.wait()


def repool_outside(field):
    which, rows, lanes = field.shape
    slabs = field.astype(jnp.float32).reshape(which, rows // (2 * SLAB), 2, SLAB, lanes)
    sums = (slabs[:, :, 0] + slabs[:, :, 1]) * root_half
    return sums.reshape(which, rows // 2, lanes).astype(jnp.bfloat16)


def swapped(block, axis, mask):
    return lax.ppermute(block, axis, [(i, i ^ mask) for i in range(lax.axis_size(axis))])


def across(block):
    count, heads = lax.axis_size("seq"), lax.axis_size("head")
    route = []
    for seq in range(count):
        end = seq in (0, count - 1)
        other = seq if end else seq + 1 if seq % 2 else seq - 1
        for head in range(heads):
            route.append((seq * heads + head, other * heads + (head ^ 1 if end else head)))
    return lax.ppermute(block, ("seq", "head"), route)


def per_device(queries, key_vectors, value_vectors, out_weight):
    rows, features = queries.shape[1:]
    queries, key_vectors, value_vectors = [
        pltpu.with_memory_space_constraint(x, pltpu.HBM)
        for x in (queries, key_vectors, value_vectors)
    ]
    pairs = features // PAIR
    seq_count, head_count = lax.axis_size("seq"), lax.axis_size("head")
    bf16 = lambda *shape: jax.ShapeDtypeStruct(shape, jnp.bfloat16)
    params = pltpu.CompilerParams(vmem_limit_bytes=32 * 1024 * 1024)

    hbm = pl.BlockSpec(memory_space=pltpu.HBM)
    vmem = pl.BlockSpec(memory_space=pltpu.VMEM)
    keys, values, ours, first, one, two = pl.pallas_call(
        pool_kernel,
        in_specs=[hbm] * 3,
        out_shape=[
            bf16(rows, features),
            bf16(rows, features),
            bf16(rows, features),
            bf16(2, BLOCK + rows // 4 - BLOCK // 4, features),
            bf16(2, rows // 2, features),
            bf16(2, rows // 4, features),
        ],
        scratch_shapes=[
            pltpu.VMEM((2, rows // BLOCK, pairs, BLOCK, PAIR), jnp.float32),
            pltpu.SemaphoreType.DMA((2, rows // BLOCK)),
            pltpu.SemaphoreType.DMA((1,)),
        ],
        compiler_params=params,
        name="pool",
    )(key_vectors, value_vectors, queries)
    second, three, four = pl.pallas_call(
        deeper_kernel,
        out_shape=[
            bf16(2, BLOCK, features),
            bf16(2, rows // 8, features),
            bf16(2, rows // 16, features),
        ],
        compiler_params=params,
        cost_estimate=pl.CostEstimate(flops=2**31, bytes_accessed=2**23, transcendentals=0),
        name="deeper",
    )(keys, values, two)

    first_in = swapped(first, "seq", 1)
    second_in = across(second)
    four_in = swapped(four, "seq", 4)
    six_in = swapped(four, "seq", 6)
    threes_in = [swapped(three, "seq", mask) for mask in (3, 2)]
    edge_q, two_q, three_q, four_q, state = pl.pallas_call(
        local_kernel,
        out_shape=[
            bf16(2, BLOCK, features),
            bf16(rows // 4, features),
            bf16(rows // 8, features),
            bf16(rows // 16, features),
            jax.ShapeDtypeStruct((3, rows, features), jnp.float32),
        ],
        scratch_shapes=[
            pltpu.VMEM((pairs, rows, PAIR), jnp.float32),
            pltpu.VMEM((pairs, rows // BLOCK, 2 * BLOCK, 3 * BLOCK), jnp.float32),
            pltpu.VMEM((pairs, rows // BLOCK // 2, 2 * BLOCK, BLOCK), jnp.float32),
        ],
        compiler_params=params,
        name="local",
    )(ours, keys, values, one, four_in)

    fours = pl.pallas_call(
        join_kernel,
        out_shape=bf16(2, rows // 8, features),
        compiler_params=params,
        cost_estimate=pl.CostEstimate(flops=2**29, bytes_accessed=2**20, transcendentals=0),
        name="join",
    )(four_in, six_in, four_q)
    fours_in = swapped(fours, "seq", 1)
    coarse, near = pl.pallas_call(
        coarse_kernel,
        out_shape=[
            jax.ShapeDtypeStruct((3, rows // 4, features), jnp.float32),
            bf16(2, rows // 16, features),
        ],
        scratch_shapes=[
            pltpu.VMEM((2, pairs, BLOCK, PAIR), jnp.float32),
            pltpu.VMEM((2, rows // 4, features), jnp.bfloat16),
            pltpu.VMEM((pairs, rows // 2, BLOCK), jnp.float32),
            pltpu.VMEM((pairs, rows // 4, BLOCK), jnp.float32),
        ],
        compiler_params=params,
        cost_estimate=pl.CostEstimate(flops=2**31, bytes_accessed=2**21, transcendentals=0),
        name="coarse",
    )(two_q, three_q, first_in, *threes_in)
    away = range(CORES, head_count)
    fine, *early = pl.pallas_call(
        mid_kernel,
        out_shape=[jax.ShapeDtypeStruct((2, rows, features), jnp.float32)]
        + [bf16(BLOCK, features) for _ in away],
        scratch_shapes=[
            pltpu.VMEM((rows // BLOCK, BLOCK, features), jnp.bfloat16),
            pltpu.VMEM((pairs, 2, 2 * BLOCK, BLOCK), jnp.float32),
        ],
        compiler_params=params,
        name="mid",
    )(edge_q, coarse, state, first_in, second_in)
    early_in = [swapped(part, "head", step) for step, part in zip(away, early)]

    far = []
    known = 8
    if known < seq_count:
        group = [four, near] + [repool_outside(field) for field in threes_in]
        group = jnp.concatenate(group + [fours, fours_in], axis=1)
        while known < seq_count:
            fresh = swapped(group, "seq", known)
            far.append(fresh)
            group = jnp.concatenate([group, fresh], axis=1)
            known *= 2

    near_parts = [bf16(BLOCK, features) for _ in range(CORES)]
    outs = pl.pallas_call(
        finish_kernel,
        out_shape=near_parts + [bf16(2 * SLAB, features) for _ in away],
        scratch_shapes=[
            pltpu.VMEM((2, rows // 16, features), jnp.float32),
            pltpu.VMEM((pairs, rows // 8, rows // 16 * seq_count), jnp.float32),
        ],
        compiler_params=params,
        name="finish",
    )(four_q, fine, four, near, *threes_in, fours, fours_in, *far)
    parts = [outs[0], swapped(outs[1], "head", 1)]
    late_in = [swapped(part, "head", step) for step, part in zip(away, outs[CORES:])]
    width = out_weight.shape[1]
    early = pl.pallas_call(
        stack_kernel,
        out_shape=jax.ShapeDtypeStruct((len(early_in), BLOCK, features), jnp.float32),
        compiler_params=params,
        cost_estimate=pl.CostEstimate(flops=2**32, bytes_accessed=2**20, transcendentals=0),
        name="stack",
    )(*early_in)
    partial = pl.pallas_call(
        partial_kernel,
        out_shape=jax.ShapeDtypeStruct((BLOCK, width), jnp.float32),
        compiler_params=params,
        name="partial",
    )(*parts, early, out_weight)
    chunk = 2 * PAIR
    result = pl.pallas_call(
        project_kernel,
        in_specs=[vmem] * (3 + len(late_in)),
        out_specs=hbm,
        out_shape=bf16(BLOCK, width),
        scratch_shapes=[
            pltpu.VMEM((width // chunk, 2, BLOCK, PAIR), jnp.float32),
            pltpu.VMEM((width // chunk, BLOCK, chunk), jnp.bfloat16),
            pltpu.SemaphoreType.DMA((width // chunk,)),
        ],
        compiler_params=params,
        name="project",
    )(partial, early, *late_in, out_weight)
    return result[None]


def solution(mesh):
    return jax.shard_map(
        per_device,
        mesh=mesh,
        in_specs=(P(None, "seq", "head"), P(None, "seq", "head"), P(None, "seq", "head"), P()),
        out_specs=P(None, ("seq", "head"), None),
        check_vma=False,
    )
```

```python
import jax
import jax.numpy as jnp
from jax import lax
from jax.experimental import pallas as pl
from jax.experimental.pallas import tpu as pltpu
from jax.sharding import PartitionSpec as P

HD = 64
BLOCK = 128
LEVELS = 4
SLAB = 8
PAIR = 2 * HD

neg_fill = -1e30
root_half = 0.7071067811865476
log2_e = 1.4426950408889634
log2_scale = HD**-0.5 * log2_e

FAN = 2**LEVELS


def slabs_of(scratch, block):
    return [scratch[pl.ds(BLOCK * block + j, SLAB, stride=FAN), :] for j in range(FAN)]


def pooled_slabs(slabs):
    return [
        ((low + high) * root_half).astype(jnp.bfloat16).astype(jnp.float32)
        for low, high in zip(slabs[0::2], slabs[1::2])
    ]


def joined(slabs):
    return jnp.concatenate(slabs, axis=0).astype(jnp.bfloat16)


def spill(source, scratch):
    for half in range(scratch.shape[0]):
        scratch[half] = source[:, half * PAIR : (half + 1) * PAIR].astype(jnp.float32)


def pool_kernel(
    k_hbm, v_hbm, k_ref, v_ref, first_ref, one_ref, two_ref, scratch, sems
):
    rows = k_ref.shape[0]
    blocks = rows // BLOCK
    arrivals = []
    for block in range(blocks):
        here = pl.ds(block * BLOCK, BLOCK)
        for which, (source, target) in enumerate(((k_hbm, k_ref), (v_hbm, v_ref))):
            copy = pltpu.make_async_copy(
                source.at[0, here, :], target.at[here, :], sems.at[which, block]
            )
            copy.start()
            arrivals.append((block, which, target, copy))
    even = lax.rem(lax.axis_index("seq"), 2) == 0
    for block, which, ref, copy in arrivals:
        copy.wait()
        here = pl.ds(block * BLOCK, BLOCK)
        spill(ref.at[here, :], scratch.at[which, block])
        for half in range(scratch.shape[2]):
            lanes = pl.ds(half * PAIR, PAIR)
            one = pooled_slabs(slabs_of(scratch.at[which, block, half], 0))
            one_ref[which, pl.ds(block * BLOCK // 2, BLOCK // 2), lanes] = joined(one)
            two_ref[which, pl.ds(block * BLOCK // 4, BLOCK // 4), lanes] = joined(pooled_slabs(one))
    inner = rows // 4 - BLOCK // 4
    for which, ref in enumerate((k_ref, v_ref)):
        first_ref[which, :BLOCK, :] = jnp.where(even, ref[rows - BLOCK :, :], ref[:BLOCK, :])
        first_ref[which, BLOCK:, :] = jnp.where(
            even, two_ref[which, :inner, :], two_ref[which, BLOCK // 4 :, :]
        )


def repooled(field):
    rows, lanes = field.shape
    slabs = field.astype(jnp.float32).reshape(rows // (2 * SLAB), 2, SLAB, lanes)
    return ((slabs[:, 0] + slabs[:, 1]) * root_half).reshape(rows // 2, lanes).astype(jnp.bfloat16)


def deeper_kernel(k_ref, v_ref, two_ref, second_ref, three_ref, four_ref):
    rows = k_ref.shape[0]
    even = lax.rem(lax.axis_index("seq"), 2) == 0
    for which, ref in enumerate((k_ref, v_ref)):
        second_ref[which] = jnp.where(even, ref[:BLOCK, :], ref[rows - BLOCK :, :])
        three = repooled(two_ref[which])
        three_ref[which] = three
        four_ref[which] = repooled(three)


def repooled(field):
    rows, lanes = field.shape
    slabs = field.astype(jnp.float32).reshape(rows // (2 * SLAB), 2, SLAB, lanes)
    return ((slabs[:, 0] + slabs[:, 1]) * root_half).reshape(rows // 2, lanes).astype(jnp.bfloat16)


def score(queries, keys, hold, is_open=None):
    rows = queries.shape[0]
    low = lax.broadcasted_iota(jnp.int32, (rows, PAIR), 1) < HD
    zero = jnp.zeros_like(queries)
    both = jnp.concatenate([jnp.where(low, queries, zero), jnp.where(low, zero, queries)], axis=0)
    raw = lax.dot_general(both, keys, (((1,), (1,)), ((), ())), preferred_element_type=jnp.float32)
    if is_open is not None:
        raw = jnp.where(is_open, raw, neg_fill)
    hold[...] = raw
    return jnp.max(raw, axis=1, keepdims=True)


def weigh(hold, top, values):
    rows = top.shape[0] // 2
    low = lax.broadcasted_iota(jnp.int32, (rows, PAIR), 1) < HD
    weights = jnp.exp2((hold[...] - top) * log2_scale).astype(jnp.bfloat16)
    result = jnp.dot(weights, values, preferred_element_type=jnp.float32)
    return (
        log2_scale * jnp.where(low, top[:rows], top[rows:]),
        jnp.where(low, result[:rows, :PAIR], result[rows:, :PAIR]),
        jnp.where(low, result[:rows, PAIR:], result[rows:, PAIR:]),
    )


def merged(fine, coarse):
    top = jnp.maximum(fine[0], coarse[0])
    keep = jnp.exp2(fine[0] - top)
    join = jnp.exp2(coarse[0] - top)
    return top, fine[1] * keep + coarse[1] * join, fine[2] * keep + coarse[2] * join


def doubled(field):
    rows, lanes = field.shape
    slabs = field.reshape(rows // SLAB, 1, SLAB, lanes)
    return jnp.broadcast_to(slabs, (rows // SLAB, 2, SLAB, lanes)).reshape(2 * rows, lanes)


def with_ones(values, weight=1.0):
    if weight != 1.0:
        values = values * jnp.bfloat16(weight)
    return jnp.concatenate([values, jnp.full(values.shape, weight, jnp.bfloat16)], axis=1)


def local_kernel(
    q_ref, k_ref, v_ref, one_ref, four_ref, edge_q, two_q, three_q, four_q, state,
    scratch, near_hold, coarse_hold,
):
    rows = q_ref.shape[0]
    blocks = rows // BLOCK
    pairs = scratch.shape[0]
    spill(q_ref, scratch)
    fine, one_q = [], []
    for pair in range(pairs):
        lanes = pl.ds(pair * PAIR, PAIR)
        ladder = [[], [], [], [], []]
        for block in range(blocks):
            slabs = slabs_of(scratch.at[pair], block)
            ladder[0].append(joined(slabs))
            for level in range(1, LEVELS + 1):
                slabs = pooled_slabs(slabs)
                ladder[level] += slabs
        edge_q[0, :, lanes] = ladder[0][0]
        edge_q[1, :, lanes] = ladder[0][-1]
        two_q[:, lanes] = joined(ladder[2])
        three_q[:, lanes] = joined(ladder[3])
        four_q[:, lanes] = joined(ladder[4])
        fine.append(ladder[0])
        one_q.append([joined(ladder[1][n : n + FAN]) for n in range(0, len(ladder[1]), FAN)])
    windows = [(max(n - 1, 0) * BLOCK, min(n + 2, blocks) * BLOCK) for n in range(blocks)]
    tops = {}
    for pair in range(pairs):
        lanes = pl.ds(pair * PAIR, PAIR)
        for half in range(blocks // 2):
            there = pl.ds((half ^ 1) * BLOCK, BLOCK)
            tops[pair, half] = score(
                one_q[pair][half], one_ref[0, there, lanes], coarse_hold.at[pair, half]
            )
            for block in (2 * half, 2 * half + 1):
                low, high = windows[block]
                hold = near_hold.at[pair, block, :, : high - low]
                tops[pair, half, block] = score(fine[pair][block], k_ref[low:high, lanes], hold)
    for pair in range(pairs):
        lanes = pl.ds(pair * PAIR, PAIR)
        for half in range(blocks // 2):
            there = pl.ds((half ^ 1) * BLOCK, BLOCK)
            coarse = weigh(
                coarse_hold.at[pair, half], tops[pair, half], with_ones(one_ref[1, there, lanes])
            )
            for block in (2 * half, 2 * half + 1):
                low, high = windows[block]
                hold = near_hold.at[pair, block, :, : high - low]
                near = weigh(hold, tops[pair, half, block], with_ones(v_ref[low:high, lanes]))
                part = slice((block - 2 * half) * BLOCK // 2, (block - 2 * half + 1) * BLOCK // 2)
                done = merged(near, [doubled(x[part]) for x in coarse])
                for index, field in enumerate(done):
                    state[index, block * BLOCK : (block + 1) * BLOCK, lanes] = field


def join_kernel(four_ref, six_ref, query_ref, out):
    sixteenth = four_ref.shape[1]
    out[:, :sixteenth, :] = four_ref[...]
    out[:, sixteenth:, :] = six_ref[...]


def coarse_kernel(
    two_q, three_q, first_ref, three_a, three_b, coarse, near_ref, scratch, two_ref, two_hold, three_hold
):
    inner = first_ref.shape[1] - BLOCK
    pairs = scratch.shape[1]
    two_ref[:, :inner, :] = first_ref[:, BLOCK:, :]
    for which in range(2):
        spill(first_ref.at[which, pl.ds(0, BLOCK), :], scratch.at[which])
        for half in range(pairs):
            lanes = pl.ds(half * PAIR, PAIR)
            slabs = slabs_of(scratch.at[which, half], 0)
            two_ref[which, inner:, lanes] = joined(pooled_slabs(pooled_slabs(slabs)))
        near_ref[which] = repooled(repooled(two_ref[which]))
    steps = {}
    for pair in range(pairs):
        lanes = pl.ds(pair * PAIR, PAIR)
        three = [
            jnp.concatenate([three_a[which, :, lanes], three_b[which, :, lanes]], axis=0)
            for which in range(2)
        ]
        steps[pair, 3] = (
            score(three_q[:, lanes], three[0], three_hold.at[pair]), with_ones(three[1])
        )
        steps[pair, 2] = (
            score(two_q[:, lanes], two_ref[0, :, lanes], two_hold.at[pair]),
            with_ones(two_ref[1, :, lanes]),
        )
    for pair in range(pairs):
        three = weigh(three_hold.at[pair], *steps[pair, 3])
        two = merged(weigh(two_hold.at[pair], *steps[pair, 2]), [doubled(x) for x in three])
        for index, field in enumerate(two):
            coarse[index, :, pl.ds(pair * PAIR, PAIR)] = field


def mid_kernel(edge_q, coarse, state, first_ref, second_ref, fine, holds):
    rows = state.shape[1]
    blocks = rows // BLOCK
    position = lax.axis_index("seq")
    last = lax.axis_size("seq") - 1
    even = lax.rem(position, 2) == 0
    opens = (position > 0, position < last)
    pairs = holds.shape[0]
    steps = {}
    for pair in range(pairs):
        lanes = pl.ds(pair * PAIR, PAIR)
        inner = [first_ref[which, :BLOCK, lanes] for which in range(2)]
        outer = [second_ref[which, :, lanes] for which in range(2)]
        for side in range(2):
            halo = [
                jnp.where(even, *((outer[which], inner[which])[:: 1 - 2 * side]))
                for which in range(2)
            ]
            steps[pair, side] = (
                score(edge_q[side, :, lanes], halo[0], holds.at[pair, side], opens[side]),
                with_ones(halo[1]),
            )
    for pair in range(pairs):
        lanes = pl.ds(pair * PAIR, PAIR)
        for block in range(blocks):
            here = slice(block * BLOCK, (block + 1) * BLOCK)
            quarter = slice(block * BLOCK // 4, (block + 1) * BLOCK // 4)
            done = merged(
                [state[index, here, lanes] for index in range(3)],
                [doubled(doubled(coarse[index, quarter, lanes])) for index in range(3)],
            )
            for side, edge in enumerate((0, blocks - 1)):
                if block == edge:
                    done = merged(done, weigh(holds.at[pair, side], *steps[pair, side]))
            fine[0, here, lanes] = done[1] / done[2]
            fine[1, here, lanes] = done[0] + jnp.log(done[2]) * log2_e


def repeated(field):
    return jnp.concatenate([field] * FAN, axis=0)


def finish_kernel(
    four_q, fine, four_ref, near_ref, three_a, three_b, fours_a, fours_b, *refs
):
    far, refs = refs[:-6], refs[-6:]
    outs, (attended, four_hold) = refs[:-2], refs[-2:]
    blocks = fine.shape[1] // BLOCK
    own = lax.axis_index("head")
    pairs = four_q.shape[1] // PAIR
    steps = {}
    for pair in range(pairs):
        lanes = pl.ds(pair * PAIR, PAIR)
        ours, theirs, beyond = [], [], []
        for which in range(2):
            ours.append(
                [four_ref[which, :, lanes], near_ref[which, :, lanes]]
                + [repooled(field[which, :, lanes]) for field in (three_a, three_b)]
            )
            theirs.append([field[which, :, lanes] for field in (fours_a, fours_b)])
            beyond.append([field[which, :, lanes] for field in far])
        steps[pair] = (
            score(
                four_q[:, lanes],
                jnp.concatenate(ours[0] + theirs[0] + beyond[0], axis=0),
                four_hold.at[pair],
            ),
            jnp.concatenate(
                [with_ones(field) for field in ours[1]]
                + [with_ones(field, 2.0) for field in theirs[1]]
                + [with_ones(field) for field in beyond[1]],
                axis=0,
            ),
        )
    for pair in range(pairs):
        lanes = pl.ds(pair * PAIR, PAIR)
        top, numer, rowsum = weigh(four_hold.at[pair], *steps[pair])
        result, log_sum = numer / rowsum, top + jnp.log(rowsum) * log2_e
        for block in range(blocks):
            here = slice(block * BLOCK, (block + 1) * BLOCK)
            few = slice(block * SLAB, (block + 1) * SLAB)
            ours = fine[0, here, lanes]
            keep = 1.0 / (1.0 + jnp.exp2(repeated(log_sum[few]) - fine[1, here, lanes]))
            theirs = repeated(result[few])
            attended[block, :, lanes] = (theirs + keep * (ours - theirs)).astype(jnp.bfloat16)
    for step, out in enumerate(outs):
        out[...] = attended[own ^ step]


def partial_kernel(own_ref, weight_ref, out_ref):
    features = own_ref.shape[1]
    start = pl.multiple_of(lax.axis_index("head") * features, features)
    out_ref[...] = jnp.dot(
        own_ref[...], weight_ref[pl.ds(start, features), :], preferred_element_type=jnp.float32
    )


def project_kernel(partial_ref, *refs):
    parts, (weight_ref, out_hbm, scratch, staged, sems) = refs[:-5], refs[-5:]
    own = lax.axis_index("head")
    features = parts[0].shape[1]
    chunk = staged.shape[2]
    copies = []
    for index in range(staged.shape[0]):
        columns = pl.ds(index * chunk, chunk)
        total = partial_ref[:, columns]
        for step, part in zip(range(len(parts), 0, -1), parts):
            start = pl.multiple_of((own ^ step) * features, features)
            total += jnp.dot(
                part[...],
                weight_ref[pl.ds(start, features), columns],
                preferred_element_type=jnp.float32,
            )
        for half in range(chunk // PAIR):
            lanes = slice(half * PAIR, (half + 1) * PAIR)
            scratch[index, half] = total[:, lanes]
            for i in range(SLAB):
                staged[index, i * FAN : (i + 1) * FAN, lanes] = scratch[
                    index, half, pl.ds(i, FAN, stride=SLAB), :
                ].astype(jnp.bfloat16)
        copy = pltpu.make_async_copy(staged.at[index], out_hbm.at[:, columns], sems.at[index])
        copy.start()
        copies.append(copy)
    for copy in copies:
        copy.wait()


def repool_outside(field):
    which, rows, lanes = field.shape
    slabs = field.astype(jnp.float32).reshape(which, rows // (2 * SLAB), 2, SLAB, lanes)
    sums = (slabs[:, :, 0] + slabs[:, :, 1]) * root_half
    return sums.reshape(which, rows // 2, lanes).astype(jnp.bfloat16)


def swapped(block, axis, mask):
    return lax.ppermute(block, axis, [(i, i ^ mask) for i in range(lax.axis_size(axis))])


def across(block):
    count, heads = lax.axis_size("seq"), lax.axis_size("head")
    route = []
    for seq in range(count):
        end = seq in (0, count - 1)
        other = seq if end else seq + 1 if seq % 2 else seq - 1
        for head in range(heads):
            route.append((seq * heads + head, other * heads + (head ^ 1 if end else head)))
    return lax.ppermute(block, ("seq", "head"), route)


def per_device(queries, key_vectors, value_vectors, out_weight):
    rows, features = queries.shape[1:]
    key_vectors, value_vectors = [
        pltpu.with_memory_space_constraint(x, pltpu.HBM) for x in (key_vectors, value_vectors)
    ]
    pairs = features // PAIR
    seq_count, head_count = lax.axis_size("seq"), lax.axis_size("head")
    bf16 = lambda *shape: jax.ShapeDtypeStruct(shape, jnp.bfloat16)
    params = pltpu.CompilerParams(vmem_limit_bytes=32 * 1024 * 1024)

    hbm = pl.BlockSpec(memory_space=pltpu.HBM)
    vmem = pl.BlockSpec(memory_space=pltpu.VMEM)
    keys, values, first, one, two = pl.pallas_call(
        pool_kernel,
        in_specs=[hbm] * 2,
        out_shape=[
            bf16(rows, features),
            bf16(rows, features),
            bf16(2, BLOCK + rows // 4 - BLOCK // 4, features),
            bf16(2, rows // 2, features),
            bf16(2, rows // 4, features),
        ],
        scratch_shapes=[
            pltpu.VMEM((2, rows // BLOCK, pairs, BLOCK, PAIR), jnp.float32),
            pltpu.SemaphoreType.DMA((2, rows // BLOCK)),
        ],
        compiler_params=params,
        name="pool",
    )(key_vectors, value_vectors)
    second, three, four = pl.pallas_call(
        deeper_kernel,
        out_shape=[
            bf16(2, BLOCK, features),
            bf16(2, rows // 8, features),
            bf16(2, rows // 16, features),
        ],
        compiler_params=params,
        cost_estimate=pl.CostEstimate(flops=2**31, bytes_accessed=2**23, transcendentals=0),
        name="deeper",
    )(keys, values, two)

    first_in = swapped(first, "seq", 1)
    second_in = across(second)
    four_in = swapped(four, "seq", 4)
    six_in = swapped(four, "seq", 6)
    threes_in = [swapped(three, "seq", mask) for mask in (3, 2)]
    edge_q, two_q, three_q, four_q, state = pl.pallas_call(
        local_kernel,
        out_shape=[
            bf16(2, BLOCK, features),
            bf16(rows // 4, features),
            bf16(rows // 8, features),
            bf16(rows // 16, features),
            jax.ShapeDtypeStruct((3, rows, features), jnp.float32),
        ],
        scratch_shapes=[
            pltpu.VMEM((pairs, rows, PAIR), jnp.float32),
            pltpu.VMEM((pairs, rows // BLOCK, 2 * BLOCK, 3 * BLOCK), jnp.float32),
            pltpu.VMEM((pairs, rows // BLOCK // 2, 2 * BLOCK, BLOCK), jnp.float32),
        ],
        compiler_params=params,
        name="local",
    )(queries[0], keys, values, one, four_in)

    fours = pl.pallas_call(
        join_kernel,
        out_shape=bf16(2, rows // 8, features),
        compiler_params=params,
        cost_estimate=pl.CostEstimate(flops=2**29, bytes_accessed=2**20, transcendentals=0),
        name="join",
    )(four_in, six_in, four_q)
    fours_in = swapped(fours, "seq", 1)
    coarse, near = pl.pallas_call(
        coarse_kernel,
        out_shape=[
            jax.ShapeDtypeStruct((3, rows // 4, features), jnp.float32),
            bf16(2, rows // 16, features),
        ],
        scratch_shapes=[
            pltpu.VMEM((2, pairs, BLOCK, PAIR), jnp.float32),
            pltpu.VMEM((2, rows // 4, features), jnp.bfloat16),
            pltpu.VMEM((pairs, rows // 2, BLOCK), jnp.float32),
            pltpu.VMEM((pairs, rows // 4, BLOCK), jnp.float32),
        ],
        compiler_params=params,
        cost_estimate=pl.CostEstimate(flops=2**31, bytes_accessed=2**21, transcendentals=0),
        name="coarse",
    )(two_q, three_q, first_in, *threes_in)
    fine = pl.pallas_call(
        mid_kernel,
        out_shape=jax.ShapeDtypeStruct((2, rows, features), jnp.float32),
        scratch_shapes=[pltpu.VMEM((pairs, 2, 2 * BLOCK, BLOCK), jnp.float32)],
        compiler_params=params,
        name="mid",
    )(edge_q, coarse, state, first_in, second_in)

    far = []
    known = 8
    if known < seq_count:
        group = [four, near] + [repool_outside(field) for field in threes_in]
        group = jnp.concatenate(group + [fours, fours_in], axis=1)
        while known < seq_count:
            fresh = swapped(group, "seq", known)
            far.append(fresh)
            group = jnp.concatenate([group, fresh], axis=1)
            known *= 2

    outs = pl.pallas_call(
        finish_kernel,
        out_shape=[bf16(BLOCK, features) for _ in range(head_count)],
        scratch_shapes=[
            pltpu.VMEM((rows // BLOCK, BLOCK, features), jnp.bfloat16),
            pltpu.VMEM((pairs, rows // 8, rows // 16 * seq_count), jnp.float32),
        ],
        compiler_params=params,
        name="finish",
    )(four_q, fine, four, near, *threes_in, fours, fours_in, *far)

    parts = [swapped(outs[step], "head", step) for step in range(head_count - 1, 0, -1)]
    width = out_weight.shape[1]
    partial = pl.pallas_call(
        partial_kernel,
        out_shape=jax.ShapeDtypeStruct((BLOCK, width), jnp.float32),
        compiler_params=params,
        name="partial",
    )(outs[0], out_weight)
    chunk = 2 * PAIR
    result = pl.pallas_call(
        project_kernel,
        in_specs=[vmem] * (len(parts) + 2),
        out_specs=hbm,
        out_shape=bf16(BLOCK, width),
        scratch_shapes=[
            pltpu.VMEM((width // chunk, 2, BLOCK, PAIR), jnp.float32),
            pltpu.VMEM((width // chunk, BLOCK, chunk), jnp.bfloat16),
            pltpu.SemaphoreType.DMA((width // chunk,)),
        ],
        compiler_params=params,
        name="project",
    )(partial, *parts, out_weight)
    return result[None]


def solution(mesh):
    return jax.shard_map(
        per_device,
        mesh=mesh,
        in_specs=(P(None, "seq", "head"), P(None, "seq", "head"), P(None, "seq", "head"), P()),
        out_specs=P(None, ("seq", "head"), None),
        check_vma=False,
    )
```

```python
import jax
import jax.numpy as jnp
from jax import lax
from jax.experimental import pallas as pl
from jax.experimental.pallas import tpu as pltpu
from jax.sharding import PartitionSpec as P

HD = 64
BLOCK = 128
LEVELS = 4
SLAB = 8
PAIR = 2 * HD

neg_fill = -1e30
root_half = 0.7071067811865476
log2_e = 1.4426950408889634
log2_scale = HD**-0.5 * log2_e
CORES = 2

FAN = 2**LEVELS


def slabs_of(scratch, block):
    return [scratch[pl.ds(BLOCK * block + j, SLAB, stride=FAN), :] for j in range(FAN)]


def pooled_slabs(slabs):
    return [
        ((low + high) * root_half).astype(jnp.bfloat16).astype(jnp.float32)
        for low, high in zip(slabs[0::2], slabs[1::2])
    ]


def joined(slabs):
    return jnp.concatenate(slabs, axis=0).astype(jnp.bfloat16)


def spill(source, scratch):
    for half in range(scratch.shape[0]):
        scratch[half] = source[:, half * PAIR : (half + 1) * PAIR].astype(jnp.float32)


def pool_kernel(
    k_hbm, v_hbm, k_ref, v_ref, first_ref, one_ref, two_ref, scratch, sems
):
    rows = k_ref.shape[0]
    blocks = rows // BLOCK
    arrivals = []
    for block in range(blocks):
        here = pl.ds(block * BLOCK, BLOCK)
        for which, (source, target) in enumerate(((k_hbm, k_ref), (v_hbm, v_ref))):
            copy = pltpu.make_async_copy(
                source.at[0, here, :], target.at[here, :], sems.at[which, block]
            )
            copy.start()
            arrivals.append((block, which, target, copy))
    even = lax.rem(lax.axis_index("seq"), 2) == 0
    for block, which, ref, copy in arrivals:
        copy.wait()
        here = pl.ds(block * BLOCK, BLOCK)
        spill(ref.at[here, :], scratch.at[which, block])
        for half in range(scratch.shape[2]):
            lanes = pl.ds(half * PAIR, PAIR)
            one = pooled_slabs(slabs_of(scratch.at[which, block, half], 0))
            one_ref[which, pl.ds(block * BLOCK // 2, BLOCK // 2), lanes] = joined(one)
            two_ref[which, pl.ds(block * BLOCK // 4, BLOCK // 4), lanes] = joined(pooled_slabs(one))
    inner = rows // 4 - BLOCK // 4
    for which, ref in enumerate((k_ref, v_ref)):
        first_ref[which, :BLOCK, :] = jnp.where(even, ref[rows - BLOCK :, :], ref[:BLOCK, :])
        first_ref[which, BLOCK:, :] = jnp.where(
            even, two_ref[which, :inner, :], two_ref[which, BLOCK // 4 :, :]
        )


def repooled(field):
    rows, lanes = field.shape
    slabs = field.astype(jnp.float32).reshape(rows // (2 * SLAB), 2, SLAB, lanes)
    return ((slabs[:, 0] + slabs[:, 1]) * root_half).reshape(rows // 2, lanes).astype(jnp.bfloat16)


def deeper_kernel(k_ref, v_ref, two_ref, second_ref, three_ref, four_ref):
    rows = k_ref.shape[0]
    even = lax.rem(lax.axis_index("seq"), 2) == 0
    for which, ref in enumerate((k_ref, v_ref)):
        second_ref[which] = jnp.where(even, ref[:BLOCK, :], ref[rows - BLOCK :, :])
        three = repooled(two_ref[which])
        three_ref[which] = three
        four_ref[which] = repooled(three)


def repooled(field):
    rows, lanes = field.shape
    slabs = field.astype(jnp.float32).reshape(rows // (2 * SLAB), 2, SLAB, lanes)
    return ((slabs[:, 0] + slabs[:, 1]) * root_half).reshape(rows // 2, lanes).astype(jnp.bfloat16)


def score(queries, keys, hold, is_open=None):
    rows = queries.shape[0]
    low = lax.broadcasted_iota(jnp.int32, (rows, PAIR), 1) < HD
    zero = jnp.zeros_like(queries)
    both = jnp.concatenate([jnp.where(low, queries, zero), jnp.where(low, zero, queries)], axis=0)
    raw = lax.dot_general(both, keys, (((1,), (1,)), ((), ())), preferred_element_type=jnp.float32)
    if is_open is not None:
        raw = jnp.where(is_open, raw, neg_fill)
    hold[...] = raw
    return jnp.max(raw, axis=1, keepdims=True)


def weigh(hold, top, values):
    rows = top.shape[0] // 2
    low = lax.broadcasted_iota(jnp.int32, (rows, PAIR), 1) < HD
    weights = jnp.exp2((hold[...] - top) * log2_scale).astype(jnp.bfloat16)
    result = jnp.dot(weights, values, preferred_element_type=jnp.float32)
    return (
        log2_scale * jnp.where(low, top[:rows], top[rows:]),
        jnp.where(low, result[:rows, :PAIR], result[rows:, :PAIR]),
        jnp.where(low, result[:rows, PAIR:], result[rows:, PAIR:]),
    )


def merged(fine, coarse):
    top = jnp.maximum(fine[0], coarse[0])
    keep = jnp.exp2(fine[0] - top)
    join = jnp.exp2(coarse[0] - top)
    return top, fine[1] * keep + coarse[1] * join, fine[2] * keep + coarse[2] * join


def doubled(field):
    rows, lanes = field.shape
    slabs = field.reshape(rows // SLAB, 1, SLAB, lanes)
    return jnp.broadcast_to(slabs, (rows // SLAB, 2, SLAB, lanes)).reshape(2 * rows, lanes)


def with_ones(values, weight=1.0):
    if weight != 1.0:
        values = values * jnp.bfloat16(weight)
    return jnp.concatenate([values, jnp.full(values.shape, weight, jnp.bfloat16)], axis=1)


def local_kernel(
    q_ref, k_ref, v_ref, one_ref, four_ref, edge_q, two_q, three_q, four_q, state,
    scratch, near_hold, coarse_hold,
):
    rows = q_ref.shape[0]
    blocks = rows // BLOCK
    pairs = scratch.shape[0]
    spill(q_ref, scratch)
    fine, one_q = [], []
    for pair in range(pairs):
        lanes = pl.ds(pair * PAIR, PAIR)
        ladder = [[], [], [], [], []]
        for block in range(blocks):
            slabs = slabs_of(scratch.at[pair], block)
            ladder[0].append(joined(slabs))
            for level in range(1, LEVELS + 1):
                slabs = pooled_slabs(slabs)
                ladder[level] += slabs
        edge_q[0, :, lanes] = ladder[0][0]
        edge_q[1, :, lanes] = ladder[0][-1]
        two_q[:, lanes] = joined(ladder[2])
        three_q[:, lanes] = joined(ladder[3])
        four_q[:, lanes] = joined(ladder[4])
        fine.append(ladder[0])
        one_q.append([joined(ladder[1][n : n + FAN]) for n in range(0, len(ladder[1]), FAN)])
    windows = [(max(n - 1, 0) * BLOCK, min(n + 2, blocks) * BLOCK) for n in range(blocks)]
    tops = {}
    for pair in range(pairs):
        lanes = pl.ds(pair * PAIR, PAIR)
        for half in range(blocks // 2):
            there = pl.ds((half ^ 1) * BLOCK, BLOCK)
            tops[pair, half] = score(
                one_q[pair][half], one_ref[0, there, lanes], coarse_hold.at[pair, half]
            )
            for block in (2 * half, 2 * half + 1):
                low, high = windows[block]
                hold = near_hold.at[pair, block, :, : high - low]
                tops[pair, half, block] = score(fine[pair][block], k_ref[low:high, lanes], hold)
    for pair in range(pairs):
        lanes = pl.ds(pair * PAIR, PAIR)
        for half in range(blocks // 2):
            there = pl.ds((half ^ 1) * BLOCK, BLOCK)
            coarse = weigh(
                coarse_hold.at[pair, half], tops[pair, half], with_ones(one_ref[1, there, lanes])
            )
            for block in (2 * half, 2 * half + 1):
                low, high = windows[block]
                hold = near_hold.at[pair, block, :, : high - low]
                near = weigh(hold, tops[pair, half, block], with_ones(v_ref[low:high, lanes]))
                part = slice((block - 2 * half) * BLOCK // 2, (block - 2 * half + 1) * BLOCK // 2)
                done = merged(near, [doubled(x[part]) for x in coarse])
                for index, field in enumerate(done):
                    state[index, block * BLOCK : (block + 1) * BLOCK, lanes] = field


def join_kernel(four_ref, six_ref, query_ref, out):
    sixteenth = four_ref.shape[1]
    out[:, :sixteenth, :] = four_ref[...]
    out[:, sixteenth:, :] = six_ref[...]


def coarse_kernel(
    two_q, three_q, first_ref, three_a, three_b, coarse, near_ref, scratch, two_ref, two_hold, three_hold
):
    inner = first_ref.shape[1] - BLOCK
    pairs = scratch.shape[1]
    two_ref[:, :inner, :] = first_ref[:, BLOCK:, :]
    for which in range(2):
        spill(first_ref.at[which, pl.ds(0, BLOCK), :], scratch.at[which])
        for half in range(pairs):
            lanes = pl.ds(half * PAIR, PAIR)
            slabs = slabs_of(scratch.at[which, half], 0)
            two_ref[which, inner:, lanes] = joined(pooled_slabs(pooled_slabs(slabs)))
        near_ref[which] = repooled(repooled(two_ref[which]))
    steps = {}
    for pair in range(pairs):
        lanes = pl.ds(pair * PAIR, PAIR)
        three = [
            jnp.concatenate([three_a[which, :, lanes], three_b[which, :, lanes]], axis=0)
            for which in range(2)
        ]
        steps[pair, 3] = (
            score(three_q[:, lanes], three[0], three_hold.at[pair]), with_ones(three[1])
        )
        steps[pair, 2] = (
            score(two_q[:, lanes], two_ref[0, :, lanes], two_hold.at[pair]),
            with_ones(two_ref[1, :, lanes]),
        )
    for pair in range(pairs):
        three = weigh(three_hold.at[pair], *steps[pair, 3])
        two = merged(weigh(two_hold.at[pair], *steps[pair, 2]), [doubled(x) for x in three])
        for index, field in enumerate(two):
            coarse[index, :, pl.ds(pair * PAIR, PAIR)] = field


def mid_kernel(edge_q, coarse, state, first_ref, second_ref, fine, holds):
    rows = state.shape[1]
    blocks = rows // BLOCK
    position = lax.axis_index("seq")
    last = lax.axis_size("seq") - 1
    even = lax.rem(position, 2) == 0
    opens = (position > 0, position < last)
    pairs = holds.shape[0]
    steps = {}
    for pair in range(pairs):
        lanes = pl.ds(pair * PAIR, PAIR)
        inner = [first_ref[which, :BLOCK, lanes] for which in range(2)]
        outer = [second_ref[which, :, lanes] for which in range(2)]
        for side in range(2):
            halo = [
                jnp.where(even, *((outer[which], inner[which])[:: 1 - 2 * side]))
                for which in range(2)
            ]
            steps[pair, side] = (
                score(edge_q[side, :, lanes], halo[0], holds.at[pair, side], opens[side]),
                with_ones(halo[1]),
            )
    for pair in range(pairs):
        lanes = pl.ds(pair * PAIR, PAIR)
        for block in range(blocks):
            here = slice(block * BLOCK, (block + 1) * BLOCK)
            quarter = slice(block * BLOCK // 4, (block + 1) * BLOCK // 4)
            done = merged(
                [state[index, here, lanes] for index in range(3)],
                [doubled(doubled(coarse[index, quarter, lanes])) for index in range(3)],
            )
            for side, edge in enumerate((0, blocks - 1)):
                if block == edge:
                    done = merged(done, weigh(holds.at[pair, side], *steps[pair, side]))
            fine[0, here, lanes] = done[1] / done[2]
            fine[1, here, lanes] = done[0] + jnp.log(done[2]) * log2_e


def repeated(field):
    return jnp.concatenate([field] * FAN, axis=0)


def finish_kernel(
    four_q, fine, four_ref, near_ref, three_a, three_b, fours_a, fours_b, *refs
):
    far, refs = refs[:-6], refs[-6:]
    outs, (attended, four_hold) = refs[:-2], refs[-2:]
    blocks = fine.shape[1] // BLOCK
    own = lax.axis_index("head")
    pairs = four_q.shape[1] // PAIR
    steps = {}
    for pair in range(pairs):
        lanes = pl.ds(pair * PAIR, PAIR)
        ours, theirs, beyond = [], [], []
        for which in range(2):
            ours.append(
                [four_ref[which, :, lanes], near_ref[which, :, lanes]]
                + [repooled(field[which, :, lanes]) for field in (three_a, three_b)]
            )
            theirs.append([field[which, :, lanes] for field in (fours_a, fours_b)])
            beyond.append([field[which, :, lanes] for field in far])
        steps[pair] = (
            score(
                four_q[:, lanes],
                jnp.concatenate(ours[0] + theirs[0] + beyond[0], axis=0),
                four_hold.at[pair],
            ),
            jnp.concatenate(
                [with_ones(field) for field in ours[1]]
                + [with_ones(field, 2.0) for field in theirs[1]]
                + [with_ones(field) for field in beyond[1]],
                axis=0,
            ),
        )
    for pair in range(pairs):
        lanes = pl.ds(pair * PAIR, PAIR)
        top, numer, rowsum = weigh(four_hold.at[pair], *steps[pair])
        result, log_sum = numer / rowsum, top + jnp.log(rowsum) * log2_e
        for block in range(blocks):
            here = slice(block * BLOCK, (block + 1) * BLOCK)
            few = slice(block * SLAB, (block + 1) * SLAB)
            ours = fine[0, here, lanes]
            keep = 1.0 / (1.0 + jnp.exp2(repeated(log_sum[few]) - fine[1, here, lanes]))
            theirs = repeated(result[few])
            attended[block, :, lanes] = (theirs + keep * (ours - theirs)).astype(jnp.bfloat16)
    for step, out in enumerate(outs):
        out[...] = attended[own ^ step]


def partial_kernel(own_ref, weight_ref, out_ref):
    features = own_ref.shape[1]
    start = pl.multiple_of(lax.axis_index("head") * features, features)
    out_ref[...] = jnp.dot(
        own_ref[...], weight_ref[pl.ds(start, features), :], preferred_element_type=jnp.float32
    )


def project_kernel(partial_ref, *refs):
    parts, (weight_ref, out_hbm, scratch, staged, sems) = refs[:-5], refs[-5:]
    own = lax.axis_index("head")
    features = parts[0].shape[1]
    chunk = staged.shape[2]
    copies = []
    for index in range(staged.shape[0]):
        columns = pl.ds(index * chunk, chunk)
        total = partial_ref[:, columns]
        count = len(parts) + 1
        for step, part in zip([*range(CORES, count), *range(1, CORES)], parts):
            start = pl.multiple_of((own ^ step) * features, features)
            total += jnp.dot(
                part[...],
                weight_ref[pl.ds(start, features), columns],
                preferred_element_type=jnp.float32,
            )
        for half in range(chunk // PAIR):
            lanes = slice(half * PAIR, (half + 1) * PAIR)
            scratch[index, half] = total[:, lanes]
            for i in range(SLAB):
                staged[index, i * FAN : (i + 1) * FAN, lanes] = scratch[
                    index, half, pl.ds(i, FAN, stride=SLAB), :
                ].astype(jnp.bfloat16)
        copy = pltpu.make_async_copy(staged.at[index], out_hbm.at[:, columns], sems.at[index])
        copy.start()
        copies.append(copy)
    for copy in copies:
        copy.wait()


def repool_outside(field):
    which, rows, lanes = field.shape
    slabs = field.astype(jnp.float32).reshape(which, rows // (2 * SLAB), 2, SLAB, lanes)
    sums = (slabs[:, :, 0] + slabs[:, :, 1]) * root_half
    return sums.reshape(which, rows // 2, lanes).astype(jnp.bfloat16)


def swapped(block, axis, mask):
    return lax.ppermute(block, axis, [(i, i ^ mask) for i in range(lax.axis_size(axis))])


def across(block):
    count, heads = lax.axis_size("seq"), lax.axis_size("head")
    route = []
    for seq in range(count):
        end = seq in (0, count - 1)
        other = seq if end else seq + 1 if seq % 2 else seq - 1
        for head in range(heads):
            route.append((seq * heads + head, other * heads + (head ^ 1 if end else head)))
    return lax.ppermute(block, ("seq", "head"), route)


def per_device(queries, key_vectors, value_vectors, out_weight):
    rows, features = queries.shape[1:]
    key_vectors, value_vectors = [
        pltpu.with_memory_space_constraint(x, pltpu.HBM) for x in (key_vectors, value_vectors)
    ]
    pairs = features // PAIR
    seq_count, head_count = lax.axis_size("seq"), lax.axis_size("head")
    bf16 = lambda *shape: jax.ShapeDtypeStruct(shape, jnp.bfloat16)
    params = pltpu.CompilerParams(vmem_limit_bytes=32 * 1024 * 1024)

    hbm = pl.BlockSpec(memory_space=pltpu.HBM)
    vmem = pl.BlockSpec(memory_space=pltpu.VMEM)
    keys, values, first, one, two = pl.pallas_call(
        pool_kernel,
        in_specs=[hbm] * 2,
        out_shape=[
            bf16(rows, features),
            bf16(rows, features),
            bf16(2, BLOCK + rows // 4 - BLOCK // 4, features),
            bf16(2, rows // 2, features),
            bf16(2, rows // 4, features),
        ],
        scratch_shapes=[
            pltpu.VMEM((2, rows // BLOCK, pairs, BLOCK, PAIR), jnp.float32),
            pltpu.SemaphoreType.DMA((2, rows // BLOCK)),
        ],
        compiler_params=params,
        name="pool",
    )(key_vectors, value_vectors)
    second, three, four = pl.pallas_call(
        deeper_kernel,
        out_shape=[
            bf16(2, BLOCK, features),
            bf16(2, rows // 8, features),
            bf16(2, rows // 16, features),
        ],
        compiler_params=params,
        cost_estimate=pl.CostEstimate(flops=2**31, bytes_accessed=2**23, transcendentals=0),
        name="deeper",
    )(keys, values, two)

    first_in = swapped(first, "seq", 1)
    second_in = across(second)
    four_in = swapped(four, "seq", 4)
    six_in = swapped(four, "seq", 6)
    threes_in = [swapped(three, "seq", mask) for mask in (3, 2)]
    edge_q, two_q, three_q, four_q, state = pl.pallas_call(
        local_kernel,
        out_shape=[
            bf16(2, BLOCK, features),
            bf16(rows // 4, features),
            bf16(rows // 8, features),
            bf16(rows // 16, features),
            jax.ShapeDtypeStruct((3, rows, features), jnp.float32),
        ],
        scratch_shapes=[
            pltpu.VMEM((pairs, rows, PAIR), jnp.float32),
            pltpu.VMEM((pairs, rows // BLOCK, 2 * BLOCK, 3 * BLOCK), jnp.float32),
            pltpu.VMEM((pairs, rows // BLOCK // 2, 2 * BLOCK, BLOCK), jnp.float32),
        ],
        compiler_params=params,
        name="local",
    )(queries[0], keys, values, one, four_in)

    fours = pl.pallas_call(
        join_kernel,
        out_shape=bf16(2, rows // 8, features),
        compiler_params=params,
        cost_estimate=pl.CostEstimate(flops=2**29, bytes_accessed=2**20, transcendentals=0),
        name="join",
    )(four_in, six_in, four_q)
    fours_in = swapped(fours, "seq", 1)
    coarse, near = pl.pallas_call(
        coarse_kernel,
        out_shape=[
            jax.ShapeDtypeStruct((3, rows // 4, features), jnp.float32),
            bf16(2, rows // 16, features),
        ],
        scratch_shapes=[
            pltpu.VMEM((2, pairs, BLOCK, PAIR), jnp.float32),
            pltpu.VMEM((2, rows // 4, features), jnp.bfloat16),
            pltpu.VMEM((pairs, rows // 2, BLOCK), jnp.float32),
            pltpu.VMEM((pairs, rows // 4, BLOCK), jnp.float32),
        ],
        compiler_params=params,
        cost_estimate=pl.CostEstimate(flops=2**31, bytes_accessed=2**21, transcendentals=0),
        name="coarse",
    )(two_q, three_q, first_in, *threes_in)
    fine = pl.pallas_call(
        mid_kernel,
        out_shape=jax.ShapeDtypeStruct((2, rows, features), jnp.float32),
        scratch_shapes=[pltpu.VMEM((pairs, 2, 2 * BLOCK, BLOCK), jnp.float32)],
        compiler_params=params,
        name="mid",
    )(edge_q, coarse, state, first_in, second_in)

    far = []
    known = 8
    if known < seq_count:
        group = [four, near] + [repool_outside(field) for field in threes_in]
        group = jnp.concatenate(group + [fours, fours_in], axis=1)
        while known < seq_count:
            fresh = swapped(group, "seq", known)
            far.append(fresh)
            group = jnp.concatenate([group, fresh], axis=1)
            known *= 2

    outs = pl.pallas_call(
        finish_kernel,
        out_shape=[bf16(BLOCK, features) for _ in range(head_count)],
        scratch_shapes=[
            pltpu.VMEM((rows // BLOCK, BLOCK, features), jnp.bfloat16),
            pltpu.VMEM((pairs, rows // 8, rows // 16 * seq_count), jnp.float32),
        ],
        compiler_params=params,
        name="finish",
    )(four_q, fine, four, near, *threes_in, fours, fours_in, *far)

    order = list(range(CORES, head_count)) + list(range(1, CORES))
    parts = [swapped(outs[step], "head", step) for step in order]
    width = out_weight.shape[1]
    partial = pl.pallas_call(
        partial_kernel,
        out_shape=jax.ShapeDtypeStruct((BLOCK, width), jnp.float32),
        compiler_params=params,
        name="partial",
    )(outs[0], out_weight)
    chunk = 2 * PAIR
    result = pl.pallas_call(
        project_kernel,
        in_specs=[vmem] * (len(parts) + 2),
        out_specs=hbm,
        out_shape=bf16(BLOCK, width),
        scratch_shapes=[
            pltpu.VMEM((width // chunk, 2, BLOCK, PAIR), jnp.float32),
            pltpu.VMEM((width // chunk, BLOCK, chunk), jnp.bfloat16),
            pltpu.SemaphoreType.DMA((width // chunk,)),
        ],
        compiler_params=params,
        name="project",
    )(partial, *parts, out_weight)
    return result[None]


def solution(mesh):
    return jax.shard_map(
        per_device,
        mesh=mesh,
        in_specs=(P(None, "seq", "head"), P(None, "seq", "head"), P(None, "seq", "head"), P()),
        out_specs=P(None, ("seq", "head"), None),
        check_vma=False,
    )
```

```python
import jax
import jax.numpy as jnp
from jax import lax
from jax.experimental import pallas as pl
from jax.experimental.pallas import tpu as pltpu
from jax.sharding import PartitionSpec as P

HD = 64
BLOCK = 128
LEVELS = 4
SLAB = 8
PAIR = 2 * HD

neg_fill = -1e30
root_half = 0.7071067811865476
log2_e = 1.4426950408889634
log2_scale = HD**-0.5 * log2_e
least_share = 2.0**-100
CORES = 2

FAN = 2**LEVELS


def slabs_of(scratch, block):
    return [scratch[pl.ds(BLOCK * block + j, SLAB, stride=FAN), :] for j in range(FAN)]


def pooled_slabs(slabs):
    return [
        ((low + high) * root_half).astype(jnp.bfloat16).astype(jnp.float32)
        for low, high in zip(slabs[0::2], slabs[1::2])
    ]


def joined(slabs):
    return jnp.concatenate(slabs, axis=0).astype(jnp.bfloat16)


def spill(source, scratch):
    for half in range(scratch.shape[0]):
        scratch[half] = source[:, half * PAIR : (half + 1) * PAIR].astype(jnp.float32)


def pool_kernel(
    k_hbm, v_hbm, k_ref, v_ref, first_ref, one_ref, two_ref, scratch, sems
):
    rows = k_ref.shape[0]
    blocks = rows // BLOCK
    arrivals = []
    for block in range(blocks):
        here = pl.ds(block * BLOCK, BLOCK)
        for which, (source, target) in enumerate(((k_hbm, k_ref), (v_hbm, v_ref))):
            copy = pltpu.make_async_copy(
                source.at[0, here, :], target.at[here, :], sems.at[which, block]
            )
            copy.start()
            arrivals.append((block, which, target, copy))
    even = lax.rem(lax.axis_index("seq"), 2) == 0
    for block, which, ref, copy in arrivals:
        copy.wait()
        here = pl.ds(block * BLOCK, BLOCK)
        spill(ref.at[here, :], scratch.at[which, block])
        for half in range(scratch.shape[2]):
            lanes = pl.ds(half * PAIR, PAIR)
            one = pooled_slabs(slabs_of(scratch.at[which, block, half], 0))
            one_ref[which, pl.ds(block * BLOCK // 2, BLOCK // 2), lanes] = joined(one)
            two_ref[which, pl.ds(block * BLOCK // 4, BLOCK // 4), lanes] = joined(pooled_slabs(one))
    inner = rows // 4 - BLOCK // 4
    for which, ref in enumerate((k_ref, v_ref)):
        first_ref[which, :BLOCK, :] = jnp.where(even, ref[rows - BLOCK :, :], ref[:BLOCK, :])
        first_ref[which, BLOCK:, :] = jnp.where(
            even, two_ref[which, :inner, :], two_ref[which, BLOCK // 4 :, :]
        )


def repooled(field):
    rows, lanes = field.shape
    slabs = field.astype(jnp.float32).reshape(rows // (2 * SLAB), 2, SLAB, lanes)
    return ((slabs[:, 0] + slabs[:, 1]) * root_half).reshape(rows // 2, lanes).astype(jnp.bfloat16)


def deeper_kernel(k_ref, v_ref, two_ref, second_ref, three_ref, four_ref):
    rows = k_ref.shape[0]
    even = lax.rem(lax.axis_index("seq"), 2) == 0
    for which, ref in enumerate((k_ref, v_ref)):
        second_ref[which] = jnp.where(even, ref[:BLOCK, :], ref[rows - BLOCK :, :])
        three = repooled(two_ref[which])
        three_ref[which] = three
        four_ref[which] = repooled(three)


def repooled(field):
    rows, lanes = field.shape
    slabs = field.astype(jnp.float32).reshape(rows // (2 * SLAB), 2, SLAB, lanes)
    return ((slabs[:, 0] + slabs[:, 1]) * root_half).reshape(rows // 2, lanes).astype(jnp.bfloat16)


def score(queries, keys, hold, is_open=None):
    rows = queries.shape[0]
    low = lax.broadcasted_iota(jnp.int32, (rows, PAIR), 1) < HD
    zero = jnp.zeros_like(queries)
    both = jnp.concatenate([jnp.where(low, queries, zero), jnp.where(low, zero, queries)], axis=0)
    raw = lax.dot_general(both, keys, (((1,), (1,)), ((), ())), preferred_element_type=jnp.float32)
    if is_open is not None:
        raw = jnp.where(is_open, raw, neg_fill)
    hold[...] = raw
    return jnp.max(raw, axis=1, keepdims=True)


def weigh(hold, top, values):
    rows = top.shape[0] // 2
    low = lax.broadcasted_iota(jnp.int32, (rows, PAIR), 1) < HD
    weights = jnp.exp2((hold[...] - top) * log2_scale).astype(jnp.bfloat16)
    result = jnp.dot(weights, values, preferred_element_type=jnp.float32)
    return (
        log2_scale * jnp.where(low, top[:rows], top[rows:]),
        jnp.where(low, result[:rows, :PAIR], result[rows:, :PAIR]),
        jnp.where(low, result[:rows, PAIR:], result[rows:, PAIR:]),
    )


def merged(fine, coarse):
    top = jnp.maximum(fine[0], coarse[0])
    keep = jnp.exp2(fine[0] - top)
    join = jnp.exp2(coarse[0] - top)
    return top, fine[1] * keep + coarse[1] * join, fine[2] * keep + coarse[2] * join


def doubled(field):
    rows, lanes = field.shape
    slabs = field.reshape(rows // SLAB, 1, SLAB, lanes)
    return jnp.broadcast_to(slabs, (rows // SLAB, 2, SLAB, lanes)).reshape(2 * rows, lanes)


def with_ones(values, weight=1.0):
    if weight != 1.0:
        values = values * jnp.bfloat16(weight)
    return jnp.concatenate([values, jnp.full(values.shape, weight, jnp.bfloat16)], axis=1)


def local_kernel(
    q_ref, k_ref, v_ref, one_ref, four_ref, edge_q, two_q, three_q, four_q, state,
    scratch, near_hold, coarse_hold,
):
    rows = q_ref.shape[0]
    blocks = rows // BLOCK
    pairs = scratch.shape[0]
    spill(q_ref, scratch)
    fine, one_q = [], []
    for pair in range(pairs):
        lanes = pl.ds(pair * PAIR, PAIR)
        ladder = [[], [], [], [], []]
        for block in range(blocks):
            slabs = slabs_of(scratch.at[pair], block)
            ladder[0].append(joined(slabs))
            for level in range(1, LEVELS + 1):
                slabs = pooled_slabs(slabs)
                ladder[level] += slabs
        edge_q[0, :, lanes] = ladder[0][0]
        edge_q[1, :, lanes] = ladder[0][-1]
        two_q[:, lanes] = joined(ladder[2])
        three_q[:, lanes] = joined(ladder[3])
        four_q[:, lanes] = joined(ladder[4])
        fine.append(ladder[0])
        one_q.append([joined(ladder[1][n : n + FAN]) for n in range(0, len(ladder[1]), FAN)])
    windows = [(max(n - 1, 0) * BLOCK, min(n + 2, blocks) * BLOCK) for n in range(blocks)]
    tops = {}
    for pair in range(pairs):
        lanes = pl.ds(pair * PAIR, PAIR)
        for half in range(blocks // 2):
            there = pl.ds((half ^ 1) * BLOCK, BLOCK)
            tops[pair, half] = score(
                one_q[pair][half], one_ref[0, there, lanes], coarse_hold.at[pair, half]
            )
            for block in (2 * half, 2 * half + 1):
                low, high = windows[block]
                hold = near_hold.at[pair, block, :, : high - low]
                tops[pair, half, block] = score(fine[pair][block], k_ref[low:high, lanes], hold)
    for pair in range(pairs):
        lanes = pl.ds(pair * PAIR, PAIR)
        for half in range(blocks // 2):
            there = pl.ds((half ^ 1) * BLOCK, BLOCK)
            coarse = weigh(
                coarse_hold.at[pair, half], tops[pair, half], with_ones(one_ref[1, there, lanes])
            )
            for block in (2 * half, 2 * half + 1):
                low, high = windows[block]
                hold = near_hold.at[pair, block, :, : high - low]
                near = weigh(hold, tops[pair, half, block], with_ones(v_ref[low:high, lanes]))
                part = slice((block - 2 * half) * BLOCK // 2, (block - 2 * half + 1) * BLOCK // 2)
                done = merged(near, [doubled(x[part]) for x in coarse])
                for index, field in enumerate(done):
                    state[index, block * BLOCK : (block + 1) * BLOCK, lanes] = field


def join_kernel(four_ref, six_ref, query_ref, out):
    sixteenth = four_ref.shape[1]
    out[:, :sixteenth, :] = four_ref[...]
    out[:, sixteenth:, :] = six_ref[...]


def coarse_kernel(
    two_q, three_q, first_ref, three_a, three_b, coarse, near_ref, scratch, two_ref, two_hold, three_hold
):
    inner = first_ref.shape[1] - BLOCK
    pairs = scratch.shape[1]
    two_ref[:, :inner, :] = first_ref[:, BLOCK:, :]
    for which in range(2):
        spill(first_ref.at[which, pl.ds(0, BLOCK), :], scratch.at[which])
        for half in range(pairs):
            lanes = pl.ds(half * PAIR, PAIR)
            slabs = slabs_of(scratch.at[which, half], 0)
            two_ref[which, inner:, lanes] = joined(pooled_slabs(pooled_slabs(slabs)))
        near_ref[which] = repooled(repooled(two_ref[which]))
    steps = {}
    for pair in range(pairs):
        lanes = pl.ds(pair * PAIR, PAIR)
        three = [
            jnp.concatenate([three_a[which, :, lanes], three_b[which, :, lanes]], axis=0)
            for which in range(2)
        ]
        steps[pair, 3] = (
            score(three_q[:, lanes], three[0], three_hold.at[pair]), with_ones(three[1])
        )
        steps[pair, 2] = (
            score(two_q[:, lanes], two_ref[0, :, lanes], two_hold.at[pair]),
            with_ones(two_ref[1, :, lanes]),
        )
    for pair in range(pairs):
        three = weigh(three_hold.at[pair], *steps[pair, 3])
        two = merged(weigh(two_hold.at[pair], *steps[pair, 2]), [doubled(x) for x in three])
        for index, field in enumerate(two):
            coarse[index, :, pl.ds(pair * PAIR, PAIR)] = field


def mid_kernel(edge_q, coarse, state, first_ref, second_ref, fine, *refs):
    outs, (ready, holds) = refs[:-2], refs[-2:]
    own = lax.axis_index("head")
    rows = state.shape[1]
    blocks = rows // BLOCK
    position = lax.axis_index("seq")
    last = lax.axis_size("seq") - 1
    even = lax.rem(position, 2) == 0
    opens = (position > 0, position < last)
    pairs = holds.shape[0]
    steps = {}
    for pair in range(pairs):
        lanes = pl.ds(pair * PAIR, PAIR)
        inner = [first_ref[which, :BLOCK, lanes] for which in range(2)]
        outer = [second_ref[which, :, lanes] for which in range(2)]
        for side in range(2):
            halo = [
                jnp.where(even, *((outer[which], inner[which])[:: 1 - 2 * side]))
                for which in range(2)
            ]
            steps[pair, side] = (
                score(edge_q[side, :, lanes], halo[0], holds.at[pair, side], opens[side]),
                with_ones(halo[1]),
            )
    for pair in range(pairs):
        lanes = pl.ds(pair * PAIR, PAIR)
        for block in range(blocks):
            here = slice(block * BLOCK, (block + 1) * BLOCK)
            quarter = slice(block * BLOCK // 4, (block + 1) * BLOCK // 4)
            done = merged(
                [state[index, here, lanes] for index in range(3)],
                [doubled(doubled(coarse[index, quarter, lanes])) for index in range(3)],
            )
            for side, edge in enumerate((0, blocks - 1)):
                if block == edge:
                    done = merged(done, weigh(holds.at[pair, side], *steps[pair, side]))
            result = done[1] / done[2]
            fine[0, here, lanes] = result
            fine[1, here, lanes] = done[0] + jnp.log(done[2]) * log2_e
            ready[block, :, lanes] = result.astype(jnp.bfloat16)
    for step, out in enumerate(outs, CORES):
        out[...] = ready[own ^ step]


def repeated(field):
    return jnp.concatenate([field] * FAN, axis=0)


def finish_kernel(
    four_q, fine, four_ref, near_ref, three_a, three_b, fours_a, fours_b, *refs
):
    refs, (coarse, four_hold) = refs[:-2], refs[-2:]
    heads = lax.axis_size("head")
    far, outs = refs[:-heads], refs[-heads:]
    own = lax.axis_index("head")
    features = four_q.shape[1]
    pairs = four_q.shape[1] // PAIR
    steps = {}
    for pair in range(pairs):
        lanes = pl.ds(pair * PAIR, PAIR)
        ours, theirs, beyond = [], [], []
        for which in range(2):
            ours.append(
                [four_ref[which, :, lanes], near_ref[which, :, lanes]]
                + [repooled(field[which, :, lanes]) for field in (three_a, three_b)]
            )
            theirs.append([field[which, :, lanes] for field in (fours_a, fours_b)])
            beyond.append([field[which, :, lanes] for field in far])
        steps[pair] = (
            score(
                four_q[:, lanes],
                jnp.concatenate(ours[0] + theirs[0] + beyond[0], axis=0),
                four_hold.at[pair],
            ),
            jnp.concatenate(
                [with_ones(field) for field in ours[1]]
                + [with_ones(field, 2.0) for field in theirs[1]]
                + [with_ones(field) for field in beyond[1]],
                axis=0,
            ),
        )
    for pair in range(pairs):
        lanes = pl.ds(pair * PAIR, PAIR)
        top, numer, rowsum = weigh(four_hold.at[pair], *steps[pair])
        coarse[0, :, lanes] = numer / rowsum
        coarse[1, :, lanes] = top + jnp.log(rowsum) * log2_e
    for step, out in enumerate(outs):
        block = own ^ step
        here = pl.ds(pl.multiple_of(block * BLOCK, BLOCK), BLOCK)
        few = pl.ds(pl.multiple_of(block * SLAB, SLAB), SLAB)
        shares = []
        for pair in range(pairs):
            lanes = pl.ds(pair * PAIR, PAIR)
            fine_sum, coarse_sum = fine[1, here, lanes], repeated(coarse[1, few, lanes])
            if step < CORES:
                keep = 1.0 / (1.0 + jnp.exp2(coarse_sum - fine_sum))
                ours, theirs = fine[0, here, lanes], repeated(coarse[0, few, lanes])
                out[:, lanes] = (theirs + keep * (ours - theirs)).astype(jnp.bfloat16)
            else:
                ratio = jnp.exp2(-jnp.abs(fine_sum - coarse_sum))
                less = jnp.maximum(ratio / (1.0 + ratio), least_share)
                shares.append(jnp.where(fine_sum <= coarse_sum, less, -less).astype(jnp.bfloat16))
        if step >= CORES:
            pick = lax.broadcasted_iota(jnp.int32, (2 * SLAB, features), 1) == HD * (
                lax.broadcasted_iota(jnp.int32, (2 * SLAB, features), 0)
            )
            by_head = lax.dot_general(
                pick.astype(jnp.bfloat16),
                jnp.concatenate(shares, axis=1),
                (((1,), (1,)), ((), ())),
                preferred_element_type=jnp.float32,
            )[:SLAB]
            blank = jnp.zeros((SLAB, features - BLOCK), jnp.float32)
            out[...] = jnp.concatenate(
                [coarse[0, few, :], jnp.concatenate([by_head, blank], axis=1)], axis=0
            ).astype(jnp.bfloat16)


def rejoin_kernel(*refs):
    outs = refs[len(refs) // 3 * 2 :]
    for early, late_ref, out in zip(refs, refs[len(outs) :], outs):
        features = early.shape[1]
        late = late_ref[...].astype(jnp.float32)
        spread = lax.broadcasted_iota(jnp.int32, (SLAB, features), 1) // HD == (
            lax.broadcasted_iota(jnp.int32, (SLAB, features), 0)
        )
        signed = lax.dot_general(
            late[SLAB:, :BLOCK].astype(jnp.bfloat16),
            spread.astype(jnp.bfloat16),
            (((0,), (0,)), ((), ())),
            preferred_element_type=jnp.float32,
        )
        keep = jnp.where(signed >= 0, signed, 1.0 + signed)
        join = jnp.where(signed >= 0, 1.0 - signed, -signed)
        result = keep * early[...].astype(jnp.float32) + join * repeated(late[:SLAB])
        out[...] = result.astype(jnp.bfloat16)


def partial_kernel(own_ref, weight_ref, out_ref):
    features = own_ref.shape[1]
    start = pl.multiple_of(lax.axis_index("head") * features, features)
    out_ref[...] = jnp.dot(
        own_ref[...], weight_ref[pl.ds(start, features), :], preferred_element_type=jnp.float32
    )


def project_kernel(partial_ref, *refs):
    parts, (weight_ref, out_hbm, scratch, staged, sems) = refs[:-5], refs[-5:]
    own = lax.axis_index("head")
    features = parts[0].shape[1]
    chunk = staged.shape[2]
    copies = []
    for index in range(staged.shape[0]):
        columns = pl.ds(index * chunk, chunk)
        total = partial_ref[:, columns]
        for step, part in enumerate(parts, 1):
            start = pl.multiple_of((own ^ step) * features, features)
            total += jnp.dot(
                part[...],
                weight_ref[pl.ds(start, features), columns],
                preferred_element_type=jnp.float32,
            )
        for half in range(chunk // PAIR):
            lanes = slice(half * PAIR, (half + 1) * PAIR)
            scratch[index, half] = total[:, lanes]
            for i in range(SLAB):
                staged[index, i * FAN : (i + 1) * FAN, lanes] = scratch[
                    index, half, pl.ds(i, FAN, stride=SLAB), :
                ].astype(jnp.bfloat16)
        copy = pltpu.make_async_copy(staged.at[index], out_hbm.at[:, columns], sems.at[index])
        copy.start()
        copies.append(copy)
    for copy in copies:
        copy.wait()


def repool_outside(field):
    which, rows, lanes = field.shape
    slabs = field.astype(jnp.float32).reshape(which, rows // (2 * SLAB), 2, SLAB, lanes)
    sums = (slabs[:, :, 0] + slabs[:, :, 1]) * root_half
    return sums.reshape(which, rows // 2, lanes).astype(jnp.bfloat16)


def swapped(block, axis, mask):
    return lax.ppermute(block, axis, [(i, i ^ mask) for i in range(lax.axis_size(axis))])


def across(block):
    count, heads = lax.axis_size("seq"), lax.axis_size("head")
    route = []
    for seq in range(count):
        end = seq in (0, count - 1)
        other = seq if end else seq + 1 if seq % 2 else seq - 1
        for head in range(heads):
            route.append((seq * heads + head, other * heads + (head ^ 1 if end else head)))
    return lax.ppermute(block, ("seq", "head"), route)


def per_device(queries, key_vectors, value_vectors, out_weight):
    rows, features = queries.shape[1:]
    key_vectors, value_vectors = [
        pltpu.with_memory_space_constraint(x, pltpu.HBM) for x in (key_vectors, value_vectors)
    ]
    pairs = features // PAIR
    seq_count, head_count = lax.axis_size("seq"), lax.axis_size("head")
    bf16 = lambda *shape: jax.ShapeDtypeStruct(shape, jnp.bfloat16)
    params = pltpu.CompilerParams(vmem_limit_bytes=32 * 1024 * 1024)

    hbm = pl.BlockSpec(memory_space=pltpu.HBM)
    vmem = pl.BlockSpec(memory_space=pltpu.VMEM)
    keys, values, first, one, two = pl.pallas_call(
        pool_kernel,
        in_specs=[hbm] * 2,
        out_shape=[
            bf16(rows, features),
            bf16(rows, features),
            bf16(2, BLOCK + rows // 4 - BLOCK // 4, features),
            bf16(2, rows // 2, features),
            bf16(2, rows // 4, features),
        ],
        scratch_shapes=[
            pltpu.VMEM((2, rows // BLOCK, pairs, BLOCK, PAIR), jnp.float32),
            pltpu.SemaphoreType.DMA((2, rows // BLOCK)),
        ],
        compiler_params=params,
        name="pool",
    )(key_vectors, value_vectors)
    second, three, four = pl.pallas_call(
        deeper_kernel,
        out_shape=[
            bf16(2, BLOCK, features),
            bf16(2, rows // 8, features),
            bf16(2, rows // 16, features),
        ],
        compiler_params=params,
        cost_estimate=pl.CostEstimate(flops=2**31, bytes_accessed=2**23, transcendentals=0),
        name="deeper",
    )(keys, values, two)

    first_in = swapped(first, "seq", 1)
    second_in = across(second)
    four_in = swapped(four, "seq", 4)
    six_in = swapped(four, "seq", 6)
    threes_in = [swapped(three, "seq", mask) for mask in (3, 2)]
    edge_q, two_q, three_q, four_q, state = pl.pallas_call(
        local_kernel,
        out_shape=[
            bf16(2, BLOCK, features),
            bf16(rows // 4, features),
            bf16(rows // 8, features),
            bf16(rows // 16, features),
            jax.ShapeDtypeStruct((3, rows, features), jnp.float32),
        ],
        scratch_shapes=[
            pltpu.VMEM((pairs, rows, PAIR), jnp.float32),
            pltpu.VMEM((pairs, rows // BLOCK, 2 * BLOCK, 3 * BLOCK), jnp.float32),
            pltpu.VMEM((pairs, rows // BLOCK // 2, 2 * BLOCK, BLOCK), jnp.float32),
        ],
        compiler_params=params,
        name="local",
    )(queries[0], keys, values, one, four_in)

    fours = pl.pallas_call(
        join_kernel,
        out_shape=bf16(2, rows // 8, features),
        compiler_params=params,
        cost_estimate=pl.CostEstimate(flops=2**29, bytes_accessed=2**20, transcendentals=0),
        name="join",
    )(four_in, six_in, four_q)
    fours_in = swapped(fours, "seq", 1)
    coarse, near = pl.pallas_call(
        coarse_kernel,
        out_shape=[
            jax.ShapeDtypeStruct((3, rows // 4, features), jnp.float32),
            bf16(2, rows // 16, features),
        ],
        scratch_shapes=[
            pltpu.VMEM((2, pairs, BLOCK, PAIR), jnp.float32),
            pltpu.VMEM((2, rows // 4, features), jnp.bfloat16),
            pltpu.VMEM((pairs, rows // 2, BLOCK), jnp.float32),
            pltpu.VMEM((pairs, rows // 4, BLOCK), jnp.float32),
        ],
        compiler_params=params,
        cost_estimate=pl.CostEstimate(flops=2**31, bytes_accessed=2**21, transcendentals=0),
        name="coarse",
    )(two_q, three_q, first_in, *threes_in)
    away = range(CORES, head_count)
    fine, *early = pl.pallas_call(
        mid_kernel,
        out_shape=[jax.ShapeDtypeStruct((2, rows, features), jnp.float32)]
        + [bf16(BLOCK, features) for _ in away],
        scratch_shapes=[
            pltpu.VMEM((rows // BLOCK, BLOCK, features), jnp.bfloat16),
            pltpu.VMEM((pairs, 2, 2 * BLOCK, BLOCK), jnp.float32),
        ],
        compiler_params=params,
        name="mid",
    )(edge_q, coarse, state, first_in, second_in)
    early_in = [swapped(part, "head", step) for step, part in zip(away, early)]

    far = []
    known = 8
    if known < seq_count:
        group = [four, near] + [repool_outside(field) for field in threes_in]
        group = jnp.concatenate(group + [fours, fours_in], axis=1)
        while known < seq_count:
            fresh = swapped(group, "seq", known)
            far.append(fresh)
            group = jnp.concatenate([group, fresh], axis=1)
            known *= 2

    near_parts = [bf16(BLOCK, features) for _ in range(CORES)]
    outs = pl.pallas_call(
        finish_kernel,
        out_shape=near_parts + [bf16(2 * SLAB, features) for _ in away],
        scratch_shapes=[
            pltpu.VMEM((2, rows // 16, features), jnp.float32),
            pltpu.VMEM((pairs, rows // 8, rows // 16 * seq_count), jnp.float32),
        ],
        compiler_params=params,
        name="finish",
    )(four_q, fine, four, near, *threes_in, fours, fours_in, *far)
    late_in = [swapped(part, "head", step) for step, part in zip(away, outs[CORES:])]
    near_in = swapped(outs[1], "head", 1)
    width = out_weight.shape[1]
    partial = pl.pallas_call(
        partial_kernel,
        out_shape=jax.ShapeDtypeStruct((BLOCK, width), jnp.float32),
        compiler_params=params,
        name="partial",
    )(outs[0], out_weight)
    rejoined = pl.pallas_call(
        rejoin_kernel,
        out_shape=[bf16(BLOCK, features) for _ in away],
        compiler_params=params,
        cost_estimate=pl.CostEstimate(flops=2**32, bytes_accessed=2**20, transcendentals=0),
        name="rejoin",
    )(*early_in, *late_in)
    chunk = 2 * PAIR
    result = pl.pallas_call(
        project_kernel,
        in_specs=[vmem] * (3 + len(rejoined)),
        out_specs=hbm,
        out_shape=bf16(BLOCK, width),
        scratch_shapes=[
            pltpu.VMEM((width // chunk, 2, BLOCK, PAIR), jnp.float32),
            pltpu.VMEM((width // chunk, BLOCK, chunk), jnp.bfloat16),
            pltpu.SemaphoreType.DMA((width // chunk,)),
        ],
        compiler_params=params,
        name="project",
    )(partial, near_in, *rejoined, out_weight)
    return result[None]


def solution(mesh):
    return jax.shard_map(
        per_device,
        mesh=mesh,
        in_specs=(P(None, "seq", "head"), P(None, "seq", "head"), P(None, "seq", "head"), P()),
        out_specs=P(None, ("seq", "head"), None),
        check_vma=False,
    )
```

```python
import jax
import jax.numpy as jnp
from jax import lax
from jax.experimental import pallas as pl
from jax.experimental.pallas import tpu as pltpu
from jax.sharding import PartitionSpec as P

HD = 64
BLOCK = 128
LEVELS = 4
SLAB = 8
PAIR = 2 * HD

neg_fill = -1e30
root_half = 0.7071067811865476
log2_e = 1.4426950408889634
log2_scale = HD**-0.5 * log2_e
least_share = 2.0**-100
AHEAD = 3

FAN = 2**LEVELS


def slabs_of(scratch, block):
    return [scratch[pl.ds(BLOCK * block + j, SLAB, stride=FAN), :] for j in range(FAN)]


def pooled_slabs(slabs):
    return [
        ((low + high) * root_half).astype(jnp.bfloat16).astype(jnp.float32)
        for low, high in zip(slabs[0::2], slabs[1::2])
    ]


def joined(slabs):
    return jnp.concatenate(slabs, axis=0).astype(jnp.bfloat16)


def spill(source, scratch):
    for half in range(scratch.shape[0]):
        scratch[half] = source[:, half * PAIR : (half + 1) * PAIR].astype(jnp.float32)


def pool_kernel(
    k_hbm, v_hbm, k_ref, v_ref, first_ref, one_ref, two_ref, scratch, sems
):
    rows = k_ref.shape[0]
    blocks = rows // BLOCK
    arrivals = []
    for block in range(blocks):
        here = pl.ds(block * BLOCK, BLOCK)
        for which, (source, target) in enumerate(((k_hbm, k_ref), (v_hbm, v_ref))):
            copy = pltpu.make_async_copy(
                source.at[0, here, :], target.at[here, :], sems.at[which, block]
            )
            copy.start()
            arrivals.append((block, which, target, copy))
    even = lax.rem(lax.axis_index("seq"), 2) == 0
    for block, which, ref, copy in arrivals:
        copy.wait()
        here = pl.ds(block * BLOCK, BLOCK)
        spill(ref.at[here, :], scratch.at[which, block])
        for half in range(scratch.shape[2]):
            lanes = pl.ds(half * PAIR, PAIR)
            one = pooled_slabs(slabs_of(scratch.at[which, block, half], 0))
            one_ref[which, pl.ds(block * BLOCK // 2, BLOCK // 2), lanes] = joined(one)
            two_ref[which, pl.ds(block * BLOCK // 4, BLOCK // 4), lanes] = joined(pooled_slabs(one))
    inner = rows // 4 - BLOCK // 4
    for which, ref in enumerate((k_ref, v_ref)):
        first_ref[which, :BLOCK, :] = jnp.where(even, ref[rows - BLOCK :, :], ref[:BLOCK, :])
        first_ref[which, BLOCK:, :] = jnp.where(
            even, two_ref[which, :inner, :], two_ref[which, BLOCK // 4 :, :]
        )


def repooled(field):
    rows, lanes = field.shape
    slabs = field.astype(jnp.float32).reshape(rows // (2 * SLAB), 2, SLAB, lanes)
    return ((slabs[:, 0] + slabs[:, 1]) * root_half).reshape(rows // 2, lanes).astype(jnp.bfloat16)


def deeper_kernel(k_ref, v_ref, two_ref, second_ref, three_ref, four_ref):
    rows = k_ref.shape[0]
    even = lax.rem(lax.axis_index("seq"), 2) == 0
    for which, ref in enumerate((k_ref, v_ref)):
        second_ref[which] = jnp.where(even, ref[:BLOCK, :], ref[rows - BLOCK :, :])
        three = repooled(two_ref[which])
        three_ref[which] = three
        four_ref[which] = repooled(three)


def repooled(field):
    rows, lanes = field.shape
    slabs = field.astype(jnp.float32).reshape(rows // (2 * SLAB), 2, SLAB, lanes)
    return ((slabs[:, 0] + slabs[:, 1]) * root_half).reshape(rows // 2, lanes).astype(jnp.bfloat16)


def score(queries, keys, hold, is_open=None):
    rows = queries.shape[0]
    low = lax.broadcasted_iota(jnp.int32, (rows, PAIR), 1) < HD
    zero = jnp.zeros_like(queries)
    both = jnp.concatenate([jnp.where(low, queries, zero), jnp.where(low, zero, queries)], axis=0)
    raw = lax.dot_general(both, keys, (((1,), (1,)), ((), ())), preferred_element_type=jnp.float32)
    if is_open is not None:
        raw = jnp.where(is_open, raw, neg_fill)
    hold[...] = raw
    return jnp.max(raw, axis=1, keepdims=True)


def weigh(hold, top, values):
    rows = top.shape[0] // 2
    low = lax.broadcasted_iota(jnp.int32, (rows, PAIR), 1) < HD
    weights = jnp.exp2((hold[...] - top) * log2_scale).astype(jnp.bfloat16)
    result = jnp.dot(weights, values, preferred_element_type=jnp.float32)
    return (
        log2_scale * jnp.where(low, top[:rows], top[rows:]),
        jnp.where(low, result[:rows, :PAIR], result[rows:, :PAIR]),
        jnp.where(low, result[:rows, PAIR:], result[rows:, PAIR:]),
    )


def merged(fine, coarse):
    top = jnp.maximum(fine[0], coarse[0])
    keep = jnp.exp2(fine[0] - top)
    join = jnp.exp2(coarse[0] - top)
    return top, fine[1] * keep + coarse[1] * join, fine[2] * keep + coarse[2] * join


def doubled(field):
    rows, lanes = field.shape
    slabs = field.reshape(rows // SLAB, 1, SLAB, lanes)
    return jnp.broadcast_to(slabs, (rows // SLAB, 2, SLAB, lanes)).reshape(2 * rows, lanes)


def with_ones(values, weight=1.0):
    if weight != 1.0:
        values = values * jnp.bfloat16(weight)
    return jnp.concatenate([values, jnp.full(values.shape, weight, jnp.bfloat16)], axis=1)


def local_kernel(
    q_ref, k_ref, v_ref, one_ref, four_ref, edge_q, two_q, three_q, four_q, state,
    scratch, near_hold, coarse_hold,
):
    rows = q_ref.shape[0]
    blocks = rows // BLOCK
    pairs = scratch.shape[0]
    spill(q_ref, scratch)
    fine, one_q = [], []
    for pair in range(pairs):
        lanes = pl.ds(pair * PAIR, PAIR)
        ladder = [[], [], [], [], []]
        for block in range(blocks):
            slabs = slabs_of(scratch.at[pair], block)
            ladder[0].append(joined(slabs))
            for level in range(1, LEVELS + 1):
                slabs = pooled_slabs(slabs)
                ladder[level] += slabs
        edge_q[0, :, lanes] = ladder[0][0]
        edge_q[1, :, lanes] = ladder[0][-1]
        two_q[:, lanes] = joined(ladder[2])
        three_q[:, lanes] = joined(ladder[3])
        four_q[:, lanes] = joined(ladder[4])
        fine.append(ladder[0])
        one_q.append([joined(ladder[1][n : n + FAN]) for n in range(0, len(ladder[1]), FAN)])
    windows = [(max(n - 1, 0) * BLOCK, min(n + 2, blocks) * BLOCK) for n in range(blocks)]
    tops = {}
    for pair in range(pairs):
        lanes = pl.ds(pair * PAIR, PAIR)
        for half in range(blocks // 2):
            there = pl.ds((half ^ 1) * BLOCK, BLOCK)
            tops[pair, half] = score(
                one_q[pair][half], one_ref[0, there, lanes], coarse_hold.at[pair, half]
            )
            for block in (2 * half, 2 * half + 1):
                low, high = windows[block]
                hold = near_hold.at[pair, block, :, : high - low]
                tops[pair, half, block] = score(fine[pair][block], k_ref[low:high, lanes], hold)
    for pair in range(pairs):
        lanes = pl.ds(pair * PAIR, PAIR)
        for half in range(blocks // 2):
            there = pl.ds((half ^ 1) * BLOCK, BLOCK)
            coarse = weigh(
                coarse_hold.at[pair, half], tops[pair, half], with_ones(one_ref[1, there, lanes])
            )
            for block in (2 * half, 2 * half + 1):
                low, high = windows[block]
                hold = near_hold.at[pair, block, :, : high - low]
                near = weigh(hold, tops[pair, half, block], with_ones(v_ref[low:high, lanes]))
                part = slice((block - 2 * half) * BLOCK // 2, (block - 2 * half + 1) * BLOCK // 2)
                done = merged(near, [doubled(x[part]) for x in coarse])
                for index, field in enumerate(done):
                    state[index, block * BLOCK : (block + 1) * BLOCK, lanes] = field


def join_kernel(four_ref, six_ref, query_ref, out):
    sixteenth = four_ref.shape[1]
    out[:, :sixteenth, :] = four_ref[...]
    out[:, sixteenth:, :] = six_ref[...]


def coarse_kernel(
    two_q, three_q, first_ref, three_a, three_b, coarse, near_ref, scratch, two_ref, two_hold, three_hold
):
    inner = first_ref.shape[1] - BLOCK
    pairs = scratch.shape[1]
    two_ref[:, :inner, :] = first_ref[:, BLOCK:, :]
    for which in range(2):
        spill(first_ref.at[which, pl.ds(0, BLOCK), :], scratch.at[which])
        for half in range(pairs):
            lanes = pl.ds(half * PAIR, PAIR)
            slabs = slabs_of(scratch.at[which, half], 0)
            two_ref[which, inner:, lanes] = joined(pooled_slabs(pooled_slabs(slabs)))
        near_ref[which] = repooled(repooled(two_ref[which]))
    steps = {}
    for pair in range(pairs):
        lanes = pl.ds(pair * PAIR, PAIR)
        three = [
            jnp.concatenate([three_a[which, :, lanes], three_b[which, :, lanes]], axis=0)
            for which in range(2)
        ]
        steps[pair, 3] = (
            score(three_q[:, lanes], three[0], three_hold.at[pair]), with_ones(three[1])
        )
        steps[pair, 2] = (
            score(two_q[:, lanes], two_ref[0, :, lanes], two_hold.at[pair]),
            with_ones(two_ref[1, :, lanes]),
        )
    for pair in range(pairs):
        three = weigh(three_hold.at[pair], *steps[pair, 3])
        two = merged(weigh(two_hold.at[pair], *steps[pair, 2]), [doubled(x) for x in three])
        for index, field in enumerate(two):
            coarse[index, :, pl.ds(pair * PAIR, PAIR)] = field


def mid_kernel(edge_q, coarse, state, first_ref, second_ref, fine, *refs):
    outs, (ready, holds) = refs[:-2], refs[-2:]
    own = lax.axis_index("head")
    rows = state.shape[1]
    blocks = rows // BLOCK
    position = lax.axis_index("seq")
    last = lax.axis_size("seq") - 1
    even = lax.rem(position, 2) == 0
    opens = (position > 0, position < last)
    pairs = holds.shape[0]
    steps = {}
    for pair in range(pairs):
        lanes = pl.ds(pair * PAIR, PAIR)
        inner = [first_ref[which, :BLOCK, lanes] for which in range(2)]
        outer = [second_ref[which, :, lanes] for which in range(2)]
        for side in range(2):
            halo = [
                jnp.where(even, *((outer[which], inner[which])[:: 1 - 2 * side]))
                for which in range(2)
            ]
            steps[pair, side] = (
                score(edge_q[side, :, lanes], halo[0], holds.at[pair, side], opens[side]),
                with_ones(halo[1]),
            )
    for pair in range(pairs):
        lanes = pl.ds(pair * PAIR, PAIR)
        for block in range(blocks):
            here = slice(block * BLOCK, (block + 1) * BLOCK)
            quarter = slice(block * BLOCK // 4, (block + 1) * BLOCK // 4)
            done = merged(
                [state[index, here, lanes] for index in range(3)],
                [doubled(doubled(coarse[index, quarter, lanes])) for index in range(3)],
            )
            for side, edge in enumerate((0, blocks - 1)):
                if block == edge:
                    done = merged(done, weigh(holds.at[pair, side], *steps[pair, side]))
            result = done[1] / done[2]
            fine[0, here, lanes] = result
            fine[1, here, lanes] = done[0] + jnp.log(done[2]) * log2_e
            ready[block, :, lanes] = result.astype(jnp.bfloat16)
    for step, out in enumerate(outs, AHEAD):
        out[...] = ready[own ^ step]


def repeated(field):
    return jnp.concatenate([field] * FAN, axis=0)


def finish_kernel(
    four_q, fine, four_ref, near_ref, three_a, three_b, fours_a, fours_b, *refs
):
    refs, (coarse, four_hold) = refs[:-2], refs[-2:]
    heads = lax.axis_size("head")
    far, outs = refs[:-heads], refs[-heads:]
    own = lax.axis_index("head")
    features = four_q.shape[1]
    pairs = four_q.shape[1] // PAIR
    steps = {}
    for pair in range(pairs):
        lanes = pl.ds(pair * PAIR, PAIR)
        ours, theirs, beyond = [], [], []
        for which in range(2):
            ours.append(
                [four_ref[which, :, lanes], near_ref[which, :, lanes]]
                + [repooled(field[which, :, lanes]) for field in (three_a, three_b)]
            )
            theirs.append([field[which, :, lanes] for field in (fours_a, fours_b)])
            beyond.append([field[which, :, lanes] for field in far])
        steps[pair] = (
            score(
                four_q[:, lanes],
                jnp.concatenate(ours[0] + theirs[0] + beyond[0], axis=0),
                four_hold.at[pair],
            ),
            jnp.concatenate(
                [with_ones(field) for field in ours[1]]
                + [with_ones(field, 2.0) for field in theirs[1]]
                + [with_ones(field) for field in beyond[1]],
                axis=0,
            ),
        )
    for pair in range(pairs):
        lanes = pl.ds(pair * PAIR, PAIR)
        top, numer, rowsum = weigh(four_hold.at[pair], *steps[pair])
        coarse[0, :, lanes] = numer / rowsum
        coarse[1, :, lanes] = top + jnp.log(rowsum) * log2_e
    for step, out in enumerate(outs):
        block = own ^ step
        here = pl.ds(pl.multiple_of(block * BLOCK, BLOCK), BLOCK)
        few = pl.ds(pl.multiple_of(block * SLAB, SLAB), SLAB)
        shares = []
        for pair in range(pairs):
            lanes = pl.ds(pair * PAIR, PAIR)
            fine_sum, coarse_sum = fine[1, here, lanes], repeated(coarse[1, few, lanes])
            if step < AHEAD:
                keep = 1.0 / (1.0 + jnp.exp2(coarse_sum - fine_sum))
                ours, theirs = fine[0, here, lanes], repeated(coarse[0, few, lanes])
                out[:, lanes] = (theirs + keep * (ours - theirs)).astype(jnp.bfloat16)
            else:
                ratio = jnp.exp2(-jnp.abs(fine_sum - coarse_sum))
                less = jnp.maximum(ratio / (1.0 + ratio), least_share)
                shares.append(jnp.where(fine_sum <= coarse_sum, less, -less).astype(jnp.bfloat16))
        if step >= AHEAD:
            pick = lax.broadcasted_iota(jnp.int32, (2 * SLAB, features), 1) == HD * (
                lax.broadcasted_iota(jnp.int32, (2 * SLAB, features), 0)
            )
            by_head = lax.dot_general(
                pick.astype(jnp.bfloat16),
                jnp.concatenate(shares, axis=1),
                (((1,), (1,)), ((), ())),
                preferred_element_type=jnp.float32,
            )[:SLAB]
            blank = jnp.zeros((SLAB, features - BLOCK), jnp.float32)
            out[...] = jnp.concatenate(
                [coarse[0, few, :], jnp.concatenate([by_head, blank], axis=1)], axis=0
            ).astype(jnp.bfloat16)


def rejoin_kernel(*refs):
    outs = refs[len(refs) // 3 * 2 :]
    for early, late_ref, out in zip(refs, refs[len(outs) :], outs):
        features = early.shape[1]
        late = late_ref[...].astype(jnp.float32)
        spread = lax.broadcasted_iota(jnp.int32, (SLAB, features), 1) // HD == (
            lax.broadcasted_iota(jnp.int32, (SLAB, features), 0)
        )
        signed = lax.dot_general(
            late[SLAB:, :BLOCK].astype(jnp.bfloat16),
            spread.astype(jnp.bfloat16),
            (((0,), (0,)), ((), ())),
            preferred_element_type=jnp.float32,
        )
        keep = jnp.where(signed >= 0, signed, 1.0 + signed)
        join = jnp.where(signed >= 0, 1.0 - signed, -signed)
        result = keep * early[...].astype(jnp.float32) + join * repeated(late[:SLAB])
        out[...] = result.astype(jnp.bfloat16)


def partial_kernel(own_ref, weight_ref, out_ref):
    features = own_ref.shape[1]
    start = pl.multiple_of(lax.axis_index("head") * features, features)
    out_ref[...] = jnp.dot(
        own_ref[...], weight_ref[pl.ds(start, features), :], preferred_element_type=jnp.float32
    )


def project_kernel(partial_ref, *refs):
    parts, (weight_ref, out_hbm, scratch, staged, sems) = refs[:-5], refs[-5:]
    steps = [*range(AHEAD - 1, 0, -1), *range(AHEAD, len(parts) + 1)]
    own = lax.axis_index("head")
    features = parts[0].shape[1]
    chunk = staged.shape[2]
    copies = []
    for index in range(staged.shape[0]):
        columns = pl.ds(index * chunk, chunk)
        total = partial_ref[:, columns]
        for step, part in zip(steps, parts):
            start = pl.multiple_of((own ^ step) * features, features)
            total += jnp.dot(
                part[...],
                weight_ref[pl.ds(start, features), columns],
                preferred_element_type=jnp.float32,
            )
        for half in range(chunk // PAIR):
            lanes = slice(half * PAIR, (half + 1) * PAIR)
            scratch[index, half] = total[:, lanes]
            for i in range(SLAB):
                staged[index, i * FAN : (i + 1) * FAN, lanes] = scratch[
                    index, half, pl.ds(i, FAN, stride=SLAB), :
                ].astype(jnp.bfloat16)
        copy = pltpu.make_async_copy(staged.at[index], out_hbm.at[:, columns], sems.at[index])
        copy.start()
        copies.append(copy)
    for copy in copies:
        copy.wait()


def repool_outside(field):
    which, rows, lanes = field.shape
    slabs = field.astype(jnp.float32).reshape(which, rows // (2 * SLAB), 2, SLAB, lanes)
    sums = (slabs[:, :, 0] + slabs[:, :, 1]) * root_half
    return sums.reshape(which, rows // 2, lanes).astype(jnp.bfloat16)


def swapped(block, axis, mask):
    return lax.ppermute(block, axis, [(i, i ^ mask) for i in range(lax.axis_size(axis))])


def across(block):
    count, heads = lax.axis_size("seq"), lax.axis_size("head")
    route = []
    for seq in range(count):
        end = seq in (0, count - 1)
        other = seq if end else seq + 1 if seq % 2 else seq - 1
        for head in range(heads):
            route.append((seq * heads + head, other * heads + (head ^ 1 if end else head)))
    return lax.ppermute(block, ("seq", "head"), route)


def per_device(queries, key_vectors, value_vectors, out_weight):
    rows, features = queries.shape[1:]
    key_vectors, value_vectors = [
        pltpu.with_memory_space_constraint(x, pltpu.HBM) for x in (key_vectors, value_vectors)
    ]
    pairs = features // PAIR
    seq_count, head_count = lax.axis_size("seq"), lax.axis_size("head")
    bf16 = lambda *shape: jax.ShapeDtypeStruct(shape, jnp.bfloat16)
    params = pltpu.CompilerParams(vmem_limit_bytes=32 * 1024 * 1024)

    hbm = pl.BlockSpec(memory_space=pltpu.HBM)
    vmem = pl.BlockSpec(memory_space=pltpu.VMEM)
    keys, values, first, one, two = pl.pallas_call(
        pool_kernel,
        in_specs=[hbm] * 2,
        out_shape=[
            bf16(rows, features),
            bf16(rows, features),
            bf16(2, BLOCK + rows // 4 - BLOCK // 4, features),
            bf16(2, rows // 2, features),
            bf16(2, rows // 4, features),
        ],
        scratch_shapes=[
            pltpu.VMEM((2, rows // BLOCK, pairs, BLOCK, PAIR), jnp.float32),
            pltpu.SemaphoreType.DMA((2, rows // BLOCK)),
        ],
        compiler_params=params,
        name="pool",
    )(key_vectors, value_vectors)
    second, three, four = pl.pallas_call(
        deeper_kernel,
        out_shape=[
            bf16(2, BLOCK, features),
            bf16(2, rows // 8, features),
            bf16(2, rows // 16, features),
        ],
        compiler_params=params,
        cost_estimate=pl.CostEstimate(flops=2**31, bytes_accessed=2**23, transcendentals=0),
        name="deeper",
    )(keys, values, two)

    first_in = swapped(first, "seq", 1)
    second_in = across(second)
    four_in = swapped(four, "seq", 4)
    six_in = swapped(four, "seq", 6)
    threes_in = [swapped(three, "seq", mask) for mask in (3, 2)]
    edge_q, two_q, three_q, four_q, state = pl.pallas_call(
        local_kernel,
        out_shape=[
            bf16(2, BLOCK, features),
            bf16(rows // 4, features),
            bf16(rows // 8, features),
            bf16(rows // 16, features),
            jax.ShapeDtypeStruct((3, rows, features), jnp.float32),
        ],
        scratch_shapes=[
            pltpu.VMEM((pairs, rows, PAIR), jnp.float32),
            pltpu.VMEM((pairs, rows // BLOCK, 2 * BLOCK, 3 * BLOCK), jnp.float32),
            pltpu.VMEM((pairs, rows // BLOCK // 2, 2 * BLOCK, BLOCK), jnp.float32),
        ],
        compiler_params=params,
        name="local",
    )(queries[0], keys, values, one, four_in)

    fours = pl.pallas_call(
        join_kernel,
        out_shape=bf16(2, rows // 8, features),
        compiler_params=params,
        cost_estimate=pl.CostEstimate(flops=2**29, bytes_accessed=2**20, transcendentals=0),
        name="join",
    )(four_in, six_in, four_q)
    fours_in = swapped(fours, "seq", 1)
    coarse, near = pl.pallas_call(
        coarse_kernel,
        out_shape=[
            jax.ShapeDtypeStruct((3, rows // 4, features), jnp.float32),
            bf16(2, rows // 16, features),
        ],
        scratch_shapes=[
            pltpu.VMEM((2, pairs, BLOCK, PAIR), jnp.float32),
            pltpu.VMEM((2, rows // 4, features), jnp.bfloat16),
            pltpu.VMEM((pairs, rows // 2, BLOCK), jnp.float32),
            pltpu.VMEM((pairs, rows // 4, BLOCK), jnp.float32),
        ],
        compiler_params=params,
        cost_estimate=pl.CostEstimate(flops=2**31, bytes_accessed=2**21, transcendentals=0),
        name="coarse",
    )(two_q, three_q, first_in, *threes_in)
    away = range(AHEAD, head_count)
    fine, *early = pl.pallas_call(
        mid_kernel,
        out_shape=[jax.ShapeDtypeStruct((2, rows, features), jnp.float32)]
        + [bf16(BLOCK, features) for _ in away],
        scratch_shapes=[
            pltpu.VMEM((rows // BLOCK, BLOCK, features), jnp.bfloat16),
            pltpu.VMEM((pairs, 2, 2 * BLOCK, BLOCK), jnp.float32),
        ],
        compiler_params=params,
        name="mid",
    )(edge_q, coarse, state, first_in, second_in)
    early_in = [swapped(part, "head", step) for step, part in zip(away, early)]

    far = []
    known = 8
    if known < seq_count:
        group = [four, near] + [repool_outside(field) for field in threes_in]
        group = jnp.concatenate(group + [fours, fours_in], axis=1)
        while known < seq_count:
            fresh = swapped(group, "seq", known)
            far.append(fresh)
            group = jnp.concatenate([group, fresh], axis=1)
            known *= 2

    near_parts = [bf16(BLOCK, features) for _ in range(AHEAD)]
    outs = pl.pallas_call(
        finish_kernel,
        out_shape=near_parts + [bf16(2 * SLAB, features) for _ in away],
        scratch_shapes=[
            pltpu.VMEM((2, rows // 16, features), jnp.float32),
            pltpu.VMEM((pairs, rows // 8, rows // 16 * seq_count), jnp.float32),
        ],
        compiler_params=params,
        name="finish",
    )(four_q, fine, four, near, *threes_in, fours, fours_in, *far)
    whole_in = [swapped(outs[step], "head", step) for step in range(AHEAD - 1, 0, -1)]
    late_in = [swapped(part, "head", step) for step, part in zip(away, outs[AHEAD:])]
    width = out_weight.shape[1]
    partial = pl.pallas_call(
        partial_kernel,
        out_shape=jax.ShapeDtypeStruct((BLOCK, width), jnp.float32),
        compiler_params=params,
        name="partial",
    )(outs[0], out_weight)
    rejoined = pl.pallas_call(
        rejoin_kernel,
        out_shape=[bf16(BLOCK, features) for _ in away],
        compiler_params=params,
        name="rejoin",
    )(*early_in, *late_in)
    chunk = 2 * PAIR
    result = pl.pallas_call(
        project_kernel,
        in_specs=[vmem] * (head_count + 1),
        out_specs=hbm,
        out_shape=bf16(BLOCK, width),
        scratch_shapes=[
            pltpu.VMEM((width // chunk, 2, BLOCK, PAIR), jnp.float32),
            pltpu.VMEM((width // chunk, BLOCK, chunk), jnp.bfloat16),
            pltpu.SemaphoreType.DMA((width // chunk,)),
        ],
        compiler_params=params,
        name="project",
    )(partial, *whole_in, *rejoined, out_weight)
    return result[None]


def solution(mesh):
    return jax.shard_map(
        per_device,
        mesh=mesh,
        in_specs=(P(None, "seq", "head"), P(None, "seq", "head"), P(None, "seq", "head"), P()),
        out_specs=P(None, ("seq", "head"), None),
        check_vma=False,
    )
```

```python
import jax
import jax.numpy as jnp
from jax import lax
from jax.experimental import pallas as pl
from jax.experimental.pallas import tpu as pltpu
from jax.sharding import PartitionSpec as P

HD = 64
BLOCK = 128
LEVELS = 4
SLAB = 8
PAIR = 2 * HD

neg_fill = -1e30
root_half = 0.7071067811865476
log2_e = 1.4426950408889634
log2_scale = HD**-0.5 * log2_e
least_share = 2.0**-100
AHEAD = 3

FAN = 2**LEVELS


def slabs_of(scratch, block):
    return [scratch[pl.ds(BLOCK * block + j, SLAB, stride=FAN), :] for j in range(FAN)]


def pooled_slabs(slabs):
    return [
        ((low + high) * root_half).astype(jnp.bfloat16).astype(jnp.float32)
        for low, high in zip(slabs[0::2], slabs[1::2])
    ]


def joined(slabs):
    return jnp.concatenate(slabs, axis=0).astype(jnp.bfloat16)


def spill(source, scratch):
    for half in range(scratch.shape[0]):
        scratch[half] = source[:, half * PAIR : (half + 1) * PAIR].astype(jnp.float32)


def pool_kernel(
    k_hbm, v_hbm, k_ref, v_ref, first_ref, one_ref, two_ref, scratch, sems
):
    rows = k_ref.shape[0]
    blocks = rows // BLOCK
    arrivals = []
    for half in range(2):
        here = pl.ds(half * rows // 2, rows // 2)
        for which, (source, target) in enumerate(((k_hbm, k_ref), (v_hbm, v_ref))):
            copy = pltpu.make_async_copy(
                source.at[0, here, :], target.at[here, :], sems.at[which, half]
            )
            copy.start()
            for block in range(half * blocks // 2, (half + 1) * blocks // 2):
                arrivals.append((block, which, target, copy))
    even = lax.rem(lax.axis_index("seq"), 2) == 0
    for block, which, ref, copy in arrivals:
        if block % (blocks // 2) == 0:
            copy.wait()
        here = pl.ds(block * BLOCK, BLOCK)
        spill(ref.at[here, :], scratch.at[which, block])
        for half in range(scratch.shape[2]):
            lanes = pl.ds(half * PAIR, PAIR)
            one = pooled_slabs(slabs_of(scratch.at[which, block, half], 0))
            one_ref[which, pl.ds(block * BLOCK // 2, BLOCK // 2), lanes] = joined(one)
            two_ref[which, pl.ds(block * BLOCK // 4, BLOCK // 4), lanes] = joined(pooled_slabs(one))
    inner = rows // 4 - BLOCK // 4
    for which, ref in enumerate((k_ref, v_ref)):
        first_ref[which, :BLOCK, :] = jnp.where(even, ref[rows - BLOCK :, :], ref[:BLOCK, :])
        first_ref[which, BLOCK:, :] = jnp.where(
            even, two_ref[which, :inner, :], two_ref[which, BLOCK // 4 :, :]
        )


def repooled(field):
    rows, lanes = field.shape
    slabs = field.astype(jnp.float32).reshape(rows // (2 * SLAB), 2, SLAB, lanes)
    return ((slabs[:, 0] + slabs[:, 1]) * root_half).reshape(rows // 2, lanes).astype(jnp.bfloat16)


def deeper_kernel(k_ref, v_ref, two_ref, second_ref, three_ref, four_ref):
    rows = k_ref.shape[0]
    even = lax.rem(lax.axis_index("seq"), 2) == 0
    for which, ref in enumerate((k_ref, v_ref)):
        second_ref[which] = jnp.where(even, ref[:BLOCK, :], ref[rows - BLOCK :, :])
        three = repooled(two_ref[which])
        three_ref[which] = three
        four_ref[which] = repooled(three)


def repooled(field):
    rows, lanes = field.shape
    slabs = field.astype(jnp.float32).reshape(rows // (2 * SLAB), 2, SLAB, lanes)
    return ((slabs[:, 0] + slabs[:, 1]) * root_half).reshape(rows // 2, lanes).astype(jnp.bfloat16)


def score(queries, keys, hold, is_open=None):
    rows = queries.shape[0]
    low = lax.broadcasted_iota(jnp.int32, (rows, PAIR), 1) < HD
    zero = jnp.zeros_like(queries)
    both = jnp.concatenate([jnp.where(low, queries, zero), jnp.where(low, zero, queries)], axis=0)
    raw = lax.dot_general(both, keys, (((1,), (1,)), ((), ())), preferred_element_type=jnp.float32)
    if is_open is not None:
        raw = jnp.where(is_open, raw, neg_fill)
    hold[...] = raw
    return jnp.max(raw, axis=1, keepdims=True)


def weigh(hold, top, values):
    rows = top.shape[0] // 2
    low = lax.broadcasted_iota(jnp.int32, (rows, PAIR), 1) < HD
    weights = jnp.exp2((hold[...] - top) * log2_scale).astype(jnp.bfloat16)
    result = jnp.dot(weights, values, preferred_element_type=jnp.float32)
    return (
        log2_scale * jnp.where(low, top[:rows], top[rows:]),
        jnp.where(low, result[:rows, :PAIR], result[rows:, :PAIR]),
        jnp.where(low, result[:rows, PAIR:], result[rows:, PAIR:]),
    )


def merged(fine, coarse):
    top = jnp.maximum(fine[0], coarse[0])
    keep = jnp.exp2(fine[0] - top)
    join = jnp.exp2(coarse[0] - top)
    return top, fine[1] * keep + coarse[1] * join, fine[2] * keep + coarse[2] * join


def doubled(field):
    rows, lanes = field.shape
    slabs = field.reshape(rows // SLAB, 1, SLAB, lanes)
    return jnp.broadcast_to(slabs, (rows // SLAB, 2, SLAB, lanes)).reshape(2 * rows, lanes)


def with_ones(values, weight=1.0):
    if weight != 1.0:
        values = values * jnp.bfloat16(weight)
    return jnp.concatenate([values, jnp.full(values.shape, weight, jnp.bfloat16)], axis=1)


def local_kernel(
    q_ref, k_ref, v_ref, one_ref, four_ref, edge_q, two_q, three_q, four_q, state,
    scratch, near_hold, coarse_hold,
):
    rows = q_ref.shape[0]
    blocks = rows // BLOCK
    pairs = scratch.shape[0]
    spill(q_ref, scratch)
    fine, one_q = [], []
    for pair in range(pairs):
        lanes = pl.ds(pair * PAIR, PAIR)
        ladder = [[], [], [], [], []]
        for block in range(blocks):
            slabs = slabs_of(scratch.at[pair], block)
            ladder[0].append(joined(slabs))
            for level in range(1, LEVELS + 1):
                slabs = pooled_slabs(slabs)
                ladder[level] += slabs
        edge_q[0, :, lanes] = ladder[0][0]
        edge_q[1, :, lanes] = ladder[0][-1]
        two_q[:, lanes] = joined(ladder[2])
        three_q[:, lanes] = joined(ladder[3])
        four_q[:, lanes] = joined(ladder[4])
        fine.append(ladder[0])
        one_q.append([joined(ladder[1][n : n + FAN]) for n in range(0, len(ladder[1]), FAN)])
    windows = [(max(n - 1, 0) * BLOCK, min(n + 2, blocks) * BLOCK) for n in range(blocks)]
    tops = {}
    for pair in range(pairs):
        lanes = pl.ds(pair * PAIR, PAIR)
        for half in range(blocks // 2):
            there = pl.ds((half ^ 1) * BLOCK, BLOCK)
            tops[pair, half] = score(
                one_q[pair][half], one_ref[0, there, lanes], coarse_hold.at[pair, half]
            )
            for block in (2 * half, 2 * half + 1):
                low, high = windows[block]
                hold = near_hold.at[pair, block, :, : high - low]
                tops[pair, half, block] = score(fine[pair][block], k_ref[low:high, lanes], hold)
    for pair in range(pairs):
        lanes = pl.ds(pair * PAIR, PAIR)
        for half in range(blocks // 2):
            there = pl.ds((half ^ 1) * BLOCK, BLOCK)
            coarse = weigh(
                coarse_hold.at[pair, half], tops[pair, half], with_ones(one_ref[1, there, lanes])
            )
            for block in (2 * half, 2 * half + 1):
                low, high = windows[block]
                hold = near_hold.at[pair, block, :, : high - low]
                near = weigh(hold, tops[pair, half, block], with_ones(v_ref[low:high, lanes]))
                part = slice((block - 2 * half) * BLOCK // 2, (block - 2 * half + 1) * BLOCK // 2)
                done = merged(near, [doubled(x[part]) for x in coarse])
                for index, field in enumerate(done):
                    state[index, block * BLOCK : (block + 1) * BLOCK, lanes] = field


def join_kernel(four_ref, six_ref, query_ref, out):
    sixteenth = four_ref.shape[1]
    out[:, :sixteenth, :] = four_ref[...]
    out[:, sixteenth:, :] = six_ref[...]


def coarse_kernel(
    two_q, three_q, first_ref, three_a, three_b, coarse, near_ref, scratch, two_ref, two_hold, three_hold
):
    inner = first_ref.shape[1] - BLOCK
    pairs = scratch.shape[1]
    two_ref[:, :inner, :] = first_ref[:, BLOCK:, :]
    for which in range(2):
        spill(first_ref.at[which, pl.ds(0, BLOCK), :], scratch.at[which])
        for half in range(pairs):
            lanes = pl.ds(half * PAIR, PAIR)
            slabs = slabs_of(scratch.at[which, half], 0)
            two_ref[which, inner:, lanes] = joined(pooled_slabs(pooled_slabs(slabs)))
        near_ref[which] = repooled(repooled(two_ref[which]))
    steps = {}
    for pair in range(pairs):
        lanes = pl.ds(pair * PAIR, PAIR)
        three = [
            jnp.concatenate([three_a[which, :, lanes], three_b[which, :, lanes]], axis=0)
            for which in range(2)
        ]
        steps[pair, 3] = (
            score(three_q[:, lanes], three[0], three_hold.at[pair]), with_ones(three[1])
        )
        steps[pair, 2] = (
            score(two_q[:, lanes], two_ref[0, :, lanes], two_hold.at[pair]),
            with_ones(two_ref[1, :, lanes]),
        )
    for pair in range(pairs):
        three = weigh(three_hold.at[pair], *steps[pair, 3])
        two = merged(weigh(two_hold.at[pair], *steps[pair, 2]), [doubled(x) for x in three])
        for index, field in enumerate(two):
            coarse[index, :, pl.ds(pair * PAIR, PAIR)] = field


def mid_kernel(edge_q, coarse, state, first_ref, second_ref, fine, *refs):
    outs, (ready, holds) = refs[:-2], refs[-2:]
    own = lax.axis_index("head")
    rows = state.shape[1]
    blocks = rows // BLOCK
    position = lax.axis_index("seq")
    last = lax.axis_size("seq") - 1
    even = lax.rem(position, 2) == 0
    opens = (position > 0, position < last)
    pairs = holds.shape[0]
    steps = {}
    for pair in range(pairs):
        lanes = pl.ds(pair * PAIR, PAIR)
        inner = [first_ref[which, :BLOCK, lanes] for which in range(2)]
        outer = [second_ref[which, :, lanes] for which in range(2)]
        for side in range(2):
            halo = [
                jnp.where(even, *((outer[which], inner[which])[:: 1 - 2 * side]))
                for which in range(2)
            ]
            steps[pair, side] = (
                score(edge_q[side, :, lanes], halo[0], holds.at[pair, side], opens[side]),
                with_ones(halo[1]),
            )
    for pair in range(pairs):
        lanes = pl.ds(pair * PAIR, PAIR)
        for block in range(blocks):
            here = slice(block * BLOCK, (block + 1) * BLOCK)
            quarter = slice(block * BLOCK // 4, (block + 1) * BLOCK // 4)
            done = merged(
                [state[index, here, lanes] for index in range(3)],
                [doubled(doubled(coarse[index, quarter, lanes])) for index in range(3)],
            )
            for side, edge in enumerate((0, blocks - 1)):
                if block == edge:
                    done = merged(done, weigh(holds.at[pair, side], *steps[pair, side]))
            result = done[1] / done[2]
            fine[0, here, lanes] = result
            fine[1, here, lanes] = done[0] + jnp.log(done[2]) * log2_e
            ready[block, :, lanes] = result.astype(jnp.bfloat16)
    for step, out in enumerate(outs, AHEAD):
        out[...] = ready[own ^ step]


def repeated(field):
    return jnp.concatenate([field] * FAN, axis=0)


def finish_blocks(fine, coarse, steps):
    own = lax.axis_index("head")
    features = fine.shape[2]
    for step, out in steps:
        block = own ^ step
        here = pl.ds(pl.multiple_of(block * BLOCK, BLOCK), BLOCK)
        few = pl.ds(pl.multiple_of(block * SLAB, SLAB), SLAB)
        shares = []
        for pair in range(features // PAIR):
            lanes = pl.ds(pair * PAIR, PAIR)
            fine_sum, coarse_sum = fine[1, here, lanes], repeated(coarse[1, few, lanes])
            if step < AHEAD:
                keep = 1.0 / (1.0 + jnp.exp2(coarse_sum - fine_sum))
                ours, theirs = fine[0, here, lanes], repeated(coarse[0, few, lanes])
                out[:, lanes] = (theirs + keep * (ours - theirs)).astype(jnp.bfloat16)
            else:
                ratio = jnp.exp2(-jnp.abs(fine_sum - coarse_sum))
                less = jnp.maximum(ratio / (1.0 + ratio), least_share)
                shares.append(jnp.where(fine_sum <= coarse_sum, less, -less).astype(jnp.bfloat16))
        if step >= AHEAD:
            pick = lax.broadcasted_iota(jnp.int32, (2 * SLAB, features), 1) == HD * (
                lax.broadcasted_iota(jnp.int32, (2 * SLAB, features), 0)
            )
            by_head = lax.dot_general(
                pick.astype(jnp.bfloat16),
                jnp.concatenate(shares, axis=1),
                (((1,), (1,)), ((), ())),
                preferred_element_type=jnp.float32,
            )[:SLAB]
            blank = jnp.zeros((SLAB, features - BLOCK), jnp.float32)
            out[...] = jnp.concatenate(
                [coarse[0, few, :], jnp.concatenate([by_head, blank], axis=1)], axis=0
            ).astype(jnp.bfloat16)


def finish_kernel(
    four_q, fine, four_ref, near_ref, three_a, three_b, fours_a, fours_b, *refs
):
    refs, (coarse, four_hold) = refs[:-2], refs[-2:]
    count = AHEAD - 2
    far, outs = refs[:-count], refs[-count:]
    pairs = four_q.shape[1] // PAIR
    steps = {}
    for pair in range(pairs):
        lanes = pl.ds(pair * PAIR, PAIR)
        ours, theirs, beyond = [], [], []
        for which in range(2):
            ours.append(
                [four_ref[which, :, lanes], near_ref[which, :, lanes]]
                + [repooled(field[which, :, lanes]) for field in (three_a, three_b)]
            )
            theirs.append([field[which, :, lanes] for field in (fours_a, fours_b)])
            beyond.append([field[which, :, lanes] for field in far])
        steps[pair] = (
            score(
                four_q[:, lanes],
                jnp.concatenate(ours[0] + theirs[0] + beyond[0], axis=0),
                four_hold.at[pair],
            ),
            jnp.concatenate(
                [with_ones(field) for field in ours[1]]
                + [with_ones(field, 2.0) for field in theirs[1]]
                + [with_ones(field) for field in beyond[1]],
                axis=0,
            ),
        )
    for pair in range(pairs):
        lanes = pl.ds(pair * PAIR, PAIR)
        top, numer, rowsum = weigh(four_hold.at[pair], *steps[pair])
        coarse[0, :, lanes] = numer / rowsum
        coarse[1, :, lanes] = top + jnp.log(rowsum) * log2_e
    finish_blocks(fine, coarse, zip(range(2, AHEAD), outs))


def rest_kernel(fine, coarse, *outs):
    steps = [0, 1, *range(AHEAD, lax.axis_size("head"))]
    finish_blocks(fine, coarse, zip(steps, outs))


def rejoin_kernel(*refs):
    outs = refs[len(refs) // 3 * 2 :]
    for early, late_ref, out in zip(refs, refs[len(outs) :], outs):
        features = early.shape[1]
        late = late_ref[...].astype(jnp.float32)
        spread = lax.broadcasted_iota(jnp.int32, (SLAB, features), 1) // HD == (
            lax.broadcasted_iota(jnp.int32, (SLAB, features), 0)
        )
        signed = lax.dot_general(
            late[SLAB:, :BLOCK].astype(jnp.bfloat16),
            spread.astype(jnp.bfloat16),
            (((0,), (0,)), ((), ())),
            preferred_element_type=jnp.float32,
        )
        keep = jnp.where(signed >= 0, signed, 1.0 + signed)
        join = jnp.where(signed >= 0, 1.0 - signed, -signed)
        result = keep * early[...] + join * repeated(late[:SLAB])
        out[...] = result.astype(jnp.bfloat16)


def widen_kernel(*refs):
    half = len(refs) // 2
    for ref, out in zip(refs[:half], refs[half:]):
        out[...] = ref[...].astype(jnp.float32)


def carry_kernel(whole_ref, *refs):
    half = len(refs) // 2
    for ref, out in zip(refs[:half], refs[half:]):
        out[...] = ref[...]


def partial_kernel(own_ref, weight_ref, out_ref):
    features = own_ref.shape[1]
    start = pl.multiple_of(lax.axis_index("head") * features, features)
    out_ref[...] = jnp.dot(
        own_ref[...], weight_ref[pl.ds(start, features), :], preferred_element_type=jnp.float32
    )


def project_kernel(partial_ref, *refs):
    parts, (weight_ref, out_hbm, scratch, staged, sems) = refs[:-5], refs[-5:]
    own = lax.axis_index("head")
    features = parts[0].shape[1]
    chunk = staged.shape[2]
    copies = []
    for index in range(staged.shape[0]):
        columns = pl.ds(index * chunk, chunk)
        total = partial_ref[:, columns]
        for step, part in zip([*range(2, len(parts) + 1), 1], parts):
            start = pl.multiple_of((own ^ step) * features, features)
            total += jnp.dot(
                part[...],
                weight_ref[pl.ds(start, features), columns],
                preferred_element_type=jnp.float32,
            )
        for half in range(chunk // PAIR):
            lanes = slice(half * PAIR, (half + 1) * PAIR)
            scratch[index, half] = total[:, lanes]
            for i in range(SLAB):
                staged[index, i * FAN : (i + 1) * FAN, lanes] = scratch[
                    index, half, pl.ds(i, FAN, stride=SLAB), :
                ].astype(jnp.bfloat16)
        copy = pltpu.make_async_copy(staged.at[index], out_hbm.at[:, columns], sems.at[index])
        copy.start()
        copies.append(copy)
    for copy in copies:
        copy.wait()


def repool_outside(field):
    which, rows, lanes = field.shape
    slabs = field.astype(jnp.float32).reshape(which, rows // (2 * SLAB), 2, SLAB, lanes)
    sums = (slabs[:, :, 0] + slabs[:, :, 1]) * root_half
    return sums.reshape(which, rows // 2, lanes).astype(jnp.bfloat16)


def swapped(block, axis, mask):
    return lax.ppermute(block, axis, [(i, i ^ mask) for i in range(lax.axis_size(axis))])


def across(block):
    count, heads = lax.axis_size("seq"), lax.axis_size("head")
    route = []
    for seq in range(count):
        end = seq in (0, count - 1)
        other = seq if end else seq + 1 if seq % 2 else seq - 1
        for head in range(heads):
            route.append((seq * heads + head, other * heads + (head ^ 1 if end else head)))
    return lax.ppermute(block, ("seq", "head"), route)


def per_device(queries, key_vectors, value_vectors, out_weight):
    rows, features = queries.shape[1:]
    key_vectors, value_vectors = [
        pltpu.with_memory_space_constraint(x, pltpu.HBM) for x in (key_vectors, value_vectors)
    ]
    pairs = features // PAIR
    seq_count, head_count = lax.axis_size("seq"), lax.axis_size("head")
    bf16 = lambda *shape: jax.ShapeDtypeStruct(shape, jnp.bfloat16)
    params = pltpu.CompilerParams(vmem_limit_bytes=32 * 1024 * 1024)

    hbm = pl.BlockSpec(memory_space=pltpu.HBM)
    vmem = pl.BlockSpec(memory_space=pltpu.VMEM)
    keys, values, first, one, two = pl.pallas_call(
        pool_kernel,
        in_specs=[hbm] * 2,
        out_shape=[
            bf16(rows, features),
            bf16(rows, features),
            bf16(2, BLOCK + rows // 4 - BLOCK // 4, features),
            bf16(2, rows // 2, features),
            bf16(2, rows // 4, features),
        ],
        scratch_shapes=[
            pltpu.VMEM((2, rows // BLOCK, pairs, BLOCK, PAIR), jnp.float32),
            pltpu.SemaphoreType.DMA((2, 2)),
        ],
        compiler_params=params,
        name="pool",
    )(key_vectors, value_vectors)
    second, three, four = pl.pallas_call(
        deeper_kernel,
        out_shape=[
            bf16(2, BLOCK, features),
            bf16(2, rows // 8, features),
            bf16(2, rows // 16, features),
        ],
        compiler_params=params,
        cost_estimate=pl.CostEstimate(flops=2**31, bytes_accessed=2**23, transcendentals=0),
        name="deeper",
    )(keys, values, two)

    first_in = swapped(first, "seq", 1)
    second_in = across(second)
    four_in = swapped(four, "seq", 4)
    six_in = swapped(four, "seq", 6)
    threes_in = [swapped(three, "seq", mask) for mask in (3, 2)]
    edge_q, two_q, three_q, four_q, state = pl.pallas_call(
        local_kernel,
        out_shape=[
            bf16(2, BLOCK, features),
            bf16(rows // 4, features),
            bf16(rows // 8, features),
            bf16(rows // 16, features),
            jax.ShapeDtypeStruct((3, rows, features), jnp.float32),
        ],
        scratch_shapes=[
            pltpu.VMEM((pairs, rows, PAIR), jnp.float32),
            pltpu.VMEM((pairs, rows // BLOCK, 2 * BLOCK, 3 * BLOCK), jnp.float32),
            pltpu.VMEM((pairs, rows // BLOCK // 2, 2 * BLOCK, BLOCK), jnp.float32),
        ],
        compiler_params=params,
        name="local",
    )(queries[0], keys, values, one, four_in)

    fours = pl.pallas_call(
        join_kernel,
        out_shape=bf16(2, rows // 8, features),
        compiler_params=params,
        cost_estimate=pl.CostEstimate(flops=2**29, bytes_accessed=2**20, transcendentals=0),
        name="join",
    )(four_in, six_in, four_q)
    fours_in = swapped(fours, "seq", 1)
    coarse, near = pl.pallas_call(
        coarse_kernel,
        out_shape=[
            jax.ShapeDtypeStruct((3, rows // 4, features), jnp.float32),
            bf16(2, rows // 16, features),
        ],
        scratch_shapes=[
            pltpu.VMEM((2, pairs, BLOCK, PAIR), jnp.float32),
            pltpu.VMEM((2, rows // 4, features), jnp.bfloat16),
            pltpu.VMEM((pairs, rows // 2, BLOCK), jnp.float32),
            pltpu.VMEM((pairs, rows // 4, BLOCK), jnp.float32),
        ],
        compiler_params=params,
        cost_estimate=pl.CostEstimate(flops=2**31, bytes_accessed=2**21, transcendentals=0),
        name="coarse",
    )(two_q, three_q, first_in, *threes_in)
    away = range(AHEAD, head_count)
    fine, *early = pl.pallas_call(
        mid_kernel,
        out_shape=[jax.ShapeDtypeStruct((2, rows, features), jnp.float32)]
        + [bf16(BLOCK, features) for _ in away],
        scratch_shapes=[
            pltpu.VMEM((rows // BLOCK, BLOCK, features), jnp.bfloat16),
            pltpu.VMEM((pairs, 2, 2 * BLOCK, BLOCK), jnp.float32),
        ],
        compiler_params=params,
        name="mid",
    )(edge_q, coarse, state, first_in, second_in)
    early_in = [swapped(part, "head", step) for step, part in zip(away, early)]

    far = []
    known = 8
    if known < seq_count:
        group = [four, near] + [repool_outside(field) for field in threes_in]
        group = jnp.concatenate(group + [fours, fours_in], axis=1)
        while known < seq_count:
            fresh = swapped(group, "seq", known)
            far.append(fresh)
            group = jnp.concatenate([group, fresh], axis=1)
            known *= 2

    parts = [bf16(BLOCK, features) for _ in range(AHEAD)]
    *outs, level_four = pl.pallas_call(
        finish_kernel,
        out_shape=parts[2:] + [jax.ShapeDtypeStruct((2, rows // 16, features), jnp.float32)],
        scratch_shapes=[pltpu.VMEM((pairs, rows // 8, rows // 16 * seq_count), jnp.float32)],
        compiler_params=params,
        name="finish",
    )(four_q, fine, four, near, *threes_in, fours, fours_in, *far)
    whole_in = [swapped(part, "head", step) for step, part in enumerate(outs, 2)]
    own_part, next_part, *late = pl.pallas_call(
        rest_kernel,
        out_shape=parts[:2] + [bf16(2 * SLAB, features) for _ in away],
        compiler_params=params,
        name="rest",
    )(fine, level_four)
    next_in = swapped(next_part, "head", 1)
    late_in = [swapped(part, "head", step) for step, part in zip(away, late)]
    width = out_weight.shape[1]
    partial = pl.pallas_call(
        partial_kernel,
        out_shape=jax.ShapeDtypeStruct((BLOCK, width), jnp.float32),
        compiler_params=params,
        name="partial",
    )(own_part, out_weight)
    heavy = pl.CostEstimate(flops=2**32, bytes_accessed=2**20, transcendentals=0)
    widened = pl.pallas_call(
        widen_kernel,
        out_shape=[jax.ShapeDtypeStruct((BLOCK, features), jnp.float32) for _ in away],
        compiler_params=params,
        cost_estimate=pl.CostEstimate(flops=2**28, bytes_accessed=2**18, transcendentals=0),
        name="widen",
    )(*early_in)
    widened = pl.pallas_call(
        carry_kernel,
        out_shape=[jax.ShapeDtypeStruct((BLOCK, features), jnp.float32) for _ in away],
        compiler_params=params,
        name="carry",
    )(whole_in[0], *widened)
    rejoined = pl.pallas_call(
        rejoin_kernel,
        out_shape=[bf16(BLOCK, features) for _ in away],
        compiler_params=params,
        cost_estimate=heavy,
        name="rejoin",
    )(*widened, *late_in)
    chunk = 2 * PAIR
    result = pl.pallas_call(
        project_kernel,
        in_specs=[vmem] * (head_count + 1),
        out_specs=hbm,
        out_shape=bf16(BLOCK, width),
        scratch_shapes=[
            pltpu.VMEM((width // chunk, 2, BLOCK, PAIR), jnp.float32),
            pltpu.VMEM((width // chunk, BLOCK, chunk), jnp.bfloat16),
            pltpu.SemaphoreType.DMA((width // chunk,)),
        ],
        compiler_params=params,
        name="project",
    )(partial, *whole_in, *rejoined, next_in, out_weight)
    return result[None]


def solution(mesh):
    return jax.shard_map(
        per_device,
        mesh=mesh,
        in_specs=(P(None, "seq", "head"), P(None, "seq", "head"), P(None, "seq", "head"), P()),
        out_specs=P(None, ("seq", "head"), None),
        check_vma=False,
    )
```

```python
import jax
import jax.numpy as jnp
from jax import lax
from jax.experimental import pallas as pl
from jax.experimental.pallas import tpu as pltpu
from jax.sharding import PartitionSpec as P

HD = 64
BLOCK = 128
LEVELS = 4
SLAB = 8
PAIR = 2 * HD

neg_fill = -1e30
root_half = 0.7071067811865476
log2_e = 1.4426950408889634
log2_scale = HD**-0.5 * log2_e
least_share = 2.0**-100
AHEAD = 3

FAN = 2**LEVELS


def slabs_of(scratch, block):
    return [scratch[pl.ds(BLOCK * block + j, SLAB, stride=FAN), :] for j in range(FAN)]


def pooled_slabs(slabs):
    return [
        ((low + high) * root_half).astype(jnp.bfloat16).astype(jnp.float32)
        for low, high in zip(slabs[0::2], slabs[1::2])
    ]


def joined(slabs):
    return jnp.concatenate(slabs, axis=0).astype(jnp.bfloat16)


def spill(source, scratch):
    for half in range(scratch.shape[0]):
        scratch[half] = source[:, half * PAIR : (half + 1) * PAIR].astype(jnp.float32)


def pool_kernel(
    k_hbm, v_hbm, q_hbm, k_ref, v_ref, q_ref, first_ref, one_ref, two_ref, scratch, sems
):
    rows = k_ref.shape[0]
    blocks = rows // BLOCK
    arrivals = []
    for which, (source, target) in enumerate(((k_hbm, k_ref), (v_hbm, v_ref), (q_hbm, q_ref))):
        copy = pltpu.make_async_copy(source.at[0], target, sems.at[which])
        copy.start()
        arrivals.append((target, copy))
    even = lax.rem(lax.axis_index("seq"), 2) == 0
    inner = rows // 4 - BLOCK // 4
    for which, (ref, copy) in enumerate(arrivals[:2]):
        copy.wait()
        for block in range(blocks):
            spill(ref.at[pl.ds(block * BLOCK, BLOCK), :], scratch.at[which, block])
            for half in range(scratch.shape[2]):
                lanes = pl.ds(half * PAIR, PAIR)
                one = pooled_slabs(slabs_of(scratch.at[which, block, half], 0))
                one_ref[which, pl.ds(block * BLOCK // 2, BLOCK // 2), lanes] = joined(one)
                two = joined(pooled_slabs(one))
                two_ref[which, pl.ds(block * BLOCK // 4, BLOCK // 4), lanes] = two
        first_ref[which, :BLOCK, :] = jnp.where(even, ref[rows - BLOCK :, :], ref[:BLOCK, :])
        first_ref[which, BLOCK : BLOCK + inner, :] = jnp.where(
            even, two_ref[which, :inner, :], two_ref[which, BLOCK // 4 :, :]
        )
    arrivals[2][1].wait()
    for block in range(blocks):
        spill(q_ref.at[pl.ds(block * BLOCK, BLOCK), :], scratch.at[2, block])
    for half in range(scratch.shape[2]):
        lanes = pl.ds(half * PAIR, PAIR)
        four = []
        for block in range(blocks):
            slabs = slabs_of(scratch.at[2, block, half], 0)
            for _ in range(LEVELS):
                slabs = pooled_slabs(slabs)
            four += slabs
        for which in range(2):
            part = four[which * blocks // 2 : (which + 1) * blocks // 2]
            first_ref[which, BLOCK + inner :, lanes] = joined(part)


def repooled(field):
    rows, lanes = field.shape
    slabs = field.astype(jnp.float32).reshape(rows // (2 * SLAB), 2, SLAB, lanes)
    return ((slabs[:, 0] + slabs[:, 1]) * root_half).reshape(rows // 2, lanes).astype(jnp.bfloat16)


def deeper_kernel(k_ref, v_ref, two_ref, second_ref, three_ref, four_ref):
    rows = k_ref.shape[0]
    even = lax.rem(lax.axis_index("seq"), 2) == 0
    for which, ref in enumerate((k_ref, v_ref)):
        second_ref[which] = jnp.where(even, ref[:BLOCK, :], ref[rows - BLOCK :, :])
        three = repooled(two_ref[which])
        three_ref[which] = three
        four_ref[which] = repooled(three)


def repooled(field):
    rows, lanes = field.shape
    slabs = field.astype(jnp.float32).reshape(rows // (2 * SLAB), 2, SLAB, lanes)
    return ((slabs[:, 0] + slabs[:, 1]) * root_half).reshape(rows // 2, lanes).astype(jnp.bfloat16)


def score(queries, keys, hold, is_open=None):
    rows = queries.shape[0]
    low = lax.broadcasted_iota(jnp.int32, (rows, PAIR), 1) < HD
    zero = jnp.zeros_like(queries)
    both = jnp.concatenate([jnp.where(low, queries, zero), jnp.where(low, zero, queries)], axis=0)
    raw = lax.dot_general(both, keys, (((1,), (1,)), ((), ())), preferred_element_type=jnp.float32)
    if is_open is not None:
        raw = jnp.where(is_open, raw, neg_fill)
    hold[...] = raw
    return jnp.max(raw, axis=1, keepdims=True)


def weigh(hold, top, values):
    rows = top.shape[0] // 2
    low = lax.broadcasted_iota(jnp.int32, (rows, PAIR), 1) < HD
    weights = jnp.exp2((hold[...] - top) * log2_scale).astype(jnp.bfloat16)
    result = jnp.dot(weights, values, preferred_element_type=jnp.float32)
    return (
        log2_scale * jnp.where(low, top[:rows], top[rows:]),
        jnp.where(low, result[:rows, :PAIR], result[rows:, :PAIR]),
        jnp.where(low, result[:rows, PAIR:], result[rows:, PAIR:]),
    )


def merged(fine, coarse):
    top = jnp.maximum(fine[0], coarse[0])
    keep = jnp.exp2(fine[0] - top)
    join = jnp.exp2(coarse[0] - top)
    return top, fine[1] * keep + coarse[1] * join, fine[2] * keep + coarse[2] * join


def doubled(field):
    rows, lanes = field.shape
    slabs = field.reshape(rows // SLAB, 1, SLAB, lanes)
    return jnp.broadcast_to(slabs, (rows // SLAB, 2, SLAB, lanes)).reshape(2 * rows, lanes)


def with_ones(values, weight=1.0):
    if weight != 1.0:
        values = values * jnp.bfloat16(weight)
    return jnp.concatenate([values, jnp.full(values.shape, weight, jnp.bfloat16)], axis=1)


def local_kernel(
    q_ref, k_ref, v_ref, one_ref, four_ref, edge_q, two_q, three_q, four_q, state,
    scratch, near_hold, coarse_hold,
):
    rows = q_ref.shape[0]
    blocks = rows // BLOCK
    pairs = scratch.shape[0]
    spill(q_ref, scratch)
    fine, one_q = [], []
    for pair in range(pairs):
        lanes = pl.ds(pair * PAIR, PAIR)
        ladder = [[], [], [], [], []]
        for block in range(blocks):
            slabs = slabs_of(scratch.at[pair], block)
            ladder[0].append(joined(slabs))
            for level in range(1, LEVELS + 1):
                slabs = pooled_slabs(slabs)
                ladder[level] += slabs
        edge_q[0, :, lanes] = ladder[0][0]
        edge_q[1, :, lanes] = ladder[0][-1]
        two_q[:, lanes] = joined(ladder[2])
        three_q[:, lanes] = joined(ladder[3])
        four_q[:, lanes] = joined(ladder[4])
        fine.append(ladder[0])
        one_q.append([joined(ladder[1][n : n + FAN]) for n in range(0, len(ladder[1]), FAN)])
    windows = [(max(n - 1, 0) * BLOCK, min(n + 2, blocks) * BLOCK) for n in range(blocks)]
    tops = {}
    for pair in range(pairs):
        lanes = pl.ds(pair * PAIR, PAIR)
        for half in range(blocks // 2):
            there = pl.ds((half ^ 1) * BLOCK, BLOCK)
            tops[pair, half] = score(
                one_q[pair][half], one_ref[0, there, lanes], coarse_hold.at[pair, half]
            )
            for block in (2 * half, 2 * half + 1):
                low, high = windows[block]
                hold = near_hold.at[pair, block, :, : high - low]
                tops[pair, half, block] = score(fine[pair][block], k_ref[low:high, lanes], hold)
    for pair in range(pairs):
        lanes = pl.ds(pair * PAIR, PAIR)
        for half in range(blocks // 2):
            there = pl.ds((half ^ 1) * BLOCK, BLOCK)
            coarse = weigh(
                coarse_hold.at[pair, half], tops[pair, half], with_ones(one_ref[1, there, lanes])
            )
            for block in (2 * half, 2 * half + 1):
                low, high = windows[block]
                hold = near_hold.at[pair, block, :, : high - low]
                near = weigh(hold, tops[pair, half, block], with_ones(v_ref[low:high, lanes]))
                part = slice((block - 2 * half) * BLOCK // 2, (block - 2 * half + 1) * BLOCK // 2)
                done = merged(near, [doubled(x[part]) for x in coarse])
                for index, field in enumerate(done):
                    state[index, block * BLOCK : (block + 1) * BLOCK, lanes] = field


def by_head(rows, features, shift=0):
    lane = lax.broadcasted_iota(jnp.int32, (rows, features), 1)
    row = lax.broadcasted_iota(jnp.int32, (rows, features), 0)
    return (lane == HD * (row - shift)).astype(jnp.bfloat16)


def answer_kernel(first_ref, four_ref, six_ref, query_ref, out, hold):
    rows, features = four_ref.shape[1:]
    heads = features // HD
    asked = first_ref.shape[1] - rows // 2
    sums = []
    for pair in range(features // PAIR):
        lanes = pl.ds(pair * PAIR, PAIR)
        queries = jnp.concatenate([first_ref[half, asked:, lanes] for half in range(2)], axis=0)
        keys = jnp.concatenate([four_ref[0, :, lanes], six_ref[0, :, lanes]], axis=0)
        values = jnp.concatenate(
            [with_ones(field[1, :, lanes], 2.0) for field in (four_ref, six_ref)], axis=0
        )
        top = score(queries, keys, hold.at[pair])
        top, numer, rowsum = weigh(hold.at[pair], top, values)
        out[:rows, lanes] = (numer / rowsum).astype(jnp.bfloat16)
        sums.append(top + jnp.log(rowsum) * log2_e)
    rest = jnp.concatenate(sums, axis=1)
    held = jnp.zeros((out.shape[0] - rows, rows), jnp.float32)
    for part in range(3):
        piece = rest.astype(jnp.bfloat16)
        rest = rest - piece.astype(jnp.float32)
        held = held + lax.dot_general(
            by_head(held.shape[0], features, part * heads),
            piece,
            (((1,), (1,)), ((), ())),
            preferred_element_type=jnp.float32,
        )
    blank = jnp.zeros((held.shape[0], features - rows), jnp.float32)
    out[rows:, :] = jnp.concatenate([held, blank], axis=1).astype(jnp.bfloat16)


def coarse_kernel(
    two_q, three_q, first_ref, three_a, three_b, coarse, near_ref, scratch, two_ref, two_hold, three_hold
):
    inner = two_ref.shape[1] - BLOCK // 4
    pairs = scratch.shape[1]
    two_ref[:, :inner, :] = first_ref[:, BLOCK : BLOCK + inner, :]
    for which in range(2):
        spill(first_ref.at[which, pl.ds(0, BLOCK), :], scratch.at[which])
        for half in range(pairs):
            lanes = pl.ds(half * PAIR, PAIR)
            slabs = slabs_of(scratch.at[which, half], 0)
            two_ref[which, inner:, lanes] = joined(pooled_slabs(pooled_slabs(slabs)))
        near_ref[which] = repooled(repooled(two_ref[which]))
    steps = {}
    for pair in range(pairs):
        lanes = pl.ds(pair * PAIR, PAIR)
        three = [
            jnp.concatenate([three_a[which, :, lanes], three_b[which, :, lanes]], axis=0)
            for which in range(2)
        ]
        steps[pair, 3] = (
            score(three_q[:, lanes], three[0], three_hold.at[pair]), with_ones(three[1])
        )
        steps[pair, 2] = (
            score(two_q[:, lanes], two_ref[0, :, lanes], two_hold.at[pair]),
            with_ones(two_ref[1, :, lanes]),
        )
    for pair in range(pairs):
        three = weigh(three_hold.at[pair], *steps[pair, 3])
        two = merged(weigh(two_hold.at[pair], *steps[pair, 2]), [doubled(x) for x in three])
        for index, field in enumerate(two):
            coarse[index, :, pl.ds(pair * PAIR, PAIR)] = field


def mid_kernel(edge_q, coarse, state, first_ref, second_ref, fine, *refs):
    outs, (ready, holds) = refs[:-2], refs[-2:]
    own = lax.axis_index("head")
    rows = state.shape[1]
    blocks = rows // BLOCK
    position = lax.axis_index("seq")
    last = lax.axis_size("seq") - 1
    even = lax.rem(position, 2) == 0
    opens = (position > 0, position < last)
    pairs = holds.shape[0]
    steps = {}
    for pair in range(pairs):
        lanes = pl.ds(pair * PAIR, PAIR)
        inner = [first_ref[which, :BLOCK, lanes] for which in range(2)]
        outer = [second_ref[which, :, lanes] for which in range(2)]
        for side in range(2):
            halo = [
                jnp.where(even, *((outer[which], inner[which])[:: 1 - 2 * side]))
                for which in range(2)
            ]
            steps[pair, side] = (
                score(edge_q[side, :, lanes], halo[0], holds.at[pair, side], opens[side]),
                with_ones(halo[1]),
            )
    for pair in range(pairs):
        lanes = pl.ds(pair * PAIR, PAIR)
        for block in range(blocks):
            here = slice(block * BLOCK, (block + 1) * BLOCK)
            quarter = slice(block * BLOCK // 4, (block + 1) * BLOCK // 4)
            done = merged(
                [state[index, here, lanes] for index in range(3)],
                [doubled(doubled(coarse[index, quarter, lanes])) for index in range(3)],
            )
            for side, edge in enumerate((0, blocks - 1)):
                if block == edge:
                    done = merged(done, weigh(holds.at[pair, side], *steps[pair, side]))
            result = done[1] / done[2]
            fine[0, here, lanes] = result
            fine[1, here, lanes] = done[0] + jnp.log(done[2]) * log2_e
            ready[block, :, lanes] = result.astype(jnp.bfloat16)
    for step, out in enumerate(outs, AHEAD):
        out[...] = ready[own ^ step]


def repeated(field):
    return jnp.concatenate([field] * FAN, axis=0)


def finish_blocks(fine, coarse, steps):
    own = lax.axis_index("head")
    features = fine.shape[2]
    for step, out in steps:
        block = own ^ step
        here = pl.ds(pl.multiple_of(block * BLOCK, BLOCK), BLOCK)
        few = pl.ds(pl.multiple_of(block * SLAB, SLAB), SLAB)
        shares = []
        for pair in range(features // PAIR):
            lanes = pl.ds(pair * PAIR, PAIR)
            fine_sum, coarse_sum = fine[1, here, lanes], repeated(coarse[1, few, lanes])
            if step < AHEAD:
                keep = 1.0 / (1.0 + jnp.exp2(coarse_sum - fine_sum))
                ours, theirs = fine[0, here, lanes], repeated(coarse[0, few, lanes])
                out[:, lanes] = (theirs + keep * (ours - theirs)).astype(jnp.bfloat16)
            else:
                ratio = jnp.exp2(-jnp.abs(fine_sum - coarse_sum))
                less = jnp.maximum(ratio / (1.0 + ratio), least_share)
                shares.append(jnp.where(fine_sum <= coarse_sum, less, -less).astype(jnp.bfloat16))
        if step >= AHEAD:
            shared = lax.dot_general(
                by_head(2 * SLAB, features),
                jnp.concatenate(shares, axis=1),
                (((1,), (1,)), ((), ())),
                preferred_element_type=jnp.float32,
            )[:SLAB]
            blank = jnp.zeros((SLAB, features - BLOCK), jnp.float32)
            out[...] = jnp.concatenate(
                [coarse[0, few, :], jnp.concatenate([shared, blank], axis=1)], axis=0
            ).astype(jnp.bfloat16)


def known_kernel(four_q, four_ref, near_ref, three_a, three_b, fours_a, fours_b, *refs):
    far, (known, four_hold) = refs[:-2], refs[-2:]
    pairs = four_q.shape[1] // PAIR
    steps = {}
    for pair in range(pairs):
        lanes = pl.ds(pair * PAIR, PAIR)
        ours, theirs, beyond = [], [], []
        for which in range(2):
            ours.append(
                [four_ref[which, :, lanes], near_ref[which, :, lanes]]
                + [repooled(field[which, :, lanes]) for field in (three_a, three_b)]
            )
            theirs.append([field[which, :, lanes] for field in (fours_a, fours_b)])
            beyond.append([field[which, :, lanes] for field in far])
        steps[pair] = (
            score(
                four_q[:, lanes],
                jnp.concatenate(ours[0] + theirs[0] + beyond[0], axis=0),
                four_hold.at[pair],
            ),
            jnp.concatenate(
                [with_ones(field) for field in ours[1]]
                + [with_ones(field, 2.0) for field in theirs[1]]
                + [with_ones(field) for field in beyond[1]],
                axis=0,
            ),
        )
    for pair in range(pairs):
        lanes = pl.ds(pair * PAIR, PAIR)
        top, numer, rowsum = weigh(four_hold.at[pair], *steps[pair])
        known[0, :, lanes] = numer / rowsum
        known[1, :, lanes] = top + jnp.log(rowsum) * log2_e


def decode_kernel(answer_ref, known, out):
    rows, features = out.shape[1:]
    heads = features // HD
    held = answer_ref[rows:, :BLOCK]
    row = lax.broadcasted_iota(jnp.int32, (held.shape[0], features), 0)
    head = lax.broadcasted_iota(jnp.int32, (held.shape[0], features), 1) // HD
    spread = (row == head) | (row == head + heads) | (row == head + 2 * heads)
    answered = lax.dot_general(
        held, spread.astype(jnp.bfloat16), (((0,), (0,)), ((), ())), preferred_element_type=jnp.float32
    )
    answer, their_sum = answer_ref[:rows, :].astype(jnp.float32), answered[:rows]
    top = jnp.maximum(known[1], their_sum)
    ours, theirs = jnp.exp2(known[1] - top), jnp.exp2(their_sum - top)
    total = ours + theirs
    out[0] = (ours * known[0] + theirs * answer) / total
    out[1] = top + jnp.log(total) * log2_e


def finish_kernel(fine, coarse, *outs):
    finish_blocks(fine, coarse, zip(range(2, AHEAD), outs))


def rest_kernel(fine, coarse, *outs):
    steps = [0, 1, *range(AHEAD, lax.axis_size("head"))]
    finish_blocks(fine, coarse, zip(steps, outs))


def rejoin_kernel(*refs):
    outs = refs[len(refs) // 3 * 2 :]
    for early, late_ref, out in zip(refs, refs[len(outs) :], outs):
        features = early.shape[1]
        late = late_ref[...].astype(jnp.float32)
        spread = lax.broadcasted_iota(jnp.int32, (SLAB, features), 1) // HD == (
            lax.broadcasted_iota(jnp.int32, (SLAB, features), 0)
        )
        signed = lax.dot_general(
            late[SLAB:, :BLOCK].astype(jnp.bfloat16),
            spread.astype(jnp.bfloat16),
            (((0,), (0,)), ((), ())),
            preferred_element_type=jnp.float32,
        )
        keep = jnp.where(signed >= 0, signed, 1.0 + signed)
        join = jnp.where(signed >= 0, 1.0 - signed, -signed)
        result = keep * early[...] + join * repeated(late[:SLAB])
        out[...] = result.astype(jnp.bfloat16)


def widen_kernel(*refs):
    half = len(refs) // 2
    for ref, out in zip(refs[:half], refs[half:]):
        out[...] = ref[...].astype(jnp.float32)


def carry_kernel(whole_ref, *refs):
    half = len(refs) // 2
    for ref, out in zip(refs[:half], refs[half:]):
        out[...] = ref[...]


def partial_kernel(own_ref, weight_ref, out_ref):
    features = own_ref.shape[1]
    start = pl.multiple_of(lax.axis_index("head") * features, features)
    out_ref[...] = jnp.dot(
        own_ref[...], weight_ref[pl.ds(start, features), :], preferred_element_type=jnp.float32
    )


def project_kernel(partial_ref, *refs):
    parts, (weight_ref, out_hbm, scratch, staged, sems) = refs[:-5], refs[-5:]
    own = lax.axis_index("head")
    features = parts[0].shape[1]
    chunk = staged.shape[2]
    copies = []
    for index in range(staged.shape[0]):
        columns = pl.ds(index * chunk, chunk)
        total = partial_ref[:, columns]
        for step, part in zip([*range(2, len(parts) + 1), 1], parts):
            start = pl.multiple_of((own ^ step) * features, features)
            total += jnp.dot(
                part[...],
                weight_ref[pl.ds(start, features), columns],
                preferred_element_type=jnp.float32,
            )
        for half in range(chunk // PAIR):
            lanes = slice(half * PAIR, (half + 1) * PAIR)
            scratch[index, half] = total[:, lanes]
            for i in range(SLAB):
                staged[index, i * FAN : (i + 1) * FAN, lanes] = scratch[
                    index, half, pl.ds(i, FAN, stride=SLAB), :
                ].astype(jnp.bfloat16)
        copy = pltpu.make_async_copy(staged.at[index], out_hbm.at[:, columns], sems.at[index])
        copy.start()
        copies.append(copy)
    for copy in copies:
        copy.wait()


def repool_outside(field):
    which, rows, lanes = field.shape
    slabs = field.astype(jnp.float32).reshape(which, rows // (2 * SLAB), 2, SLAB, lanes)
    sums = (slabs[:, :, 0] + slabs[:, :, 1]) * root_half
    return sums.reshape(which, rows // 2, lanes).astype(jnp.bfloat16)


def swapped(block, axis, mask):
    return lax.ppermute(block, axis, [(i, i ^ mask) for i in range(lax.axis_size(axis))])


def across(block):
    count, heads = lax.axis_size("seq"), lax.axis_size("head")
    route = []
    for seq in range(count):
        end = seq in (0, count - 1)
        other = seq if end else seq + 1 if seq % 2 else seq - 1
        for head in range(heads):
            route.append((seq * heads + head, other * heads + (head ^ 1 if end else head)))
    return lax.ppermute(block, ("seq", "head"), route)


def per_device(queries, key_vectors, value_vectors, out_weight):
    rows, features = queries.shape[1:]
    queries, key_vectors, value_vectors = [
        pltpu.with_memory_space_constraint(x, pltpu.HBM)
        for x in (queries, key_vectors, value_vectors)
    ]
    pairs = features // PAIR
    seq_count, head_count = lax.axis_size("seq"), lax.axis_size("head")
    bf16 = lambda *shape: jax.ShapeDtypeStruct(shape, jnp.bfloat16)
    params = pltpu.CompilerParams(vmem_limit_bytes=32 * 1024 * 1024)

    hbm = pl.BlockSpec(memory_space=pltpu.HBM)
    vmem = pl.BlockSpec(memory_space=pltpu.VMEM)
    keys, values, ours, first, one, two = pl.pallas_call(
        pool_kernel,
        in_specs=[hbm] * 3,
        out_shape=[
            bf16(rows, features),
            bf16(rows, features),
            bf16(rows, features),
            bf16(2, BLOCK + rows // 4 - BLOCK // 4 + rows // 32, features),
            bf16(2, rows // 2, features),
            bf16(2, rows // 4, features),
        ],
        scratch_shapes=[
            pltpu.VMEM((3, rows // BLOCK, pairs, BLOCK, PAIR), jnp.float32),
            pltpu.SemaphoreType.DMA((3,)),
        ],
        compiler_params=params,
        name="pool",
    )(key_vectors, value_vectors, queries)
    second, three, four = pl.pallas_call(
        deeper_kernel,
        out_shape=[
            bf16(2, BLOCK, features),
            bf16(2, rows // 8, features),
            bf16(2, rows // 16, features),
        ],
        compiler_params=params,
        cost_estimate=pl.CostEstimate(flops=2**31, bytes_accessed=2**23, transcendentals=0),
        name="deeper",
    )(keys, values, two)

    first_in = swapped(first, "seq", 1)
    second_in = across(second)
    four_in = swapped(four, "seq", 4)
    six_in = swapped(four, "seq", 6)
    threes_in = [swapped(three, "seq", mask) for mask in (2, 3)]
    edge_q, two_q, three_q, four_q, state = pl.pallas_call(
        local_kernel,
        out_shape=[
            bf16(2, BLOCK, features),
            bf16(rows // 4, features),
            bf16(rows // 8, features),
            bf16(rows // 16, features),
            jax.ShapeDtypeStruct((3, rows, features), jnp.float32),
        ],
        scratch_shapes=[
            pltpu.VMEM((pairs, rows, PAIR), jnp.float32),
            pltpu.VMEM((pairs, rows // BLOCK, 2 * BLOCK, 3 * BLOCK), jnp.float32),
            pltpu.VMEM((pairs, rows // BLOCK // 2, 2 * BLOCK, BLOCK), jnp.float32),
        ],
        compiler_params=params,
        name="local",
    )(ours, keys, values, one, four_in)

    answer = pl.pallas_call(
        answer_kernel,
        out_shape=bf16(rows // 16 + 2 * SLAB, features),
        scratch_shapes=[pltpu.VMEM((pairs, rows // 8, rows // 8), jnp.float32)],
        compiler_params=params,
        cost_estimate=pl.CostEstimate(flops=2**29, bytes_accessed=2**20, transcendentals=0),
        name="answer",
    )(first_in, four_in, six_in, four_q)
    answer_in = swapped(answer, "seq", 1)
    coarse, near = pl.pallas_call(
        coarse_kernel,
        out_shape=[
            jax.ShapeDtypeStruct((3, rows // 4, features), jnp.float32),
            bf16(2, rows // 16, features),
        ],
        scratch_shapes=[
            pltpu.VMEM((2, pairs, BLOCK, PAIR), jnp.float32),
            pltpu.VMEM((2, rows // 4, features), jnp.bfloat16),
            pltpu.VMEM((pairs, rows // 2, BLOCK), jnp.float32),
            pltpu.VMEM((pairs, rows // 4, BLOCK), jnp.float32),
        ],
        compiler_params=params,
        cost_estimate=pl.CostEstimate(flops=2**31, bytes_accessed=2**21, transcendentals=0),
        name="coarse",
    )(two_q, three_q, first_in, *threes_in)
    away = range(AHEAD, head_count)
    fine, *early = pl.pallas_call(
        mid_kernel,
        out_shape=[jax.ShapeDtypeStruct((2, rows, features), jnp.float32)]
        + [bf16(BLOCK, features) for _ in away],
        scratch_shapes=[
            pltpu.VMEM((rows // BLOCK, BLOCK, features), jnp.bfloat16),
            pltpu.VMEM((pairs, 2, 2 * BLOCK, BLOCK), jnp.float32),
        ],
        compiler_params=params,
        name="mid",
    )(edge_q, coarse, state, first_in, second_in)
    early_in = [swapped(part, "head", step) for step, part in zip(away, early)]

    far = []
    reach = 8
    if reach < seq_count:
        group = [four, near] + [repool_outside(field) for field in threes_in]
        fours = jnp.concatenate([four_in, six_in], axis=1)
        group = jnp.concatenate(group + [fours, swapped(fours, "seq", 1)], axis=1)
        while reach < seq_count:
            fresh = swapped(group, "seq", reach)
            far.append(fresh)
            group = jnp.concatenate([group, fresh], axis=1)
            reach *= 2

    parts = [bf16(BLOCK, features) for _ in range(AHEAD)]
    heavy = pl.CostEstimate(flops=2**32, bytes_accessed=2**20, transcendentals=0)
    sums = jax.ShapeDtypeStruct((2, rows // 16, features), jnp.float32)
    known = pl.pallas_call(
        known_kernel,
        out_shape=sums,
        scratch_shapes=[pltpu.VMEM((pairs, rows // 8, rows // 16 * (seq_count - 2)), jnp.float32)],
        compiler_params=params,
        name="known",
    )(four_q, four, near, *threes_in, four_in, six_in, *far)
    level_four = pl.pallas_call(
        decode_kernel,
        out_shape=sums,
        compiler_params=params,
        cost_estimate=heavy,
        name="decode",
    )(answer_in, known)
    outs = pl.pallas_call(
        finish_kernel,
        out_shape=parts[2:],
        compiler_params=params,
        name="finish",
    )(fine, level_four)
    whole_in = [swapped(part, "head", step) for step, part in enumerate(outs, 2)]
    own_part, next_part, *late = pl.pallas_call(
        rest_kernel,
        out_shape=parts[:2] + [bf16(2 * SLAB, features) for _ in away],
        compiler_params=params,
        name="rest",
    )(fine, level_four)
    next_in = swapped(next_part, "head", 1)
    late_in = [swapped(part, "head", step) for step, part in zip(away, late)]
    width = out_weight.shape[1]
    partial = pl.pallas_call(
        partial_kernel,
        out_shape=jax.ShapeDtypeStruct((BLOCK, width), jnp.float32),
        compiler_params=params,
        name="partial",
    )(own_part, out_weight)
    widened = pl.pallas_call(
        widen_kernel,
        out_shape=[jax.ShapeDtypeStruct((BLOCK, features), jnp.float32) for _ in away],
        compiler_params=params,
        cost_estimate=pl.CostEstimate(flops=2**28, bytes_accessed=2**18, transcendentals=0),
        name="widen",
    )(*early_in)
    widened = pl.pallas_call(
        carry_kernel,
        out_shape=[jax.ShapeDtypeStruct((BLOCK, features), jnp.float32) for _ in away],
        compiler_params=params,
        name="carry",
    )(whole_in[0], *widened)
    rejoined = pl.pallas_call(
        rejoin_kernel,
        out_shape=[bf16(BLOCK, features) for _ in away],
        compiler_params=params,
        cost_estimate=heavy,
        name="rejoin",
    )(*widened, *late_in)
    chunk = 2 * PAIR
    result = pl.pallas_call(
        project_kernel,
        in_specs=[vmem] * (head_count + 1),
        out_specs=hbm,
        out_shape=bf16(BLOCK, width),
        scratch_shapes=[
            pltpu.VMEM((width // chunk, 2, BLOCK, PAIR), jnp.float32),
            pltpu.VMEM((width // chunk, BLOCK, chunk), jnp.bfloat16),
            pltpu.SemaphoreType.DMA((width // chunk,)),
        ],
        compiler_params=params,
        name="project",
    )(partial, *whole_in, *rejoined, next_in, out_weight)
    return result[None]


def solution(mesh):
    return jax.shard_map(
        per_device,
        mesh=mesh,
        in_specs=(P(None, "seq", "head"), P(None, "seq", "head"), P(None, "seq", "head"), P()),
        out_specs=P(None, ("seq", "head"), None),
        check_vma=False,
    )
```

```python
import jax
import jax.numpy as jnp
from jax import lax
from jax.experimental import pallas as pl
from jax.experimental.pallas import tpu as pltpu
from jax.sharding import PartitionSpec as P

HD = 64
BLOCK = 128
LEVELS = 4
SLAB = 8
PAIR = 2 * HD

neg_fill = -1e30
root_half = 0.7071067811865476
log2_e = 1.4426950408889634
log2_scale = HD**-0.5 * log2_e
least_share = 2.0**-100
AHEAD = 3

FAN = 2**LEVELS


def slabs_of(scratch, block):
    return [scratch[pl.ds(BLOCK * block + j, SLAB, stride=FAN), :] for j in range(FAN)]


def pooled_slabs(slabs):
    return [
        ((low + high) * root_half).astype(jnp.bfloat16).astype(jnp.float32)
        for low, high in zip(slabs[0::2], slabs[1::2])
    ]


def joined(slabs):
    return jnp.concatenate(slabs, axis=0).astype(jnp.bfloat16)


def spill(source, scratch):
    for half in range(scratch.shape[0]):
        scratch[half] = source[:, half * PAIR : (half + 1) * PAIR].astype(jnp.float32)


def pool_kernel(
    k_hbm, v_hbm, k_ref, v_ref, first_ref, one_ref, two_ref, scratch, sems
):
    rows = k_ref.shape[0]
    blocks = rows // BLOCK
    arrivals = []
    for half in range(2):
        here = pl.ds(half * rows // 2, rows // 2)
        for which, (source, target) in enumerate(((k_hbm, k_ref), (v_hbm, v_ref))):
            copy = pltpu.make_async_copy(
                source.at[0, here, :], target.at[here, :], sems.at[which, half]
            )
            copy.start()
            for block in range(half * blocks // 2, (half + 1) * blocks // 2):
                arrivals.append((block, which, target, copy))
    even = lax.rem(lax.axis_index("seq"), 2) == 0
    for block, which, ref, copy in arrivals:
        if block % (blocks // 2) == 0:
            copy.wait()
        here = pl.ds(block * BLOCK, BLOCK)
        spill(ref.at[here, :], scratch.at[which, block])
        for half in range(scratch.shape[2]):
            lanes = pl.ds(half * PAIR, PAIR)
            one = pooled_slabs(slabs_of(scratch.at[which, block, half], 0))
            one_ref[which, pl.ds(block * BLOCK // 2, BLOCK // 2), lanes] = joined(one)
            two_ref[which, pl.ds(block * BLOCK // 4, BLOCK // 4), lanes] = joined(pooled_slabs(one))
    inner = rows // 4 - BLOCK // 4
    for which, ref in enumerate((k_ref, v_ref)):
        first_ref[which, :BLOCK, :] = jnp.where(even, ref[rows - BLOCK :, :], ref[:BLOCK, :])
        first_ref[which, BLOCK:, :] = jnp.where(
            even, two_ref[which, :inner, :], two_ref[which, BLOCK // 4 :, :]
        )


def repooled(field):
    rows, lanes = field.shape
    slabs = field.astype(jnp.float32).reshape(rows // (2 * SLAB), 2, SLAB, lanes)
    return ((slabs[:, 0] + slabs[:, 1]) * root_half).reshape(rows // 2, lanes).astype(jnp.bfloat16)


def deeper_kernel(k_ref, v_ref, two_ref, second_ref, three_ref, four_ref):
    rows = k_ref.shape[0]
    even = lax.rem(lax.axis_index("seq"), 2) == 0
    for which, ref in enumerate((k_ref, v_ref)):
        second_ref[which] = jnp.where(even, ref[:BLOCK, :], ref[rows - BLOCK :, :])
        three = repooled(two_ref[which])
        three_ref[which] = three
        four_ref[which] = repooled(three)


def repooled(field):
    rows, lanes = field.shape
    slabs = field.astype(jnp.float32).reshape(rows // (2 * SLAB), 2, SLAB, lanes)
    return ((slabs[:, 0] + slabs[:, 1]) * root_half).reshape(rows // 2, lanes).astype(jnp.bfloat16)


def score(queries, keys, hold, is_open=None):
    rows = queries.shape[0]
    low = lax.broadcasted_iota(jnp.int32, (rows, PAIR), 1) < HD
    zero = jnp.zeros_like(queries)
    both = jnp.concatenate([jnp.where(low, queries, zero), jnp.where(low, zero, queries)], axis=0)
    raw = lax.dot_general(both, keys, (((1,), (1,)), ((), ())), preferred_element_type=jnp.float32)
    if is_open is not None:
        raw = jnp.where(is_open, raw, neg_fill)
    hold[...] = raw
    return jnp.max(raw, axis=1, keepdims=True)


def weigh(hold, top, values):
    rows = top.shape[0] // 2
    low = lax.broadcasted_iota(jnp.int32, (rows, PAIR), 1) < HD
    weights = jnp.exp2((hold[...] - top) * log2_scale).astype(jnp.bfloat16)
    result = jnp.dot(weights, values, preferred_element_type=jnp.float32)
    return (
        log2_scale * jnp.where(low, top[:rows], top[rows:]),
        jnp.where(low, result[:rows, :PAIR], result[rows:, :PAIR]),
        jnp.where(low, result[:rows, PAIR:], result[rows:, PAIR:]),
    )


def merged(fine, coarse):
    top = jnp.maximum(fine[0], coarse[0])
    keep = jnp.exp2(fine[0] - top)
    join = jnp.exp2(coarse[0] - top)
    return top, fine[1] * keep + coarse[1] * join, fine[2] * keep + coarse[2] * join


def doubled(field):
    rows, lanes = field.shape
    slabs = field.reshape(rows // SLAB, 1, SLAB, lanes)
    return jnp.broadcast_to(slabs, (rows // SLAB, 2, SLAB, lanes)).reshape(2 * rows, lanes)


def with_ones(values, weight=1.0):
    if weight != 1.0:
        values = values * jnp.bfloat16(weight)
    return jnp.concatenate([values, jnp.full(values.shape, weight, jnp.bfloat16)], axis=1)


def local_kernel(
    q_ref, k_ref, v_ref, one_ref, four_ref, edge_q, two_q, three_q, four_q, state,
    scratch, near_hold, coarse_hold,
):
    rows = q_ref.shape[0]
    blocks = rows // BLOCK
    pairs = scratch.shape[0]
    spill(q_ref, scratch)
    fine, one_q = [], []
    for pair in range(pairs):
        lanes = pl.ds(pair * PAIR, PAIR)
        ladder = [[], [], [], [], []]
        for block in range(blocks):
            slabs = slabs_of(scratch.at[pair], block)
            ladder[0].append(joined(slabs))
            for level in range(1, LEVELS + 1):
                slabs = pooled_slabs(slabs)
                ladder[level] += slabs
        edge_q[0, :, lanes] = ladder[0][0]
        edge_q[1, :, lanes] = ladder[0][-1]
        two_q[:, lanes] = joined(ladder[2])
        three_q[:, lanes] = joined(ladder[3])
        four_q[:, lanes] = joined(ladder[4])
        fine.append(ladder[0])
        one_q.append([joined(ladder[1][n : n + FAN]) for n in range(0, len(ladder[1]), FAN)])
    windows = [(max(n - 1, 0) * BLOCK, min(n + 2, blocks) * BLOCK) for n in range(blocks)]
    tops = {}
    for pair in range(pairs):
        lanes = pl.ds(pair * PAIR, PAIR)
        for half in range(blocks // 2):
            there = pl.ds((half ^ 1) * BLOCK, BLOCK)
            tops[pair, half] = score(
                one_q[pair][half], one_ref[0, there, lanes], coarse_hold.at[pair, half]
            )
            for block in (2 * half, 2 * half + 1):
                low, high = windows[block]
                hold = near_hold.at[pair, block, :, : high - low]
                tops[pair, half, block] = score(fine[pair][block], k_ref[low:high, lanes], hold)
    for pair in range(pairs):
        lanes = pl.ds(pair * PAIR, PAIR)
        for half in range(blocks // 2):
            there = pl.ds((half ^ 1) * BLOCK, BLOCK)
            coarse = weigh(
                coarse_hold.at[pair, half], tops[pair, half], with_ones(one_ref[1, there, lanes])
            )
            for block in (2 * half, 2 * half + 1):
                low, high = windows[block]
                hold = near_hold.at[pair, block, :, : high - low]
                near = weigh(hold, tops[pair, half, block], with_ones(v_ref[low:high, lanes]))
                part = slice((block - 2 * half) * BLOCK // 2, (block - 2 * half + 1) * BLOCK // 2)
                done = merged(near, [doubled(x[part]) for x in coarse])
                for index, field in enumerate(done):
                    state[index, block * BLOCK : (block + 1) * BLOCK, lanes] = field


def join_kernel(four_ref, six_ref, query_ref, out):
    sixteenth = four_ref.shape[1]
    out[:, :sixteenth, :] = four_ref[...]
    out[:, sixteenth:, :] = six_ref[...]


def coarse_kernel(
    two_q, three_q, first_ref, three_a, three_b, coarse, near_ref, scratch, two_ref, two_hold, three_hold
):
    inner = first_ref.shape[1] - BLOCK
    pairs = scratch.shape[1]
    two_ref[:, :inner, :] = first_ref[:, BLOCK:, :]
    for which in range(2):
        spill(first_ref.at[which, pl.ds(0, BLOCK), :], scratch.at[which])
        for half in range(pairs):
            lanes = pl.ds(half * PAIR, PAIR)
            slabs = slabs_of(scratch.at[which, half], 0)
            two_ref[which, inner:, lanes] = joined(pooled_slabs(pooled_slabs(slabs)))
        near_ref[which] = repooled(repooled(two_ref[which]))
    steps = {}
    for pair in range(pairs):
        lanes = pl.ds(pair * PAIR, PAIR)
        three = [
            jnp.concatenate([three_a[which, :, lanes], three_b[which, :, lanes]], axis=0)
            for which in range(2)
        ]
        steps[pair, 3] = (
            score(three_q[:, lanes], three[0], three_hold.at[pair]), with_ones(three[1])
        )
        steps[pair, 2] = (
            score(two_q[:, lanes], two_ref[0, :, lanes], two_hold.at[pair]),
            with_ones(two_ref[1, :, lanes]),
        )
    for pair in range(pairs):
        three = weigh(three_hold.at[pair], *steps[pair, 3])
        two = merged(weigh(two_hold.at[pair], *steps[pair, 2]), [doubled(x) for x in three])
        for index, field in enumerate(two):
            coarse[index, :, pl.ds(pair * PAIR, PAIR)] = field


def mid_kernel(edge_q, coarse, state, first_ref, second_ref, fine, *refs):
    outs, (ready, holds) = refs[:-2], refs[-2:]
    own = lax.axis_index("head")
    rows = state.shape[1]
    blocks = rows // BLOCK
    position = lax.axis_index("seq")
    last = lax.axis_size("seq") - 1
    even = lax.rem(position, 2) == 0
    opens = (position > 0, position < last)
    pairs = holds.shape[0]
    steps = {}
    for pair in range(pairs):
        lanes = pl.ds(pair * PAIR, PAIR)
        inner = [first_ref[which, :BLOCK, lanes] for which in range(2)]
        outer = [second_ref[which, :, lanes] for which in range(2)]
        for side in range(2):
            halo = [
                jnp.where(even, *((outer[which], inner[which])[:: 1 - 2 * side]))
                for which in range(2)
            ]
            steps[pair, side] = (
                score(edge_q[side, :, lanes], halo[0], holds.at[pair, side], opens[side]),
                with_ones(halo[1]),
            )
    for pair in range(pairs):
        lanes = pl.ds(pair * PAIR, PAIR)
        for block in range(blocks):
            here = slice(block * BLOCK, (block + 1) * BLOCK)
            quarter = slice(block * BLOCK // 4, (block + 1) * BLOCK // 4)
            done = merged(
                [state[index, here, lanes] for index in range(3)],
                [doubled(doubled(coarse[index, quarter, lanes])) for index in range(3)],
            )
            for side, edge in enumerate((0, blocks - 1)):
                if block == edge:
                    done = merged(done, weigh(holds.at[pair, side], *steps[pair, side]))
            result = done[1] / done[2]
            fine[0, here, lanes] = result
            fine[1, here, lanes] = done[0] + jnp.log(done[2]) * log2_e
            ready[block, :, lanes] = result.astype(jnp.bfloat16)
    for step, out in enumerate(outs, AHEAD):
        out[...] = ready[own ^ step]


def repeated(field):
    return jnp.concatenate([field] * FAN, axis=0)


def finish_blocks(fine, coarse, steps):
    own = lax.axis_index("head")
    features = fine.shape[2]
    for step, out in steps:
        block = own ^ step
        here = pl.ds(pl.multiple_of(block * BLOCK, BLOCK), BLOCK)
        few = pl.ds(pl.multiple_of(block * SLAB, SLAB), SLAB)
        shares = []
        for pair in range(features // PAIR):
            lanes = pl.ds(pair * PAIR, PAIR)
            fine_sum, coarse_sum = fine[1, here, lanes], repeated(coarse[1, few, lanes])
            if step < AHEAD:
                keep = 1.0 / (1.0 + jnp.exp2(coarse_sum - fine_sum))
                ours, theirs = fine[0, here, lanes], repeated(coarse[0, few, lanes])
                out[:, lanes] = (theirs + keep * (ours - theirs)).astype(jnp.bfloat16)
            else:
                ratio = jnp.exp2(-jnp.abs(fine_sum - coarse_sum))
                less = jnp.maximum(ratio / (1.0 + ratio), least_share)
                shares.append(jnp.where(fine_sum <= coarse_sum, less, -less).astype(jnp.bfloat16))
        if step >= AHEAD:
            pick = lax.broadcasted_iota(jnp.int32, (2 * SLAB, features), 1) == HD * (
                lax.broadcasted_iota(jnp.int32, (2 * SLAB, features), 0)
            )
            by_head = lax.dot_general(
                pick.astype(jnp.bfloat16),
                jnp.concatenate(shares, axis=1),
                (((1,), (1,)), ((), ())),
                preferred_element_type=jnp.float32,
            )[:SLAB]
            blank = jnp.zeros((SLAB, features - BLOCK), jnp.float32)
            out[...] = jnp.concatenate(
                [coarse[0, few, :], jnp.concatenate([by_head, blank], axis=1)], axis=0
            ).astype(jnp.bfloat16)


def finish_kernel(
    four_q, fine, four_ref, near_ref, three_a, three_b, fours_a, fours_b, *refs
):
    refs, (coarse, four_hold) = refs[:-2], refs[-2:]
    steps_out = range(2, lax.axis_size("head"))
    far, outs = refs[: -len(steps_out)], refs[-len(steps_out) :]
    pairs = four_q.shape[1] // PAIR
    steps = {}
    for pair in range(pairs):
        lanes = pl.ds(pair * PAIR, PAIR)
        ours, theirs, beyond = [], [], []
        for which in range(2):
            ours.append(
                [four_ref[which, :, lanes], near_ref[which, :, lanes]]
                + [repooled(field[which, :, lanes]) for field in (three_a, three_b)]
            )
            theirs.append([field[which, :, lanes] for field in (fours_a, fours_b)])
            beyond.append([field[which, :, lanes] for field in far])
        steps[pair] = (
            score(
                four_q[:, lanes],
                jnp.concatenate(ours[0] + theirs[0] + beyond[0], axis=0),
                four_hold.at[pair],
            ),
            jnp.concatenate(
                [with_ones(field) for field in ours[1]]
                + [with_ones(field, 2.0) for field in theirs[1]]
                + [with_ones(field) for field in beyond[1]],
                axis=0,
            ),
        )
    for pair in range(pairs):
        lanes = pl.ds(pair * PAIR, PAIR)
        top, numer, rowsum = weigh(four_hold.at[pair], *steps[pair])
        coarse[0, :, lanes] = numer / rowsum
        coarse[1, :, lanes] = top + jnp.log(rowsum) * log2_e
    finish_blocks(fine, coarse, zip(steps_out, outs))


def rest_kernel(fine, coarse, *outs):
    finish_blocks(fine, coarse, enumerate(outs))


def rejoin_kernel(*refs):
    outs = refs[len(refs) // 3 * 2 :]
    for early, late_ref, out in zip(refs, refs[len(outs) :], outs):
        features = early.shape[1]
        late = late_ref[...].astype(jnp.float32)
        spread = lax.broadcasted_iota(jnp.int32, (SLAB, features), 1) // HD == (
            lax.broadcasted_iota(jnp.int32, (SLAB, features), 0)
        )
        signed = lax.dot_general(
            late[SLAB:, :BLOCK].astype(jnp.bfloat16),
            spread.astype(jnp.bfloat16),
            (((0,), (0,)), ((), ())),
            preferred_element_type=jnp.float32,
        )
        keep = jnp.where(signed >= 0, signed, 1.0 + signed)
        join = jnp.where(signed >= 0, 1.0 - signed, -signed)
        result = keep * early[...] + join * repeated(late[:SLAB])
        out[...] = result.astype(jnp.bfloat16)


def widen_kernel(*refs):
    half = len(refs) // 2
    for ref, out in zip(refs[:half], refs[half:]):
        out[...] = ref[...].astype(jnp.float32)


def carry_kernel(whole_ref, *refs):
    half = len(refs) // 2
    for ref, out in zip(refs[:half], refs[half:]):
        out[...] = ref[...]


def partial_kernel(own_ref, weight_ref, out_ref):
    features = own_ref.shape[1]
    start = pl.multiple_of(lax.axis_index("head") * features, features)
    out_ref[...] = jnp.dot(
        own_ref[...], weight_ref[pl.ds(start, features), :], preferred_element_type=jnp.float32
    )


def project_kernel(partial_ref, *refs):
    parts, (weight_ref, out_hbm, scratch, staged, sems) = refs[:-5], refs[-5:]
    own = lax.axis_index("head")
    features = parts[0].shape[1]
    chunk = staged.shape[2]
    copies = []
    for index in range(staged.shape[0]):
        columns = pl.ds(index * chunk, chunk)
        total = partial_ref[:, columns]
        for step, part in zip([*range(2, len(parts) + 1), 1], parts):
            start = pl.multiple_of((own ^ step) * features, features)
            total += jnp.dot(
                part[...],
                weight_ref[pl.ds(start, features), columns],
                preferred_element_type=jnp.float32,
            )
        for half in range(chunk // PAIR):
            lanes = slice(half * PAIR, (half + 1) * PAIR)
            scratch[index, half] = total[:, lanes]
            for i in range(SLAB):
                staged[index, i * FAN : (i + 1) * FAN, lanes] = scratch[
                    index, half, pl.ds(i, FAN, stride=SLAB), :
                ].astype(jnp.bfloat16)
        copy = pltpu.make_async_copy(staged.at[index], out_hbm.at[:, columns], sems.at[index])
        copy.start()
        copies.append(copy)
    for copy in copies:
        copy.wait()


def repool_outside(field):
    which, rows, lanes = field.shape
    slabs = field.astype(jnp.float32).reshape(which, rows // (2 * SLAB), 2, SLAB, lanes)
    sums = (slabs[:, :, 0] + slabs[:, :, 1]) * root_half
    return sums.reshape(which, rows // 2, lanes).astype(jnp.bfloat16)


def swapped(block, axis, mask):
    return lax.ppermute(block, axis, [(i, i ^ mask) for i in range(lax.axis_size(axis))])


def across(block):
    count, heads = lax.axis_size("seq"), lax.axis_size("head")
    route = []
    for seq in range(count):
        end = seq in (0, count - 1)
        other = seq if end else seq + 1 if seq % 2 else seq - 1
        for head in range(heads):
            route.append((seq * heads + head, other * heads + (head ^ 1 if end else head)))
    return lax.ppermute(block, ("seq", "head"), route)


def per_device(queries, key_vectors, value_vectors, out_weight):
    rows, features = queries.shape[1:]
    key_vectors, value_vectors = [
        pltpu.with_memory_space_constraint(x, pltpu.HBM) for x in (key_vectors, value_vectors)
    ]
    pairs = features // PAIR
    seq_count, head_count = lax.axis_size("seq"), lax.axis_size("head")
    bf16 = lambda *shape: jax.ShapeDtypeStruct(shape, jnp.bfloat16)
    params = pltpu.CompilerParams(vmem_limit_bytes=32 * 1024 * 1024)

    hbm = pl.BlockSpec(memory_space=pltpu.HBM)
    vmem = pl.BlockSpec(memory_space=pltpu.VMEM)
    keys, values, first, one, two = pl.pallas_call(
        pool_kernel,
        in_specs=[hbm] * 2,
        out_shape=[
            bf16(rows, features),
            bf16(rows, features),
            bf16(2, BLOCK + rows // 4 - BLOCK // 4, features),
            bf16(2, rows // 2, features),
            bf16(2, rows // 4, features),
        ],
        scratch_shapes=[
            pltpu.VMEM((2, rows // BLOCK, pairs, BLOCK, PAIR), jnp.float32),
            pltpu.SemaphoreType.DMA((2, 2)),
        ],
        compiler_params=params,
        name="pool",
    )(key_vectors, value_vectors)
    second, three, four = pl.pallas_call(
        deeper_kernel,
        out_shape=[
            bf16(2, BLOCK, features),
            bf16(2, rows // 8, features),
            bf16(2, rows // 16, features),
        ],
        compiler_params=params,
        cost_estimate=pl.CostEstimate(flops=2**31, bytes_accessed=2**23, transcendentals=0),
        name="deeper",
    )(keys, values, two)

    first_in = swapped(first, "seq", 1)
    second_in = across(second)
    four_in = swapped(four, "seq", 4)
    six_in = swapped(four, "seq", 6)
    threes_in = [swapped(three, "seq", mask) for mask in (3, 2)]
    edge_q, two_q, three_q, four_q, state = pl.pallas_call(
        local_kernel,
        out_shape=[
            bf16(2, BLOCK, features),
            bf16(rows // 4, features),
            bf16(rows // 8, features),
            bf16(rows // 16, features),
            jax.ShapeDtypeStruct((3, rows, features), jnp.float32),
        ],
        scratch_shapes=[
            pltpu.VMEM((pairs, rows, PAIR), jnp.float32),
            pltpu.VMEM((pairs, rows // BLOCK, 2 * BLOCK, 3 * BLOCK), jnp.float32),
            pltpu.VMEM((pairs, rows // BLOCK // 2, 2 * BLOCK, BLOCK), jnp.float32),
        ],
        compiler_params=params,
        name="local",
    )(queries[0], keys, values, one, four_in)

    fours = pl.pallas_call(
        join_kernel,
        out_shape=bf16(2, rows // 8, features),
        compiler_params=params,
        cost_estimate=pl.CostEstimate(flops=2**29, bytes_accessed=2**20, transcendentals=0),
        name="join",
    )(four_in, six_in, four_q)
    fours_in = swapped(fours, "seq", 1)
    coarse, near = pl.pallas_call(
        coarse_kernel,
        out_shape=[
            jax.ShapeDtypeStruct((3, rows // 4, features), jnp.float32),
            bf16(2, rows // 16, features),
        ],
        scratch_shapes=[
            pltpu.VMEM((2, pairs, BLOCK, PAIR), jnp.float32),
            pltpu.VMEM((2, rows // 4, features), jnp.bfloat16),
            pltpu.VMEM((pairs, rows // 2, BLOCK), jnp.float32),
            pltpu.VMEM((pairs, rows // 4, BLOCK), jnp.float32),
        ],
        compiler_params=params,
        cost_estimate=pl.CostEstimate(flops=2**31, bytes_accessed=2**21, transcendentals=0),
        name="coarse",
    )(two_q, three_q, first_in, *threes_in)
    away = range(AHEAD, head_count)
    fine, *early = pl.pallas_call(
        mid_kernel,
        out_shape=[jax.ShapeDtypeStruct((2, rows, features), jnp.float32)]
        + [bf16(BLOCK, features) for _ in away],
        scratch_shapes=[
            pltpu.VMEM((rows // BLOCK, BLOCK, features), jnp.bfloat16),
            pltpu.VMEM((pairs, 2, 2 * BLOCK, BLOCK), jnp.float32),
        ],
        compiler_params=params,
        name="mid",
    )(edge_q, coarse, state, first_in, second_in)
    early_in = [swapped(part, "head", step) for step, part in zip(away, early)]

    far = []
    known = 8
    if known < seq_count:
        group = [four, near] + [repool_outside(field) for field in threes_in]
        group = jnp.concatenate(group + [fours, fours_in], axis=1)
        while known < seq_count:
            fresh = swapped(group, "seq", known)
            far.append(fresh)
            group = jnp.concatenate([group, fresh], axis=1)
            known *= 2

    parts = [bf16(BLOCK, features) for _ in range(AHEAD)]
    *outs, level_four = pl.pallas_call(
        finish_kernel,
        out_shape=parts[2:]
        + [bf16(2 * SLAB, features) for _ in away]
        + [jax.ShapeDtypeStruct((2, rows // 16, features), jnp.float32)],
        scratch_shapes=[pltpu.VMEM((pairs, rows // 8, rows // 16 * seq_count), jnp.float32)],
        compiler_params=params,
        name="finish",
    )(four_q, fine, four, near, *threes_in, fours, fours_in, *far)
    whole_in = [swapped(part, "head", step) for step, part in zip(range(2, AHEAD), outs)]
    late_in = [swapped(part, "head", step) for step, part in zip(away, outs[AHEAD - 2 :])]
    own_part, next_part = pl.pallas_call(
        rest_kernel,
        out_shape=parts[:2],
        compiler_params=params,
        name="rest",
    )(fine, level_four)
    next_in = swapped(next_part, "head", 1)
    width = out_weight.shape[1]
    partial = pl.pallas_call(
        partial_kernel,
        out_shape=jax.ShapeDtypeStruct((BLOCK, width), jnp.float32),
        compiler_params=params,
        name="partial",
    )(own_part, out_weight)
    heavy = pl.CostEstimate(flops=2**32, bytes_accessed=2**20, transcendentals=0)
    widened = pl.pallas_call(
        widen_kernel,
        out_shape=[jax.ShapeDtypeStruct((BLOCK, features), jnp.float32) for _ in away],
        compiler_params=params,
        cost_estimate=pl.CostEstimate(flops=2**22, bytes_accessed=2**10, transcendentals=0),
        name="widen",
    )(*early_in)
    widened = pl.pallas_call(
        carry_kernel,
        out_shape=[jax.ShapeDtypeStruct((BLOCK, features), jnp.float32) for _ in away],
        compiler_params=params,
        name="carry",
    )(whole_in[0], *widened)
    rejoined = pl.pallas_call(
        rejoin_kernel,
        out_shape=[bf16(BLOCK, features) for _ in away],
        compiler_params=params,
        cost_estimate=heavy,
        name="rejoin",
    )(*widened, *late_in)
    chunk = 2 * PAIR
    result = pl.pallas_call(
        project_kernel,
        in_specs=[vmem] * (head_count + 1),
        out_specs=hbm,
        out_shape=bf16(BLOCK, width),
        scratch_shapes=[
            pltpu.VMEM((width // chunk, 2, BLOCK, PAIR), jnp.float32),
            pltpu.VMEM((width // chunk, BLOCK, chunk), jnp.bfloat16),
            pltpu.SemaphoreType.DMA((width // chunk,)),
        ],
        compiler_params=params,
        name="project",
    )(partial, *whole_in, *rejoined, next_in, out_weight)
    return result[None]


def solution(mesh):
    return jax.shard_map(
        per_device,
        mesh=mesh,
        in_specs=(P(None, "seq", "head"), P(None, "seq", "head"), P(None, "seq", "head"), P()),
        out_specs=P(None, ("seq", "head"), None),
        check_vma=False,
    )
```

```python
import jax
import jax.numpy as jnp
from jax import lax
from jax.experimental import pallas as pl
from jax.experimental.pallas import tpu as pltpu
from jax.sharding import PartitionSpec as P

HD = 64
BLOCK = 128
LEVELS = 4
SLAB = 8
PAIR = 2 * HD

neg_fill = -1e30
root_half = 0.7071067811865476
log2_e = 1.4426950408889634
log2_scale = HD**-0.5 * log2_e
least_share = 2.0**-100
AHEAD = 3

FAN = 2**LEVELS


def slabs_of(scratch, block):
    return [scratch[pl.ds(BLOCK * block + j, SLAB, stride=FAN), :] for j in range(FAN)]


def pooled_slabs(slabs):
    return [
        ((low + high) * root_half).astype(jnp.bfloat16).astype(jnp.float32)
        for low, high in zip(slabs[0::2], slabs[1::2])
    ]


def joined(slabs):
    return jnp.concatenate(slabs, axis=0).astype(jnp.bfloat16)


def spill(source, scratch):
    for half in range(scratch.shape[0]):
        scratch[half] = source[:, half * PAIR : (half + 1) * PAIR].astype(jnp.float32)


def pool_kernel(
    k_hbm, v_hbm, k_ref, v_ref, first_ref, one_ref, two_ref, scratch, sems
):
    rows = k_ref.shape[0]
    blocks = rows // BLOCK
    arrivals = []
    for half in range(2):
        here = pl.ds(half * rows // 2, rows // 2)
        for which, (source, target) in enumerate(((k_hbm, k_ref), (v_hbm, v_ref))):
            copy = pltpu.make_async_copy(
                source.at[0, here, :], target.at[here, :], sems.at[which, half]
            )
            copy.start()
            for block in range(half * blocks // 2, (half + 1) * blocks // 2):
                arrivals.append((block, which, target, copy))
    even = lax.rem(lax.axis_index("seq"), 2) == 0
    for block, which, ref, copy in arrivals:
        if block % (blocks // 2) == 0:
            copy.wait()
        here = pl.ds(block * BLOCK, BLOCK)
        spill(ref.at[here, :], scratch.at[which, block])
        for half in range(scratch.shape[2]):
            lanes = pl.ds(half * PAIR, PAIR)
            one = pooled_slabs(slabs_of(scratch.at[which, block, half], 0))
            one_ref[which, pl.ds(block * BLOCK // 2, BLOCK // 2), lanes] = joined(one)
            two_ref[which, pl.ds(block * BLOCK // 4, BLOCK // 4), lanes] = joined(pooled_slabs(one))
    inner = rows // 4 - BLOCK // 4
    for which, ref in enumerate((k_ref, v_ref)):
        first_ref[which, :BLOCK, :] = jnp.where(even, ref[rows - BLOCK :, :], ref[:BLOCK, :])
        first_ref[which, BLOCK:, :] = jnp.where(
            even, two_ref[which, :inner, :], two_ref[which, BLOCK // 4 :, :]
        )


def repooled(field):
    rows, lanes = field.shape
    slabs = field.astype(jnp.float32).reshape(rows // (2 * SLAB), 2, SLAB, lanes)
    return ((slabs[:, 0] + slabs[:, 1]) * root_half).reshape(rows // 2, lanes).astype(jnp.bfloat16)


def deeper_kernel(k_ref, v_ref, two_ref, second_ref, three_ref, four_ref):
    rows = k_ref.shape[0]
    even = lax.rem(lax.axis_index("seq"), 2) == 0
    for which, ref in enumerate((k_ref, v_ref)):
        second_ref[which] = jnp.where(even, ref[:BLOCK, :], ref[rows - BLOCK :, :])
        three = repooled(two_ref[which])
        three_ref[which] = three
        four_ref[which] = repooled(three)


def repooled(field):
    rows, lanes = field.shape
    slabs = field.astype(jnp.float32).reshape(rows // (2 * SLAB), 2, SLAB, lanes)
    return ((slabs[:, 0] + slabs[:, 1]) * root_half).reshape(rows // 2, lanes).astype(jnp.bfloat16)


def score(queries, keys, hold, is_open=None):
    rows = queries.shape[0]
    low = lax.broadcasted_iota(jnp.int32, (rows, PAIR), 1) < HD
    zero = jnp.zeros_like(queries)
    both = jnp.concatenate([jnp.where(low, queries, zero), jnp.where(low, zero, queries)], axis=0)
    raw = lax.dot_general(both, keys, (((1,), (1,)), ((), ())), preferred_element_type=jnp.float32)
    if is_open is not None:
        raw = jnp.where(is_open, raw, neg_fill)
    hold[...] = raw
    return jnp.max(raw, axis=1, keepdims=True)


def weigh(hold, top, values):
    rows = top.shape[0] // 2
    low = lax.broadcasted_iota(jnp.int32, (rows, PAIR), 1) < HD
    weights = jnp.exp2((hold[...] - top) * log2_scale).astype(jnp.bfloat16)
    result = jnp.dot(weights, values, preferred_element_type=jnp.float32)
    return (
        log2_scale * jnp.where(low, top[:rows], top[rows:]),
        jnp.where(low, result[:rows, :PAIR], result[rows:, :PAIR]),
        jnp.where(low, result[:rows, PAIR:], result[rows:, PAIR:]),
    )


def merged(fine, coarse):
    top = jnp.maximum(fine[0], coarse[0])
    keep = jnp.exp2(fine[0] - top)
    join = jnp.exp2(coarse[0] - top)
    return top, fine[1] * keep + coarse[1] * join, fine[2] * keep + coarse[2] * join


def doubled(field):
    rows, lanes = field.shape
    slabs = field.reshape(rows // SLAB, 1, SLAB, lanes)
    return jnp.broadcast_to(slabs, (rows // SLAB, 2, SLAB, lanes)).reshape(2 * rows, lanes)


def with_ones(values, weight=1.0):
    if weight != 1.0:
        values = values * jnp.bfloat16(weight)
    return jnp.concatenate([values, jnp.full(values.shape, weight, jnp.bfloat16)], axis=1)


def local_kernel(
    q_ref, k_ref, v_ref, one_ref, four_ref, edge_q, two_q, three_q, four_q, state,
    scratch, near_hold, coarse_hold,
):
    rows = q_ref.shape[0]
    blocks = rows // BLOCK
    pairs = scratch.shape[0]
    spill(q_ref, scratch)
    fine, one_q = [], []
    for pair in range(pairs):
        lanes = pl.ds(pair * PAIR, PAIR)
        ladder = [[], [], [], [], []]
        for block in range(blocks):
            slabs = slabs_of(scratch.at[pair], block)
            ladder[0].append(joined(slabs))
            for level in range(1, LEVELS + 1):
                slabs = pooled_slabs(slabs)
                ladder[level] += slabs
        edge_q[0, :, lanes] = ladder[0][0]
        edge_q[1, :, lanes] = ladder[0][-1]
        two_q[:, lanes] = joined(ladder[2])
        three_q[:, lanes] = joined(ladder[3])
        four_q[:, lanes] = joined(ladder[4])
        fine.append(ladder[0])
        one_q.append([joined(ladder[1][n : n + FAN]) for n in range(0, len(ladder[1]), FAN)])
    windows = [(max(n - 1, 0) * BLOCK, min(n + 2, blocks) * BLOCK) for n in range(blocks)]
    tops = {}
    for pair in range(pairs):
        lanes = pl.ds(pair * PAIR, PAIR)
        for half in range(blocks // 2):
            there = pl.ds((half ^ 1) * BLOCK, BLOCK)
            tops[pair, half] = score(
                one_q[pair][half], one_ref[0, there, lanes], coarse_hold.at[pair, half]
            )
            for block in (2 * half, 2 * half + 1):
                low, high = windows[block]
                hold = near_hold.at[pair, block, :, : high - low]
                tops[pair, half, block] = score(fine[pair][block], k_ref[low:high, lanes], hold)
    for pair in range(pairs):
        lanes = pl.ds(pair * PAIR, PAIR)
        for half in range(blocks // 2):
            there = pl.ds((half ^ 1) * BLOCK, BLOCK)
            coarse = weigh(
                coarse_hold.at[pair, half], tops[pair, half], with_ones(one_ref[1, there, lanes])
            )
            for block in (2 * half, 2 * half + 1):
                low, high = windows[block]
                hold = near_hold.at[pair, block, :, : high - low]
                near = weigh(hold, tops[pair, half, block], with_ones(v_ref[low:high, lanes]))
                part = slice((block - 2 * half) * BLOCK // 2, (block - 2 * half + 1) * BLOCK // 2)
                done = merged(near, [doubled(x[part]) for x in coarse])
                for index, field in enumerate(done):
                    state[index, block * BLOCK : (block + 1) * BLOCK, lanes] = field


def join_kernel(four_ref, six_ref, query_ref, out):
    sixteenth = four_ref.shape[1]
    out[:, :sixteenth, :] = four_ref[...]
    out[:, sixteenth:, :] = six_ref[...]


def coarse_kernel(
    two_q, three_q, first_ref, three_a, three_b, coarse, near_ref, scratch, two_ref, two_hold, three_hold
):
    inner = first_ref.shape[1] - BLOCK
    pairs = scratch.shape[1]
    two_ref[:, :inner, :] = first_ref[:, BLOCK:, :]
    for which in range(2):
        spill(first_ref.at[which, pl.ds(0, BLOCK), :], scratch.at[which])
        for half in range(pairs):
            lanes = pl.ds(half * PAIR, PAIR)
            slabs = slabs_of(scratch.at[which, half], 0)
            two_ref[which, inner:, lanes] = joined(pooled_slabs(pooled_slabs(slabs)))
        near_ref[which] = repooled(repooled(two_ref[which]))
    steps = {}
    for pair in range(pairs):
        lanes = pl.ds(pair * PAIR, PAIR)
        three = [
            jnp.concatenate([three_a[which, :, lanes], three_b[which, :, lanes]], axis=0)
            for which in range(2)
        ]
        steps[pair, 3] = (
            score(three_q[:, lanes], three[0], three_hold.at[pair]), with_ones(three[1])
        )
        steps[pair, 2] = (
            score(two_q[:, lanes], two_ref[0, :, lanes], two_hold.at[pair]),
            with_ones(two_ref[1, :, lanes]),
        )
    for pair in range(pairs):
        three = weigh(three_hold.at[pair], *steps[pair, 3])
        two = merged(weigh(two_hold.at[pair], *steps[pair, 2]), [doubled(x) for x in three])
        for index, field in enumerate(two):
            coarse[index, :, pl.ds(pair * PAIR, PAIR)] = field


def mid_kernel(edge_q, coarse, state, first_ref, second_ref, known, fine, *refs):
    outs, (ready, holds) = refs[:-2], refs[-2:]
    own = lax.axis_index("head")
    rows = state.shape[1]
    blocks = rows // BLOCK
    position = lax.axis_index("seq")
    last = lax.axis_size("seq") - 1
    even = lax.rem(position, 2) == 0
    opens = (position > 0, position < last)
    pairs = holds.shape[0]
    steps = {}
    for pair in range(pairs):
        lanes = pl.ds(pair * PAIR, PAIR)
        inner = [first_ref[which, :BLOCK, lanes] for which in range(2)]
        outer = [second_ref[which, :, lanes] for which in range(2)]
        for side in range(2):
            halo = [
                jnp.where(even, *((outer[which], inner[which])[:: 1 - 2 * side]))
                for which in range(2)
            ]
            steps[pair, side] = (
                score(edge_q[side, :, lanes], halo[0], holds.at[pair, side], opens[side]),
                with_ones(halo[1]),
            )
    for pair in range(pairs):
        lanes = pl.ds(pair * PAIR, PAIR)
        for block in range(blocks):
            here = slice(block * BLOCK, (block + 1) * BLOCK)
            quarter = slice(block * BLOCK // 4, (block + 1) * BLOCK // 4)
            done = merged(
                [state[index, here, lanes] for index in range(3)],
                [doubled(doubled(coarse[index, quarter, lanes])) for index in range(3)],
            )
            for side, edge in enumerate((0, blocks - 1)):
                if block == edge:
                    done = merged(done, weigh(holds.at[pair, side], *steps[pair, side]))
            result = done[1] / done[2]
            fine[0, here, lanes] = result
            fine[1, here, lanes] = done[0] + jnp.log(done[2]) * log2_e
            ready[block, :, lanes] = result.astype(jnp.bfloat16)
    for step, out in enumerate(outs, AHEAD):
        out[...] = ready[own ^ step]


def repeated(field):
    return jnp.concatenate([field] * FAN, axis=0)


def finish_blocks(fine, coarse, steps):
    own = lax.axis_index("head")
    features = fine.shape[2]
    for step, out in steps:
        block = own ^ step
        here = pl.ds(pl.multiple_of(block * BLOCK, BLOCK), BLOCK)
        few = pl.ds(pl.multiple_of(block * SLAB, SLAB), SLAB)
        shares = []
        for pair in range(features // PAIR):
            lanes = pl.ds(pair * PAIR, PAIR)
            fine_sum, coarse_sum = fine[1, here, lanes], repeated(coarse[1, few, lanes])
            if step < AHEAD:
                keep = 1.0 / (1.0 + jnp.exp2(coarse_sum - fine_sum))
                ours, theirs = fine[0, here, lanes], repeated(coarse[0, few, lanes])
                out[:, lanes] = (theirs + keep * (ours - theirs)).astype(jnp.bfloat16)
            else:
                ratio = jnp.exp2(-jnp.abs(fine_sum - coarse_sum))
                less = jnp.maximum(ratio / (1.0 + ratio), least_share)
                shares.append(jnp.where(fine_sum <= coarse_sum, less, -less).astype(jnp.bfloat16))
        if step >= AHEAD:
            pick = lax.broadcasted_iota(jnp.int32, (2 * SLAB, features), 1) == HD * (
                lax.broadcasted_iota(jnp.int32, (2 * SLAB, features), 0)
            )
            by_head = lax.dot_general(
                pick.astype(jnp.bfloat16),
                jnp.concatenate(shares, axis=1),
                (((1,), (1,)), ((), ())),
                preferred_element_type=jnp.float32,
            )[:SLAB]
            blank = jnp.zeros((SLAB, features - BLOCK), jnp.float32)
            out[...] = jnp.concatenate(
                [coarse[0, few, :], jnp.concatenate([by_head, blank], axis=1)], axis=0
            ).astype(jnp.bfloat16)


def known_kernel(four_q, four_ref, near_ref, three_a, three_b, fours_ref, *refs):
    far, (known, hold) = refs[:-2], refs[-2:]
    pairs = four_q.shape[1] // PAIR
    steps = {}
    for pair in range(pairs):
        lanes = pl.ds(pair * PAIR, PAIR)
        ours, beyond = [], []
        for which in range(2):
            ours.append(
                [four_ref[which, :, lanes], near_ref[which, :, lanes]]
                + [repooled(field[which, :, lanes]) for field in (three_a, three_b)]
            )
            beyond.append([field[which, :, lanes] for field in far])
        keys = jnp.concatenate(ours[0] + [fours_ref[0, :, lanes]] + beyond[0], axis=0)
        steps[pair] = (
            score(four_q[:, lanes], keys, hold.at[pair]),
            jnp.concatenate(
                [with_ones(field) for field in ours[1]]
                + [with_ones(fours_ref[1, :, lanes], 2.0)]
                + [with_ones(field) for field in beyond[1]],
                axis=0,
            ),
        )
    for pair in range(pairs):
        for index, field in enumerate(weigh(hold.at[pair], *steps[pair])):
            known[index, :, pl.ds(pair * PAIR, PAIR)] = field


def finish_kernel(four_q, fours_ref, known, fine, *refs):
    outs, (coarse, hold) = refs[:-2], refs[-2:]
    pairs = four_q.shape[1] // PAIR
    lanes = [pl.ds(pair * PAIR, PAIR) for pair in range(pairs)]
    tops = [
        score(four_q[:, lanes[pair]], fours_ref[0, :, lanes[pair]], hold.at[pair])
        for pair in range(pairs)
    ]
    for pair in range(pairs):
        values = with_ones(fours_ref[1, :, lanes[pair]], 2.0)
        top, numer, rowsum = merged(
            weigh(hold.at[pair], tops[pair], values),
            [known[index, :, lanes[pair]] for index in range(3)],
        )
        coarse[0, :, lanes[pair]] = numer / rowsum
        coarse[1, :, lanes[pair]] = top + jnp.log(rowsum) * log2_e
    finish_blocks(fine, coarse, zip(range(2, lax.axis_size("head")), outs))


def rest_kernel(fine, coarse, *outs):
    finish_blocks(fine, coarse, enumerate(outs))


def rejoin_kernel(further_ref, *refs):
    outs = refs[len(refs) // 3 * 2 :]
    for early, late_ref, out in zip(refs, refs[len(outs) :], outs):
        features = early.shape[1]
        late = late_ref[...].astype(jnp.float32)
        spread = lax.broadcasted_iota(jnp.int32, (SLAB, features), 1) // HD == (
            lax.broadcasted_iota(jnp.int32, (SLAB, features), 0)
        )
        signed = lax.dot_general(
            late[SLAB:, :BLOCK].astype(jnp.bfloat16),
            spread.astype(jnp.bfloat16),
            (((0,), (0,)), ((), ())),
            preferred_element_type=jnp.float32,
        )
        keep = jnp.where(signed >= 0, signed, 1.0 + signed)
        join = jnp.where(signed >= 0, 1.0 - signed, -signed)
        result = keep * early[...] + join * repeated(late[:SLAB])
        out[...] = result.astype(jnp.bfloat16)


def widen_kernel(*refs):
    half = len(refs) // 2
    for ref, out in zip(refs[:half], refs[half:]):
        out[...] = ref[...].astype(jnp.float32)


def partial_kernel(own_ref, weight_ref, out_ref):
    features = own_ref.shape[1]
    start = pl.multiple_of(lax.axis_index("head") * features, features)
    out_ref[...] = jnp.dot(
        own_ref[...], weight_ref[pl.ds(start, features), :], preferred_element_type=jnp.float32
    )


def further_kernel(widened_ref, partial_ref, weight_ref, *refs):
    parts, out_ref = refs[:-1], refs[-1]
    own = lax.axis_index("head")
    total = partial_ref[...]
    for step, part in enumerate(parts, 2):
        features = part.shape[1]
        start = pl.multiple_of((own ^ step) * features, features)
        total += jnp.dot(
            part[...], weight_ref[pl.ds(start, features), :], preferred_element_type=jnp.float32
        )
    out_ref[...] = total


def project_kernel(partial_ref, *refs):
    parts, (weight_ref, out_hbm, scratch, staged, sems) = refs[:-5], refs[-5:]
    own = lax.axis_index("head")
    features = parts[0].shape[1]
    chunk = staged.shape[2]
    copies = []
    for index in range(staged.shape[0]):
        columns = pl.ds(index * chunk, chunk)
        total = partial_ref[:, columns]
        for step, part in zip([*range(AHEAD, AHEAD + len(parts) - 1), 1], parts):
            start = pl.multiple_of((own ^ step) * features, features)
            total += jnp.dot(
                part[...],
                weight_ref[pl.ds(start, features), columns],
                preferred_element_type=jnp.float32,
            )
        for half in range(chunk // PAIR):
            lanes = slice(half * PAIR, (half + 1) * PAIR)
            scratch[index, half] = total[:, lanes]
            for i in range(SLAB):
                staged[index, i * FAN : (i + 1) * FAN, lanes] = scratch[
                    index, half, pl.ds(i, FAN, stride=SLAB), :
                ].astype(jnp.bfloat16)
        copy = pltpu.make_async_copy(staged.at[index], out_hbm.at[:, columns], sems.at[index])
        copy.start()
        copies.append(copy)
    for copy in copies:
        copy.wait()


def repool_outside(field):
    which, rows, lanes = field.shape
    slabs = field.astype(jnp.float32).reshape(which, rows // (2 * SLAB), 2, SLAB, lanes)
    sums = (slabs[:, :, 0] + slabs[:, :, 1]) * root_half
    return sums.reshape(which, rows // 2, lanes).astype(jnp.bfloat16)


def swapped(block, axis, mask):
    return lax.ppermute(block, axis, [(i, i ^ mask) for i in range(lax.axis_size(axis))])


def across(block):
    count, heads = lax.axis_size("seq"), lax.axis_size("head")
    route = []
    for seq in range(count):
        end = seq in (0, count - 1)
        other = seq if end else seq + 1 if seq % 2 else seq - 1
        for head in range(heads):
            route.append((seq * heads + head, other * heads + (head ^ 1 if end else head)))
    return lax.ppermute(block, ("seq", "head"), route)


def per_device(queries, key_vectors, value_vectors, out_weight):
    rows, features = queries.shape[1:]
    key_vectors, value_vectors = [
        pltpu.with_memory_space_constraint(x, pltpu.HBM) for x in (key_vectors, value_vectors)
    ]
    pairs = features // PAIR
    seq_count, head_count = lax.axis_size("seq"), lax.axis_size("head")
    bf16 = lambda *shape: jax.ShapeDtypeStruct(shape, jnp.bfloat16)
    params = pltpu.CompilerParams(vmem_limit_bytes=32 * 1024 * 1024)

    hbm = pl.BlockSpec(memory_space=pltpu.HBM)
    vmem = pl.BlockSpec(memory_space=pltpu.VMEM)
    keys, values, first, one, two = pl.pallas_call(
        pool_kernel,
        in_specs=[hbm] * 2,
        out_shape=[
            bf16(rows, features),
            bf16(rows, features),
            bf16(2, BLOCK + rows // 4 - BLOCK // 4, features),
            bf16(2, rows // 2, features),
            bf16(2, rows // 4, features),
        ],
        scratch_shapes=[
            pltpu.VMEM((2, rows // BLOCK, pairs, BLOCK, PAIR), jnp.float32),
            pltpu.SemaphoreType.DMA((2, 2)),
        ],
        compiler_params=params,
        name="pool",
    )(key_vectors, value_vectors)
    second, three, four = pl.pallas_call(
        deeper_kernel,
        out_shape=[
            bf16(2, BLOCK, features),
            bf16(2, rows // 8, features),
            bf16(2, rows // 16, features),
        ],
        compiler_params=params,
        cost_estimate=pl.CostEstimate(flops=2**31, bytes_accessed=2**23, transcendentals=0),
        name="deeper",
    )(keys, values, two)

    first_in = swapped(first, "seq", 1)
    second_in = across(second)
    four_in = swapped(four, "seq", 4)
    six_in = swapped(four, "seq", 6)
    threes_in = [swapped(three, "seq", mask) for mask in (2, 3)]
    edge_q, two_q, three_q, four_q, state = pl.pallas_call(
        local_kernel,
        out_shape=[
            bf16(2, BLOCK, features),
            bf16(rows // 4, features),
            bf16(rows // 8, features),
            bf16(rows // 16, features),
            jax.ShapeDtypeStruct((3, rows, features), jnp.float32),
        ],
        scratch_shapes=[
            pltpu.VMEM((pairs, rows, PAIR), jnp.float32),
            pltpu.VMEM((pairs, rows // BLOCK, 2 * BLOCK, 3 * BLOCK), jnp.float32),
            pltpu.VMEM((pairs, rows // BLOCK // 2, 2 * BLOCK, BLOCK), jnp.float32),
        ],
        compiler_params=params,
        name="local",
    )(queries[0], keys, values, one, four_in)

    fours = pl.pallas_call(
        join_kernel,
        out_shape=bf16(2, rows // 8, features),
        compiler_params=params,
        cost_estimate=pl.CostEstimate(flops=2**29, bytes_accessed=2**20, transcendentals=0),
        name="join",
    )(four_in, six_in, four_q)
    fours_in = swapped(fours, "seq", 1)
    coarse, near = pl.pallas_call(
        coarse_kernel,
        out_shape=[
            jax.ShapeDtypeStruct((3, rows // 4, features), jnp.float32),
            bf16(2, rows // 16, features),
        ],
        scratch_shapes=[
            pltpu.VMEM((2, pairs, BLOCK, PAIR), jnp.float32),
            pltpu.VMEM((2, rows // 4, features), jnp.bfloat16),
            pltpu.VMEM((pairs, rows // 2, BLOCK), jnp.float32),
            pltpu.VMEM((pairs, rows // 4, BLOCK), jnp.float32),
        ],
        compiler_params=params,
        cost_estimate=pl.CostEstimate(flops=2**31, bytes_accessed=2**21, transcendentals=0),
        name="coarse",
    )(two_q, three_q, first_in, *threes_in)
    far = []
    reach = 8
    if reach < seq_count:
        group = [four, near] + [repool_outside(field) for field in threes_in]
        group = jnp.concatenate(group + [fours, fours_in], axis=1)
        while reach < seq_count:
            fresh = swapped(group, "seq", reach)
            far.append(fresh)
            group = jnp.concatenate([group, fresh], axis=1)
            reach *= 2

    known = pl.pallas_call(
        known_kernel,
        out_shape=jax.ShapeDtypeStruct((3, rows // 16, features), jnp.float32),
        scratch_shapes=[pltpu.VMEM((pairs, rows // 8, rows // 16 * (seq_count - 2)), jnp.float32)],
        compiler_params=params,
        name="known",
    )(four_q, four, near, *threes_in, fours, *far)
    away = range(AHEAD, head_count)
    fine, *early = pl.pallas_call(
        mid_kernel,
        out_shape=[jax.ShapeDtypeStruct((2, rows, features), jnp.float32)]
        + [bf16(BLOCK, features) for _ in away],
        scratch_shapes=[
            pltpu.VMEM((rows // BLOCK, BLOCK, features), jnp.bfloat16),
            pltpu.VMEM((pairs, 2, 2 * BLOCK, BLOCK), jnp.float32),
        ],
        compiler_params=params,
        name="mid",
    )(edge_q, coarse, state, first_in, second_in, known)
    early_in = [swapped(part, "head", step) for step, part in zip(away, early)]

    parts = [bf16(BLOCK, features) for _ in range(AHEAD)]
    *outs, level_four = pl.pallas_call(
        finish_kernel,
        out_shape=parts[2:]
        + [bf16(2 * SLAB, features) for _ in away]
        + [jax.ShapeDtypeStruct((2, rows // 16, features), jnp.float32)],
        scratch_shapes=[pltpu.VMEM((pairs, rows // 8, rows // 8), jnp.float32)],
        compiler_params=params,
        name="finish",
    )(four_q, fours_in, known, fine)
    whole_in = [swapped(part, "head", step) for step, part in zip(range(2, AHEAD), outs)]
    late_in = [swapped(part, "head", step) for step, part in zip(away, outs[AHEAD - 2 :])]
    own_part, next_part = pl.pallas_call(
        rest_kernel,
        out_shape=parts[:2],
        compiler_params=params,
        name="rest",
    )(fine, level_four)
    next_in = swapped(next_part, "head", 1)
    width = out_weight.shape[1]
    partial = pl.pallas_call(
        partial_kernel,
        out_shape=jax.ShapeDtypeStruct((BLOCK, width), jnp.float32),
        compiler_params=params,
        name="partial",
    )(own_part, out_weight)
    heavy = pl.CostEstimate(flops=2**32, bytes_accessed=2**20, transcendentals=0)
    widened = pl.pallas_call(
        widen_kernel,
        out_shape=[jax.ShapeDtypeStruct((BLOCK, features), jnp.float32) for _ in away],
        compiler_params=params,
        cost_estimate=pl.CostEstimate(flops=2**22, bytes_accessed=2**10, transcendentals=0),
        name="widen",
    )(*early_in)
    further = pl.pallas_call(
        further_kernel,
        out_shape=jax.ShapeDtypeStruct((BLOCK, width), jnp.float32),
        compiler_params=params,
        name="further",
    )(widened[0], partial, out_weight, *whole_in)
    rejoined = pl.pallas_call(
        rejoin_kernel,
        out_shape=[bf16(BLOCK, features) for _ in away],
        compiler_params=params,
        cost_estimate=heavy,
        name="rejoin",
    )(further, *widened, *late_in)
    chunk = 2 * PAIR
    result = pl.pallas_call(
        project_kernel,
        in_specs=[vmem] * (len(rejoined) + 3),
        out_specs=hbm,
        out_shape=bf16(BLOCK, width),
        scratch_shapes=[
            pltpu.VMEM((width // chunk, 2, BLOCK, PAIR), jnp.float32),
            pltpu.VMEM((width // chunk, BLOCK, chunk), jnp.bfloat16),
            pltpu.SemaphoreType.DMA((width // chunk,)),
        ],
        compiler_params=params,
        name="project",
    )(further, *rejoined, next_in, out_weight)
    return result[None]


def solution(mesh):
    return jax.shard_map(
        per_device,
        mesh=mesh,
        in_specs=(P(None, "seq", "head"), P(None, "seq", "head"), P(None, "seq", "head"), P()),
        out_specs=P(None, ("seq", "head"), None),
        check_vma=False,
    )
```

```python
import jax
import jax.numpy as jnp
from jax import lax
from jax.experimental import pallas as pl
from jax.experimental.pallas import tpu as pltpu
from jax.sharding import PartitionSpec as P

HD = 64
BLOCK = 128
LEVELS = 4
SLAB = 8
PAIR = 2 * HD

neg_fill = -1e30
root_half = 0.7071067811865476
log2_e = 1.4426950408889634
log2_scale = HD**-0.5 * log2_e
least_share = 2.0**-100
AHEAD = 3

FAN = 2**LEVELS


def slabs_of(scratch, block):
    return [scratch[pl.ds(BLOCK * block + j, SLAB, stride=FAN), :] for j in range(FAN)]


def pooled_slabs(slabs):
    return [
        ((low + high) * root_half).astype(jnp.bfloat16).astype(jnp.float32)
        for low, high in zip(slabs[0::2], slabs[1::2])
    ]


def joined(slabs):
    return jnp.concatenate(slabs, axis=0).astype(jnp.bfloat16)


def spill(source, scratch):
    for half in range(scratch.shape[0]):
        scratch[half] = source[:, half * PAIR : (half + 1) * PAIR].astype(jnp.float32)


def pool_kernel(
    k_hbm, v_hbm, k_ref, v_ref, first_ref, one_ref, two_ref, scratch, sems
):
    rows = k_ref.shape[0]
    blocks = rows // BLOCK
    arrivals = []
    for half in range(2):
        here = pl.ds(half * rows // 2, rows // 2)
        for which, (source, target) in enumerate(((k_hbm, k_ref), (v_hbm, v_ref))):
            copy = pltpu.make_async_copy(
                source.at[0, here, :], target.at[here, :], sems.at[which, half]
            )
            copy.start()
            for block in range(half * blocks // 2, (half + 1) * blocks // 2):
                arrivals.append((block, which, target, copy))
    even = lax.rem(lax.axis_index("seq"), 2) == 0
    for block, which, ref, copy in arrivals:
        if block % (blocks // 2) == 0:
            copy.wait()
        here = pl.ds(block * BLOCK, BLOCK)
        spill(ref.at[here, :], scratch.at[which, block])
        for half in range(scratch.shape[2]):
            lanes = pl.ds(half * PAIR, PAIR)
            one = pooled_slabs(slabs_of(scratch.at[which, block, half], 0))
            one_ref[which, pl.ds(block * BLOCK // 2, BLOCK // 2), lanes] = joined(one)
            two_ref[which, pl.ds(block * BLOCK // 4, BLOCK // 4), lanes] = joined(pooled_slabs(one))
    inner = rows // 4 - BLOCK // 4
    for which, ref in enumerate((k_ref, v_ref)):
        first_ref[which, :BLOCK, :] = jnp.where(even, ref[rows - BLOCK :, :], ref[:BLOCK, :])
        first_ref[which, BLOCK:, :] = jnp.where(
            even, two_ref[which, :inner, :], two_ref[which, BLOCK // 4 :, :]
        )


def repooled(field):
    rows, lanes = field.shape
    slabs = field.astype(jnp.float32).reshape(rows // (2 * SLAB), 2, SLAB, lanes)
    return ((slabs[:, 0] + slabs[:, 1]) * root_half).reshape(rows // 2, lanes).astype(jnp.bfloat16)


def deeper_kernel(k_ref, v_ref, two_ref, second_ref, three_ref, four_ref):
    rows = k_ref.shape[0]
    even = lax.rem(lax.axis_index("seq"), 2) == 0
    for which, ref in enumerate((k_ref, v_ref)):
        second_ref[which] = jnp.where(even, ref[:BLOCK, :], ref[rows - BLOCK :, :])
        three = repooled(two_ref[which])
        three_ref[which] = three
        four_ref[which] = repooled(three)


def repooled(field):
    rows, lanes = field.shape
    slabs = field.astype(jnp.float32).reshape(rows // (2 * SLAB), 2, SLAB, lanes)
    return ((slabs[:, 0] + slabs[:, 1]) * root_half).reshape(rows // 2, lanes).astype(jnp.bfloat16)


def score(queries, keys, hold, is_open=None):
    rows = queries.shape[0]
    low = lax.broadcasted_iota(jnp.int32, (rows, PAIR), 1) < HD
    zero = jnp.zeros_like(queries)
    both = jnp.concatenate([jnp.where(low, queries, zero), jnp.where(low, zero, queries)], axis=0)
    raw = lax.dot_general(both, keys, (((1,), (1,)), ((), ())), preferred_element_type=jnp.float32)
    if is_open is not None:
        raw = jnp.where(is_open, raw, neg_fill)
    hold[...] = raw
    return jnp.max(raw, axis=1, keepdims=True)


def weigh(hold, top, values):
    rows = top.shape[0] // 2
    low = lax.broadcasted_iota(jnp.int32, (rows, PAIR), 1) < HD
    weights = jnp.exp2((hold[...] - top) * log2_scale).astype(jnp.bfloat16)
    result = jnp.dot(weights, values, preferred_element_type=jnp.float32)
    return (
        log2_scale * jnp.where(low, top[:rows], top[rows:]),
        jnp.where(low, result[:rows, :PAIR], result[rows:, :PAIR]),
        jnp.where(low, result[:rows, PAIR:], result[rows:, PAIR:]),
    )


def merged(fine, coarse):
    top = jnp.maximum(fine[0], coarse[0])
    keep = jnp.exp2(fine[0] - top)
    join = jnp.exp2(coarse[0] - top)
    return top, fine[1] * keep + coarse[1] * join, fine[2] * keep + coarse[2] * join


def doubled(field):
    rows, lanes = field.shape
    slabs = field.reshape(rows // SLAB, 1, SLAB, lanes)
    return jnp.broadcast_to(slabs, (rows // SLAB, 2, SLAB, lanes)).reshape(2 * rows, lanes)


def with_ones(values, weight=1.0):
    if weight != 1.0:
        values = values * jnp.bfloat16(weight)
    return jnp.concatenate([values, jnp.full(values.shape, weight, jnp.bfloat16)], axis=1)


def local_kernel(
    q_ref, k_ref, v_ref, one_ref, four_ref, edge_q, two_q, three_q, four_q, state,
    scratch, near_hold, coarse_hold,
):
    rows = q_ref.shape[0]
    blocks = rows // BLOCK
    pairs = scratch.shape[0]
    spill(q_ref, scratch)
    fine, one_q = [], []
    for pair in range(pairs):
        lanes = pl.ds(pair * PAIR, PAIR)
        ladder = [[], [], [], [], []]
        for block in range(blocks):
            slabs = slabs_of(scratch.at[pair], block)
            ladder[0].append(joined(slabs))
            for level in range(1, LEVELS + 1):
                slabs = pooled_slabs(slabs)
                ladder[level] += slabs
        edge_q[0, :, lanes] = ladder[0][0]
        edge_q[1, :, lanes] = ladder[0][-1]
        two_q[:, lanes] = joined(ladder[2])
        three_q[:, lanes] = joined(ladder[3])
        four_q[:, lanes] = joined(ladder[4])
        fine.append(ladder[0])
        one_q.append([joined(ladder[1][n : n + FAN]) for n in range(0, len(ladder[1]), FAN)])
    windows = [(max(n - 1, 0) * BLOCK, min(n + 2, blocks) * BLOCK) for n in range(blocks)]
    tops = {}
    for pair in range(pairs):
        lanes = pl.ds(pair * PAIR, PAIR)
        for half in range(blocks // 2):
            there = pl.ds((half ^ 1) * BLOCK, BLOCK)
            tops[pair, half] = score(
                one_q[pair][half], one_ref[0, there, lanes], coarse_hold.at[pair, half]
            )
            for block in (2 * half, 2 * half + 1):
                low, high = windows[block]
                hold = near_hold.at[pair, block, :, : high - low]
                tops[pair, half, block] = score(fine[pair][block], k_ref[low:high, lanes], hold)
    for pair in range(pairs):
        lanes = pl.ds(pair * PAIR, PAIR)
        for half in range(blocks // 2):
            there = pl.ds((half ^ 1) * BLOCK, BLOCK)
            coarse = weigh(
                coarse_hold.at[pair, half], tops[pair, half], with_ones(one_ref[1, there, lanes])
            )
            for block in (2 * half, 2 * half + 1):
                low, high = windows[block]
                hold = near_hold.at[pair, block, :, : high - low]
                near = weigh(hold, tops[pair, half, block], with_ones(v_ref[low:high, lanes]))
                part = slice((block - 2 * half) * BLOCK // 2, (block - 2 * half + 1) * BLOCK // 2)
                done = merged(near, [doubled(x[part]) for x in coarse])
                for index, field in enumerate(done):
                    state[index, block * BLOCK : (block + 1) * BLOCK, lanes] = field


def join_kernel(four_ref, six_ref, query_ref, out):
    sixteenth = four_ref.shape[1]
    out[:, :sixteenth, :] = four_ref[...]
    out[:, sixteenth:, :] = six_ref[...]


def coarse_kernel(
    two_q, three_q, first_ref, three_a, three_b, coarse, near_ref, scratch, two_ref, two_hold, three_hold
):
    inner = first_ref.shape[1] - BLOCK
    pairs = scratch.shape[1]
    two_ref[:, :inner, :] = first_ref[:, BLOCK:, :]
    for which in range(2):
        spill(first_ref.at[which, pl.ds(0, BLOCK), :], scratch.at[which])
        for half in range(pairs):
            lanes = pl.ds(half * PAIR, PAIR)
            slabs = slabs_of(scratch.at[which, half], 0)
            two_ref[which, inner:, lanes] = joined(pooled_slabs(pooled_slabs(slabs)))
        near_ref[which] = repooled(repooled(two_ref[which]))
    steps = {}
    for pair in range(pairs):
        lanes = pl.ds(pair * PAIR, PAIR)
        three = [
            jnp.concatenate([three_a[which, :, lanes], three_b[which, :, lanes]], axis=0)
            for which in range(2)
        ]
        steps[pair, 3] = (
            score(three_q[:, lanes], three[0], three_hold.at[pair]), with_ones(three[1])
        )
        steps[pair, 2] = (
            score(two_q[:, lanes], two_ref[0, :, lanes], two_hold.at[pair]),
            with_ones(two_ref[1, :, lanes]),
        )
    for pair in range(pairs):
        three = weigh(three_hold.at[pair], *steps[pair, 3])
        two = merged(weigh(two_hold.at[pair], *steps[pair, 2]), [doubled(x) for x in three])
        for index, field in enumerate(two):
            coarse[index, :, pl.ds(pair * PAIR, PAIR)] = field


def mid_kernel(edge_q, coarse, state, first_ref, second_ref, fine, *refs):
    outs, (ready, holds) = refs[:-2], refs[-2:]
    own = lax.axis_index("head")
    rows = state.shape[1]
    blocks = rows // BLOCK
    position = lax.axis_index("seq")
    last = lax.axis_size("seq") - 1
    even = lax.rem(position, 2) == 0
    opens = (position > 0, position < last)
    pairs = holds.shape[0]
    steps = {}
    for pair in range(pairs):
        lanes = pl.ds(pair * PAIR, PAIR)
        inner = [first_ref[which, :BLOCK, lanes] for which in range(2)]
        outer = [second_ref[which, :, lanes] for which in range(2)]
        for side in range(2):
            halo = [
                jnp.where(even, *((outer[which], inner[which])[:: 1 - 2 * side]))
                for which in range(2)
            ]
            steps[pair, side] = (
                score(edge_q[side, :, lanes], halo[0], holds.at[pair, side], opens[side]),
                with_ones(halo[1]),
            )
    for pair in range(pairs):
        lanes = pl.ds(pair * PAIR, PAIR)
        for block in range(blocks):
            here = slice(block * BLOCK, (block + 1) * BLOCK)
            quarter = slice(block * BLOCK // 4, (block + 1) * BLOCK // 4)
            done = merged(
                [state[index, here, lanes] for index in range(3)],
                [doubled(doubled(coarse[index, quarter, lanes])) for index in range(3)],
            )
            for side, edge in enumerate((0, blocks - 1)):
                if block == edge:
                    done = merged(done, weigh(holds.at[pair, side], *steps[pair, side]))
            result = done[1] / done[2]
            fine[0, here, lanes] = result
            fine[1, here, lanes] = done[0] + jnp.log(done[2]) * log2_e
            ready[block, :, lanes] = result.astype(jnp.bfloat16)
    for step, out in enumerate(outs, AHEAD):
        out[...] = ready[own ^ step]


def repeated(field):
    return jnp.concatenate([field] * FAN, axis=0)


def finish_blocks(fine, coarse, steps):
    own = lax.axis_index("head")
    features = fine.shape[2]
    for step, out in steps:
        block = own ^ step
        here = pl.ds(pl.multiple_of(block * BLOCK, BLOCK), BLOCK)
        few = pl.ds(pl.multiple_of(block * SLAB, SLAB), SLAB)
        shares = []
        for pair in range(features // PAIR):
            lanes = pl.ds(pair * PAIR, PAIR)
            fine_sum, coarse_sum = fine[1, here, lanes], repeated(coarse[1, few, lanes])
            if step < AHEAD:
                keep = 1.0 / (1.0 + jnp.exp2(coarse_sum - fine_sum))
                ours, theirs = fine[0, here, lanes], repeated(coarse[0, few, lanes])
                out[:, lanes] = (theirs + keep * (ours - theirs)).astype(jnp.bfloat16)
            else:
                ratio = jnp.exp2(-jnp.abs(fine_sum - coarse_sum))
                less = jnp.maximum(ratio / (1.0 + ratio), least_share)
                shares.append(jnp.where(fine_sum <= coarse_sum, less, -less).astype(jnp.bfloat16))
        if step >= AHEAD:
            pick = lax.broadcasted_iota(jnp.int32, (2 * SLAB, features), 1) == HD * (
                lax.broadcasted_iota(jnp.int32, (2 * SLAB, features), 0)
            )
            by_head = lax.dot_general(
                pick.astype(jnp.bfloat16),
                jnp.concatenate(shares, axis=1),
                (((1,), (1,)), ((), ())),
                preferred_element_type=jnp.float32,
            )[:SLAB]
            blank = jnp.zeros((SLAB, features - BLOCK), jnp.float32)
            out[...] = jnp.concatenate(
                [coarse[0, few, :], jnp.concatenate([by_head, blank], axis=1)], axis=0
            ).astype(jnp.bfloat16)


def finish_kernel(
    four_q, fine, four_ref, near_ref, three_a, three_b, fours_a, fours_b, *refs
):
    refs, (coarse, four_hold) = refs[:-2], refs[-2:]
    steps_out = range(2, lax.axis_size("head"))
    far, outs = refs[: -len(steps_out)], refs[-len(steps_out) :]
    pairs = four_q.shape[1] // PAIR
    steps = {}
    for pair in range(pairs):
        lanes = pl.ds(pair * PAIR, PAIR)
        ours, theirs, beyond = [], [], []
        for which in range(2):
            ours.append(
                [four_ref[which, :, lanes], near_ref[which, :, lanes]]
                + [repooled(field[which, :, lanes]) for field in (three_a, three_b)]
            )
            theirs.append([field[which, :, lanes] for field in (fours_a, fours_b)])
            beyond.append([field[which, :, lanes] for field in far])
        steps[pair] = (
            score(
                four_q[:, lanes],
                jnp.concatenate(ours[0] + theirs[0] + beyond[0], axis=0),
                four_hold.at[pair],
            ),
            jnp.concatenate(
                [with_ones(field) for field in ours[1]]
                + [with_ones(field, 2.0) for field in theirs[1]]
                + [with_ones(field) for field in beyond[1]],
                axis=0,
            ),
        )
    for pair in range(pairs):
        lanes = pl.ds(pair * PAIR, PAIR)
        top, numer, rowsum = weigh(four_hold.at[pair], *steps[pair])
        coarse[0, :, lanes] = numer / rowsum
        coarse[1, :, lanes] = top + jnp.log(rowsum) * log2_e
    finish_blocks(fine, coarse, zip(steps_out, outs))


def rest_kernel(fine, coarse, *outs):
    finish_blocks(fine, coarse, enumerate(outs))


def rejoin_kernel(further_ref, *refs):
    outs = refs[len(refs) // 3 * 2 :]
    for early, late_ref, out in zip(refs, refs[len(outs) :], outs):
        features = early.shape[1]
        late = late_ref[...].astype(jnp.float32)
        spread = lax.broadcasted_iota(jnp.int32, (SLAB, features), 1) // HD == (
            lax.broadcasted_iota(jnp.int32, (SLAB, features), 0)
        )
        signed = lax.dot_general(
            late[SLAB:, :BLOCK].astype(jnp.bfloat16),
            spread.astype(jnp.bfloat16),
            (((0,), (0,)), ((), ())),
            preferred_element_type=jnp.float32,
        )
        keep = jnp.where(signed >= 0, signed, 1.0 + signed)
        join = jnp.where(signed >= 0, 1.0 - signed, -signed)
        result = keep * early[...] + join * repeated(late[:SLAB])
        out[...] = result.astype(jnp.bfloat16)


def widen_kernel(*refs):
    half = len(refs) // 2
    for ref, out in zip(refs[:half], refs[half:]):
        out[...] = ref[...].astype(jnp.float32)


def partial_kernel(own_ref, weight_ref, out_ref):
    features = own_ref.shape[1]
    start = pl.multiple_of(lax.axis_index("head") * features, features)
    out_ref[...] = jnp.dot(
        own_ref[...], weight_ref[pl.ds(start, features), :], preferred_element_type=jnp.float32
    )


def further_kernel(widened_ref, partial_ref, weight_ref, *refs):
    parts, out_ref = refs[:-1], refs[-1]
    own = lax.axis_index("head")
    total = partial_ref[...]
    for step, part in enumerate(parts, 2):
        features = part.shape[1]
        start = pl.multiple_of((own ^ step) * features, features)
        total += jnp.dot(
            part[...], weight_ref[pl.ds(start, features), :], preferred_element_type=jnp.float32
        )
    out_ref[...] = total


def project_kernel(partial_ref, *refs):
    parts, (weight_ref, out_hbm, scratch, staged, sems) = refs[:-5], refs[-5:]
    own = lax.axis_index("head")
    features = parts[0].shape[1]
    chunk = staged.shape[2]
    copies = []
    for index in range(staged.shape[0]):
        columns = pl.ds(index * chunk, chunk)
        total = partial_ref[:, columns]
        for step, part in zip([*range(AHEAD, AHEAD + len(parts) - 1), 1], parts):
            start = pl.multiple_of((own ^ step) * features, features)
            total += jnp.dot(
                part[...],
                weight_ref[pl.ds(start, features), columns],
                preferred_element_type=jnp.float32,
            )
        for half in range(chunk // PAIR):
            lanes = slice(half * PAIR, (half + 1) * PAIR)
            scratch[index, half] = total[:, lanes]
            for i in range(SLAB):
                staged[index, i * FAN : (i + 1) * FAN, lanes] = scratch[
                    index, half, pl.ds(i, FAN, stride=SLAB), :
                ].astype(jnp.bfloat16)
        copy = pltpu.make_async_copy(staged.at[index], out_hbm.at[:, columns], sems.at[index])
        copy.start()
        copies.append(copy)
    for copy in copies:
        copy.wait()


def repool_outside(field):
    which, rows, lanes = field.shape
    slabs = field.astype(jnp.float32).reshape(which, rows // (2 * SLAB), 2, SLAB, lanes)
    sums = (slabs[:, :, 0] + slabs[:, :, 1]) * root_half
    return sums.reshape(which, rows // 2, lanes).astype(jnp.bfloat16)


def swapped(block, axis, mask):
    return lax.ppermute(block, axis, [(i, i ^ mask) for i in range(lax.axis_size(axis))])


def across(block):
    count, heads = lax.axis_size("seq"), lax.axis_size("head")
    route = []
    for seq in range(count):
        end = seq in (0, count - 1)
        other = seq if end else seq + 1 if seq % 2 else seq - 1
        for head in range(heads):
            route.append((seq * heads + head, other * heads + (head ^ 1 if end else head)))
    return lax.ppermute(block, ("seq", "head"), route)


def per_device(queries, key_vectors, value_vectors, out_weight):
    rows, features = queries.shape[1:]
    key_vectors, value_vectors = [
        pltpu.with_memory_space_constraint(x, pltpu.HBM) for x in (key_vectors, value_vectors)
    ]
    pairs = features // PAIR
    seq_count, head_count = lax.axis_size("seq"), lax.axis_size("head")
    bf16 = lambda *shape: jax.ShapeDtypeStruct(shape, jnp.bfloat16)
    params = pltpu.CompilerParams(vmem_limit_bytes=32 * 1024 * 1024)

    hbm = pl.BlockSpec(memory_space=pltpu.HBM)
    vmem = pl.BlockSpec(memory_space=pltpu.VMEM)
    keys, values, first, one, two = pl.pallas_call(
        pool_kernel,
        in_specs=[hbm] * 2,
        out_shape=[
            bf16(rows, features),
            bf16(rows, features),
            bf16(2, BLOCK + rows // 4 - BLOCK // 4, features),
            bf16(2, rows // 2, features),
            bf16(2, rows // 4, features),
        ],
        scratch_shapes=[
            pltpu.VMEM((2, rows // BLOCK, pairs, BLOCK, PAIR), jnp.float32),
            pltpu.SemaphoreType.DMA((2, 2)),
        ],
        compiler_params=params,
        name="pool",
    )(key_vectors, value_vectors)
    second, three, four = pl.pallas_call(
        deeper_kernel,
        out_shape=[
            bf16(2, BLOCK, features),
            bf16(2, rows // 8, features),
            bf16(2, rows // 16, features),
        ],
        compiler_params=params,
        cost_estimate=pl.CostEstimate(flops=2**31, bytes_accessed=2**23, transcendentals=0),
        name="deeper",
    )(keys, values, two)

    first_in = swapped(first, "seq", 1)
    second_in = across(second)
    four_in = swapped(four, "seq", 4)
    six_in = swapped(four, "seq", 6)
    threes_in = [swapped(three, "seq", mask) for mask in (3, 2)]
    edge_q, two_q, three_q, four_q, state = pl.pallas_call(
        local_kernel,
        out_shape=[
            bf16(2, BLOCK, features),
            bf16(rows // 4, features),
            bf16(rows // 8, features),
            bf16(rows // 16, features),
            jax.ShapeDtypeStruct((3, rows, features), jnp.float32),
        ],
        scratch_shapes=[
            pltpu.VMEM((pairs, rows, PAIR), jnp.float32),
            pltpu.VMEM((pairs, rows // BLOCK, 2 * BLOCK, 3 * BLOCK), jnp.float32),
            pltpu.VMEM((pairs, rows // BLOCK // 2, 2 * BLOCK, BLOCK), jnp.float32),
        ],
        compiler_params=params,
        name="local",
    )(queries[0], keys, values, one, four_in)

    fours = pl.pallas_call(
        join_kernel,
        out_shape=bf16(2, rows // 8, features),
        compiler_params=params,
        cost_estimate=pl.CostEstimate(flops=2**29, bytes_accessed=2**20, transcendentals=0),
        name="join",
    )(four_in, six_in, four_q)
    fours_in = swapped(fours, "seq", 1)
    coarse, near = pl.pallas_call(
        coarse_kernel,
        out_shape=[
            jax.ShapeDtypeStruct((3, rows // 4, features), jnp.float32),
            bf16(2, rows // 16, features),
        ],
        scratch_shapes=[
            pltpu.VMEM((2, pairs, BLOCK, PAIR), jnp.float32),
            pltpu.VMEM((2, rows // 4, features), jnp.bfloat16),
            pltpu.VMEM((pairs, rows // 2, BLOCK), jnp.float32),
            pltpu.VMEM((pairs, rows // 4, BLOCK), jnp.float32),
        ],
        compiler_params=params,
        cost_estimate=pl.CostEstimate(flops=2**31, bytes_accessed=2**21, transcendentals=0),
        name="coarse",
    )(two_q, three_q, first_in, *threes_in)
    away = range(AHEAD, head_count)
    fine, *early = pl.pallas_call(
        mid_kernel,
        out_shape=[jax.ShapeDtypeStruct((2, rows, features), jnp.float32)]
        + [bf16(BLOCK, features) for _ in away],
        scratch_shapes=[
            pltpu.VMEM((rows // BLOCK, BLOCK, features), jnp.bfloat16),
            pltpu.VMEM((pairs, 2, 2 * BLOCK, BLOCK), jnp.float32),
        ],
        compiler_params=params,
        name="mid",
    )(edge_q, coarse, state, first_in, second_in)
    early_in = [swapped(part, "head", step) for step, part in zip(away, early)]

    far = []
    known = 8
    if known < seq_count:
        group = [four, near] + [repool_outside(field) for field in threes_in]
        group = jnp.concatenate(group + [fours, fours_in], axis=1)
        while known < seq_count:
            fresh = swapped(group, "seq", known)
            far.append(fresh)
            group = jnp.concatenate([group, fresh], axis=1)
            known *= 2

    parts = [bf16(BLOCK, features) for _ in range(AHEAD)]
    *outs, level_four = pl.pallas_call(
        finish_kernel,
        out_shape=parts[2:]
        + [bf16(2 * SLAB, features) for _ in away]
        + [jax.ShapeDtypeStruct((2, rows // 16, features), jnp.float32)],
        scratch_shapes=[pltpu.VMEM((pairs, rows // 8, rows // 16 * seq_count), jnp.float32)],
        compiler_params=params,
        name="finish",
    )(four_q, fine, four, near, *threes_in, fours, fours_in, *far)
    whole_in = [swapped(part, "head", step) for step, part in zip(range(2, AHEAD), outs)]
    late_in = [swapped(part, "head", step) for step, part in zip(away, outs[AHEAD - 2 :])]
    own_part, next_part = pl.pallas_call(
        rest_kernel,
        out_shape=parts[:2],
        compiler_params=params,
        name="rest",
    )(fine, level_four)
    next_in = swapped(next_part, "head", 1)
    width = out_weight.shape[1]
    partial = pl.pallas_call(
        partial_kernel,
        out_shape=jax.ShapeDtypeStruct((BLOCK, width), jnp.float32),
        compiler_params=params,
        name="partial",
    )(own_part, out_weight)
    heavy = pl.CostEstimate(flops=2**32, bytes_accessed=2**20, transcendentals=0)
    widened = pl.pallas_call(
        widen_kernel,
        out_shape=[jax.ShapeDtypeStruct((BLOCK, features), jnp.float32) for _ in away],
        compiler_params=params,
        cost_estimate=pl.CostEstimate(flops=2**22, bytes_accessed=2**10, transcendentals=0),
        name="widen",
    )(*early_in)
    further = pl.pallas_call(
        further_kernel,
        out_shape=jax.ShapeDtypeStruct((BLOCK, width), jnp.float32),
        compiler_params=params,
        name="further",
    )(widened[0], partial, out_weight, *whole_in)
    rejoined = pl.pallas_call(
        rejoin_kernel,
        out_shape=[bf16(BLOCK, features) for _ in away],
        compiler_params=params,
        cost_estimate=heavy,
        name="rejoin",
    )(further, *widened, *late_in)
    chunk = 2 * PAIR
    result = pl.pallas_call(
        project_kernel,
        in_specs=[vmem] * (len(rejoined) + 3),
        out_specs=hbm,
        out_shape=bf16(BLOCK, width),
        scratch_shapes=[
            pltpu.VMEM((width // chunk, 2, BLOCK, PAIR), jnp.float32),
            pltpu.VMEM((width // chunk, BLOCK, chunk), jnp.bfloat16),
            pltpu.SemaphoreType.DMA((width // chunk,)),
        ],
        compiler_params=params,
        name="project",
    )(further, *rejoined, next_in, out_weight)
    return result[None]


def solution(mesh):
    return jax.shard_map(
        per_device,
        mesh=mesh,
        in_specs=(P(None, "seq", "head"), P(None, "seq", "head"), P(None, "seq", "head"), P()),
        out_specs=P(None, ("seq", "head"), None),
        check_vma=False,
    )
```

```python
import jax
import jax.numpy as jnp
from jax import lax
from jax.experimental import pallas as pl
from jax.experimental.pallas import tpu as pltpu
from jax.sharding import PartitionSpec as P

HD = 64
BLOCK = 128
LEVELS = 4
SLAB = 8
PAIR = 2 * HD

neg_fill = -1e30
root_half = 0.7071067811865476
log2_e = 1.4426950408889634
log2_scale = HD**-0.5 * log2_e
least_share = 2.0**-100
AHEAD = 3

FAN = 2**LEVELS


def slabs_of(scratch, block):
    return [scratch[pl.ds(BLOCK * block + j, SLAB, stride=FAN), :] for j in range(FAN)]


def pooled_slabs(slabs):
    return [
        ((low + high) * root_half).astype(jnp.bfloat16).astype(jnp.float32)
        for low, high in zip(slabs[0::2], slabs[1::2])
    ]


def joined(slabs):
    return jnp.concatenate(slabs, axis=0).astype(jnp.bfloat16)


def spill(source, scratch):
    for half in range(scratch.shape[0]):
        scratch[half] = source[:, half * PAIR : (half + 1) * PAIR].astype(jnp.float32)


def first_level(block):
    row = lax.broadcasted_iota(jnp.int32, (BLOCK // 2, BLOCK), 0)
    column = lax.broadcasted_iota(jnp.int32, (BLOCK // 2, BLOCK), 1)
    pairs = column // 2 == FAN // 2 * (row % SLAB) + row // SLAB
    sums = jnp.dot(pairs.astype(jnp.bfloat16), block, preferred_element_type=jnp.float32)
    return (sums * root_half).astype(jnp.bfloat16)


def pool_kernel(k_hbm, v_hbm, k_ref, v_ref, first_ref, one_ref, two_ref, sems):
    rows = k_ref.shape[0]
    blocks = rows // BLOCK
    arrivals = []
    for half in range(2):
        here = pl.ds(half * rows // 2, rows // 2)
        for which, (source, target) in enumerate(((k_hbm, k_ref), (v_hbm, v_ref))):
            copy = pltpu.make_async_copy(
                source.at[0, here, :], target.at[here, :], sems.at[which, half]
            )
            copy.start()
            for block in range(half * blocks // 2, (half + 1) * blocks // 2):
                arrivals.append((block, which, target, copy))
    even = lax.rem(lax.axis_index("seq"), 2) == 0
    for block, which, ref, copy in arrivals:
        if block % (blocks // 2) == 0:
            copy.wait()
        one = first_level(ref[pl.ds(block * BLOCK, BLOCK), :])
        one_ref[which, pl.ds(block * BLOCK // 2, BLOCK // 2), :] = one
        two_ref[which, pl.ds(block * BLOCK // 4, BLOCK // 4), :] = repooled(one)
    inner = rows // 4 - BLOCK // 4
    for which, ref in enumerate((k_ref, v_ref)):
        first_ref[which, :BLOCK, :] = jnp.where(even, ref[rows - BLOCK :, :], ref[:BLOCK, :])
        first_ref[which, BLOCK:, :] = jnp.where(
            even, two_ref[which, :inner, :], two_ref[which, BLOCK // 4 :, :]
        )


def repooled(field):
    rows, lanes = field.shape
    slabs = field.astype(jnp.float32).reshape(rows // (2 * SLAB), 2, SLAB, lanes)
    return ((slabs[:, 0] + slabs[:, 1]) * root_half).reshape(rows // 2, lanes).astype(jnp.bfloat16)


def deeper_kernel(k_ref, v_ref, two_ref, second_ref, three_ref, four_ref):
    rows = k_ref.shape[0]
    even = lax.rem(lax.axis_index("seq"), 2) == 0
    for which, ref in enumerate((k_ref, v_ref)):
        second_ref[which] = jnp.where(even, ref[:BLOCK, :], ref[rows - BLOCK :, :])
        three = repooled(two_ref[which])
        three_ref[which] = three
        four_ref[which] = repooled(three)


def repooled(field):
    rows, lanes = field.shape
    slabs = field.astype(jnp.float32).reshape(rows // (2 * SLAB), 2, SLAB, lanes)
    return ((slabs[:, 0] + slabs[:, 1]) * root_half).reshape(rows // 2, lanes).astype(jnp.bfloat16)


def score(queries, keys, hold, is_open=None):
    rows = queries.shape[0]
    low = lax.broadcasted_iota(jnp.int32, (rows, PAIR), 1) < HD
    zero = jnp.zeros_like(queries)
    both = jnp.concatenate([jnp.where(low, queries, zero), jnp.where(low, zero, queries)], axis=0)
    raw = lax.dot_general(both, keys, (((1,), (1,)), ((), ())), preferred_element_type=jnp.float32)
    if is_open is not None:
        raw = jnp.where(is_open, raw, neg_fill)
    hold[...] = raw
    return jnp.max(raw, axis=1, keepdims=True)


def weigh(hold, top, values):
    rows = top.shape[0] // 2
    low = lax.broadcasted_iota(jnp.int32, (rows, PAIR), 1) < HD
    weights = jnp.exp2((hold[...] - top) * log2_scale).astype(jnp.bfloat16)
    result = jnp.dot(weights, values, preferred_element_type=jnp.float32)
    return (
        log2_scale * jnp.where(low, top[:rows], top[rows:]),
        jnp.where(low, result[:rows, :PAIR], result[rows:, :PAIR]),
        jnp.where(low, result[:rows, PAIR:], result[rows:, PAIR:]),
    )


def merged(fine, coarse):
    top = jnp.maximum(fine[0], coarse[0])
    keep = jnp.exp2(fine[0] - top)
    join = jnp.exp2(coarse[0] - top)
    return top, fine[1] * keep + coarse[1] * join, fine[2] * keep + coarse[2] * join


def doubled(field):
    rows, lanes = field.shape
    slabs = field.reshape(rows // SLAB, 1, SLAB, lanes)
    return jnp.broadcast_to(slabs, (rows // SLAB, 2, SLAB, lanes)).reshape(2 * rows, lanes)


def with_ones(values, weight=1.0):
    if weight != 1.0:
        values = values * jnp.bfloat16(weight)
    return jnp.concatenate([values, jnp.full(values.shape, weight, jnp.bfloat16)], axis=1)


def local_kernel(
    q_ref, k_ref, v_ref, one_ref, four_ref, edge_q, two_q, three_q, four_q, state,
    scratch, near_hold, coarse_hold,
):
    rows = q_ref.shape[0]
    blocks = rows // BLOCK
    pairs = scratch.shape[0]
    spill(q_ref, scratch)
    fine, one_q = [], []
    for pair in range(pairs):
        lanes = pl.ds(pair * PAIR, PAIR)
        ladder = [[], [], [], [], []]
        for block in range(blocks):
            slabs = slabs_of(scratch.at[pair], block)
            ladder[0].append(joined(slabs))
            for level in range(1, LEVELS + 1):
                slabs = pooled_slabs(slabs)
                ladder[level] += slabs
        edge_q[0, :, lanes] = ladder[0][0]
        edge_q[1, :, lanes] = ladder[0][-1]
        two_q[:, lanes] = joined(ladder[2])
        three_q[:, lanes] = joined(ladder[3])
        four_q[:, lanes] = joined(ladder[4])
        fine.append(ladder[0])
        one_q.append([joined(ladder[1][n : n + FAN]) for n in range(0, len(ladder[1]), FAN)])
    windows = [(max(n - 1, 0) * BLOCK, min(n + 2, blocks) * BLOCK) for n in range(blocks)]
    tops = {}
    for pair in range(pairs):
        lanes = pl.ds(pair * PAIR, PAIR)
        for half in range(blocks // 2):
            there = pl.ds((half ^ 1) * BLOCK, BLOCK)
            tops[pair, half] = score(
                one_q[pair][half], one_ref[0, there, lanes], coarse_hold.at[pair, half]
            )
            for block in (2 * half, 2 * half + 1):
                low, high = windows[block]
                hold = near_hold.at[pair, block, :, : high - low]
                tops[pair, half, block] = score(fine[pair][block], k_ref[low:high, lanes], hold)
    for pair in range(pairs):
        lanes = pl.ds(pair * PAIR, PAIR)
        for half in range(blocks // 2):
            there = pl.ds((half ^ 1) * BLOCK, BLOCK)
            coarse = weigh(
                coarse_hold.at[pair, half], tops[pair, half], with_ones(one_ref[1, there, lanes])
            )
            for block in (2 * half, 2 * half + 1):
                low, high = windows[block]
                hold = near_hold.at[pair, block, :, : high - low]
                near = weigh(hold, tops[pair, half, block], with_ones(v_ref[low:high, lanes]))
                part = slice((block - 2 * half) * BLOCK // 2, (block - 2 * half + 1) * BLOCK // 2)
                done = merged(near, [doubled(x[part]) for x in coarse])
                for index, field in enumerate(done):
                    state[index, block * BLOCK : (block + 1) * BLOCK, lanes] = field


def join_kernel(four_ref, six_ref, query_ref, out):
    sixteenth = four_ref.shape[1]
    out[:, :sixteenth, :] = four_ref[...]
    out[:, sixteenth:, :] = six_ref[...]


def coarse_kernel(
    two_q, three_q, first_ref, three_a, three_b, coarse, near_ref, two_ref, two_hold, three_hold
):
    inner = first_ref.shape[1] - BLOCK
    pairs = two_q.shape[1] // PAIR
    two_ref[:, :inner, :] = first_ref[:, BLOCK:, :]
    for which in range(2):
        two_ref[which, inner:, :] = repooled(first_level(first_ref[which, :BLOCK, :]))
        near_ref[which] = repooled(repooled(two_ref[which]))
    steps = {}
    for pair in range(pairs):
        lanes = pl.ds(pair * PAIR, PAIR)
        three = [
            jnp.concatenate([three_a[which, :, lanes], three_b[which, :, lanes]], axis=0)
            for which in range(2)
        ]
        steps[pair, 3] = (
            score(three_q[:, lanes], three[0], three_hold.at[pair]), with_ones(three[1])
        )
        steps[pair, 2] = (
            score(two_q[:, lanes], two_ref[0, :, lanes], two_hold.at[pair]),
            with_ones(two_ref[1, :, lanes]),
        )
    for pair in range(pairs):
        three = weigh(three_hold.at[pair], *steps[pair, 3])
        two = merged(weigh(two_hold.at[pair], *steps[pair, 2]), [doubled(x) for x in three])
        for index, field in enumerate(two):
            coarse[index, :, pl.ds(pair * PAIR, PAIR)] = field


def mid_kernel(edge_q, coarse, state, first_ref, second_ref, fine, *refs):
    outs, (ready, holds) = refs[:-2], refs[-2:]
    own = lax.axis_index("head")
    rows = state.shape[1]
    blocks = rows // BLOCK
    position = lax.axis_index("seq")
    last = lax.axis_size("seq") - 1
    even = lax.rem(position, 2) == 0
    opens = (position > 0, position < last)
    pairs = holds.shape[0]
    steps = {}
    for pair in range(pairs):
        lanes = pl.ds(pair * PAIR, PAIR)
        inner = [first_ref[which, :BLOCK, lanes] for which in range(2)]
        outer = [second_ref[which, :, lanes] for which in range(2)]
        for side in range(2):
            halo = [
                jnp.where(even, *((outer[which], inner[which])[:: 1 - 2 * side]))
                for which in range(2)
            ]
            steps[pair, side] = (
                score(edge_q[side, :, lanes], halo[0], holds.at[pair, side], opens[side]),
                with_ones(halo[1]),
            )
    for pair in range(pairs):
        lanes = pl.ds(pair * PAIR, PAIR)
        for block in range(blocks):
            here = slice(block * BLOCK, (block + 1) * BLOCK)
            quarter = slice(block * BLOCK // 4, (block + 1) * BLOCK // 4)
            done = merged(
                [state[index, here, lanes] for index in range(3)],
                [doubled(doubled(coarse[index, quarter, lanes])) for index in range(3)],
            )
            for side, edge in enumerate((0, blocks - 1)):
                if block == edge:
                    done = merged(done, weigh(holds.at[pair, side], *steps[pair, side]))
            result = done[1] / done[2]
            fine[0, here, lanes] = result
            fine[1, here, lanes] = done[0] + jnp.log(done[2]) * log2_e
            ready[block, :, lanes] = result.astype(jnp.bfloat16)
    for step, out in enumerate(outs, AHEAD):
        out[...] = ready[own ^ step]


def repeated(field):
    return jnp.concatenate([field] * FAN, axis=0)


def finish_blocks(fine, coarse, steps):
    own = lax.axis_index("head")
    features = fine.shape[2]
    for step, out in steps:
        block = own ^ step
        here = pl.ds(pl.multiple_of(block * BLOCK, BLOCK), BLOCK)
        few = pl.ds(pl.multiple_of(block * SLAB, SLAB), SLAB)
        shares = []
        for pair in range(features // PAIR):
            lanes = pl.ds(pair * PAIR, PAIR)
            fine_sum, coarse_sum = fine[1, here, lanes], repeated(coarse[1, few, lanes])
            if step < AHEAD:
                keep = 1.0 / (1.0 + jnp.exp2(coarse_sum - fine_sum))
                ours, theirs = fine[0, here, lanes], repeated(coarse[0, few, lanes])
                out[:, lanes] = (theirs + keep * (ours - theirs)).astype(jnp.bfloat16)
            else:
                ratio = jnp.exp2(-jnp.abs(fine_sum - coarse_sum))
                less = jnp.maximum(ratio / (1.0 + ratio), least_share)
                shares.append(jnp.where(fine_sum <= coarse_sum, less, -less).astype(jnp.bfloat16))
        if step >= AHEAD:
            pick = lax.broadcasted_iota(jnp.int32, (2 * SLAB, features), 1) == HD * (
                lax.broadcasted_iota(jnp.int32, (2 * SLAB, features), 0)
            )
            by_head = lax.dot_general(
                pick.astype(jnp.bfloat16),
                jnp.concatenate(shares, axis=1),
                (((1,), (1,)), ((), ())),
                preferred_element_type=jnp.float32,
            )[:SLAB]
            blank = jnp.zeros((SLAB, features - BLOCK), jnp.float32)
            out[...] = jnp.concatenate(
                [coarse[0, few, :], jnp.concatenate([by_head, blank], axis=1)], axis=0
            ).astype(jnp.bfloat16)


def finish_kernel(
    four_q, fine, four_ref, near_ref, three_a, three_b, fours_a, fours_b, *refs
):
    refs, (coarse, four_hold) = refs[:-2], refs[-2:]
    steps_out = range(2, lax.axis_size("head"))
    far, outs = refs[: -len(steps_out)], refs[-len(steps_out) :]
    pairs = four_q.shape[1] // PAIR
    steps = {}
    for pair in range(pairs):
        lanes = pl.ds(pair * PAIR, PAIR)
        ours, theirs, beyond = [], [], []
        for which in range(2):
            ours.append(
                [four_ref[which, :, lanes], near_ref[which, :, lanes]]
                + [repooled(field[which, :, lanes]) for field in (three_a, three_b)]
            )
            theirs.append([field[which, :, lanes] for field in (fours_a, fours_b)])
            beyond.append([field[which, :, lanes] for field in far])
        steps[pair] = (
            score(
                four_q[:, lanes],
                jnp.concatenate(ours[0] + theirs[0] + beyond[0], axis=0),
                four_hold.at[pair],
            ),
            jnp.concatenate(
                [with_ones(field) for field in ours[1]]
                + [with_ones(field, 2.0) for field in theirs[1]]
                + [with_ones(field) for field in beyond[1]],
                axis=0,
            ),
        )
    for pair in range(pairs):
        lanes = pl.ds(pair * PAIR, PAIR)
        top, numer, rowsum = weigh(four_hold.at[pair], *steps[pair])
        coarse[0, :, lanes] = numer / rowsum
        coarse[1, :, lanes] = top + jnp.log(rowsum) * log2_e
    finish_blocks(fine, coarse, zip(steps_out, outs))


def rest_kernel(fine, coarse, *outs):
    finish_blocks(fine, coarse, enumerate(outs))


def rejoin_kernel(further_ref, *refs):
    outs = refs[len(refs) // 3 * 2 :]
    for early, late_ref, out in zip(refs, refs[len(outs) :], outs):
        features = early.shape[1]
        late = late_ref[...].astype(jnp.float32)
        spread = lax.broadcasted_iota(jnp.int32, (SLAB, features), 1) // HD == (
            lax.broadcasted_iota(jnp.int32, (SLAB, features), 0)
        )
        signed = lax.dot_general(
            late[SLAB:, :BLOCK].astype(jnp.bfloat16),
            spread.astype(jnp.bfloat16),
            (((0,), (0,)), ((), ())),
            preferred_element_type=jnp.float32,
        )
        keep = jnp.where(signed >= 0, signed, 1.0 + signed)
        join = jnp.where(signed >= 0, 1.0 - signed, -signed)
        result = keep * early[...] + join * repeated(late[:SLAB])
        out[...] = result.astype(jnp.bfloat16)


def widen_kernel(*refs):
    half = len(refs) // 2
    for ref, out in zip(refs[:half], refs[half:]):
        out[...] = ref[...].astype(jnp.float32)


def partial_kernel(own_ref, weight_ref, out_ref):
    features = own_ref.shape[1]
    start = pl.multiple_of(lax.axis_index("head") * features, features)
    out_ref[...] = jnp.dot(
        own_ref[...], weight_ref[pl.ds(start, features), :], preferred_element_type=jnp.float32
    )


def further_kernel(widened_ref, partial_ref, weight_ref, *refs):
    parts, out_ref = refs[:-1], refs[-1]
    own = lax.axis_index("head")
    total = partial_ref[...]
    for step, part in enumerate(parts, 2):
        features = part.shape[1]
        start = pl.multiple_of((own ^ step) * features, features)
        total += jnp.dot(
            part[...], weight_ref[pl.ds(start, features), :], preferred_element_type=jnp.float32
        )
    out_ref[...] = total


def project_kernel(partial_ref, *refs):
    parts, (weight_ref, out_hbm, scratch, staged, sems) = refs[:-5], refs[-5:]
    own = lax.axis_index("head")
    features = parts[0].shape[1]
    chunk = staged.shape[2]
    copies = []
    for index in range(staged.shape[0]):
        columns = pl.ds(index * chunk, chunk)
        total = partial_ref[:, columns]
        for step, part in zip([*range(AHEAD, AHEAD + len(parts) - 1), 1], parts):
            start = pl.multiple_of((own ^ step) * features, features)
            total += jnp.dot(
                part[...],
                weight_ref[pl.ds(start, features), columns],
                preferred_element_type=jnp.float32,
            )
        for half in range(chunk // PAIR):
            lanes = slice(half * PAIR, (half + 1) * PAIR)
            scratch[index, half] = total[:, lanes]
            for i in range(SLAB):
                staged[index, i * FAN : (i + 1) * FAN, lanes] = scratch[
                    index, half, pl.ds(i, FAN, stride=SLAB), :
                ].astype(jnp.bfloat16)
        copy = pltpu.make_async_copy(staged.at[index], out_hbm.at[:, columns], sems.at[index])
        copy.start()
        copies.append(copy)
    for copy in copies:
        copy.wait()


def repool_outside(field):
    which, rows, lanes = field.shape
    slabs = field.astype(jnp.float32).reshape(which, rows // (2 * SLAB), 2, SLAB, lanes)
    sums = (slabs[:, :, 0] + slabs[:, :, 1]) * root_half
    return sums.reshape(which, rows // 2, lanes).astype(jnp.bfloat16)


def swapped(block, axis, mask):
    return lax.ppermute(block, axis, [(i, i ^ mask) for i in range(lax.axis_size(axis))])


def across(block):
    count, heads = lax.axis_size("seq"), lax.axis_size("head")
    route = []
    for seq in range(count):
        end = seq in (0, count - 1)
        other = seq if end else seq + 1 if seq % 2 else seq - 1
        for head in range(heads):
            route.append((seq * heads + head, other * heads + (head ^ 1 if end else head)))
    return lax.ppermute(block, ("seq", "head"), route)


def per_device(queries, key_vectors, value_vectors, out_weight):
    rows, features = queries.shape[1:]
    key_vectors, value_vectors = [
        pltpu.with_memory_space_constraint(x, pltpu.HBM) for x in (key_vectors, value_vectors)
    ]
    pairs = features // PAIR
    seq_count, head_count = lax.axis_size("seq"), lax.axis_size("head")
    bf16 = lambda *shape: jax.ShapeDtypeStruct(shape, jnp.bfloat16)
    params = pltpu.CompilerParams(vmem_limit_bytes=32 * 1024 * 1024)

    hbm = pl.BlockSpec(memory_space=pltpu.HBM)
    vmem = pl.BlockSpec(memory_space=pltpu.VMEM)
    keys, values, first, one, two = pl.pallas_call(
        pool_kernel,
        in_specs=[hbm] * 2,
        out_shape=[
            bf16(rows, features),
            bf16(rows, features),
            bf16(2, BLOCK + rows // 4 - BLOCK // 4, features),
            bf16(2, rows // 2, features),
            bf16(2, rows // 4, features),
        ],
        scratch_shapes=[
            pltpu.SemaphoreType.DMA((2, 2)),
        ],
        compiler_params=params,
        name="pool",
    )(key_vectors, value_vectors)
    second, three, four = pl.pallas_call(
        deeper_kernel,
        out_shape=[
            bf16(2, BLOCK, features),
            bf16(2, rows // 8, features),
            bf16(2, rows // 16, features),
        ],
        compiler_params=params,
        cost_estimate=pl.CostEstimate(flops=2**31, bytes_accessed=2**23, transcendentals=0),
        name="deeper",
    )(keys, values, two)

    first_in = swapped(first, "seq", 1)
    second_in = across(second)
    four_in = swapped(four, "seq", 4)
    six_in = swapped(four, "seq", 6)
    threes_in = [swapped(three, "seq", mask) for mask in (3, 2)]
    edge_q, two_q, three_q, four_q, state = pl.pallas_call(
        local_kernel,
        out_shape=[
            bf16(2, BLOCK, features),
            bf16(rows // 4, features),
            bf16(rows // 8, features),
            bf16(rows // 16, features),
            jax.ShapeDtypeStruct((3, rows, features), jnp.float32),
        ],
        scratch_shapes=[
            pltpu.VMEM((pairs, rows, PAIR), jnp.float32),
            pltpu.VMEM((pairs, rows // BLOCK, 2 * BLOCK, 3 * BLOCK), jnp.float32),
            pltpu.VMEM((pairs, rows // BLOCK // 2, 2 * BLOCK, BLOCK), jnp.float32),
        ],
        compiler_params=params,
        name="local",
    )(queries[0], keys, values, one, four_in)

    fours = pl.pallas_call(
        join_kernel,
        out_shape=bf16(2, rows // 8, features),
        compiler_params=params,
        cost_estimate=pl.CostEstimate(flops=2**29, bytes_accessed=2**20, transcendentals=0),
        name="join",
    )(four_in, six_in, four_q)
    fours_in = swapped(fours, "seq", 1)
    coarse, near = pl.pallas_call(
        coarse_kernel,
        out_shape=[
            jax.ShapeDtypeStruct((3, rows // 4, features), jnp.float32),
            bf16(2, rows // 16, features),
        ],
        scratch_shapes=[
            pltpu.VMEM((2, rows // 4, features), jnp.bfloat16),
            pltpu.VMEM((pairs, rows // 2, BLOCK), jnp.float32),
            pltpu.VMEM((pairs, rows // 4, BLOCK), jnp.float32),
        ],
        compiler_params=params,
        cost_estimate=pl.CostEstimate(flops=2**31, bytes_accessed=2**21, transcendentals=0),
        name="coarse",
    )(two_q, three_q, first_in, *threes_in)
    away = range(AHEAD, head_count)
    fine, *early = pl.pallas_call(
        mid_kernel,
        out_shape=[jax.ShapeDtypeStruct((2, rows, features), jnp.float32)]
        + [bf16(BLOCK, features) for _ in away],
        scratch_shapes=[
            pltpu.VMEM((rows // BLOCK, BLOCK, features), jnp.bfloat16),
            pltpu.VMEM((pairs, 2, 2 * BLOCK, BLOCK), jnp.float32),
        ],
        compiler_params=params,
        name="mid",
    )(edge_q, coarse, state, first_in, second_in)
    early_in = [swapped(part, "head", step) for step, part in zip(away, early)]

    far = []
    known = 8
    if known < seq_count:
        group = [four, near] + [repool_outside(field) for field in threes_in]
        group = jnp.concatenate(group + [fours, fours_in], axis=1)
        while known < seq_count:
            fresh = swapped(group, "seq", known)
            far.append(fresh)
            group = jnp.concatenate([group, fresh], axis=1)
            known *= 2

    parts = [bf16(BLOCK, features) for _ in range(AHEAD)]
    *outs, level_four = pl.pallas_call(
        finish_kernel,
        out_shape=parts[2:]
        + [bf16(2 * SLAB, features) for _ in away]
        + [jax.ShapeDtypeStruct((2, rows // 16, features), jnp.float32)],
        scratch_shapes=[pltpu.VMEM((pairs, rows // 8, rows // 16 * seq_count), jnp.float32)],
        compiler_params=params,
        name="finish",
    )(four_q, fine, four, near, *threes_in, fours, fours_in, *far)
    whole_in = [swapped(part, "head", step) for step, part in zip(range(2, AHEAD), outs)]
    late_in = [swapped(part, "head", step) for step, part in zip(away, outs[AHEAD - 2 :])]
    own_part, next_part = pl.pallas_call(
        rest_kernel,
        out_shape=parts[:2],
        compiler_params=params,
        name="rest",
    )(fine, level_four)
    next_in = swapped(next_part, "head", 1)
    width = out_weight.shape[1]
    partial = pl.pallas_call(
        partial_kernel,
        out_shape=jax.ShapeDtypeStruct((BLOCK, width), jnp.float32),
        compiler_params=params,
        name="partial",
    )(own_part, out_weight)
    heavy = pl.CostEstimate(flops=2**32, bytes_accessed=2**20, transcendentals=0)
    widened = pl.pallas_call(
        widen_kernel,
        out_shape=[jax.ShapeDtypeStruct((BLOCK, features), jnp.float32) for _ in away],
        compiler_params=params,
        cost_estimate=pl.CostEstimate(flops=2**22, bytes_accessed=2**10, transcendentals=0),
        name="widen",
    )(*early_in)
    further = pl.pallas_call(
        further_kernel,
        out_shape=jax.ShapeDtypeStruct((BLOCK, width), jnp.float32),
        compiler_params=params,
        name="further",
    )(widened[0], partial, out_weight, *whole_in)
    rejoined = pl.pallas_call(
        rejoin_kernel,
        out_shape=[bf16(BLOCK, features) for _ in away],
        compiler_params=params,
        cost_estimate=heavy,
        name="rejoin",
    )(further, *widened, *late_in)
    chunk = 2 * PAIR
    result = pl.pallas_call(
        project_kernel,
        in_specs=[vmem] * (len(rejoined) + 3),
        out_specs=hbm,
        out_shape=bf16(BLOCK, width),
        scratch_shapes=[
            pltpu.VMEM((width // chunk, 2, BLOCK, PAIR), jnp.float32),
            pltpu.VMEM((width // chunk, BLOCK, chunk), jnp.bfloat16),
            pltpu.SemaphoreType.DMA((width // chunk,)),
        ],
        compiler_params=params,
        name="project",
    )(further, *rejoined, next_in, out_weight)
    return result[None]


def solution(mesh):
    return jax.shard_map(
        per_device,
        mesh=mesh,
        in_specs=(P(None, "seq", "head"), P(None, "seq", "head"), P(None, "seq", "head"), P()),
        out_specs=P(None, ("seq", "head"), None),
        check_vma=False,
    )
```

```python
import jax
import jax.numpy as jnp
from jax import lax
from jax.experimental import pallas as pl
from jax.experimental.pallas import tpu as pltpu
from jax.sharding import PartitionSpec as P

HD = 64
BLOCK = 128
LEVELS = 4
SLAB = 8
PAIR = 2 * HD

neg_fill = -1e30
root_half = 0.7071067811865476
log2_e = 1.4426950408889634
log2_scale = HD**-0.5 * log2_e
least_share = 2.0**-100
AHEAD = 2

FAN = 2**LEVELS


def slabs_of(scratch, block):
    return [scratch[pl.ds(BLOCK * block + j, SLAB, stride=FAN), :] for j in range(FAN)]


def pooled_slabs(slabs):
    return [
        ((low + high) * root_half).astype(jnp.bfloat16).astype(jnp.float32)
        for low, high in zip(slabs[0::2], slabs[1::2])
    ]


def joined(slabs):
    return jnp.concatenate(slabs, axis=0).astype(jnp.bfloat16)


def spill(source, scratch):
    for half in range(scratch.shape[0]):
        scratch[half] = source[:, half * PAIR : (half + 1) * PAIR].astype(jnp.float32)


def pool_kernel(
    k_hbm, v_hbm, k_ref, v_ref, first_ref, one_ref, two_ref, scratch, sems
):
    rows = k_ref.shape[0]
    blocks = rows // BLOCK
    arrivals = []
    for half in range(2):
        here = pl.ds(half * rows // 2, rows // 2)
        for which, (source, target) in enumerate(((k_hbm, k_ref), (v_hbm, v_ref))):
            copy = pltpu.make_async_copy(
                source.at[0, here, :], target.at[here, :], sems.at[which, half]
            )
            copy.start()
            for block in range(half * blocks // 2, (half + 1) * blocks // 2):
                arrivals.append((block, which, target, copy))
    even = lax.rem(lax.axis_index("seq"), 2) == 0
    for block, which, ref, copy in arrivals:
        if block % (blocks // 2) == 0:
            copy.wait()
        here = pl.ds(block * BLOCK, BLOCK)
        spill(ref.at[here, :], scratch.at[which, block])
        for half in range(scratch.shape[2]):
            lanes = pl.ds(half * PAIR, PAIR)
            one = pooled_slabs(slabs_of(scratch.at[which, block, half], 0))
            one_ref[which, pl.ds(block * BLOCK // 2, BLOCK // 2), lanes] = joined(one)
            two_ref[which, pl.ds(block * BLOCK // 4, BLOCK // 4), lanes] = joined(pooled_slabs(one))
    inner = rows // 4 - BLOCK // 4
    for which, ref in enumerate((k_ref, v_ref)):
        first_ref[which, :BLOCK, :] = jnp.where(even, ref[rows - BLOCK :, :], ref[:BLOCK, :])
        first_ref[which, BLOCK:, :] = jnp.where(
            even, two_ref[which, :inner, :], two_ref[which, BLOCK // 4 :, :]
        )


def repooled(field):
    rows, lanes = field.shape
    slabs = field.astype(jnp.float32).reshape(rows // (2 * SLAB), 2, SLAB, lanes)
    return ((slabs[:, 0] + slabs[:, 1]) * root_half).reshape(rows // 2, lanes).astype(jnp.bfloat16)


def deeper_kernel(k_ref, v_ref, two_ref, second_ref, three_ref, four_ref):
    rows = k_ref.shape[0]
    even = lax.rem(lax.axis_index("seq"), 2) == 0
    for which, ref in enumerate((k_ref, v_ref)):
        second_ref[which] = jnp.where(even, ref[:BLOCK, :], ref[rows - BLOCK :, :])
        three = repooled(two_ref[which])
        three_ref[which] = three
        four_ref[which] = repooled(three)


def repooled(field):
    rows, lanes = field.shape
    slabs = field.astype(jnp.float32).reshape(rows // (2 * SLAB), 2, SLAB, lanes)
    return ((slabs[:, 0] + slabs[:, 1]) * root_half).reshape(rows // 2, lanes).astype(jnp.bfloat16)


def score(queries, keys, hold, is_open=None):
    rows = queries.shape[0]
    low = lax.broadcasted_iota(jnp.int32, (rows, PAIR), 1) < HD
    zero = jnp.zeros_like(queries)
    both = jnp.concatenate([jnp.where(low, queries, zero), jnp.where(low, zero, queries)], axis=0)
    raw = lax.dot_general(both, keys, (((1,), (1,)), ((), ())), preferred_element_type=jnp.float32)
    if is_open is not None:
        raw = jnp.where(is_open, raw, neg_fill)
    hold[...] = raw
    return jnp.max(raw, axis=1, keepdims=True)


def weigh(hold, top, values):
    rows = top.shape[0] // 2
    low = lax.broadcasted_iota(jnp.int32, (rows, PAIR), 1) < HD
    weights = jnp.exp2((hold[...] - top) * log2_scale).astype(jnp.bfloat16)
    result = jnp.dot(weights, values, preferred_element_type=jnp.float32)
    return (
        log2_scale * jnp.where(low, top[:rows], top[rows:]),
        jnp.where(low, result[:rows, :PAIR], result[rows:, :PAIR]),
        jnp.where(low, result[:rows, PAIR:], result[rows:, PAIR:]),
    )


def merged(fine, coarse):
    top = jnp.maximum(fine[0], coarse[0])
    keep = jnp.exp2(fine[0] - top)
    join = jnp.exp2(coarse[0] - top)
    return top, fine[1] * keep + coarse[1] * join, fine[2] * keep + coarse[2] * join


def doubled(field):
    rows, lanes = field.shape
    slabs = field.reshape(rows // SLAB, 1, SLAB, lanes)
    return jnp.broadcast_to(slabs, (rows // SLAB, 2, SLAB, lanes)).reshape(2 * rows, lanes)


def with_ones(values, weight=1.0):
    if weight != 1.0:
        values = values * jnp.bfloat16(weight)
    return jnp.concatenate([values, jnp.full(values.shape, weight, jnp.bfloat16)], axis=1)


def local_kernel(
    q_ref, k_ref, v_ref, one_ref, four_ref, edge_q, two_q, three_q, four_q, state,
    scratch, near_hold, coarse_hold,
):
    rows = q_ref.shape[0]
    blocks = rows // BLOCK
    pairs = scratch.shape[0]
    spill(q_ref, scratch)
    fine, one_q = [], []
    for pair in range(pairs):
        lanes = pl.ds(pair * PAIR, PAIR)
        ladder = [[], [], [], [], []]
        for block in range(blocks):
            slabs = slabs_of(scratch.at[pair], block)
            ladder[0].append(joined(slabs))
            for level in range(1, LEVELS + 1):
                slabs = pooled_slabs(slabs)
                ladder[level] += slabs
        edge_q[0, :, lanes] = ladder[0][0]
        edge_q[1, :, lanes] = ladder[0][-1]
        two_q[:, lanes] = joined(ladder[2])
        three_q[:, lanes] = joined(ladder[3])
        four_q[:, lanes] = joined(ladder[4])
        fine.append(ladder[0])
        one_q.append([joined(ladder[1][n : n + FAN]) for n in range(0, len(ladder[1]), FAN)])
    windows = [(max(n - 1, 0) * BLOCK, min(n + 2, blocks) * BLOCK) for n in range(blocks)]
    tops = {}
    for pair in range(pairs):
        lanes = pl.ds(pair * PAIR, PAIR)
        for half in range(blocks // 2):
            there = pl.ds((half ^ 1) * BLOCK, BLOCK)
            tops[pair, half] = score(
                one_q[pair][half], one_ref[0, there, lanes], coarse_hold.at[pair, half]
            )
            for block in (2 * half, 2 * half + 1):
                low, high = windows[block]
                hold = near_hold.at[pair, block, :, : high - low]
                tops[pair, half, block] = score(fine[pair][block], k_ref[low:high, lanes], hold)
    for pair in range(pairs):
        lanes = pl.ds(pair * PAIR, PAIR)
        for half in range(blocks // 2):
            there = pl.ds((half ^ 1) * BLOCK, BLOCK)
            coarse = weigh(
                coarse_hold.at[pair, half], tops[pair, half], with_ones(one_ref[1, there, lanes])
            )
            for block in (2 * half, 2 * half + 1):
                low, high = windows[block]
                hold = near_hold.at[pair, block, :, : high - low]
                near = weigh(hold, tops[pair, half, block], with_ones(v_ref[low:high, lanes]))
                part = slice((block - 2 * half) * BLOCK // 2, (block - 2 * half + 1) * BLOCK // 2)
                done = merged(near, [doubled(x[part]) for x in coarse])
                for index, field in enumerate(done):
                    state[index, block * BLOCK : (block + 1) * BLOCK, lanes] = field


def join_kernel(four_ref, six_ref, query_ref, out):
    sixteenth = four_ref.shape[1]
    out[:, :sixteenth, :] = four_ref[...]
    out[:, sixteenth:, :] = six_ref[...]


def coarse_kernel(
    two_q, three_q, first_ref, three_a, three_b, coarse, near_ref, scratch, two_ref, two_hold, three_hold
):
    inner = first_ref.shape[1] - BLOCK
    pairs = scratch.shape[1]
    two_ref[:, :inner, :] = first_ref[:, BLOCK:, :]
    for which in range(2):
        spill(first_ref.at[which, pl.ds(0, BLOCK), :], scratch.at[which])
        for half in range(pairs):
            lanes = pl.ds(half * PAIR, PAIR)
            slabs = slabs_of(scratch.at[which, half], 0)
            two_ref[which, inner:, lanes] = joined(pooled_slabs(pooled_slabs(slabs)))
        near_ref[which] = repooled(repooled(two_ref[which]))
    steps = {}
    for pair in range(pairs):
        lanes = pl.ds(pair * PAIR, PAIR)
        three = [
            jnp.concatenate([three_a[which, :, lanes], three_b[which, :, lanes]], axis=0)
            for which in range(2)
        ]
        steps[pair, 3] = (
            score(three_q[:, lanes], three[0], three_hold.at[pair]), with_ones(three[1])
        )
        steps[pair, 2] = (
            score(two_q[:, lanes], two_ref[0, :, lanes], two_hold.at[pair]),
            with_ones(two_ref[1, :, lanes]),
        )
    for pair in range(pairs):
        three = weigh(three_hold.at[pair], *steps[pair, 3])
        two = merged(weigh(two_hold.at[pair], *steps[pair, 2]), [doubled(x) for x in three])
        for index, field in enumerate(two):
            coarse[index, :, pl.ds(pair * PAIR, PAIR)] = field


def mid_kernel(edge_q, coarse, state, first_ref, second_ref, fine, *refs):
    outs, (ready, holds) = refs[:-2], refs[-2:]
    own = lax.axis_index("head")
    rows = state.shape[1]
    blocks = rows // BLOCK
    position = lax.axis_index("seq")
    last = lax.axis_size("seq") - 1
    even = lax.rem(position, 2) == 0
    opens = (position > 0, position < last)
    pairs = holds.shape[0]
    steps = {}
    for pair in range(pairs):
        lanes = pl.ds(pair * PAIR, PAIR)
        inner = [first_ref[which, :BLOCK, lanes] for which in range(2)]
        outer = [second_ref[which, :, lanes] for which in range(2)]
        for side in range(2):
            halo = [
                jnp.where(even, *((outer[which], inner[which])[:: 1 - 2 * side]))
                for which in range(2)
            ]
            steps[pair, side] = (
                score(edge_q[side, :, lanes], halo[0], holds.at[pair, side], opens[side]),
                with_ones(halo[1]),
            )
    for pair in range(pairs):
        lanes = pl.ds(pair * PAIR, PAIR)
        for block in range(blocks):
            here = slice(block * BLOCK, (block + 1) * BLOCK)
            quarter = slice(block * BLOCK // 4, (block + 1) * BLOCK // 4)
            done = merged(
                [state[index, here, lanes] for index in range(3)],
                [doubled(doubled(coarse[index, quarter, lanes])) for index in range(3)],
            )
            for side, edge in enumerate((0, blocks - 1)):
                if block == edge:
                    done = merged(done, weigh(holds.at[pair, side], *steps[pair, side]))
            result = done[1] / done[2]
            fine[0, here, lanes] = result
            fine[1, here, lanes] = done[0] + jnp.log(done[2]) * log2_e
            ready[block, :, lanes] = result.astype(jnp.bfloat16)
    for step, out in enumerate(outs, AHEAD):
        out[...] = ready[own ^ step]


def repeated(field):
    return jnp.concatenate([field] * FAN, axis=0)


def finish_blocks(fine, coarse, steps):
    own = lax.axis_index("head")
    features = fine.shape[2]
    for step, out in steps:
        block = own ^ step
        here = pl.ds(pl.multiple_of(block * BLOCK, BLOCK), BLOCK)
        few = pl.ds(pl.multiple_of(block * SLAB, SLAB), SLAB)
        shares = []
        for pair in range(features // PAIR):
            lanes = pl.ds(pair * PAIR, PAIR)
            fine_sum, coarse_sum = fine[1, here, lanes], repeated(coarse[1, few, lanes])
            if step < AHEAD:
                keep = 1.0 / (1.0 + jnp.exp2(coarse_sum - fine_sum))
                ours, theirs = fine[0, here, lanes], repeated(coarse[0, few, lanes])
                out[:, lanes] = (theirs + keep * (ours - theirs)).astype(jnp.bfloat16)
            else:
                ratio = jnp.exp2(-jnp.abs(fine_sum - coarse_sum))
                less = jnp.maximum(ratio / (1.0 + ratio), least_share)
                shares.append(jnp.where(fine_sum <= coarse_sum, less, -less).astype(jnp.bfloat16))
        if step >= AHEAD:
            pick = lax.broadcasted_iota(jnp.int32, (2 * SLAB, features), 1) == HD * (
                lax.broadcasted_iota(jnp.int32, (2 * SLAB, features), 0)
            )
            by_head = lax.dot_general(
                pick.astype(jnp.bfloat16),
                jnp.concatenate(shares, axis=1),
                (((1,), (1,)), ((), ())),
                preferred_element_type=jnp.float32,
            )[:SLAB]
            blank = jnp.zeros((SLAB, features - BLOCK), jnp.float32)
            out[...] = jnp.concatenate(
                [coarse[0, few, :], jnp.concatenate([by_head, blank], axis=1)], axis=0
            ).astype(jnp.bfloat16)


def finish_kernel(
    four_q, fine, four_ref, near_ref, three_a, three_b, fours_a, fours_b, *refs
):
    refs, (coarse, four_hold) = refs[:-2], refs[-2:]
    steps_out = range(2, lax.axis_size("head"))
    far, outs = refs[: -len(steps_out)], refs[-len(steps_out) :]
    pairs = four_q.shape[1] // PAIR
    steps = {}
    for pair in range(pairs):
        lanes = pl.ds(pair * PAIR, PAIR)
        ours, theirs, beyond = [], [], []
        for which in range(2):
            ours.append(
                [four_ref[which, :, lanes], near_ref[which, :, lanes]]
                + [repooled(field[which, :, lanes]) for field in (three_a, three_b)]
            )
            theirs.append([field[which, :, lanes] for field in (fours_a, fours_b)])
            beyond.append([field[which, :, lanes] for field in far])
        steps[pair] = (
            score(
                four_q[:, lanes],
                jnp.concatenate(ours[0] + theirs[0] + beyond[0], axis=0),
                four_hold.at[pair],
            ),
            jnp.concatenate(
                [with_ones(field) for field in ours[1]]
                + [with_ones(field, 2.0) for field in theirs[1]]
                + [with_ones(field) for field in beyond[1]],
                axis=0,
            ),
        )
    for pair in range(pairs):
        lanes = pl.ds(pair * PAIR, PAIR)
        top, numer, rowsum = weigh(four_hold.at[pair], *steps[pair])
        coarse[0, :, lanes] = numer / rowsum
        coarse[1, :, lanes] = top + jnp.log(rowsum) * log2_e
    finish_blocks(fine, coarse, zip(steps_out, outs))


def rest_kernel(fine, coarse, *outs):
    finish_blocks(fine, coarse, enumerate(outs))


def rejoin_kernel(partial_ref, *refs):
    outs = refs[len(refs) // 3 * 2 :]
    for early, late_ref, out in zip(refs, refs[len(outs) :], outs):
        features = early.shape[1]
        late = late_ref[...].astype(jnp.float32)
        spread = lax.broadcasted_iota(jnp.int32, (SLAB, features), 1) // HD == (
            lax.broadcasted_iota(jnp.int32, (SLAB, features), 0)
        )
        signed = lax.dot_general(
            late[SLAB:, :BLOCK].astype(jnp.bfloat16),
            spread.astype(jnp.bfloat16),
            (((0,), (0,)), ((), ())),
            preferred_element_type=jnp.float32,
        )
        keep = jnp.where(signed >= 0, signed, 1.0 + signed)
        join = jnp.where(signed >= 0, 1.0 - signed, -signed)
        result = keep * early[...] + join * repeated(late[:SLAB])
        out[...] = result.astype(jnp.bfloat16)


def widen_kernel(*refs):
    half = len(refs) // 2
    for ref, out in zip(refs[:half], refs[half:]):
        out[...] = ref[...].astype(jnp.float32)


def partial_kernel(own_ref, weight_ref, out_ref):
    features = own_ref.shape[1]
    start = pl.multiple_of(lax.axis_index("head") * features, features)
    out_ref[...] = jnp.dot(
        own_ref[...], weight_ref[pl.ds(start, features), :], preferred_element_type=jnp.float32
    )


def project_kernel(partial_ref, *refs):
    parts, (weight_ref, out_hbm, scratch, staged, sems) = refs[:-5], refs[-5:]
    own = lax.axis_index("head")
    features = parts[0].shape[1]
    chunk = staged.shape[2]
    copies = []
    for index in range(staged.shape[0]):
        columns = pl.ds(index * chunk, chunk)
        total = partial_ref[:, columns]
        for step, part in zip([*range(AHEAD, AHEAD + len(parts) - 1), 1], parts):
            start = pl.multiple_of((own ^ step) * features, features)
            total += jnp.dot(
                part[...],
                weight_ref[pl.ds(start, features), columns],
                preferred_element_type=jnp.float32,
            )
        for half in range(chunk // PAIR):
            lanes = slice(half * PAIR, (half + 1) * PAIR)
            scratch[index, half] = total[:, lanes]
            for i in range(SLAB):
                staged[index, i * FAN : (i + 1) * FAN, lanes] = scratch[
                    index, half, pl.ds(i, FAN, stride=SLAB), :
                ].astype(jnp.bfloat16)
        copy = pltpu.make_async_copy(staged.at[index], out_hbm.at[:, columns], sems.at[index])
        copy.start()
        copies.append(copy)
    for copy in copies:
        copy.wait()


def repool_outside(field):
    which, rows, lanes = field.shape
    slabs = field.astype(jnp.float32).reshape(which, rows // (2 * SLAB), 2, SLAB, lanes)
    sums = (slabs[:, :, 0] + slabs[:, :, 1]) * root_half
    return sums.reshape(which, rows // 2, lanes).astype(jnp.bfloat16)


def swapped(block, axis, mask):
    return lax.ppermute(block, axis, [(i, i ^ mask) for i in range(lax.axis_size(axis))])


def across(block):
    count, heads = lax.axis_size("seq"), lax.axis_size("head")
    route = []
    for seq in range(count):
        end = seq in (0, count - 1)
        other = seq if end else seq + 1 if seq % 2 else seq - 1
        for head in range(heads):
            route.append((seq * heads + head, other * heads + (head ^ 1 if end else head)))
    return lax.ppermute(block, ("seq", "head"), route)


def per_device(queries, key_vectors, value_vectors, out_weight):
    rows, features = queries.shape[1:]
    key_vectors, value_vectors = [
        pltpu.with_memory_space_constraint(x, pltpu.HBM) for x in (key_vectors, value_vectors)
    ]
    pairs = features // PAIR
    seq_count, head_count = lax.axis_size("seq"), lax.axis_size("head")
    bf16 = lambda *shape: jax.ShapeDtypeStruct(shape, jnp.bfloat16)
    params = pltpu.CompilerParams(vmem_limit_bytes=32 * 1024 * 1024)

    hbm = pl.BlockSpec(memory_space=pltpu.HBM)
    vmem = pl.BlockSpec(memory_space=pltpu.VMEM)
    keys, values, first, one, two = pl.pallas_call(
        pool_kernel,
        in_specs=[hbm] * 2,
        out_shape=[
            bf16(rows, features),
            bf16(rows, features),
            bf16(2, BLOCK + rows // 4 - BLOCK // 4, features),
            bf16(2, rows // 2, features),
            bf16(2, rows // 4, features),
        ],
        scratch_shapes=[
            pltpu.VMEM((2, rows // BLOCK, pairs, BLOCK, PAIR), jnp.float32),
            pltpu.SemaphoreType.DMA((2, 2)),
        ],
        compiler_params=params,
        name="pool",
    )(key_vectors, value_vectors)
    second, three, four = pl.pallas_call(
        deeper_kernel,
        out_shape=[
            bf16(2, BLOCK, features),
            bf16(2, rows // 8, features),
            bf16(2, rows // 16, features),
        ],
        compiler_params=params,
        cost_estimate=pl.CostEstimate(flops=2**31, bytes_accessed=2**23, transcendentals=0),
        name="deeper",
    )(keys, values, two)

    first_in = swapped(first, "seq", 1)
    second_in = across(second)
    four_in = swapped(four, "seq", 4)
    six_in = swapped(four, "seq", 6)
    threes_in = [swapped(three, "seq", mask) for mask in (3, 2)]
    edge_q, two_q, three_q, four_q, state = pl.pallas_call(
        local_kernel,
        out_shape=[
            bf16(2, BLOCK, features),
            bf16(rows // 4, features),
            bf16(rows // 8, features),
            bf16(rows // 16, features),
            jax.ShapeDtypeStruct((3, rows, features), jnp.float32),
        ],
        scratch_shapes=[
            pltpu.VMEM((pairs, rows, PAIR), jnp.float32),
            pltpu.VMEM((pairs, rows // BLOCK, 2 * BLOCK, 3 * BLOCK), jnp.float32),
            pltpu.VMEM((pairs, rows // BLOCK // 2, 2 * BLOCK, BLOCK), jnp.float32),
        ],
        compiler_params=params,
        name="local",
    )(queries[0], keys, values, one, four_in)

    fours = pl.pallas_call(
        join_kernel,
        out_shape=bf16(2, rows // 8, features),
        compiler_params=params,
        cost_estimate=pl.CostEstimate(flops=2**29, bytes_accessed=2**20, transcendentals=0),
        name="join",
    )(four_in, six_in, four_q)
    fours_in = swapped(fours, "seq", 1)
    coarse, near = pl.pallas_call(
        coarse_kernel,
        out_shape=[
            jax.ShapeDtypeStruct((3, rows // 4, features), jnp.float32),
            bf16(2, rows // 16, features),
        ],
        scratch_shapes=[
            pltpu.VMEM((2, pairs, BLOCK, PAIR), jnp.float32),
            pltpu.VMEM((2, rows // 4, features), jnp.bfloat16),
            pltpu.VMEM((pairs, rows // 2, BLOCK), jnp.float32),
            pltpu.VMEM((pairs, rows // 4, BLOCK), jnp.float32),
        ],
        compiler_params=params,
        cost_estimate=pl.CostEstimate(flops=2**31, bytes_accessed=2**21, transcendentals=0),
        name="coarse",
    )(two_q, three_q, first_in, *threes_in)
    away = range(AHEAD, head_count)
    fine, *early = pl.pallas_call(
        mid_kernel,
        out_shape=[jax.ShapeDtypeStruct((2, rows, features), jnp.float32)]
        + [bf16(BLOCK, features) for _ in away],
        scratch_shapes=[
            pltpu.VMEM((rows // BLOCK, BLOCK, features), jnp.bfloat16),
            pltpu.VMEM((pairs, 2, 2 * BLOCK, BLOCK), jnp.float32),
        ],
        compiler_params=params,
        name="mid",
    )(edge_q, coarse, state, first_in, second_in)
    early_in = [swapped(part, "head", step) for step, part in zip(away, early)]

    far = []
    known = 8
    if known < seq_count:
        group = [four, near] + [repool_outside(field) for field in threes_in]
        group = jnp.concatenate(group + [fours, fours_in], axis=1)
        while known < seq_count:
            fresh = swapped(group, "seq", known)
            far.append(fresh)
            group = jnp.concatenate([group, fresh], axis=1)
            known *= 2

    parts = [bf16(BLOCK, features) for _ in range(AHEAD)]
    *outs, level_four = pl.pallas_call(
        finish_kernel,
        out_shape=[bf16(2 * SLAB, features) for _ in away]
        + [jax.ShapeDtypeStruct((2, rows // 16, features), jnp.float32)],
        scratch_shapes=[pltpu.VMEM((pairs, rows // 8, rows // 16 * seq_count), jnp.float32)],
        compiler_params=params,
        name="finish",
    )(four_q, fine, four, near, *threes_in, fours, fours_in, *far)
    late_in = [swapped(part, "head", step) for step, part in zip(away, outs)]
    own_part, next_part = pl.pallas_call(
        rest_kernel,
        out_shape=parts[:2],
        compiler_params=params,
        name="rest",
    )(fine, level_four)
    next_in = swapped(next_part, "head", 1)
    width = out_weight.shape[1]
    partial = pl.pallas_call(
        partial_kernel,
        out_shape=jax.ShapeDtypeStruct((BLOCK, width), jnp.float32),
        compiler_params=params,
        name="partial",
    )(own_part, out_weight)
    heavy = pl.CostEstimate(flops=2**32, bytes_accessed=2**20, transcendentals=0)
    widened = pl.pallas_call(
        widen_kernel,
        out_shape=[jax.ShapeDtypeStruct((BLOCK, features), jnp.float32) for _ in away],
        compiler_params=params,
        cost_estimate=pl.CostEstimate(flops=2**22, bytes_accessed=2**10, transcendentals=0),
        name="widen",
    )(*early_in[::-1])
    rejoined = pl.pallas_call(
        rejoin_kernel,
        out_shape=[bf16(BLOCK, features) for _ in away],
        compiler_params=params,
        cost_estimate=heavy,
        name="rejoin",
    )(partial, *widened, *late_in[::-1])
    chunk = 2 * PAIR
    result = pl.pallas_call(
        project_kernel,
        in_specs=[vmem] * (len(rejoined) + 3),
        out_specs=hbm,
        out_shape=bf16(BLOCK, width),
        scratch_shapes=[
            pltpu.VMEM((width // chunk, 2, BLOCK, PAIR), jnp.float32),
            pltpu.VMEM((width // chunk, BLOCK, chunk), jnp.bfloat16),
            pltpu.SemaphoreType.DMA((width // chunk,)),
        ],
        compiler_params=params,
        name="project",
    )(partial, *rejoined[::-1], next_in, out_weight)
    return result[None]


def solution(mesh):
    return jax.shard_map(
        per_device,
        mesh=mesh,
        in_specs=(P(None, "seq", "head"), P(None, "seq", "head"), P(None, "seq", "head"), P()),
        out_specs=P(None, ("seq", "head"), None),
        check_vma=False,
    )
```

```python
import jax
import jax.numpy as jnp
from jax import lax
from jax.experimental import pallas as pl
from jax.experimental.pallas import tpu as pltpu
from jax.sharding import PartitionSpec as P

HD = 64
BLOCK = 128
LEVELS = 4
SLAB = 8
PAIR = 2 * HD

neg_fill = -1e30
root_half = 0.7071067811865476
log2_e = 1.4426950408889634
log2_scale = HD**-0.5 * log2_e
least_share = 2.0**-100
AHEAD = 3

FAN = 2**LEVELS


def slabs_of(scratch, block):
    return [scratch[pl.ds(BLOCK * block + j, SLAB, stride=FAN), :] for j in range(FAN)]


def pooled_slabs(slabs):
    return [
        ((low + high) * root_half).astype(jnp.bfloat16).astype(jnp.float32)
        for low, high in zip(slabs[0::2], slabs[1::2])
    ]


def joined(slabs):
    return jnp.concatenate(slabs, axis=0).astype(jnp.bfloat16)


def spill(source, scratch):
    for half in range(scratch.shape[0]):
        scratch[half] = source[:, half * PAIR : (half + 1) * PAIR].astype(jnp.float32)


def pool_kernel(
    k_hbm, v_hbm, k_ref, v_ref, first_ref, one_ref, two_ref, scratch, sems
):
    rows = k_ref.shape[0]
    blocks = rows // BLOCK
    arrivals = []
    for half in range(2):
        here = pl.ds(half * rows // 2, rows // 2)
        for which, (source, target) in enumerate(((k_hbm, k_ref), (v_hbm, v_ref))):
            copy = pltpu.make_async_copy(
                source.at[0, here, :], target.at[here, :], sems.at[which, half]
            )
            copy.start()
            for block in range(half * blocks // 2, (half + 1) * blocks // 2):
                arrivals.append((block, which, target, copy))
    even = lax.rem(lax.axis_index("seq"), 2) == 0
    for block, which, ref, copy in arrivals:
        if block % (blocks // 2) == 0:
            copy.wait()
        here = pl.ds(block * BLOCK, BLOCK)
        spill(ref.at[here, :], scratch.at[which, block])
        for half in range(scratch.shape[2]):
            lanes = pl.ds(half * PAIR, PAIR)
            one = pooled_slabs(slabs_of(scratch.at[which, block, half], 0))
            one_ref[which, pl.ds(block * BLOCK // 2, BLOCK // 2), lanes] = joined(one)
            two_ref[which, pl.ds(block * BLOCK // 4, BLOCK // 4), lanes] = joined(pooled_slabs(one))
    inner = rows // 4 - BLOCK // 4
    for which, ref in enumerate((k_ref, v_ref)):
        first_ref[which, :BLOCK, :] = jnp.where(even, ref[rows - BLOCK :, :], ref[:BLOCK, :])
        first_ref[which, BLOCK:, :] = jnp.where(
            even, two_ref[which, :inner, :], two_ref[which, BLOCK // 4 :, :]
        )


def repooled(field):
    rows, lanes = field.shape
    slabs = field.astype(jnp.float32).reshape(rows // (2 * SLAB), 2, SLAB, lanes)
    return ((slabs[:, 0] + slabs[:, 1]) * root_half).reshape(rows // 2, lanes).astype(jnp.bfloat16)


def deeper_kernel(k_ref, v_ref, two_ref, second_ref, three_ref, four_ref):
    rows = k_ref.shape[0]
    even = lax.rem(lax.axis_index("seq"), 2) == 0
    for which, ref in enumerate((k_ref, v_ref)):
        second_ref[which] = jnp.where(even, ref[:BLOCK, :], ref[rows - BLOCK :, :])
        three = repooled(two_ref[which])
        three_ref[which] = three
        four_ref[which] = repooled(three)


def repooled(field):
    rows, lanes = field.shape
    slabs = field.astype(jnp.float32).reshape(rows // (2 * SLAB), 2, SLAB, lanes)
    return ((slabs[:, 0] + slabs[:, 1]) * root_half).reshape(rows // 2, lanes).astype(jnp.bfloat16)


def score(queries, keys, hold, is_open=None):
    rows = queries.shape[0]
    low = lax.broadcasted_iota(jnp.int32, (rows, PAIR), 1) < HD
    zero = jnp.zeros_like(queries)
    both = jnp.concatenate([jnp.where(low, queries, zero), jnp.where(low, zero, queries)], axis=0)
    raw = lax.dot_general(both, keys, (((1,), (1,)), ((), ())), preferred_element_type=jnp.float32)
    if is_open is not None:
        raw = jnp.where(is_open, raw, neg_fill)
    hold[...] = raw
    return jnp.max(raw, axis=1, keepdims=True)


def weigh(hold, top, values):
    rows = top.shape[0] // 2
    low = lax.broadcasted_iota(jnp.int32, (rows, PAIR), 1) < HD
    weights = jnp.exp2((hold[...] - top) * log2_scale).astype(jnp.bfloat16)
    result = jnp.dot(weights, values, preferred_element_type=jnp.float32)
    return (
        log2_scale * jnp.where(low, top[:rows], top[rows:]),
        jnp.where(low, result[:rows, :PAIR], result[rows:, :PAIR]),
        jnp.where(low, result[:rows, PAIR:], result[rows:, PAIR:]),
    )


def merged(fine, coarse):
    top = jnp.maximum(fine[0], coarse[0])
    keep = jnp.exp2(fine[0] - top)
    join = jnp.exp2(coarse[0] - top)
    return top, fine[1] * keep + coarse[1] * join, fine[2] * keep + coarse[2] * join


def doubled(field):
    rows, lanes = field.shape
    slabs = field.reshape(rows // SLAB, 1, SLAB, lanes)
    return jnp.broadcast_to(slabs, (rows // SLAB, 2, SLAB, lanes)).reshape(2 * rows, lanes)


def with_ones(values, weight=1.0):
    if weight != 1.0:
        values = values * jnp.bfloat16(weight)
    return jnp.concatenate([values, jnp.full(values.shape, weight, jnp.bfloat16)], axis=1)


def local_kernel(
    q_ref, k_ref, v_ref, one_ref, four_ref, edge_q, two_q, three_q, four_q, state,
    scratch, near_hold, coarse_hold,
):
    rows = q_ref.shape[0]
    blocks = rows // BLOCK
    pairs = scratch.shape[0]
    spill(q_ref, scratch)
    fine, one_q = [], []
    for pair in range(pairs):
        lanes = pl.ds(pair * PAIR, PAIR)
        ladder = [[], [], [], [], []]
        for block in range(blocks):
            slabs = slabs_of(scratch.at[pair], block)
            ladder[0].append(joined(slabs))
            for level in range(1, LEVELS + 1):
                slabs = pooled_slabs(slabs)
                ladder[level] += slabs
        edge_q[0, :, lanes] = ladder[0][0]
        edge_q[1, :, lanes] = ladder[0][-1]
        two_q[:, lanes] = joined(ladder[2])
        three_q[:, lanes] = joined(ladder[3])
        four_q[:, lanes] = joined(ladder[4])
        fine.append(ladder[0])
        one_q.append([joined(ladder[1][n : n + FAN]) for n in range(0, len(ladder[1]), FAN)])
    windows = [(max(n - 1, 0) * BLOCK, min(n + 2, blocks) * BLOCK) for n in range(blocks)]
    tops = {}
    for pair in range(pairs):
        lanes = pl.ds(pair * PAIR, PAIR)
        for half in range(blocks // 2):
            there = pl.ds((half ^ 1) * BLOCK, BLOCK)
            tops[pair, half] = score(
                one_q[pair][half], one_ref[0, there, lanes], coarse_hold.at[pair, half]
            )
            for block in (2 * half, 2 * half + 1):
                low, high = windows[block]
                hold = near_hold.at[pair, block, :, : high - low]
                tops[pair, half, block] = score(fine[pair][block], k_ref[low:high, lanes], hold)
    for pair in range(pairs):
        lanes = pl.ds(pair * PAIR, PAIR)
        for half in range(blocks // 2):
            there = pl.ds((half ^ 1) * BLOCK, BLOCK)
            coarse = weigh(
                coarse_hold.at[pair, half], tops[pair, half], with_ones(one_ref[1, there, lanes])
            )
            for block in (2 * half, 2 * half + 1):
                low, high = windows[block]
                hold = near_hold.at[pair, block, :, : high - low]
                near = weigh(hold, tops[pair, half, block], with_ones(v_ref[low:high, lanes]))
                part = slice((block - 2 * half) * BLOCK // 2, (block - 2 * half + 1) * BLOCK // 2)
                done = merged(near, [doubled(x[part]) for x in coarse])
                for index, field in enumerate(done):
                    state[index, block * BLOCK : (block + 1) * BLOCK, lanes] = field


def join_kernel(four_ref, six_ref, query_ref, out):
    sixteenth = four_ref.shape[1]
    out[:, :sixteenth, :] = four_ref[...]
    out[:, sixteenth:, :] = six_ref[...]


def coarse_kernel(
    two_q, three_q, first_ref, three_a, three_b, coarse, near_ref, scratch, two_ref, two_hold, three_hold
):
    inner = first_ref.shape[1] - BLOCK
    pairs = scratch.shape[1]
    two_ref[:, :inner, :] = first_ref[:, BLOCK:, :]
    for which in range(2):
        spill(first_ref.at[which, pl.ds(0, BLOCK), :], scratch.at[which])
        for half in range(pairs):
            lanes = pl.ds(half * PAIR, PAIR)
            slabs = slabs_of(scratch.at[which, half], 0)
            two_ref[which, inner:, lanes] = joined(pooled_slabs(pooled_slabs(slabs)))
        near_ref[which] = repooled(repooled(two_ref[which]))
    steps = {}
    for pair in range(pairs):
        lanes = pl.ds(pair * PAIR, PAIR)
        three = [
            jnp.concatenate([three_a[which, :, lanes], three_b[which, :, lanes]], axis=0)
            for which in range(2)
        ]
        steps[pair, 3] = (
            score(three_q[:, lanes], three[0], three_hold.at[pair]), with_ones(three[1])
        )
        steps[pair, 2] = (
            score(two_q[:, lanes], two_ref[0, :, lanes], two_hold.at[pair]),
            with_ones(two_ref[1, :, lanes]),
        )
    for pair in range(pairs):
        three = weigh(three_hold.at[pair], *steps[pair, 3])
        two = merged(weigh(two_hold.at[pair], *steps[pair, 2]), [doubled(x) for x in three])
        for index, field in enumerate(two):
            coarse[index, :, pl.ds(pair * PAIR, PAIR)] = field


def mid_kernel(edge_q, coarse, state, first_ref, second_ref, fine, *refs):
    outs, (ready, holds) = refs[:-2], refs[-2:]
    own = lax.axis_index("head")
    rows = state.shape[1]
    blocks = rows // BLOCK
    position = lax.axis_index("seq")
    last = lax.axis_size("seq") - 1
    even = lax.rem(position, 2) == 0
    opens = (position > 0, position < last)
    pairs = holds.shape[0]
    steps = {}
    for pair in range(pairs):
        lanes = pl.ds(pair * PAIR, PAIR)
        inner = [first_ref[which, :BLOCK, lanes] for which in range(2)]
        outer = [second_ref[which, :, lanes] for which in range(2)]
        for side in range(2):
            halo = [
                jnp.where(even, *((outer[which], inner[which])[:: 1 - 2 * side]))
                for which in range(2)
            ]
            steps[pair, side] = (
                score(edge_q[side, :, lanes], halo[0], holds.at[pair, side], opens[side]),
                with_ones(halo[1]),
            )
    for pair in range(pairs):
        lanes = pl.ds(pair * PAIR, PAIR)
        for block in range(blocks):
            here = slice(block * BLOCK, (block + 1) * BLOCK)
            quarter = slice(block * BLOCK // 4, (block + 1) * BLOCK // 4)
            done = merged(
                [state[index, here, lanes] for index in range(3)],
                [doubled(doubled(coarse[index, quarter, lanes])) for index in range(3)],
            )
            for side, edge in enumerate((0, blocks - 1)):
                if block == edge:
                    done = merged(done, weigh(holds.at[pair, side], *steps[pair, side]))
            result = done[1] / done[2]
            fine[0, here, lanes] = result
            fine[1, here, lanes] = done[0] + jnp.log(done[2]) * log2_e
            ready[block, :, lanes] = result.astype(jnp.bfloat16)
    for step, out in enumerate(outs, AHEAD):
        out[...] = ready[own ^ step]


def repeated(field):
    return jnp.concatenate([field] * FAN, axis=0)


def finish_blocks(fine, coarse, steps):
    own = lax.axis_index("head")
    features = fine.shape[2]
    for step, out in steps:
        block = own ^ step
        here = pl.ds(pl.multiple_of(block * BLOCK, BLOCK), BLOCK)
        few = pl.ds(pl.multiple_of(block * SLAB, SLAB), SLAB)
        shares = []
        for pair in range(features // PAIR):
            lanes = pl.ds(pair * PAIR, PAIR)
            fine_sum, coarse_sum = fine[1, here, lanes], repeated(coarse[1, few, lanes])
            if step < AHEAD:
                keep = 1.0 / (1.0 + jnp.exp2(coarse_sum - fine_sum))
                ours, theirs = fine[0, here, lanes], repeated(coarse[0, few, lanes])
                out[:, lanes] = (theirs + keep * (ours - theirs)).astype(jnp.bfloat16)
            else:
                ratio = jnp.exp2(-jnp.abs(fine_sum - coarse_sum))
                less = jnp.maximum(ratio / (1.0 + ratio), least_share)
                shares.append(jnp.where(fine_sum <= coarse_sum, less, -less).astype(jnp.bfloat16))
        if step >= AHEAD:
            pick = lax.broadcasted_iota(jnp.int32, (2 * SLAB, features), 1) == HD * (
                lax.broadcasted_iota(jnp.int32, (2 * SLAB, features), 0)
            )
            by_head = lax.dot_general(
                pick.astype(jnp.bfloat16),
                jnp.concatenate(shares, axis=1),
                (((1,), (1,)), ((), ())),
                preferred_element_type=jnp.float32,
            )[:SLAB]
            blank = jnp.zeros((SLAB, features - BLOCK), jnp.float32)
            out[...] = jnp.concatenate(
                [coarse[0, few, :], jnp.concatenate([by_head, blank], axis=1)], axis=0
            ).astype(jnp.bfloat16)


def finish_kernel(
    four_q, fine, four_ref, near_ref, three_a, three_b, fours_a, fours_b, *refs
):
    refs, (coarse, four_hold) = refs[:-2], refs[-2:]
    steps_out = range(2, lax.axis_size("head"))
    far, outs = refs[: -len(steps_out)], refs[-len(steps_out) :]
    pairs = four_q.shape[1] // PAIR
    steps = {}
    for pair in range(pairs):
        lanes = pl.ds(pair * PAIR, PAIR)
        ours, theirs, beyond = [], [], []
        for which in range(2):
            ours.append(
                [four_ref[which, :, lanes], near_ref[which, :, lanes]]
                + [repooled(field[which, :, lanes]) for field in (three_a, three_b)]
            )
            theirs.append([field[which, :, lanes] for field in (fours_a, fours_b)])
            beyond.append([field[which, :, lanes] for field in far])
        steps[pair] = (
            score(
                four_q[:, lanes],
                jnp.concatenate(ours[0] + theirs[0] + beyond[0], axis=0),
                four_hold.at[pair],
            ),
            jnp.concatenate(
                [with_ones(field) for field in ours[1]]
                + [with_ones(field, 2.0) for field in theirs[1]]
                + [with_ones(field) for field in beyond[1]],
                axis=0,
            ),
        )
    for pair in range(pairs):
        lanes = pl.ds(pair * PAIR, PAIR)
        top, numer, rowsum = weigh(four_hold.at[pair], *steps[pair])
        coarse[0, :, lanes] = numer / rowsum
        coarse[1, :, lanes] = top + jnp.log(rowsum) * log2_e
    finish_blocks(fine, coarse, [*zip(steps_out, outs)][::-1])


def rest_kernel(fine, coarse, *outs):
    finish_blocks(fine, coarse, enumerate(outs))


def rejoin_kernel(further_ref, *refs):
    outs = refs[len(refs) // 3 * 2 :]
    for early, late_ref, out in zip(refs, refs[len(outs) :], outs):
        features = early.shape[1]
        late = late_ref[...].astype(jnp.float32)
        spread = lax.broadcasted_iota(jnp.int32, (SLAB, features), 1) // HD == (
            lax.broadcasted_iota(jnp.int32, (SLAB, features), 0)
        )
        signed = lax.dot_general(
            late[SLAB:, :BLOCK].astype(jnp.bfloat16),
            spread.astype(jnp.bfloat16),
            (((0,), (0,)), ((), ())),
            preferred_element_type=jnp.float32,
        )
        keep = jnp.where(signed >= 0, signed, 1.0 + signed)
        join = jnp.where(signed >= 0, 1.0 - signed, -signed)
        result = keep * early[...] + join * repeated(late[:SLAB])
        out[...] = result.astype(jnp.bfloat16)


def widen_kernel(*refs):
    half = len(refs) // 2
    for ref, out in zip(refs[:half], refs[half:]):
        out[...] = ref[...].astype(jnp.float32)


def partial_kernel(own_ref, weight_ref, out_ref):
    features = own_ref.shape[1]
    start = pl.multiple_of(lax.axis_index("head") * features, features)
    out_ref[...] = jnp.dot(
        own_ref[...], weight_ref[pl.ds(start, features), :], preferred_element_type=jnp.float32
    )


def further_kernel(widened_ref, partial_ref, weight_ref, *refs):
    parts, out_ref = refs[:-1], refs[-1]
    own = lax.axis_index("head")
    total = partial_ref[...]
    for step, part in enumerate(parts, 2):
        features = part.shape[1]
        start = pl.multiple_of((own ^ step) * features, features)
        total += jnp.dot(
            part[...], weight_ref[pl.ds(start, features), :], preferred_element_type=jnp.float32
        )
    out_ref[...] = total


def project_kernel(partial_ref, *refs):
    parts, (weight_ref, out_hbm, scratch, staged, sems) = refs[:-5], refs[-5:]
    own = lax.axis_index("head")
    features = parts[0].shape[1]
    chunk = staged.shape[2]
    copies = []
    for index in range(staged.shape[0]):
        columns = pl.ds(index * chunk, chunk)
        total = partial_ref[:, columns]
        for step, part in zip([*range(AHEAD, AHEAD + len(parts) - 1), 1], parts):
            start = pl.multiple_of((own ^ step) * features, features)
            total += jnp.dot(
                part[...],
                weight_ref[pl.ds(start, features), columns],
                preferred_element_type=jnp.float32,
            )
        for half in range(chunk // PAIR):
            lanes = slice(half * PAIR, (half + 1) * PAIR)
            scratch[index, half] = total[:, lanes]
            for i in range(SLAB):
                staged[index, i * FAN : (i + 1) * FAN, lanes] = scratch[
                    index, half, pl.ds(i, FAN, stride=SLAB), :
                ].astype(jnp.bfloat16)
        copy = pltpu.make_async_copy(staged.at[index], out_hbm.at[:, columns], sems.at[index])
        copy.start()
        copies.append(copy)
    for copy in copies:
        copy.wait()


def repool_outside(field):
    which, rows, lanes = field.shape
    slabs = field.astype(jnp.float32).reshape(which, rows // (2 * SLAB), 2, SLAB, lanes)
    sums = (slabs[:, :, 0] + slabs[:, :, 1]) * root_half
    return sums.reshape(which, rows // 2, lanes).astype(jnp.bfloat16)


def swapped(block, axis, mask):
    return lax.ppermute(block, axis, [(i, i ^ mask) for i in range(lax.axis_size(axis))])


def across(block):
    count, heads = lax.axis_size("seq"), lax.axis_size("head")
    route = []
    for seq in range(count):
        end = seq in (0, count - 1)
        other = seq if end else seq + 1 if seq % 2 else seq - 1
        for head in range(heads):
            route.append((seq * heads + head, other * heads + (head ^ 1 if end else head)))
    return lax.ppermute(block, ("seq", "head"), route)


def per_device(queries, key_vectors, value_vectors, out_weight):
    rows, features = queries.shape[1:]
    key_vectors, value_vectors = [
        pltpu.with_memory_space_constraint(x, pltpu.HBM) for x in (key_vectors, value_vectors)
    ]
    pairs = features // PAIR
    seq_count, head_count = lax.axis_size("seq"), lax.axis_size("head")
    bf16 = lambda *shape: jax.ShapeDtypeStruct(shape, jnp.bfloat16)
    params = pltpu.CompilerParams(vmem_limit_bytes=32 * 1024 * 1024)

    hbm = pl.BlockSpec(memory_space=pltpu.HBM)
    vmem = pl.BlockSpec(memory_space=pltpu.VMEM)
    keys, values, first, one, two = pl.pallas_call(
        pool_kernel,
        in_specs=[hbm] * 2,
        out_shape=[
            bf16(rows, features),
            bf16(rows, features),
            bf16(2, BLOCK + rows // 4 - BLOCK // 4, features),
            bf16(2, rows // 2, features),
            bf16(2, rows // 4, features),
        ],
        scratch_shapes=[
            pltpu.VMEM((2, rows // BLOCK, pairs, BLOCK, PAIR), jnp.float32),
            pltpu.SemaphoreType.DMA((2, 2)),
        ],
        compiler_params=params,
        name="pool",
    )(key_vectors, value_vectors)
    second, three, four = pl.pallas_call(
        deeper_kernel,
        out_shape=[
            bf16(2, BLOCK, features),
            bf16(2, rows // 8, features),
            bf16(2, rows // 16, features),
        ],
        compiler_params=params,
        cost_estimate=pl.CostEstimate(flops=2**31, bytes_accessed=2**23, transcendentals=0),
        name="deeper",
    )(keys, values, two)

    first_in = swapped(first, "seq", 1)
    second_in = across(second)
    four_in = swapped(four, "seq", 4)
    six_in = swapped(four, "seq", 6)
    threes_in = [swapped(three, "seq", mask) for mask in (3, 2)]
    edge_q, two_q, three_q, four_q, state = pl.pallas_call(
        local_kernel,
        out_shape=[
            bf16(2, BLOCK, features),
            bf16(rows // 4, features),
            bf16(rows // 8, features),
            bf16(rows // 16, features),
            jax.ShapeDtypeStruct((3, rows, features), jnp.float32),
        ],
        scratch_shapes=[
            pltpu.VMEM((pairs, rows, PAIR), jnp.float32),
            pltpu.VMEM((pairs, rows // BLOCK, 2 * BLOCK, 3 * BLOCK), jnp.float32),
            pltpu.VMEM((pairs, rows // BLOCK // 2, 2 * BLOCK, BLOCK), jnp.float32),
        ],
        compiler_params=params,
        name="local",
    )(queries[0], keys, values, one, four_in)

    fours = pl.pallas_call(
        join_kernel,
        out_shape=bf16(2, rows // 8, features),
        compiler_params=params,
        cost_estimate=pl.CostEstimate(flops=2**29, bytes_accessed=2**20, transcendentals=0),
        name="join",
    )(four_in, six_in, four_q)
    fours_in = swapped(fours, "seq", 1)
    coarse, near = pl.pallas_call(
        coarse_kernel,
        out_shape=[
            jax.ShapeDtypeStruct((3, rows // 4, features), jnp.float32),
            bf16(2, rows // 16, features),
        ],
        scratch_shapes=[
            pltpu.VMEM((2, pairs, BLOCK, PAIR), jnp.float32),
            pltpu.VMEM((2, rows // 4, features), jnp.bfloat16),
            pltpu.VMEM((pairs, rows // 2, BLOCK), jnp.float32),
            pltpu.VMEM((pairs, rows // 4, BLOCK), jnp.float32),
        ],
        compiler_params=params,
        cost_estimate=pl.CostEstimate(flops=2**31, bytes_accessed=2**21, transcendentals=0),
        name="coarse",
    )(two_q, three_q, first_in, *threes_in)
    away = range(AHEAD, head_count)
    fine, *early = pl.pallas_call(
        mid_kernel,
        out_shape=[jax.ShapeDtypeStruct((2, rows, features), jnp.float32)]
        + [bf16(BLOCK, features) for _ in away],
        scratch_shapes=[
            pltpu.VMEM((rows // BLOCK, BLOCK, features), jnp.bfloat16),
            pltpu.VMEM((pairs, 2, 2 * BLOCK, BLOCK), jnp.float32),
        ],
        compiler_params=params,
        name="mid",
    )(edge_q, coarse, state, first_in, second_in)
    early_in = [swapped(part, "head", step) for step, part in zip(away, early)]

    far = []
    known = 8
    if known < seq_count:
        group = [four, near] + [repool_outside(field) for field in threes_in]
        group = jnp.concatenate(group + [fours, fours_in], axis=1)
        while known < seq_count:
            fresh = swapped(group, "seq", known)
            far.append(fresh)
            group = jnp.concatenate([group, fresh], axis=1)
            known *= 2

    parts = [bf16(BLOCK, features) for _ in range(AHEAD)]
    *outs, level_four = pl.pallas_call(
        finish_kernel,
        out_shape=parts[2:]
        + [bf16(2 * SLAB, features) for _ in away]
        + [jax.ShapeDtypeStruct((2, rows // 16, features), jnp.float32)],
        scratch_shapes=[pltpu.VMEM((pairs, rows // 8, rows // 16 * seq_count), jnp.float32)],
        compiler_params=params,
        name="finish",
    )(four_q, fine, four, near, *threes_in, fours, fours_in, *far)
    whole_in = [swapped(part, "head", step) for step, part in zip(range(2, AHEAD), outs)]
    late_in = [swapped(part, "head", step) for step, part in zip(away, outs[AHEAD - 2 :])]
    own_part, next_part = pl.pallas_call(
        rest_kernel,
        out_shape=parts[:2],
        compiler_params=params,
        name="rest",
    )(fine, level_four)
    next_in = swapped(next_part, "head", 1)
    width = out_weight.shape[1]
    partial = pl.pallas_call(
        partial_kernel,
        out_shape=jax.ShapeDtypeStruct((BLOCK, width), jnp.float32),
        compiler_params=params,
        name="partial",
    )(own_part, out_weight)
    heavy = pl.CostEstimate(flops=2**32, bytes_accessed=2**20, transcendentals=0)
    widened = pl.pallas_call(
        widen_kernel,
        out_shape=[jax.ShapeDtypeStruct((BLOCK, features), jnp.float32) for _ in away],
        compiler_params=params,
        cost_estimate=pl.CostEstimate(flops=2**22, bytes_accessed=2**10, transcendentals=0),
        name="widen",
    )(*early_in)
    further = pl.pallas_call(
        further_kernel,
        out_shape=jax.ShapeDtypeStruct((BLOCK, width), jnp.float32),
        compiler_params=params,
        name="further",
    )(widened[0], partial, out_weight, *whole_in)
    rejoined = pl.pallas_call(
        rejoin_kernel,
        out_shape=[bf16(BLOCK, features) for _ in away],
        compiler_params=params,
        cost_estimate=heavy,
        name="rejoin",
    )(further, *widened, *late_in)
    chunk = 4 * PAIR
    result = pl.pallas_call(
        project_kernel,
        in_specs=[vmem] * (len(rejoined) + 3),
        out_specs=hbm,
        out_shape=bf16(BLOCK, width),
        scratch_shapes=[
            pltpu.VMEM((width // chunk, chunk // PAIR, BLOCK, PAIR), jnp.float32),
            pltpu.VMEM((width // chunk, BLOCK, chunk), jnp.bfloat16),
            pltpu.SemaphoreType.DMA((width // chunk,)),
        ],
        compiler_params=params,
        name="project",
    )(further, *rejoined, next_in, out_weight)
    return result[None]


def solution(mesh):
    return jax.shard_map(
        per_device,
        mesh=mesh,
        in_specs=(P(None, "seq", "head"), P(None, "seq", "head"), P(None, "seq", "head"), P()),
        out_specs=P(None, ("seq", "head"), None),
        check_vma=False,
    )
```

```python
import jax
import jax.numpy as jnp
from jax import lax
from jax.experimental import pallas as pl
from jax.experimental.pallas import tpu as pltpu
from jax.sharding import PartitionSpec as P

HD = 64
BLOCK = 128
LEVELS = 4
SLAB = 8
PAIR = 2 * HD

neg_fill = -1e30
root_half = 0.7071067811865476
log2_e = 1.4426950408889634
log2_scale = HD**-0.5 * log2_e
least_share = 2.0**-100
AHEAD = 3

FAN = 2**LEVELS


def slabs_of(scratch, block):
    return [scratch[pl.ds(BLOCK * block + j, SLAB, stride=FAN), :] for j in range(FAN)]


def pooled_slabs(slabs):
    return [
        ((low + high) * root_half).astype(jnp.bfloat16).astype(jnp.float32)
        for low, high in zip(slabs[0::2], slabs[1::2])
    ]


def joined(slabs):
    return jnp.concatenate(slabs, axis=0).astype(jnp.bfloat16)


def spill(source, scratch):
    for half in range(scratch.shape[0]):
        scratch[half] = source[:, half * PAIR : (half + 1) * PAIR].astype(jnp.float32)


def pool_kernel(
    k_hbm, v_hbm, k_ref, v_ref, first_ref, one_ref, two_ref, scratch, sems
):
    rows = k_ref.shape[0]
    blocks = rows // BLOCK
    arrivals = []
    for half in range(2):
        here = pl.ds(half * rows // 2, rows // 2)
        for which, (source, target) in enumerate(((k_hbm, k_ref), (v_hbm, v_ref))):
            copy = pltpu.make_async_copy(
                source.at[0, here, :], target.at[here, :], sems.at[which, half]
            )
            copy.start()
            for block in range(half * blocks // 2, (half + 1) * blocks // 2):
                arrivals.append((block, which, target, copy))
    even = lax.rem(lax.axis_index("seq"), 2) == 0
    for block, which, ref, copy in arrivals:
        if block % (blocks // 2) == 0:
            copy.wait()
        here = pl.ds(block * BLOCK, BLOCK)
        spill(ref.at[here, :], scratch.at[which, block])
        for half in range(scratch.shape[2]):
            lanes = pl.ds(half * PAIR, PAIR)
            one = pooled_slabs(slabs_of(scratch.at[which, block, half], 0))
            one_ref[which, pl.ds(block * BLOCK // 2, BLOCK // 2), lanes] = joined(one)
            two_ref[which, pl.ds(block * BLOCK // 4, BLOCK // 4), lanes] = joined(pooled_slabs(one))
    inner = rows // 4 - BLOCK // 4
    for which, ref in enumerate((k_ref, v_ref)):
        first_ref[which, :BLOCK, :] = jnp.where(even, ref[rows - BLOCK :, :], ref[:BLOCK, :])
        first_ref[which, BLOCK:, :] = jnp.where(
            even, two_ref[which, :inner, :], two_ref[which, BLOCK // 4 :, :]
        )


def repooled(field):
    rows, lanes = field.shape
    slabs = field.astype(jnp.float32).reshape(rows // (2 * SLAB), 2, SLAB, lanes)
    return ((slabs[:, 0] + slabs[:, 1]) * root_half).reshape(rows // 2, lanes).astype(jnp.bfloat16)


def deeper_kernel(k_ref, v_ref, two_ref, second_ref, three_ref, four_ref):
    rows = k_ref.shape[0]
    even = lax.rem(lax.axis_index("seq"), 2) == 0
    for which, ref in enumerate((k_ref, v_ref)):
        second_ref[which] = jnp.where(even, ref[:BLOCK, :], ref[rows - BLOCK :, :])
        three = repooled(two_ref[which])
        three_ref[which] = three
        four_ref[which] = repooled(three)


def repooled(field):
    rows, lanes = field.shape
    slabs = field.astype(jnp.float32).reshape(rows // (2 * SLAB), 2, SLAB, lanes)
    return ((slabs[:, 0] + slabs[:, 1]) * root_half).reshape(rows // 2, lanes).astype(jnp.bfloat16)


def score(queries, keys, hold, is_open=None):
    rows = queries.shape[0]
    low = lax.broadcasted_iota(jnp.int32, (rows, PAIR), 1) < HD
    zero = jnp.zeros_like(queries)
    both = jnp.concatenate([jnp.where(low, queries, zero), jnp.where(low, zero, queries)], axis=0)
    raw = lax.dot_general(both, keys, (((1,), (1,)), ((), ())), preferred_element_type=jnp.float32)
    if is_open is not None:
        raw = jnp.where(is_open, raw, neg_fill)
    hold[...] = raw
    return jnp.max(raw, axis=1, keepdims=True)


def weigh(hold, top, values):
    rows = top.shape[0] // 2
    low = lax.broadcasted_iota(jnp.int32, (rows, PAIR), 1) < HD
    weights = jnp.exp2((hold[...] - top) * log2_scale).astype(jnp.bfloat16)
    result = jnp.dot(weights, values, preferred_element_type=jnp.float32)
    return (
        log2_scale * jnp.where(low, top[:rows], top[rows:]),
        jnp.where(low, result[:rows, :PAIR], result[rows:, :PAIR]),
        jnp.where(low, result[:rows, PAIR:], result[rows:, PAIR:]),
    )


def merged(fine, coarse):
    top = jnp.maximum(fine[0], coarse[0])
    keep = jnp.exp2(fine[0] - top)
    join = jnp.exp2(coarse[0] - top)
    return top, fine[1] * keep + coarse[1] * join, fine[2] * keep + coarse[2] * join


def doubled(field):
    rows, lanes = field.shape
    slabs = field.reshape(rows // SLAB, 1, SLAB, lanes)
    return jnp.broadcast_to(slabs, (rows // SLAB, 2, SLAB, lanes)).reshape(2 * rows, lanes)


def with_ones(values, weight=1.0):
    if weight != 1.0:
        values = values * jnp.bfloat16(weight)
    return jnp.concatenate([values, jnp.full(values.shape, weight, jnp.bfloat16)], axis=1)


def local_kernel(
    q_ref, k_ref, v_ref, one_ref, four_ref, edge_q, two_q, three_q, four_q, state,
    scratch, near_hold, coarse_hold,
):
    rows = q_ref.shape[0]
    blocks = rows // BLOCK
    pairs = scratch.shape[0]
    spill(q_ref, scratch)
    fine, one_q = [], []
    for pair in range(pairs):
        lanes = pl.ds(pair * PAIR, PAIR)
        ladder = [[], [], [], [], []]
        for block in range(blocks):
            slabs = slabs_of(scratch.at[pair], block)
            ladder[0].append(joined(slabs))
            for level in range(1, LEVELS + 1):
                slabs = pooled_slabs(slabs)
                ladder[level] += slabs
        edge_q[0, :, lanes] = ladder[0][0]
        edge_q[1, :, lanes] = ladder[0][-1]
        two_q[:, lanes] = joined(ladder[2])
        three_q[:, lanes] = joined(ladder[3])
        four_q[:, lanes] = joined(ladder[4])
        fine.append(ladder[0])
        one_q.append([joined(ladder[1][n : n + FAN]) for n in range(0, len(ladder[1]), FAN)])
    windows = [(max(n - 1, 0) * BLOCK, min(n + 2, blocks) * BLOCK) for n in range(blocks)]
    tops = {}
    for pair in range(pairs):
        lanes = pl.ds(pair * PAIR, PAIR)
        for half in range(blocks // 2):
            there = pl.ds((half ^ 1) * BLOCK, BLOCK)
            tops[pair, half] = score(
                one_q[pair][half], one_ref[0, there, lanes], coarse_hold.at[pair, half]
            )
            for block in (2 * half, 2 * half + 1):
                low, high = windows[block]
                hold = near_hold.at[pair, block, :, : high - low]
                tops[pair, half, block] = score(fine[pair][block], k_ref[low:high, lanes], hold)
    for pair in range(pairs):
        lanes = pl.ds(pair * PAIR, PAIR)
        for half in range(blocks // 2):
            there = pl.ds((half ^ 1) * BLOCK, BLOCK)
            coarse = weigh(
                coarse_hold.at[pair, half], tops[pair, half], with_ones(one_ref[1, there, lanes])
            )
            for block in (2 * half, 2 * half + 1):
                low, high = windows[block]
                hold = near_hold.at[pair, block, :, : high - low]
                near = weigh(hold, tops[pair, half, block], with_ones(v_ref[low:high, lanes]))
                part = slice((block - 2 * half) * BLOCK // 2, (block - 2 * half + 1) * BLOCK // 2)
                done = merged(near, [doubled(x[part]) for x in coarse])
                for index, field in enumerate(done):
                    state[index, block * BLOCK : (block + 1) * BLOCK, lanes] = field


def join_kernel(four_ref, six_ref, query_ref, out):
    sixteenth = four_ref.shape[1]
    out[:, :sixteenth, :] = four_ref[...]
    out[:, sixteenth:, :] = six_ref[...]


def coarse_kernel(
    two_q, three_q, first_ref, three_a, three_b, coarse, near_ref, scratch, two_ref, two_hold, three_hold
):
    inner = first_ref.shape[1] - BLOCK
    pairs = scratch.shape[1]
    two_ref[:, :inner, :] = first_ref[:, BLOCK:, :]
    for which in range(2):
        spill(first_ref.at[which, pl.ds(0, BLOCK), :], scratch.at[which])
        for half in range(pairs):
            lanes = pl.ds(half * PAIR, PAIR)
            slabs = slabs_of(scratch.at[which, half], 0)
            two_ref[which, inner:, lanes] = joined(pooled_slabs(pooled_slabs(slabs)))
        near_ref[which] = repooled(repooled(two_ref[which]))
    steps = {}
    for pair in range(pairs):
        lanes = pl.ds(pair * PAIR, PAIR)
        three = [
            jnp.concatenate([three_a[which, :, lanes], three_b[which, :, lanes]], axis=0)
            for which in range(2)
        ]
        steps[pair, 3] = (
            score(three_q[:, lanes], three[0], three_hold.at[pair]), with_ones(three[1])
        )
        steps[pair, 2] = (
            score(two_q[:, lanes], two_ref[0, :, lanes], two_hold.at[pair]),
            with_ones(two_ref[1, :, lanes]),
        )
    for pair in range(pairs):
        three = weigh(three_hold.at[pair], *steps[pair, 3])
        two = merged(weigh(two_hold.at[pair], *steps[pair, 2]), [doubled(x) for x in three])
        for index, field in enumerate(two):
            coarse[index, :, pl.ds(pair * PAIR, PAIR)] = field


def mid_kernel(edge_q, coarse, state, first_ref, second_ref, fine, *refs):
    outs, (ready, holds) = refs[:-2], refs[-2:]
    own = lax.axis_index("head")
    rows = state.shape[1]
    blocks = rows // BLOCK
    position = lax.axis_index("seq")
    last = lax.axis_size("seq") - 1
    even = lax.rem(position, 2) == 0
    opens = (position > 0, position < last)
    pairs = holds.shape[0]
    steps = {}
    for pair in range(pairs):
        lanes = pl.ds(pair * PAIR, PAIR)
        inner = [first_ref[which, :BLOCK, lanes] for which in range(2)]
        outer = [second_ref[which, :, lanes] for which in range(2)]
        for side in range(2):
            halo = [
                jnp.where(even, *((outer[which], inner[which])[:: 1 - 2 * side]))
                for which in range(2)
            ]
            steps[pair, side] = (
                score(edge_q[side, :, lanes], halo[0], holds.at[pair, side], opens[side]),
                with_ones(halo[1]),
            )
    for pair in range(pairs):
        lanes = pl.ds(pair * PAIR, PAIR)
        for block in range(blocks):
            here = slice(block * BLOCK, (block + 1) * BLOCK)
            quarter = slice(block * BLOCK // 4, (block + 1) * BLOCK // 4)
            done = merged(
                [state[index, here, lanes] for index in range(3)],
                [doubled(doubled(coarse[index, quarter, lanes])) for index in range(3)],
            )
            for side, edge in enumerate((0, blocks - 1)):
                if block == edge:
                    done = merged(done, weigh(holds.at[pair, side], *steps[pair, side]))
            result = done[1] / done[2]
            fine[0, here, lanes] = result
            fine[1, here, lanes] = done[0] + jnp.log(done[2]) * log2_e
            ready[block, :, lanes] = result.astype(jnp.bfloat16)
    for step, out in enumerate(outs, AHEAD):
        out[...] = ready[own ^ step]


def repeated(field):
    return jnp.concatenate([field] * FAN, axis=0)


def finish_blocks(fine, coarse, steps):
    own = lax.axis_index("head")
    features = fine.shape[2]
    for step, out in steps:
        block = own ^ step
        here = pl.ds(pl.multiple_of(block * BLOCK, BLOCK), BLOCK)
        few = pl.ds(pl.multiple_of(block * SLAB, SLAB), SLAB)
        shares = []
        for pair in range(features // PAIR):
            lanes = pl.ds(pair * PAIR, PAIR)
            fine_sum, coarse_sum = fine[1, here, lanes], repeated(coarse[1, few, lanes])
            if step < AHEAD:
                keep = 1.0 / (1.0 + jnp.exp2(coarse_sum - fine_sum))
                ours, theirs = fine[0, here, lanes], repeated(coarse[0, few, lanes])
                out[:, lanes] = (theirs + keep * (ours - theirs)).astype(jnp.bfloat16)
            else:
                ratio = jnp.exp2(-jnp.abs(fine_sum - coarse_sum))
                less = jnp.maximum(ratio / (1.0 + ratio), least_share)
                shares.append(jnp.where(fine_sum <= coarse_sum, less, -less).astype(jnp.bfloat16))
        if step >= AHEAD:
            pick = lax.broadcasted_iota(jnp.int32, (2 * SLAB, features), 1) == HD * (
                lax.broadcasted_iota(jnp.int32, (2 * SLAB, features), 0)
            )
            by_head = lax.dot_general(
                pick.astype(jnp.bfloat16),
                jnp.concatenate(shares, axis=1),
                (((1,), (1,)), ((), ())),
                preferred_element_type=jnp.float32,
            )[:SLAB]
            blank = jnp.zeros((SLAB, features - BLOCK), jnp.float32)
            out[...] = jnp.concatenate(
                [coarse[0, few, :], jnp.concatenate([by_head, blank], axis=1)], axis=0
            ).astype(jnp.bfloat16)


def finish_kernel(
    four_q, fine, four_ref, near_ref, three_a, three_b, fours_a, fours_b, *refs
):
    refs, (coarse, four_hold) = refs[:-2], refs[-2:]
    steps_out = range(2, lax.axis_size("head"))
    far, outs = refs[: -len(steps_out)], refs[-len(steps_out) :]
    pairs = four_q.shape[1] // PAIR
    steps = {}
    for pair in range(pairs):
        lanes = pl.ds(pair * PAIR, PAIR)
        ours, theirs, beyond = [], [], []
        for which in range(2):
            ours.append(
                [four_ref[which, :, lanes], near_ref[which, :, lanes]]
                + [repooled(field[which, :, lanes]) for field in (three_a, three_b)]
            )
            theirs.append([field[which, :, lanes] for field in (fours_a, fours_b)])
            beyond.append([field[which, :, lanes] for field in far])
        steps[pair] = (
            score(
                four_q[:, lanes],
                jnp.concatenate(ours[0] + theirs[0] + beyond[0], axis=0),
                four_hold.at[pair],
            ),
            jnp.concatenate(
                [with_ones(field) for field in ours[1]]
                + [with_ones(field, 2.0) for field in theirs[1]]
                + [with_ones(field) for field in beyond[1]],
                axis=0,
            ),
        )
    for pair in range(pairs):
        lanes = pl.ds(pair * PAIR, PAIR)
        top, numer, rowsum = weigh(four_hold.at[pair], *steps[pair])
        coarse[0, :, lanes] = numer / rowsum
        coarse[1, :, lanes] = top + jnp.log(rowsum) * log2_e
    finish_blocks(fine, coarse, zip(steps_out, outs))


def rest_kernel(fine, coarse, *outs):
    finish_blocks(fine, coarse, enumerate(outs))


def gate_kernel(further_ref, *refs):
    half = len(refs) // 2
    for ref, out in zip(refs[:half], refs[half:]):
        out[...] = ref[...]


def rejoined(early, late_ref):
    features = early.shape[1]
    late = late_ref[...].astype(jnp.float32)
    spread = lax.broadcasted_iota(jnp.int32, (SLAB, features), 1) // HD == (
        lax.broadcasted_iota(jnp.int32, (SLAB, features), 0)
    )
    signed = lax.dot_general(
        late[SLAB:, :BLOCK].astype(jnp.bfloat16),
        spread.astype(jnp.bfloat16),
        (((0,), (0,)), ((), ())),
        preferred_element_type=jnp.float32,
    )
    keep = jnp.where(signed >= 0, signed, 1.0 + signed)
    join = jnp.where(signed >= 0, 1.0 - signed, -signed)
    result = keep * early + join * repeated(late[:SLAB])
    return result.astype(jnp.bfloat16)


def widen_kernel(*refs):
    half = len(refs) // 2
    for ref, out in zip(refs[:half], refs[half:]):
        out[...] = ref[...].astype(jnp.float32)


def partial_kernel(own_ref, weight_ref, out_ref):
    features = own_ref.shape[1]
    start = pl.multiple_of(lax.axis_index("head") * features, features)
    out_ref[...] = jnp.dot(
        own_ref[...], weight_ref[pl.ds(start, features), :], preferred_element_type=jnp.float32
    )


def further_kernel(widened_ref, partial_ref, weight_ref, *refs):
    parts, out_ref = refs[:-1], refs[-1]
    own = lax.axis_index("head")
    total = partial_ref[...]
    for step, part in enumerate(parts, 2):
        features = part.shape[1]
        start = pl.multiple_of((own ^ step) * features, features)
        total += jnp.dot(
            part[...], weight_ref[pl.ds(start, features), :], preferred_element_type=jnp.float32
        )
    out_ref[...] = total


def project_kernel(partial_ref, *refs):
    refs, (next_ref, weight_ref, out_hbm, scratch, staged, sems) = refs[:-6], refs[-6:]
    own = lax.axis_index("head")
    half = len(refs) // 2
    parts = [next_ref[...]]
    parts += [rejoined(early[...], late) for early, late in zip(refs[:half], refs[half:])]
    features = next_ref.shape[1]
    chunk = staged.shape[2]
    copies = []
    for index in range(staged.shape[0]):
        columns = pl.ds(index * chunk, chunk)
        total = partial_ref[:, columns]
        for step, part in zip([1, *range(AHEAD, AHEAD + half)], parts):
            start = pl.multiple_of((own ^ step) * features, features)
            total += jnp.dot(
                part,
                weight_ref[pl.ds(start, features), columns],
                preferred_element_type=jnp.float32,
            )
        for half in range(chunk // PAIR):
            lanes = slice(half * PAIR, (half + 1) * PAIR)
            scratch[index, half] = total[:, lanes]
            for i in range(SLAB):
                staged[index, i * FAN : (i + 1) * FAN, lanes] = scratch[
                    index, half, pl.ds(i, FAN, stride=SLAB), :
                ].astype(jnp.bfloat16)
        copy = pltpu.make_async_copy(staged.at[index], out_hbm.at[:, columns], sems.at[index])
        copy.start()
        copies.append(copy)
    for copy in copies:
        copy.wait()


def repool_outside(field):
    which, rows, lanes = field.shape
    slabs = field.astype(jnp.float32).reshape(which, rows // (2 * SLAB), 2, SLAB, lanes)
    sums = (slabs[:, :, 0] + slabs[:, :, 1]) * root_half
    return sums.reshape(which, rows // 2, lanes).astype(jnp.bfloat16)


def swapped(block, axis, mask):
    return lax.ppermute(block, axis, [(i, i ^ mask) for i in range(lax.axis_size(axis))])


def across(block):
    count, heads = lax.axis_size("seq"), lax.axis_size("head")
    route = []
    for seq in range(count):
        end = seq in (0, count - 1)
        other = seq if end else seq + 1 if seq % 2 else seq - 1
        for head in range(heads):
            route.append((seq * heads + head, other * heads + (head ^ 1 if end else head)))
    return lax.ppermute(block, ("seq", "head"), route)


def per_device(queries, key_vectors, value_vectors, out_weight):
    rows, features = queries.shape[1:]
    key_vectors, value_vectors = [
        pltpu.with_memory_space_constraint(x, pltpu.HBM) for x in (key_vectors, value_vectors)
    ]
    pairs = features // PAIR
    seq_count, head_count = lax.axis_size("seq"), lax.axis_size("head")
    bf16 = lambda *shape: jax.ShapeDtypeStruct(shape, jnp.bfloat16)
    params = pltpu.CompilerParams(vmem_limit_bytes=32 * 1024 * 1024)

    hbm = pl.BlockSpec(memory_space=pltpu.HBM)
    vmem = pl.BlockSpec(memory_space=pltpu.VMEM)
    keys, values, first, one, two = pl.pallas_call(
        pool_kernel,
        in_specs=[hbm] * 2,
        out_shape=[
            bf16(rows, features),
            bf16(rows, features),
            bf16(2, BLOCK + rows // 4 - BLOCK // 4, features),
            bf16(2, rows // 2, features),
            bf16(2, rows // 4, features),
        ],
        scratch_shapes=[
            pltpu.VMEM((2, rows // BLOCK, pairs, BLOCK, PAIR), jnp.float32),
            pltpu.SemaphoreType.DMA((2, 2)),
        ],
        compiler_params=params,
        name="pool",
    )(key_vectors, value_vectors)
    second, three, four = pl.pallas_call(
        deeper_kernel,
        out_shape=[
            bf16(2, BLOCK, features),
            bf16(2, rows // 8, features),
            bf16(2, rows // 16, features),
        ],
        compiler_params=params,
        cost_estimate=pl.CostEstimate(flops=2**31, bytes_accessed=2**23, transcendentals=0),
        name="deeper",
    )(keys, values, two)

    first_in = swapped(first, "seq", 1)
    second_in = across(second)
    four_in = swapped(four, "seq", 4)
    six_in = swapped(four, "seq", 6)
    threes_in = [swapped(three, "seq", mask) for mask in (3, 2)]
    edge_q, two_q, three_q, four_q, state = pl.pallas_call(
        local_kernel,
        out_shape=[
            bf16(2, BLOCK, features),
            bf16(rows // 4, features),
            bf16(rows // 8, features),
            bf16(rows // 16, features),
            jax.ShapeDtypeStruct((3, rows, features), jnp.float32),
        ],
        scratch_shapes=[
            pltpu.VMEM((pairs, rows, PAIR), jnp.float32),
            pltpu.VMEM((pairs, rows // BLOCK, 2 * BLOCK, 3 * BLOCK), jnp.float32),
            pltpu.VMEM((pairs, rows // BLOCK // 2, 2 * BLOCK, BLOCK), jnp.float32),
        ],
        compiler_params=params,
        name="local",
    )(queries[0], keys, values, one, four_in)

    fours = pl.pallas_call(
        join_kernel,
        out_shape=bf16(2, rows // 8, features),
        compiler_params=params,
        cost_estimate=pl.CostEstimate(flops=2**29, bytes_accessed=2**20, transcendentals=0),
        name="join",
    )(four_in, six_in, four_q)
    fours_in = swapped(fours, "seq", 1)
    coarse, near = pl.pallas_call(
        coarse_kernel,
        out_shape=[
            jax.ShapeDtypeStruct((3, rows // 4, features), jnp.float32),
            bf16(2, rows // 16, features),
        ],
        scratch_shapes=[
            pltpu.VMEM((2, pairs, BLOCK, PAIR), jnp.float32),
            pltpu.VMEM((2, rows // 4, features), jnp.bfloat16),
            pltpu.VMEM((pairs, rows // 2, BLOCK), jnp.float32),
            pltpu.VMEM((pairs, rows // 4, BLOCK), jnp.float32),
        ],
        compiler_params=params,
        cost_estimate=pl.CostEstimate(flops=2**31, bytes_accessed=2**21, transcendentals=0),
        name="coarse",
    )(two_q, three_q, first_in, *threes_in)
    away = range(AHEAD, head_count)
    fine, *early = pl.pallas_call(
        mid_kernel,
        out_shape=[jax.ShapeDtypeStruct((2, rows, features), jnp.float32)]
        + [bf16(BLOCK, features) for _ in away],
        scratch_shapes=[
            pltpu.VMEM((rows // BLOCK, BLOCK, features), jnp.bfloat16),
            pltpu.VMEM((pairs, 2, 2 * BLOCK, BLOCK), jnp.float32),
        ],
        compiler_params=params,
        name="mid",
    )(edge_q, coarse, state, first_in, second_in)
    early_in = [swapped(part, "head", step) for step, part in zip(away, early)]

    far = []
    known = 8
    if known < seq_count:
        group = [four, near] + [repool_outside(field) for field in threes_in]
        group = jnp.concatenate(group + [fours, fours_in], axis=1)
        while known < seq_count:
            fresh = swapped(group, "seq", known)
            far.append(fresh)
            group = jnp.concatenate([group, fresh], axis=1)
            known *= 2

    parts = [bf16(BLOCK, features) for _ in range(AHEAD)]
    *outs, level_four = pl.pallas_call(
        finish_kernel,
        out_shape=parts[2:]
        + [bf16(2 * SLAB, features) for _ in away]
        + [jax.ShapeDtypeStruct((2, rows // 16, features), jnp.float32)],
        scratch_shapes=[pltpu.VMEM((pairs, rows // 8, rows // 16 * seq_count), jnp.float32)],
        compiler_params=params,
        name="finish",
    )(four_q, fine, four, near, *threes_in, fours, fours_in, *far)
    whole_in = [swapped(part, "head", step) for step, part in zip(range(2, AHEAD), outs)]
    late_in = [swapped(part, "head", step) for step, part in zip(away, outs[AHEAD - 2 :])]
    own_part, next_part = pl.pallas_call(
        rest_kernel,
        out_shape=parts[:2],
        compiler_params=params,
        name="rest",
    )(fine, level_four)
    next_in = swapped(next_part, "head", 1)
    width = out_weight.shape[1]
    partial = pl.pallas_call(
        partial_kernel,
        out_shape=jax.ShapeDtypeStruct((BLOCK, width), jnp.float32),
        compiler_params=params,
        name="partial",
    )(own_part, out_weight)
    heavy = pl.CostEstimate(flops=2**32, bytes_accessed=2**20, transcendentals=0)
    widened = pl.pallas_call(
        widen_kernel,
        out_shape=[jax.ShapeDtypeStruct((BLOCK, features), jnp.float32) for _ in away],
        compiler_params=params,
        cost_estimate=pl.CostEstimate(flops=2**22, bytes_accessed=2**10, transcendentals=0),
        name="widen",
    )(*early_in)
    further = pl.pallas_call(
        further_kernel,
        out_shape=jax.ShapeDtypeStruct((BLOCK, width), jnp.float32),
        compiler_params=params,
        name="further",
    )(widened[0], partial, out_weight, *whole_in)
    gated = pl.pallas_call(
        gate_kernel,
        out_shape=[bf16(2 * SLAB, features) for _ in away],
        compiler_params=params,
        cost_estimate=heavy,
        name="gate",
    )(further, *late_in)
    chunk = 4 * PAIR
    result = pl.pallas_call(
        project_kernel,
        in_specs=[vmem] * (2 * len(gated) + 3),
        out_specs=hbm,
        out_shape=bf16(BLOCK, width),
        scratch_shapes=[
            pltpu.VMEM((width // chunk, chunk // PAIR, BLOCK, PAIR), jnp.float32),
            pltpu.VMEM((width // chunk, BLOCK, chunk), jnp.bfloat16),
            pltpu.SemaphoreType.DMA((width // chunk,)),
        ],
        compiler_params=params,
        name="project",
    )(further, *widened, *gated, next_in, out_weight)
    return result[None]


def solution(mesh):
    return jax.shard_map(
        per_device,
        mesh=mesh,
        in_specs=(P(None, "seq", "head"), P(None, "seq", "head"), P(None, "seq", "head"), P()),
        out_specs=P(None, ("seq", "head"), None),
        check_vma=False,
    )
```

```python
import jax
import jax.numpy as jnp
from jax import lax
from jax.experimental import pallas as pl
from jax.experimental.pallas import tpu as pltpu
from jax.sharding import PartitionSpec as P

HD = 64
BLOCK = 128
LEVELS = 4
SLAB = 8
PAIR = 2 * HD

neg_fill = -1e30
root_half = 0.7071067811865476
log2_e = 1.4426950408889634
log2_scale = HD**-0.5 * log2_e
least_share = 2.0**-100
AHEAD = 3

FAN = 2**LEVELS


def slabs_of(scratch, block):
    return [scratch[pl.ds(BLOCK * block + j, SLAB, stride=FAN), :] for j in range(FAN)]


def pooled_slabs(slabs):
    return [
        ((low + high) * root_half).astype(jnp.bfloat16).astype(jnp.float32)
        for low, high in zip(slabs[0::2], slabs[1::2])
    ]


def joined(slabs):
    return jnp.concatenate(slabs, axis=0).astype(jnp.bfloat16)


def spill(source, scratch):
    for half in range(scratch.shape[0]):
        scratch[half] = source[:, half * PAIR : (half + 1) * PAIR].astype(jnp.float32)


def pool_kernel(
    k_hbm, v_hbm, k_ref, v_ref, first_ref, one_ref, second_ref, three_ref, four_ref,
    two_ref, scratch, sems,
):
    rows = k_ref.shape[0]
    blocks = rows // BLOCK
    arrivals = []
    for half in range(2):
        here = pl.ds(half * rows // 2, rows // 2)
        for which, (source, target) in enumerate(((k_hbm, k_ref), (v_hbm, v_ref))):
            copy = pltpu.make_async_copy(
                source.at[0, here, :], target.at[here, :], sems.at[which, half]
            )
            copy.start()
            for block in range(half * blocks // 2, (half + 1) * blocks // 2):
                arrivals.append((block, which, target, copy))
    even = lax.rem(lax.axis_index("seq"), 2) == 0
    for block, which, ref, copy in arrivals:
        if block % (blocks // 2) == 0:
            copy.wait()
        here = pl.ds(block * BLOCK, BLOCK)
        spill(ref.at[here, :], scratch.at[which, block])
        for half in range(scratch.shape[2]):
            lanes = pl.ds(half * PAIR, PAIR)
            one = pooled_slabs(slabs_of(scratch.at[which, block, half], 0))
            one_ref[which, pl.ds(block * BLOCK // 2, BLOCK // 2), lanes] = joined(one)
            two_ref[which, pl.ds(block * BLOCK // 4, BLOCK // 4), lanes] = joined(pooled_slabs(one))
    inner = rows // 4 - BLOCK // 4
    for which, ref in enumerate((k_ref, v_ref)):
        first_ref[which, :BLOCK, :] = jnp.where(even, ref[rows - BLOCK :, :], ref[:BLOCK, :])
        first_ref[which, BLOCK:, :] = jnp.where(
            even, two_ref[which, :inner, :], two_ref[which, BLOCK // 4 :, :]
        )
        second_ref[which] = jnp.where(even, ref[:BLOCK, :], ref[rows - BLOCK :, :])
        three = repooled(two_ref[which])
        three_ref[which] = three
        four_ref[which] = repooled(three)


def repooled(field):
    rows, lanes = field.shape
    slabs = field.astype(jnp.float32).reshape(rows // (2 * SLAB), 2, SLAB, lanes)
    return ((slabs[:, 0] + slabs[:, 1]) * root_half).reshape(rows // 2, lanes).astype(jnp.bfloat16)


def score(queries, keys, hold, is_open=None):
    rows = queries.shape[0]
    low = lax.broadcasted_iota(jnp.int32, (rows, PAIR), 1) < HD
    zero = jnp.zeros_like(queries)
    both = jnp.concatenate([jnp.where(low, queries, zero), jnp.where(low, zero, queries)], axis=0)
    raw = lax.dot_general(both, keys, (((1,), (1,)), ((), ())), preferred_element_type=jnp.float32)
    if is_open is not None:
        raw = jnp.where(is_open, raw, neg_fill)
    hold[...] = raw
    return jnp.max(raw, axis=1, keepdims=True)


def weigh(hold, top, values):
    rows = top.shape[0] // 2
    low = lax.broadcasted_iota(jnp.int32, (rows, PAIR), 1) < HD
    weights = jnp.exp2((hold[...] - top) * log2_scale).astype(jnp.bfloat16)
    result = jnp.dot(weights, values, preferred_element_type=jnp.float32)
    return (
        log2_scale * jnp.where(low, top[:rows], top[rows:]),
        jnp.where(low, result[:rows, :PAIR], result[rows:, :PAIR]),
        jnp.where(low, result[:rows, PAIR:], result[rows:, PAIR:]),
    )


def merged(fine, coarse):
    top = jnp.maximum(fine[0], coarse[0])
    keep = jnp.exp2(fine[0] - top)
    join = jnp.exp2(coarse[0] - top)
    return top, fine[1] * keep + coarse[1] * join, fine[2] * keep + coarse[2] * join


def doubled(field):
    rows, lanes = field.shape
    slabs = field.reshape(rows // SLAB, 1, SLAB, lanes)
    return jnp.broadcast_to(slabs, (rows // SLAB, 2, SLAB, lanes)).reshape(2 * rows, lanes)


def with_ones(values, weight=1.0):
    if weight != 1.0:
        values = values * jnp.bfloat16(weight)
    return jnp.concatenate([values, jnp.full(values.shape, weight, jnp.bfloat16)], axis=1)


def local_kernel(
    q_ref, k_ref, v_ref, one_ref, four_ref, edge_q, two_q, three_q, four_q, state,
    scratch, near_hold, coarse_hold,
):
    rows = q_ref.shape[0]
    blocks = rows // BLOCK
    pairs = scratch.shape[0]
    spill(q_ref, scratch)
    fine, one_q = [], []
    for pair in range(pairs):
        lanes = pl.ds(pair * PAIR, PAIR)
        ladder = [[], [], [], [], []]
        for block in range(blocks):
            slabs = slabs_of(scratch.at[pair], block)
            ladder[0].append(joined(slabs))
            for level in range(1, LEVELS + 1):
                slabs = pooled_slabs(slabs)
                ladder[level] += slabs
        edge_q[0, :, lanes] = ladder[0][0]
        edge_q[1, :, lanes] = ladder[0][-1]
        two_q[:, lanes] = joined(ladder[2])
        three_q[:, lanes] = joined(ladder[3])
        four_q[:, lanes] = joined(ladder[4])
        fine.append(ladder[0])
        one_q.append([joined(ladder[1][n : n + FAN]) for n in range(0, len(ladder[1]), FAN)])
    windows = [(max(n - 1, 0) * BLOCK, min(n + 2, blocks) * BLOCK) for n in range(blocks)]
    tops = {}
    for pair in range(pairs):
        lanes = pl.ds(pair * PAIR, PAIR)
        for half in range(blocks // 2):
            there = pl.ds((half ^ 1) * BLOCK, BLOCK)
            tops[pair, half] = score(
                one_q[pair][half], one_ref[0, there, lanes], coarse_hold.at[pair, half]
            )
            for block in (2 * half, 2 * half + 1):
                low, high = windows[block]
                hold = near_hold.at[pair, block, :, : high - low]
                tops[pair, half, block] = score(fine[pair][block], k_ref[low:high, lanes], hold)
    for pair in range(pairs):
        lanes = pl.ds(pair * PAIR, PAIR)
        for half in range(blocks // 2):
            there = pl.ds((half ^ 1) * BLOCK, BLOCK)
            coarse = weigh(
                coarse_hold.at[pair, half], tops[pair, half], with_ones(one_ref[1, there, lanes])
            )
            for block in (2 * half, 2 * half + 1):
                low, high = windows[block]
                hold = near_hold.at[pair, block, :, : high - low]
                near = weigh(hold, tops[pair, half, block], with_ones(v_ref[low:high, lanes]))
                part = slice((block - 2 * half) * BLOCK // 2, (block - 2 * half + 1) * BLOCK // 2)
                done = merged(near, [doubled(x[part]) for x in coarse])
                for index, field in enumerate(done):
                    state[index, block * BLOCK : (block + 1) * BLOCK, lanes] = field


def join_kernel(four_ref, six_ref, query_ref, out):
    sixteenth = four_ref.shape[1]
    out[:, :sixteenth, :] = four_ref[...]
    out[:, sixteenth:, :] = six_ref[...]


def coarse_kernel(
    two_q, three_q, first_ref, three_a, three_b, coarse, near_ref, scratch, two_ref, two_hold, three_hold
):
    inner = first_ref.shape[1] - BLOCK
    pairs = scratch.shape[1]
    two_ref[:, :inner, :] = first_ref[:, BLOCK:, :]
    for which in range(2):
        spill(first_ref.at[which, pl.ds(0, BLOCK), :], scratch.at[which])
        for half in range(pairs):
            lanes = pl.ds(half * PAIR, PAIR)
            slabs = slabs_of(scratch.at[which, half], 0)
            two_ref[which, inner:, lanes] = joined(pooled_slabs(pooled_slabs(slabs)))
        near_ref[which] = repooled(repooled(two_ref[which]))
    steps = {}
    for pair in range(pairs):
        lanes = pl.ds(pair * PAIR, PAIR)
        three = [
            jnp.concatenate([three_a[which, :, lanes], three_b[which, :, lanes]], axis=0)
            for which in range(2)
        ]
        steps[pair, 3] = (
            score(three_q[:, lanes], three[0], three_hold.at[pair]), with_ones(three[1])
        )
        steps[pair, 2] = (
            score(two_q[:, lanes], two_ref[0, :, lanes], two_hold.at[pair]),
            with_ones(two_ref[1, :, lanes]),
        )
    for pair in range(pairs):
        three = weigh(three_hold.at[pair], *steps[pair, 3])
        two = merged(weigh(two_hold.at[pair], *steps[pair, 2]), [doubled(x) for x in three])
        for index, field in enumerate(two):
            coarse[index, :, pl.ds(pair * PAIR, PAIR)] = field


def mid_kernel(edge_q, coarse, state, first_ref, second_ref, fine, *refs):
    outs, (ready, holds) = refs[:-2], refs[-2:]
    own = lax.axis_index("head")
    rows = state.shape[1]
    blocks = rows // BLOCK
    position = lax.axis_index("seq")
    last = lax.axis_size("seq") - 1
    even = lax.rem(position, 2) == 0
    opens = (position > 0, position < last)
    pairs = holds.shape[0]
    steps = {}
    for pair in range(pairs):
        lanes = pl.ds(pair * PAIR, PAIR)
        inner = [first_ref[which, :BLOCK, lanes] for which in range(2)]
        outer = [second_ref[which, :, lanes] for which in range(2)]
        for side in range(2):
            halo = [
                jnp.where(even, *((outer[which], inner[which])[:: 1 - 2 * side]))
                for which in range(2)
            ]
            steps[pair, side] = (
                score(edge_q[side, :, lanes], halo[0], holds.at[pair, side], opens[side]),
                with_ones(halo[1]),
            )
    for pair in range(pairs):
        lanes = pl.ds(pair * PAIR, PAIR)
        for block in range(blocks):
            here = slice(block * BLOCK, (block + 1) * BLOCK)
            quarter = slice(block * BLOCK // 4, (block + 1) * BLOCK // 4)
            done = merged(
                [state[index, here, lanes] for index in range(3)],
                [doubled(doubled(coarse[index, quarter, lanes])) for index in range(3)],
            )
            for side, edge in enumerate((0, blocks - 1)):
                if block == edge:
                    done = merged(done, weigh(holds.at[pair, side], *steps[pair, side]))
            result = done[1] / done[2]
            fine[0, here, lanes] = result
            fine[1, here, lanes] = done[0] + jnp.log(done[2]) * log2_e
            ready[block, :, lanes] = result.astype(jnp.bfloat16)
    for step, out in enumerate(outs, AHEAD):
        out[...] = ready[own ^ step]


def repeated(field):
    return jnp.concatenate([field] * FAN, axis=0)


def finish_blocks(fine, coarse, steps):
    own = lax.axis_index("head")
    features = fine.shape[2]
    for step, out in steps:
        block = own ^ step
        here = pl.ds(pl.multiple_of(block * BLOCK, BLOCK), BLOCK)
        few = pl.ds(pl.multiple_of(block * SLAB, SLAB), SLAB)
        shares = []
        for pair in range(features // PAIR):
            lanes = pl.ds(pair * PAIR, PAIR)
            fine_sum, coarse_sum = fine[1, here, lanes], repeated(coarse[1, few, lanes])
            if step < AHEAD:
                keep = 1.0 / (1.0 + jnp.exp2(coarse_sum - fine_sum))
                ours, theirs = fine[0, here, lanes], repeated(coarse[0, few, lanes])
                out[:, lanes] = (theirs + keep * (ours - theirs)).astype(jnp.bfloat16)
            else:
                ratio = jnp.exp2(-jnp.abs(fine_sum - coarse_sum))
                less = jnp.maximum(ratio / (1.0 + ratio), least_share)
                shares.append(jnp.where(fine_sum <= coarse_sum, less, -less).astype(jnp.bfloat16))
        if step >= AHEAD:
            pick = lax.broadcasted_iota(jnp.int32, (2 * SLAB, features), 1) == HD * (
                lax.broadcasted_iota(jnp.int32, (2 * SLAB, features), 0)
            )
            by_head = lax.dot_general(
                pick.astype(jnp.bfloat16),
                jnp.concatenate(shares, axis=1),
                (((1,), (1,)), ((), ())),
                preferred_element_type=jnp.float32,
            )[:SLAB]
            blank = jnp.zeros((SLAB, features - BLOCK), jnp.float32)
            out[...] = jnp.concatenate(
                [coarse[0, few, :], jnp.concatenate([by_head, blank], axis=1)], axis=0
            ).astype(jnp.bfloat16)


def finish_kernel(
    four_q, fine, four_ref, near_ref, three_a, three_b, fours_a, fours_b, *refs
):
    refs, (coarse, four_hold) = refs[:-2], refs[-2:]
    steps_out = range(2, lax.axis_size("head"))
    far, outs = refs[: -len(steps_out)], refs[-len(steps_out) :]
    pairs = four_q.shape[1] // PAIR
    steps = {}
    for pair in range(pairs):
        lanes = pl.ds(pair * PAIR, PAIR)
        ours, theirs, beyond = [], [], []
        for which in range(2):
            ours.append(
                [four_ref[which, :, lanes], near_ref[which, :, lanes]]
                + [repooled(field[which, :, lanes]) for field in (three_a, three_b)]
            )
            theirs.append([field[which, :, lanes] for field in (fours_a, fours_b)])
            beyond.append([field[which, :, lanes] for field in far])
        steps[pair] = (
            score(
                four_q[:, lanes],
                jnp.concatenate(ours[0] + theirs[0] + beyond[0], axis=0),
                four_hold.at[pair],
            ),
            jnp.concatenate(
                [with_ones(field) for field in ours[1]]
                + [with_ones(field, 2.0) for field in theirs[1]]
                + [with_ones(field) for field in beyond[1]],
                axis=0,
            ),
        )
    for pair in range(pairs):
        lanes = pl.ds(pair * PAIR, PAIR)
        top, numer, rowsum = weigh(four_hold.at[pair], *steps[pair])
        coarse[0, :, lanes] = numer / rowsum
        coarse[1, :, lanes] = top + jnp.log(rowsum) * log2_e
    finish_blocks(fine, coarse, zip(steps_out, outs))


def rest_kernel(fine, coarse, *outs):
    finish_blocks(fine, coarse, enumerate(outs))


def rejoin_kernel(further_ref, *refs):
    outs = refs[len(refs) // 3 * 2 :]
    for early, late_ref, out in zip(refs, refs[len(outs) :], outs):
        features = early.shape[1]
        late = late_ref[...].astype(jnp.float32)
        spread = lax.broadcasted_iota(jnp.int32, (SLAB, features), 1) // HD == (
            lax.broadcasted_iota(jnp.int32, (SLAB, features), 0)
        )
        signed = lax.dot_general(
            late[SLAB:, :BLOCK].astype(jnp.bfloat16),
            spread.astype(jnp.bfloat16),
            (((0,), (0,)), ((), ())),
            preferred_element_type=jnp.float32,
        )
        keep = jnp.where(signed >= 0, signed, 1.0 + signed)
        join = jnp.where(signed >= 0, 1.0 - signed, -signed)
        result = keep * early[...] + join * repeated(late[:SLAB])
        out[...] = result.astype(jnp.bfloat16)


def widen_kernel(*refs):
    half = len(refs) // 2
    for ref, out in zip(refs[:half], refs[half:]):
        out[...] = ref[...].astype(jnp.float32)


def partial_kernel(own_ref, weight_ref, out_ref):
    features = own_ref.shape[1]
    start = pl.multiple_of(lax.axis_index("head") * features, features)
    out_ref[...] = jnp.dot(
        own_ref[...], weight_ref[pl.ds(start, features), :], preferred_element_type=jnp.float32
    )


def further_kernel(widened_ref, partial_ref, weight_ref, *refs):
    parts, out_ref = refs[:-1], refs[-1]
    own = lax.axis_index("head")
    total = partial_ref[...]
    for step, part in enumerate(parts, 2):
        features = part.shape[1]
        start = pl.multiple_of((own ^ step) * features, features)
        total += jnp.dot(
            part[...], weight_ref[pl.ds(start, features), :], preferred_element_type=jnp.float32
        )
    out_ref[...] = total


def project_kernel(partial_ref, *refs):
    parts, (weight_ref, out_hbm, scratch, staged, sems) = refs[:-5], refs[-5:]
    own = lax.axis_index("head")
    features = parts[0].shape[1]
    chunk = staged.shape[2]
    copies = []
    for index in range(staged.shape[0]):
        columns = pl.ds(index * chunk, chunk)
        total = partial_ref[:, columns]
        for step, part in zip([*range(AHEAD, AHEAD + len(parts) - 1), 1], parts):
            start = pl.multiple_of((own ^ step) * features, features)
            total += jnp.dot(
                part[...],
                weight_ref[pl.ds(start, features), columns],
                preferred_element_type=jnp.float32,
            )
        for half in range(chunk // PAIR):
            lanes = slice(half * PAIR, (half + 1) * PAIR)
            scratch[index, half] = total[:, lanes]
            for i in range(SLAB):
                staged[index, i * FAN : (i + 1) * FAN, lanes] = scratch[
                    index, half, pl.ds(i, FAN, stride=SLAB), :
                ].astype(jnp.bfloat16)
        copy = pltpu.make_async_copy(staged.at[index], out_hbm.at[:, columns], sems.at[index])
        copy.start()
        copies.append(copy)
    for copy in copies:
        copy.wait()


def repool_outside(field):
    which, rows, lanes = field.shape
    slabs = field.astype(jnp.float32).reshape(which, rows // (2 * SLAB), 2, SLAB, lanes)
    sums = (slabs[:, :, 0] + slabs[:, :, 1]) * root_half
    return sums.reshape(which, rows // 2, lanes).astype(jnp.bfloat16)


def swapped(block, axis, mask):
    return lax.ppermute(block, axis, [(i, i ^ mask) for i in range(lax.axis_size(axis))])


def across(block):
    count, heads = lax.axis_size("seq"), lax.axis_size("head")
    route = []
    for seq in range(count):
        end = seq in (0, count - 1)
        other = seq if end else seq + 1 if seq % 2 else seq - 1
        for head in range(heads):
            route.append((seq * heads + head, other * heads + (head ^ 1 if end else head)))
    return lax.ppermute(block, ("seq", "head"), route)


def per_device(queries, key_vectors, value_vectors, out_weight):
    rows, features = queries.shape[1:]
    key_vectors, value_vectors = [
        pltpu.with_memory_space_constraint(x, pltpu.HBM) for x in (key_vectors, value_vectors)
    ]
    pairs = features // PAIR
    seq_count, head_count = lax.axis_size("seq"), lax.axis_size("head")
    bf16 = lambda *shape: jax.ShapeDtypeStruct(shape, jnp.bfloat16)
    params = pltpu.CompilerParams(vmem_limit_bytes=32 * 1024 * 1024)

    hbm = pl.BlockSpec(memory_space=pltpu.HBM)
    vmem = pl.BlockSpec(memory_space=pltpu.VMEM)
    keys, values, first, one, second, three, four = pl.pallas_call(
        pool_kernel,
        in_specs=[hbm] * 2,
        out_shape=[
            bf16(rows, features),
            bf16(rows, features),
            bf16(2, BLOCK + rows // 4 - BLOCK // 4, features),
            bf16(2, rows // 2, features),
            bf16(2, BLOCK, features),
            bf16(2, rows // 8, features),
            bf16(2, rows // 16, features),
        ],
        scratch_shapes=[
            pltpu.VMEM((2, rows // 4, features), jnp.bfloat16),
            pltpu.VMEM((2, rows // BLOCK, pairs, BLOCK, PAIR), jnp.float32),
            pltpu.SemaphoreType.DMA((2, 2)),
        ],
        compiler_params=params,
        name="pool",
    )(key_vectors, value_vectors)
    first_in = swapped(first, "seq", 1)
    second_in = across(second)
    four_in = swapped(four, "seq", 4)
    six_in = swapped(four, "seq", 6)
    threes_in = [swapped(three, "seq", mask) for mask in (3, 2)]
    edge_q, two_q, three_q, four_q, state = pl.pallas_call(
        local_kernel,
        out_shape=[
            bf16(2, BLOCK, features),
            bf16(rows // 4, features),
            bf16(rows // 8, features),
            bf16(rows // 16, features),
            jax.ShapeDtypeStruct((3, rows, features), jnp.float32),
        ],
        scratch_shapes=[
            pltpu.VMEM((pairs, rows, PAIR), jnp.float32),
            pltpu.VMEM((pairs, rows // BLOCK, 2 * BLOCK, 3 * BLOCK), jnp.float32),
            pltpu.VMEM((pairs, rows // BLOCK // 2, 2 * BLOCK, BLOCK), jnp.float32),
        ],
        compiler_params=params,
        name="local",
    )(queries[0], keys, values, one, four_in)

    fours = pl.pallas_call(
        join_kernel,
        out_shape=bf16(2, rows // 8, features),
        compiler_params=params,
        cost_estimate=pl.CostEstimate(flops=2**29, bytes_accessed=2**20, transcendentals=0),
        name="join",
    )(four_in, six_in, four_q)
    fours_in = swapped(fours, "seq", 1)
    coarse, near = pl.pallas_call(
        coarse_kernel,
        out_shape=[
            jax.ShapeDtypeStruct((3, rows // 4, features), jnp.float32),
            bf16(2, rows // 16, features),
        ],
        scratch_shapes=[
            pltpu.VMEM((2, pairs, BLOCK, PAIR), jnp.float32),
            pltpu.VMEM((2, rows // 4, features), jnp.bfloat16),
            pltpu.VMEM((pairs, rows // 2, BLOCK), jnp.float32),
            pltpu.VMEM((pairs, rows // 4, BLOCK), jnp.float32),
        ],
        compiler_params=params,
        cost_estimate=pl.CostEstimate(flops=2**31, bytes_accessed=2**21, transcendentals=0),
        name="coarse",
    )(two_q, three_q, first_in, *threes_in)
    away = range(AHEAD, head_count)
    fine, *early = pl.pallas_call(
        mid_kernel,
        out_shape=[jax.ShapeDtypeStruct((2, rows, features), jnp.float32)]
        + [bf16(BLOCK, features) for _ in away],
        scratch_shapes=[
            pltpu.VMEM((rows // BLOCK, BLOCK, features), jnp.bfloat16),
            pltpu.VMEM((pairs, 2, 2 * BLOCK, BLOCK), jnp.float32),
        ],
        compiler_params=params,
        name="mid",
    )(edge_q, coarse, state, first_in, second_in)
    early_in = [swapped(part, "head", step) for step, part in zip(away, early)]

    far = []
    known = 8
    if known < seq_count:
        group = [four, near] + [repool_outside(field) for field in threes_in]
        group = jnp.concatenate(group + [fours, fours_in], axis=1)
        while known < seq_count:
            fresh = swapped(group, "seq", known)
            far.append(fresh)
            group = jnp.concatenate([group, fresh], axis=1)
            known *= 2

    parts = [bf16(BLOCK, features) for _ in range(AHEAD)]
    *outs, level_four = pl.pallas_call(
        finish_kernel,
        out_shape=parts[2:]
        + [bf16(2 * SLAB, features) for _ in away]
        + [jax.ShapeDtypeStruct((2, rows // 16, features), jnp.float32)],
        scratch_shapes=[pltpu.VMEM((pairs, rows // 8, rows // 16 * seq_count), jnp.float32)],
        compiler_params=params,
        name="finish",
    )(four_q, fine, four, near, *threes_in, fours, fours_in, *far)
    whole_in = [swapped(part, "head", step) for step, part in zip(range(2, AHEAD), outs)]
    late_in = [swapped(part, "head", step) for step, part in zip(away, outs[AHEAD - 2 :])]
    own_part, next_part = pl.pallas_call(
        rest_kernel,
        out_shape=parts[:2],
        compiler_params=params,
        name="rest",
    )(fine, level_four)
    next_in = swapped(next_part, "head", 1)
    width = out_weight.shape[1]
    partial = pl.pallas_call(
        partial_kernel,
        out_shape=jax.ShapeDtypeStruct((BLOCK, width), jnp.float32),
        compiler_params=params,
        name="partial",
    )(own_part, out_weight)
    heavy = pl.CostEstimate(flops=2**32, bytes_accessed=2**20, transcendentals=0)
    widened = pl.pallas_call(
        widen_kernel,
        out_shape=[jax.ShapeDtypeStruct((BLOCK, features), jnp.float32) for _ in away],
        compiler_params=params,
        cost_estimate=pl.CostEstimate(flops=2**22, bytes_accessed=2**10, transcendentals=0),
        name="widen",
    )(*early_in)
    further = pl.pallas_call(
        further_kernel,
        out_shape=jax.ShapeDtypeStruct((BLOCK, width), jnp.float32),
        compiler_params=params,
        name="further",
    )(widened[0], partial, out_weight, *whole_in)
    rejoined = pl.pallas_call(
        rejoin_kernel,
        out_shape=[bf16(BLOCK, features) for _ in away],
        compiler_params=params,
        cost_estimate=heavy,
        name="rejoin",
    )(further, *widened, *late_in)
    chunk = 2 * PAIR
    result = pl.pallas_call(
        project_kernel,
        in_specs=[vmem] * (len(rejoined) + 3),
        out_specs=hbm,
        out_shape=bf16(BLOCK, width),
        scratch_shapes=[
            pltpu.VMEM((width // chunk, 2, BLOCK, PAIR), jnp.float32),
            pltpu.VMEM((width // chunk, BLOCK, chunk), jnp.bfloat16),
            pltpu.SemaphoreType.DMA((width // chunk,)),
        ],
        compiler_params=params,
        name="project",
    )(further, *rejoined, next_in, out_weight)
    return result[None]


def solution(mesh):
    return jax.shard_map(
        per_device,
        mesh=mesh,
        in_specs=(P(None, "seq", "head"), P(None, "seq", "head"), P(None, "seq", "head"), P()),
        out_specs=P(None, ("seq", "head"), None),
        check_vma=False,
    )
```
